32 devices in a mesh: fsdp: 8 (over y, x, core), tp: 4 (over z).
Axes of the slice: x: 2, y: 2, z: 4, core: 2. Of those that a mesh axis runs over, the one named last changes fastest.
Arguments:
- hidden_in: bfloat16 [4096, 2048], P(('fsdp', 'tp')), may hold values from -6 to 6
- out_grad: bfloat16 [4096, 2048], P(('fsdp', 'tp')), may hold values from -6 to 6
- segment_ids: int32 [8, 512], P('fsdp'), may hold values from 0 to 3, never falling along the last dimension, each value on 1 to 256 neighbouring positions
- expert_ids: int32 [4096, 4], P('fsdp'), may hold values from 0 to 7, all different within a row; in each aligned block of 512 rows (0 to 511, 512 to 1023, ...) at most 384 rows name the same one
- route_weights: float32 [4096, 4], P('fsdp'), may hold values from 0.05 to 0.6
- attn_gain: float32 [2048], replicated, may hold values from 0.5 to 1.5
- ffn_gain: float32 [2048], replicated, may hold values from 0.5 to 1.5
- qkv_weight: bfloat16 [2048, 3, 16, 128], P('fsdp', None, 'tp'), may hold values from -0.125 to 0.125
- qkv_bias: float32 [3, 16, 128], P(None, 'tp', 'fsdp'), may hold values from -0.6 to 0.6
- out_weight: bfloat16 [2048, 2048], P('tp', 'fsdp'), may hold values from -0.75 to 0.75
- shared_gate_up: bfloat16 [2048, 2, 5632], P('fsdp', None, 'tp'), may hold values from -0.125 to 0.125
- shared_down: bfloat16 [5632, 2048], P('tp', 'fsdp'), may hold values from -0.15625 to 0.15625
- shared_gate_vec: float32 [2048], replicated, may hold values from -0.125 to 0.125
- expert_gate_up: bfloat16 [8, 2048, 2, 1408], P('fsdp', None, None, 'tp'), may hold values from -0.125 to 0.125
- expert_down: bfloat16 [8, 1408, 2048], P('fsdp', 'tp'), may hold values from -0.3125 to 0.3125
Outputs:
- hidden_out: bfloat16 [4096, 2048], P(('fsdp', 'tp'))
- hidden_grad: float32 [4096, 2048], P(('fsdp', 'tp'))
- route_grad: float32 [4096, 4], P(('fsdp', 'tp'))
- attn_gain_grad: float32 [2048], P(('fsdp', 'tp'))
- ffn_gain_grad: float32 [2048], P(('fsdp', 'tp'))
- qkv_weight_grad: float32 [2048, 3, 16, 128], P('fsdp', None, 'tp')
- qkv_bias_grad: float32 [3, 16, 128], P(None, 'tp', 'fsdp')
- out_weight_grad: float32 [2048, 2048], P('tp', 'fsdp')
- shared_gate_up_grad: float32 [2048, 2, 5632], P('fsdp', None, 'tp')
- shared_down_grad: float32 [5632, 2048], P('tp', 'fsdp')
- shared_gate_vec_grad: float32 [2048], P(('fsdp', 'tp'))
- expert_gate_up_grad: float32 [8, 2048, 2, 1408], P('fsdp', None, None, 'tp')
- expert_down_grad: float32 [8, 1408, 2048], P('fsdp', 'tp')
The draws below stay inside these ranges and needn't reach their ends.
Inputs may be any that keep to these rules, and one draw needn't show every extreme that they name: `segment_ids`: within each pack the numbers never fall; each document holds 1 to 256 positions. `expert_ids`: each row names 4 different experts; among the 512 rows of one pack no expert is named by more than 384 rows, and in every draw some pack names some expert exactly 384 times.
All inputs are finite; a program needn't handle non-finite values.
Results may differ from the reference program's by a relative error of at most 0.033.
Values may be sent and summed in bfloat16 or wider, within the bound.
A program may use at most 320 MiB of HBM per device.

```python
import math
from functools import partial
import jax
import jax.numpy as jnp
import numpy as np
from jax import lax

D = 2048
H = 16
HD = 128
FFS = 5632
FFE = 1408
TOP = 4
LEN = 512
DOCS = 4
EXPERTS = 8
PACKS = 8
TOKENS = 4096
CAP = 384
N_FSDP = 8
N_TP = 4


def steps_of(key, extent, pieces, smallest, high):
    factor_of = 1.0
    for position, blocks in pieces:
        draws = jax.random.uniform(jax.random.fold_in(jax.random.fold_in(key, 6), position), (blocks,), jnp.float32, smallest / len(pieces), high / len(pieces))
        factor_of = factor_of * jnp.repeat(jnp.exp(draws), extent[position] // blocks).reshape((-1,) + (1,) * (len(extent) - 1 - position))
    return factor_of


def split_up(number_of, total, reach, slope):
    portions = [(1 << 20) // math.isqrt(grade ** slope) + 1 for grade in range(2, number_of + 1)]
    spare, holding = total - reach - (number_of - 1), [1] * (number_of - 1)
    while spare > 0:
        movable = [i for i in range(number_of - 1) if holding[i] < reach]
        whole, budget = sum([portions[i] for i in movable]), spare
        for i in movable:
            extra = min(reach - holding[i], max(1, budget * portions[i] // whole), spare)
            holding[i] = holding[i] + extra
            spare = spare - extra
    return np.array([reach] + holding)


def uneven(key, amount, total, reach, lean):
    if amount == 2:
        one = jax.random.randint(key, (), max(1, total - reach), min(reach, total - 1) + 1)
        return jnp.stack([one, total - one])
    sizes = jnp.asarray(split_up(amount, total, reach, lean), jnp.int32)
    twos = (amount - 1) // 2
    source_of, sink = sizes[1:1 + 2 * twos:2], sizes[2:2 + 2 * twos:2]
    room = jnp.minimum(source_of - 1, reach - sink)
    moved = jax.random.randint(jax.random.fold_in(key, 1), (twos,), 0, 1 << 20) % (room + 1)
    sizes = sizes.at[1:1 + 2 * twos:2].set(source_of - moved).at[2:2 + 2 * twos:2].set(sink + moved)
    return sizes[jax.random.permutation(jax.random.fold_in(key, 2), amount)]


def routed_block(key, own, number, rows, number_of, top, bound, slope):
    sequence = jax.random.permutation(key, number_of)
    packed, usual = load_shares(number_of, rows * top, bound, slope, True), load_shares(number_of, rows * top, bound, slope, False)
    places = jnp.arange(number_of)

    def named(lengths, offset_by):
        used = int((lengths > 0).sum())
        fixed = max(1, used // 4)
        moved = fixed + (places - fixed + offset_by * (used - fixed)) % max(1, number_of - fixed)
        return jnp.zeros((number_of,), jnp.int32).at[sequence[jnp.where(places < fixed, places, moved)]].set(jnp.asarray(lengths, jnp.int32))

    lengths = jnp.where(number % 4 == 0, named(packed, number // 4), named(usual, number - number // 4 - 1))
    mixed = jax.random.permutation(jax.random.fold_in(own, 3), number_of)
    donor, sink = mixed[0:number_of // 2 * 2:2], mixed[1:number_of // 2 * 2:2]
    room = jnp.minimum(lengths[donor] - 1, bound - lengths[sink]) // 2
    room = jnp.where((donor == sequence[0]) | (sink == sequence[0]) | (lengths[sink] == 0), 0, jnp.maximum(room, 0))
    moved = jax.random.randint(jax.random.fold_in(own, 4), (number_of // 2,), 0, 1 << 20) % (room + 1)
    lengths = lengths.at[donor].add(-moved).at[sink].add(moved)
    members = jnp.searchsorted(jnp.cumsum(lengths), jnp.arange(rows * top), side="right").astype(jnp.int32)
    grid = members.reshape(top, rows).T
    grid = grid[jax.random.permutation(jax.random.fold_in(own, 1), rows)]
    offset_by = jax.random.randint(jax.random.fold_in(own, 2), (rows, 1), 0, top)
    return jnp.take_along_axis(grid, (jnp.arange(top)[None, :] + offset_by) % top, axis=1)


def load_shares(count, total, bound, skew, full):
    loads = [(1 << 20) // math.isqrt(standing ** skew) + 1 for standing in range(1, count + 1)]
    largest = bound if full else min(bound, max(-(-total // count), total * loads[0] // sum(loads)))
    least = 1 if total - largest >= count - 1 else 0
    given, surplus = [largest] + [least] * (count - 1), total - largest - least * (count - 1)
    while surplus > 0:
        candidates = [i for i in range(1, count) if given[i] < largest] or [i for i in range(1, count) if given[i] < bound]
        whole, budget = sum([loads[i] for i in candidates]), surplus
        for i in candidates:
            extra = min(bound - given[i], max(1, budget * loads[i] // whole), surplus)
            given[i] = given[i] + extra
            surplus = surplus - extra
    return np.array(given)


def gaussian(key, extent, width, reach, pieces=(), kind=jnp.bfloat16):
    result = width * jax.random.normal(key, extent, jnp.float32)
    if pieces:
        result = result * steps_of(key, extent, pieces, -0.22, 0.18)
    return jnp.clip(result, -reach, reach).astype(kind)


def setup_inputs(seed: int = 0) -> dict:
    streams_of = jax.random.split(jax.random.key(seed), 16)
    hidden_in = gaussian(streams_of[0], (TOKENS, D), 1.0, 6.0, ((0, 32),))
    out_grad = gaussian(streams_of[1], (TOKENS, D), 1.0, 6.0, ((0, 32),))
    segment_ids = jax.vmap(lambda own: jnp.searchsorted(jnp.cumsum(uneven(own, DOCS, LEN, LEN // 2, 1)), jnp.arange(LEN), side="right"))(jax.random.split(streams_of[2], PACKS)).reshape((PACKS, LEN)).astype(jnp.int32)
    expert_ids_keys = jax.random.split(jax.random.fold_in(streams_of[3], 1), TOKENS // LEN)
    expert_ids_turns = jax.random.permutation(jax.random.fold_in(streams_of[3], 3), TOKENS // LEN)
    expert_ids = jax.vmap(lambda own, number: routed_block(jax.random.fold_in(streams_of[3], 2), own, number, LEN, EXPERTS, TOP, CAP, 1))(expert_ids_keys, expert_ids_turns).reshape((TOKENS, TOP))
    route_weights = jnp.clip(0.05 + 0.55 * jax.random.uniform(streams_of[4], (TOKENS, TOP), jnp.float32) ** steps_of(streams_of[4], (TOKENS, TOP), ((0, 8),), -0.2, 0.2), 0.05, 0.6)
    attn_gain = jnp.clip(1.0 + 0.1 * jax.random.normal(streams_of[5], (D,), jnp.float32), 0.5, 1.5)
    ffn_gain = jnp.clip(1.0 + 0.1 * jax.random.normal(streams_of[6], (D,), jnp.float32), 0.5, 1.5)
    qkv_weight = gaussian(streams_of[7], (D, 3, H, HD), D ** -0.5, 0.125, ((0, 8), (2, 4)))
    qkv_bias = gaussian(streams_of[8], (3, H, HD), 0.1, 0.6, ((1, 4), (2, 8)), jnp.float32)
    out_weight = gaussian(streams_of[9], (D, D), (D // 32) ** -0.5, 0.75, ((0, 4), (1, 8)))
    shared_gate_up = gaussian(streams_of[10], (D, 2, FFS), D ** -0.5, 0.125, ((0, 8), (2, 4)))
    shared_down = gaussian(streams_of[11], (FFS, D), (FFS // 4) ** -0.5, 0.15625, ((0, 4), (1, 8)))
    shared_gate_vec = gaussian(streams_of[12], (D,), D ** -0.5, 0.125, (), jnp.float32)
    expert_gate_up = gaussian(streams_of[13], (EXPERTS, D, 2, FFE), D ** -0.5, 0.125, ((0, 8), (3, 4)))
    expert_down = gaussian(streams_of[14], (EXPERTS, FFE, D), (FFE // 4) ** -0.5, 0.3125, ((0, 8), (1, 4)))
    return dict(hidden_in=hidden_in, out_grad=out_grad, segment_ids=segment_ids, expert_ids=expert_ids, route_weights=route_weights, attn_gain=attn_gain, ffn_gain=ffn_gain, qkv_weight=qkv_weight, qkv_bias=qkv_bias, out_weight=out_weight, shared_gate_up=shared_gate_up, shared_down=shared_down, shared_gate_vec=shared_gate_vec, expert_gate_up=expert_gate_up, expert_down=expert_down)


epsilon = 1e-06

def rounded(tensor):
    return lax.optimization_barrier(tensor.astype(jnp.bfloat16)).astype(jnp.float32)

def rope_tables(length, head_dim):
    half_dim = head_dim // 2
    ratios = jnp.arange(half_dim, dtype=jnp.float32) * (2.0 / head_dim)
    frequency = jnp.exp(-jnp.log(10000.0) * ratios)
    angles = jnp.arange(length, dtype=jnp.float32)[:, None] * frequency[None, :]
    return (jnp.cos(angles)[:, None, :], jnp.sin(angles)[:, None, :])

def rotate(tensor, cos_table, sin_table):
    half_dim = tensor.shape[-1] // 2
    front_half = tensor[..., :half_dim]
    back_half = tensor[..., half_dim:]
    return jnp.concatenate([front_half * cos_table - back_half * sin_table, back_half * cos_table + front_half * sin_table], axis=-1)

def unrotate(tensor, cos_table, sin_table):
    half_dim = tensor.shape[-1] // 2
    front_half = tensor[..., :half_dim]
    back_half = tensor[..., half_dim:]
    return jnp.concatenate([front_half * cos_table + back_half * sin_table, back_half * cos_table - front_half * sin_table], axis=-1)

def silu_parts(gate_in):
    sigmoid_value = jax.nn.sigmoid(gate_in)
    return (gate_in * sigmoid_value, sigmoid_value * (1.0 + gate_in * (1.0 - sigmoid_value)))

def slot_table(route_ids, experts, capacity):
    flat_ids = route_ids.reshape(-1)
    onehot = (flat_ids[:, None] == jnp.arange(experts, dtype=jnp.int32)[None, :]).astype(jnp.int32)
    before = jnp.cumsum(onehot, axis=0, dtype=jnp.int32) - onehot
    ranks = lax.optimization_barrier(jnp.sum(before * onehot, axis=1, dtype=jnp.int32))
    places = flat_ids * capacity + ranks
    filler = jnp.arange(flat_ids.shape[0], dtype=jnp.int32) + 1
    slot_rows = jnp.zeros((experts * capacity,), jnp.int32).at[places].set(filler)
    return (places.reshape(route_ids.shape), slot_rows.reshape(experts, capacity))

def allowed_pairs(segments):
    positions = jnp.arange(segments.shape[0], dtype=jnp.int32)
    return (positions[:, None] >= positions[None, :]) & (segments[:, None] == segments[None, :])

def inverse_rms(tensor):
    return lax.rsqrt(lax.optimization_barrier(jnp.mean(tensor * tensor, axis=-1, keepdims=True)) + epsilon)

def norm_backward(d_normed, hat_rows, inverse, gain_vec):
    d_hat = d_normed * gain_vec
    return inverse * (d_hat - hat_rows * lax.optimization_barrier(jnp.mean(d_hat * hat_rows, axis=-1, keepdims=True)))

def scores_of(query, keys, segments):
    raw = jnp.einsum('qhd,khd->hqk', query, keys, precision=lax.Precision.HIGHEST) * HD ** (-0.5)
    return jnp.where(allowed_pairs(segments)[None], raw, -1e+30)

def take_rows(rows, index):
    return rows[index]

def gather_sum(table, index):
    return lax.optimization_barrier(jnp.sum(table[index], axis=1))

def expert_forward(inputs):
    rows, gate_up, down = inputs
    quarter = FFE // N_TP
    pre_act = jnp.dot(rows, gate_up.reshape(D, 2 * FFE), preferred_element_type=jnp.float32)
    act_value, act_slope = silu_parts(pre_act[:, :FFE])
    hidden = rounded(act_value * pre_act[:, FFE:])
    parts = jnp.einsum('rjq,jqd->jrd', hidden.reshape(-1, N_TP, quarter), down.reshape(N_TP, quarter, D).astype(jnp.float32), precision=lax.Precision.HIGHEST)
    return lax.optimization_barrier(jnp.sum(rounded(parts), axis=0))

def expert_backward(inputs):
    rows, grads, gate_up, down = inputs
    quarter = FFE // N_TP
    pre_act = jnp.dot(rows, gate_up.reshape(D, 2 * FFE), preferred_element_type=jnp.float32)
    act_value, act_slope = silu_parts(pre_act[:, :FFE])
    upper = pre_act[:, FFE:]
    hidden = (act_value * upper).astype(jnp.bfloat16)
    d_hidden = jnp.dot(grads, down.T, preferred_element_type=jnp.float32)
    d_gate = (d_hidden * upper * act_slope).astype(jnp.bfloat16)
    d_upper = (d_hidden * act_value).astype(jnp.bfloat16)
    g_down = jnp.dot(hidden.T, grads, preferred_element_type=jnp.float32)
    d_cat = jnp.stack([d_gate, d_upper], axis=1)
    g_gate_up = jnp.dot(rows.T, d_cat.reshape(-1, 2 * FFE), preferred_element_type=jnp.float32).reshape(D, 2, FFE)
    parts = jnp.einsum('rsjq,dsjq->jrd', d_cat.reshape(-1, 2, N_TP, quarter).astype(jnp.float32), gate_up.reshape(D, 2, N_TP, quarter).astype(jnp.float32), precision=lax.Precision.HIGHEST)
    return (g_gate_up, g_down, lax.optimization_barrier(jnp.sum(rounded(parts), axis=0)))

def reference(hidden_in, out_grad, segment_ids, expert_ids, route_weights, attn_gain, ffn_gain, qkv_weight, qkv_bias, out_weight, shared_gate_up, shared_down, shared_gate_vec, expert_gate_up, expert_down):
    highest = lax.Precision.HIGHEST
    cos_table, sin_table = rope_tables(LEN, HD)
    pack_rows = hidden_in.reshape(N_FSDP, LEN, D)
    pack_grads = out_grad.reshape(N_FSDP, LEN, D)
    pack_ids = expert_ids.reshape(N_FSDP, LEN, TOP)
    pack_weights = route_weights.reshape(N_FSDP, LEN, TOP)

    def attend_pack(inputs):
        rows, segments = inputs
        row_float = rows.astype(jnp.float32)
        inverse = inverse_rms(row_float)
        normed = (row_float * inverse * attn_gain).astype(jnp.bfloat16)
        qkv = jnp.dot(normed, qkv_weight.reshape(D, 3 * D), preferred_element_type=jnp.float32).reshape(LEN, 3, H, HD) + qkv_bias
        query = rounded(rotate(qkv[:, 0], cos_table, sin_table))
        keys = rounded(rotate(qkv[:, 1], cos_table, sin_table))
        values = rounded(qkv[:, 2])
        scores = scores_of(query, keys, segments)
        row_peak = lax.optimization_barrier(jnp.max(scores, axis=-1, keepdims=True))
        log_total = row_peak + jnp.log(lax.optimization_barrier(jnp.sum(jnp.exp(scores - row_peak), axis=-1, keepdims=True)))
        probs = rounded(jnp.exp(scores - log_total))
        heads_out = jnp.einsum('hqk,khd->qhd', probs, values, precision=highest).astype(jnp.bfloat16).reshape(LEN, D)
        mixed = jnp.dot(heads_out, out_weight, preferred_element_type=jnp.float32)
        return (row_float + mixed, normed, query.astype(jnp.bfloat16), keys.astype(jnp.bfloat16), values.astype(jnp.bfloat16), log_total, heads_out)
    middle, normed_one, queries, keys_all, values_all, log_totals, heads_all = lax.map(attend_pack, (pack_rows, segment_ids))
    ffn_inverse = inverse_rms(middle)
    normed_two = (middle * ffn_inverse * ffn_gain).astype(jnp.bfloat16)
    places, slot_rows = jax.vmap(partial(slot_table, experts=EXPERTS, capacity=CAP))(pack_ids)
    filled = slot_rows > 0
    route_index = jnp.maximum(slot_rows - 1, 0)
    token_index = route_index // TOP
    expert_in = jnp.where(filled[..., None], jax.vmap(take_rows)(normed_two, token_index), jnp.zeros((), jnp.bfloat16))
    expert_in = expert_in.transpose(1, 0, 2, 3).reshape(EXPERTS, N_FSDP * CAP, D)
    expert_out = lax.map(expert_forward, (expert_in, expert_gate_up, expert_down))
    expert_flat = expert_out.reshape(-1, D)
    expert_of = places // CAP
    slot_of = places % CAP
    global_rows = (expert_of * N_FSDP + jnp.arange(N_FSDP, dtype=jnp.int32)[:, None, None]) * CAP + slot_of
    gate_up_flat = shared_gate_up.reshape(D, 2 * FFS)

    def shared_pack(running, inputs):
        normed, mid_rows, grads, rows_index, weights = inputs
        grad_float = grads.astype(jnp.float32)
        normed_float = normed.astype(jnp.float32)
        gate_prob = jax.nn.sigmoid(lax.optimization_barrier(jnp.sum(normed_float * shared_gate_vec, axis=-1)))
        shared_pre = jnp.dot(normed, gate_up_flat, preferred_element_type=jnp.float32)
        shared_act, shared_slope = silu_parts(shared_pre[:, :FFS])
        shared_upper = shared_pre[:, FFS:]
        shared_hidden = (shared_act * shared_upper).astype(jnp.bfloat16)
        shared_out = jnp.dot(shared_hidden, shared_down, preferred_element_type=jnp.float32)
        picked = expert_flat[rows_index]
        moe_out = lax.optimization_barrier(jnp.sum(weights[:, :, None] * picked, axis=1))
        block_out = (mid_rows + gate_prob[:, None] * shared_out + moe_out).astype(jnp.bfloat16)
        route_part = lax.optimization_barrier(jnp.sum(grad_float[:, None, :] * picked, axis=-1))
        gate_grad = lax.optimization_barrier(jnp.sum(grad_float * shared_out, axis=-1))
        logit_grad = gate_grad * gate_prob * (1.0 - gate_prob)
        scaled = (gate_prob[:, None] * grad_float).astype(jnp.bfloat16)
        d_hidden = jnp.dot(scaled, shared_down.T, preferred_element_type=jnp.float32)
        d_cat = jnp.concatenate([(d_hidden * shared_upper * shared_slope).astype(jnp.bfloat16), (d_hidden * shared_act).astype(jnp.bfloat16)], axis=1)
        g_down = jnp.dot(shared_hidden.T, scaled, preferred_element_type=jnp.float32)
        g_gate_up = jnp.dot(normed.T, d_cat, preferred_element_type=jnp.float32)
        d_normed = jnp.dot(d_cat, gate_up_flat.T, preferred_element_type=jnp.float32) + logit_grad[:, None] * shared_gate_vec
        g_vec = lax.optimization_barrier(jnp.sum(normed_float * logit_grad[:, None], axis=0))
        running = (running[0] + g_gate_up, running[1] + g_down, running[2] + g_vec)
        return (running, (block_out, route_part, d_normed))
    start = (jnp.zeros((D, 2 * FFS), jnp.float32), jnp.zeros((FFS, D), jnp.float32), jnp.zeros((D,), jnp.float32))
    shared_sums, (block_out, route_part, d_normed_two) = lax.scan(shared_pack, start, (normed_two, middle, pack_grads, global_rows, pack_weights))
    flat_weights = pack_weights.reshape(N_FSDP, LEN * TOP)
    slot_weights = jnp.where(filled, jax.vmap(take_rows)(flat_weights, route_index), 0.0)
    grad_rows = jax.vmap(take_rows)(pack_grads, token_index).astype(jnp.float32)
    expert_grad_in = (slot_weights[..., None] * grad_rows).astype(jnp.bfloat16)
    expert_grad_in = expert_grad_in.transpose(1, 0, 2, 3).reshape(EXPERTS, N_FSDP * CAP, D)
    g_expert_gate_up, g_expert_down, d_expert_in = lax.map(expert_backward, (expert_in, expert_grad_in, expert_gate_up, expert_down))
    d_expert_flat = d_expert_in.reshape(-1, D)
    moe_back = lax.map(partial(gather_sum, d_expert_flat), global_rows)
    d_normed_two = d_normed_two + moe_back
    hat_two = middle * ffn_inverse
    g_ffn_gain = lax.optimization_barrier(jnp.sum(d_normed_two * hat_two, axis=(0, 1)))
    middle_grad = pack_grads.astype(jnp.float32) + norm_backward(d_normed_two, hat_two, ffn_inverse, ffn_gain)

    def attend_back(running, inputs):
        d_middle, rows, normed, query_b, keys_b, values_b, log_total, heads_out, segments = inputs
        query = query_b.astype(jnp.float32)
        keys = keys_b.astype(jnp.float32)
        values = values_b.astype(jnp.float32)
        d_rows = d_middle.astype(jnp.bfloat16)
        g_out = jnp.dot(heads_out.T, d_rows, preferred_element_type=jnp.float32)
        d_heads = jnp.dot(d_rows, out_weight.T, preferred_element_type=jnp.float32).astype(jnp.bfloat16)
        heads_float = heads_out.reshape(LEN, H, HD).astype(jnp.float32)
        d_heads_float = d_heads.reshape(LEN, H, HD).astype(jnp.float32)
        scores = scores_of(query, keys, segments)
        probs = jnp.exp(scores - log_total)
        probs_b = rounded(probs)
        d_values = jnp.einsum('hqk,qhd->khd', probs_b, d_heads_float, precision=highest)
        d_probs = jnp.einsum('qhd,khd->hqk', d_heads_float, values, precision=highest)
        delta = lax.optimization_barrier(jnp.sum(d_heads_float * heads_float, axis=-1))
        d_scores = rounded(probs * (d_probs - delta.T[:, :, None]))
        d_query = jnp.einsum('hqk,khd->qhd', d_scores, keys, precision=highest) * HD ** (-0.5)
        d_keys = jnp.einsum('hqk,qhd->khd', d_scores, query, precision=highest) * HD ** (-0.5)
        d_qkv = jnp.stack([unrotate(d_query, cos_table, sin_table), unrotate(d_keys, cos_table, sin_table), d_values], axis=1)
        g_bias = lax.optimization_barrier(jnp.sum(d_qkv, axis=0))
        d_qkv_b = d_qkv.astype(jnp.bfloat16).reshape(LEN, 3 * D)
        g_qkv = jnp.dot(normed.T, d_qkv_b, preferred_element_type=jnp.float32)
        d_normed = jnp.dot(d_qkv_b, qkv_weight.reshape(D, 3 * D).T, preferred_element_type=jnp.float32)
        row_float = rows.astype(jnp.float32)
        inverse = inverse_rms(row_float)
        hat_one = row_float * inverse
        g_gain = lax.optimization_barrier(jnp.sum(d_normed * hat_one, axis=0))
        d_input = d_middle + norm_backward(d_normed, hat_one, inverse, attn_gain)
        running = jax.tree.map(jnp.add, running, (g_qkv, g_bias, g_out, g_gain))
        return (running, d_input)
    start = (jnp.zeros((D, 3 * D), jnp.float32), jnp.zeros((3, H, HD), jnp.float32), jnp.zeros((D, D), jnp.float32), jnp.zeros((D,), jnp.float32))
    attn_sums, d_input = lax.scan(attend_back, start, (middle_grad, pack_rows, normed_one, queries, keys_all, values_all, log_totals, heads_all, segment_ids))
    g_qkv, g_bias, g_out, g_attn_gain = attn_sums
    g_gate_up, g_down, g_vec = shared_sums
    return (block_out.reshape(TOKENS, D), d_input.reshape(TOKENS, D), route_part.reshape(TOKENS, TOP), g_attn_gain, g_ffn_gain, g_qkv.reshape(D, 3, H, HD), g_bias, g_out, g_gate_up.reshape(D, 2, FFS), g_down, g_vec, g_expert_gate_up, g_expert_down)
```

```python
import jax
import jax.numpy as jnp
from jax import lax
from jax.sharding import PartitionSpec as P

epsilon = 1e-06


def rope_tables(length, head_dim):
    half_dim = head_dim // 2
    ratios = jnp.arange(half_dim, dtype=jnp.float32) * (2.0 / head_dim)
    frequency = jnp.exp(-jnp.log(10000.0) * ratios)
    angles = jnp.arange(length, dtype=jnp.float32)[:, None] * frequency[None, :]
    return (jnp.cos(angles)[:, None, :], jnp.sin(angles)[:, None, :])


def rotate(tensor, cos_table, sin_table):
    half_dim = tensor.shape[-1] // 2
    front_half = tensor[..., :half_dim]
    back_half = tensor[..., half_dim:]
    return jnp.concatenate(
        [
            front_half * cos_table - back_half * sin_table,
            back_half * cos_table + front_half * sin_table,
        ],
        axis=-1,
    )


def unrotate(tensor, cos_table, sin_table):
    half_dim = tensor.shape[-1] // 2
    front_half = tensor[..., :half_dim]
    back_half = tensor[..., half_dim:]
    return jnp.concatenate(
        [
            front_half * cos_table + back_half * sin_table,
            back_half * cos_table - front_half * sin_table,
        ],
        axis=-1,
    )


def silu_parts(gate_in):
    sigmoid_value = jax.nn.sigmoid(gate_in)
    return (gate_in * sigmoid_value, sigmoid_value * (1.0 + gate_in * (1.0 - sigmoid_value)))


def slot_table(route_ids, experts, capacity):
    flat_ids = route_ids.reshape(-1)
    onehot = (flat_ids[:, None] == jnp.arange(experts, dtype=jnp.int32)[None, :]).astype(jnp.int32)
    before = jnp.cumsum(onehot, axis=0, dtype=jnp.int32) - onehot
    ranks = jnp.sum(before * onehot, axis=1, dtype=jnp.int32)
    places = flat_ids * capacity + ranks
    filler = jnp.arange(flat_ids.shape[0], dtype=jnp.int32) + 1
    slot_rows = jnp.zeros((experts * capacity,), jnp.int32).at[places].set(filler)
    return (places.reshape(route_ids.shape), slot_rows.reshape(experts, capacity))


def inverse_rms(tensor):
    return lax.rsqrt(jnp.mean(tensor * tensor, axis=-1, keepdims=True) + epsilon)


def norm_backward(d_normed, hat_rows, inverse, gain_vec):
    d_hat = d_normed * gain_vec
    return inverse * (d_hat - hat_rows * jnp.mean(d_hat * hat_rows, axis=-1, keepdims=True))


def masked_scores(query, keys, allowed, score_scale):
    raw = jnp.einsum("qhd,khd->hqk", query, keys, preferred_element_type=jnp.float32) * score_scale
    return jnp.where(allowed[None], raw, -1e30)


def spread(rows):
    return lax.all_gather(rows, "tp", axis=0, tiled=True)


def head_total(partial_rows):
    return lax.psum_scatter(
        partial_rows.astype(jnp.bfloat16), "tp", scatter_dimension=0, tiled=True
    ).astype(jnp.float32)


def to_experts(buffer):
    return lax.all_to_all(buffer, "fsdp", split_axis=0, concat_axis=0, tiled=True)


def from_experts(buffer):
    return lax.all_to_all(buffer, "fsdp", split_axis=0, concat_axis=0, tiled=True)


def routed_plan(
    hidden_in,
    out_grad,
    segment_ids,
    expert_ids,
    route_weights,
    attn_gain,
    ffn_gain,
    qkv_weight,
    qkv_bias,
    out_weight,
    shared_gate_up,
    shared_down,
    shared_gate_vec,
    expert_gate_up,
    expert_down,
):
    tp_rank = lax.axis_index("tp")
    experts = lax.axis_size("fsdp")
    length = segment_ids.shape[1]
    top_count = expert_ids.shape[1]
    capacity = 3 * length * top_count // (2 * experts)
    own_rows = hidden_in.shape[0]
    model_width = hidden_in.shape[1]
    qkv_full, bias_full, out_full, shared_full, shared_down_full = (
        lax.all_gather(qkv_weight, "fsdp", axis=0, tiled=True),
        lax.all_gather(qkv_bias.astype(jnp.bfloat16), "fsdp", axis=2, tiled=True).astype(
            qkv_bias.dtype
        ),
        lax.all_gather(out_weight, "fsdp", axis=1, tiled=True),
        lax.all_gather(shared_gate_up, "fsdp", axis=0, tiled=True),
        lax.all_gather(shared_down, "fsdp", axis=1, tiled=True),
    )
    local_heads = qkv_full.shape[2]
    head_dim = qkv_full.shape[3]
    score_scale = head_dim ** (-0.5)
    cos_table, sin_table = rope_tables(length, head_dim)
    positions = jnp.arange(length, dtype=jnp.int32)
    segments = segment_ids[0]
    allowed = (positions[:, None] >= positions[None, :]) & (segments[:, None] == segments[None, :])
    hidden_float = hidden_in.astype(jnp.float32)
    attn_inverse = inverse_rms(hidden_float)
    normed_one = spread((hidden_float * attn_inverse * attn_gain).astype(jnp.bfloat16))
    qkv_flat = qkv_full.reshape(model_width, -1)
    qkv = (
        jnp.dot(normed_one, qkv_flat, preferred_element_type=jnp.float32).reshape(
            length, 3, local_heads, head_dim
        )
        + bias_full
    )
    query = rotate(qkv[:, 0], cos_table, sin_table).astype(jnp.bfloat16)
    keys = rotate(qkv[:, 1], cos_table, sin_table).astype(jnp.bfloat16)
    values = qkv[:, 2].astype(jnp.bfloat16)
    scores = masked_scores(query, keys, allowed, score_scale)
    row_peak = jnp.max(scores, axis=-1, keepdims=True)
    log_total = row_peak + jnp.log(jnp.sum(jnp.exp(scores - row_peak), axis=-1, keepdims=True))
    probs_b = jnp.exp(scores - log_total).astype(jnp.bfloat16)
    heads_out = (
        jnp.einsum("hqk,khd->qhd", probs_b, values, preferred_element_type=jnp.float32)
        .astype(jnp.bfloat16)
        .reshape(length, -1)
    )
    middle = hidden_float + head_total(
        jnp.dot(heads_out, out_full, preferred_element_type=jnp.float32)
    )
    ffn_inverse = inverse_rms(middle)
    normed_two_own = (middle * ffn_inverse * ffn_gain).astype(jnp.bfloat16)
    normed_two = spread(normed_two_own)
    gate_prob = jax.nn.sigmoid(jnp.sum(normed_two.astype(jnp.float32) * shared_gate_vec, axis=-1))
    shared_flat = shared_full.reshape(model_width, -1)
    shared_width = shared_full.shape[2]
    shared_pre = jnp.dot(normed_two, shared_flat, preferred_element_type=jnp.float32)
    shared_act, shared_slope = silu_parts(shared_pre[:, :shared_width])
    shared_upper = shared_pre[:, shared_width:]
    shared_hidden = (shared_act * shared_upper).astype(jnp.bfloat16)
    shared_part = jnp.dot(shared_hidden, shared_down_full, preferred_element_type=jnp.float32)
    places, slot_rows = slot_table(expert_ids, experts, capacity)
    filled = slot_rows > 0
    route_index = jnp.maximum(slot_rows - 1, 0)
    source_rows = route_index // top_count
    flat_weights = route_weights.reshape(-1)
    slot_weights = jnp.where(filled, flat_weights[route_index], 0.0)
    send_rows = jnp.where(filled[:, :, None], normed_two[source_rows], jnp.zeros((), jnp.bfloat16))
    arrived = to_experts(send_rows).reshape(-1, model_width)
    expert_flat = expert_gate_up[0].reshape(model_width, -1)
    expert_width = expert_gate_up.shape[3]
    down_local = expert_down[0]
    expert_pre = jnp.dot(arrived, expert_flat, preferred_element_type=jnp.float32)
    expert_act, expert_slope = silu_parts(expert_pre[:, :expert_width])
    expert_upper = expert_pre[:, expert_width:]
    expert_hidden = (expert_act * expert_upper).astype(jnp.bfloat16)
    expert_part = jnp.dot(expert_hidden, down_local, preferred_element_type=jnp.float32).astype(
        jnp.bfloat16
    )
    returned = from_experts(expert_part.reshape(experts, capacity, model_width)).reshape(
        experts * capacity, model_width
    )
    picked = returned[places].astype(jnp.float32)
    token_term = gate_prob[:, None] * shared_part + jnp.sum(
        route_weights[:, :, None] * picked, axis=1
    )
    own_extra = 0.0
    total = (
        lax.psum_scatter(
            token_term.astype(jnp.bfloat16), "tp", scatter_dimension=0, tiled=True
        ).astype(jnp.float32)
        + own_extra
    )
    hidden_out = (middle + total).astype(jnp.bfloat16)
    grad_rows = spread(out_grad)
    grad_float = grad_rows.astype(jnp.float32)
    gate_part = jnp.sum(grad_float * shared_part, axis=-1)
    scaled_grad = (gate_prob[:, None] * grad_float).astype(jnp.bfloat16)
    shared_d_hidden = jnp.dot(scaled_grad, shared_down_full.T, preferred_element_type=jnp.float32)
    shared_d_cat = jnp.concatenate(
        [
            (shared_d_hidden * shared_upper * shared_slope).astype(jnp.bfloat16),
            (shared_d_hidden * shared_act).astype(jnp.bfloat16),
        ],
        axis=1,
    )
    g_shared_down = jnp.dot(shared_hidden.T, scaled_grad, preferred_element_type=jnp.float32)
    g_shared_gate_up = jnp.dot(
        normed_two.T, shared_d_cat, preferred_element_type=jnp.float32
    ).reshape(shared_full.shape)
    d_normed_part = jnp.dot(shared_d_cat, shared_flat.T, preferred_element_type=jnp.float32)
    expert_grad_in = (slot_weights[:, :, None] * grad_float[source_rows]).astype(jnp.bfloat16)
    arrived_grad = to_experts(expert_grad_in).reshape(-1, model_width)
    back_act, back_slope, back_upper, back_hidden = (
        expert_act,
        expert_slope,
        expert_upper,
        expert_hidden,
    )
    expert_d_hidden = jnp.dot(arrived_grad, down_local.T, preferred_element_type=jnp.float32)
    expert_d_cat = jnp.concatenate(
        [
            (expert_d_hidden * back_upper * back_slope).astype(jnp.bfloat16),
            (expert_d_hidden * back_act).astype(jnp.bfloat16),
        ],
        axis=1,
    )
    g_expert_down = jnp.dot(back_hidden.T, arrived_grad, preferred_element_type=jnp.float32)[None]
    g_expert_gate_up = jnp.dot(arrived.T, expert_d_cat, preferred_element_type=jnp.float32).reshape(
        expert_gate_up.shape
    )
    expert_d_part = jnp.dot(expert_d_cat, expert_flat.T, preferred_element_type=jnp.float32).astype(
        jnp.bfloat16
    )
    route_part = jnp.sum(grad_float[:, None, :] * picked, axis=-1)
    returned_grad = from_experts(expert_d_part.reshape(experts, capacity, model_width)).reshape(
        experts * capacity, model_width
    )
    d_normed_part = d_normed_part + jnp.sum(returned_grad[places].astype(jnp.float32), axis=1)
    d_normed_two, route_grad, gate_grad = (
        lax.psum_scatter(
            d_normed_part.astype(jnp.bfloat16), "tp", scatter_dimension=0, tiled=True
        ).astype(jnp.float32),
        lax.psum_scatter(
            route_part.astype(jnp.bfloat16), "tp", scatter_dimension=0, tiled=True
        ).astype(jnp.float32),
        lax.psum_scatter(
            gate_part.astype(jnp.bfloat16), "tp", scatter_dimension=0, tiled=True
        ).astype(jnp.float32),
    )
    own_gate = lax.dynamic_slice_in_dim(gate_prob, tp_rank * own_rows, own_rows)
    logit_grad = gate_grad * own_gate * (1.0 - own_gate)
    d_normed_two = d_normed_two + logit_grad[:, None] * shared_gate_vec
    g_gate_vec = jnp.sum(normed_two_own.astype(jnp.float32) * logit_grad[:, None], axis=0)
    hat_two = middle * ffn_inverse
    g_ffn_gain = jnp.sum(d_normed_two * hat_two, axis=0)
    middle_grad = out_grad.astype(jnp.float32) + norm_backward(
        d_normed_two, hat_two, ffn_inverse, ffn_gain
    )
    d_rows = spread(middle_grad.astype(jnp.bfloat16))
    g_out = jnp.dot(heads_out.T, d_rows, preferred_element_type=jnp.float32)
    d_heads = (
        jnp.dot(d_rows, out_full.T, preferred_element_type=jnp.float32)
        .astype(jnp.bfloat16)
        .reshape(length, local_heads, head_dim)
    )
    heads_three = heads_out.reshape(length, local_heads, head_dim)
    scores_again = masked_scores(query, keys, allowed, score_scale)
    probs_full = jnp.exp(scores_again - log_total)
    probs_again = probs_full.astype(jnp.bfloat16)
    d_values = jnp.einsum("hqk,qhd->khd", probs_again, d_heads, preferred_element_type=jnp.float32)
    d_probs = jnp.einsum("qhd,khd->hqk", d_heads, values, preferred_element_type=jnp.float32)
    delta = jnp.sum(d_heads.astype(jnp.float32) * heads_three.astype(jnp.float32), axis=-1)
    d_scores = (probs_full * (d_probs - delta.T[:, :, None])).astype(jnp.bfloat16)
    d_query = (
        jnp.einsum("hqk,khd->qhd", d_scores, keys, preferred_element_type=jnp.float32) * score_scale
    )
    d_keys = (
        jnp.einsum("hqk,qhd->khd", d_scores, query, preferred_element_type=jnp.float32)
        * score_scale
    )
    d_qkv = jnp.stack(
        [unrotate(d_query, cos_table, sin_table), unrotate(d_keys, cos_table, sin_table), d_values],
        axis=1,
    )
    g_bias = jnp.sum(d_qkv, axis=0)
    d_qkv_b = d_qkv.astype(jnp.bfloat16).reshape(length, -1)
    g_qkv = jnp.dot(normed_one.T, d_qkv_b, preferred_element_type=jnp.float32).reshape(
        qkv_full.shape
    )
    d_normed_one = head_total(jnp.dot(d_qkv_b, qkv_flat.T, preferred_element_type=jnp.float32))
    hat_one = hidden_float * attn_inverse
    g_attn_gain = jnp.sum(d_normed_one * hat_one, axis=0)
    hidden_grad = middle_grad + norm_backward(d_normed_one, hat_one, attn_inverse, attn_gain)
    g_qkv, g_bias, g_out, g_shared_gate_up, g_shared_down = (
        lax.psum_scatter(
            g_qkv.astype(jnp.bfloat16), "fsdp", scatter_dimension=0, tiled=True
        ).astype(jnp.float32),
        lax.psum_scatter(
            g_bias.astype(jnp.bfloat16), "fsdp", scatter_dimension=2, tiled=True
        ).astype(jnp.float32),
        lax.psum_scatter(
            g_out.astype(jnp.bfloat16), "fsdp", scatter_dimension=1, tiled=True
        ).astype(jnp.float32),
        lax.psum_scatter(
            g_shared_gate_up.astype(jnp.bfloat16), "fsdp", scatter_dimension=0, tiled=True
        ).astype(jnp.float32),
        lax.psum_scatter(
            g_shared_down.astype(jnp.bfloat16), "fsdp", scatter_dimension=1, tiled=True
        ).astype(jnp.float32),
    )
    g_attn_gain, g_ffn_gain, g_gate_vec = (
        lax.psum_scatter(g_attn_gain, ("fsdp", "tp"), scatter_dimension=0, tiled=True),
        lax.psum_scatter(g_ffn_gain, ("fsdp", "tp"), scatter_dimension=0, tiled=True),
        lax.psum_scatter(g_gate_vec, ("fsdp", "tp"), scatter_dimension=0, tiled=True),
    )
    return (
        hidden_out,
        hidden_grad,
        route_grad,
        g_attn_gain,
        g_ffn_gain,
        g_qkv,
        g_bias,
        g_out,
        g_shared_gate_up,
        g_shared_down,
        g_gate_vec,
        g_expert_gate_up,
        g_expert_down,
    )


def dense_plan(
    hidden_in,
    out_grad,
    segment_ids,
    expert_ids,
    route_weights,
    attn_gain,
    ffn_gain,
    qkv_weight,
    qkv_bias,
    out_weight,
    shared_gate_up,
    shared_down,
    shared_gate_vec,
    expert_gate_up,
    expert_down,
):
    every = ("fsdp", "tp")
    tp_rank = lax.axis_index("tp")
    experts = lax.axis_size("fsdp")
    packs = experts
    length = segment_ids.shape[1]
    own_rows = hidden_in.shape[0]
    model_width = hidden_in.shape[1]
    bf16 = jnp.bfloat16
    f32 = jnp.float32

    grad_all = lax.all_gather(out_grad, every, axis=0, tiled=True)
    qkv_full = lax.all_gather(qkv_weight, "fsdp", axis=0, tiled=True)
    bias_full = lax.all_gather(qkv_bias.astype(bf16), "fsdp", axis=2, tiled=True).astype(f32)
    out_full = lax.all_gather(out_weight, "fsdp", axis=1, tiled=True)
    shared_up = lax.all_to_all(shared_gate_up, "fsdp", split_axis=2, concat_axis=0, tiled=True)
    shared_dn = lax.all_to_all(shared_down, "fsdp", split_axis=0, concat_axis=1, tiled=True)
    expert_up = expert_gate_up[0]
    expert_dn = expert_down[0]
    expert_width = expert_up.shape[2]
    shared_width = shared_up.shape[2]

    chosen = expert_ids[:, :, None] == jnp.arange(experts, dtype=jnp.int32)
    table = jnp.sum(jnp.where(chosen, route_weights[:, :, None], 0.0), axis=1)
    expert_scale = lax.all_to_all(table.T, "fsdp", split_axis=0, concat_axis=0, tiled=True)
    expert_scale = expert_scale.reshape(-1)

    local_heads = qkv_full.shape[2]
    head_dim = qkv_full.shape[3]
    score_scale = head_dim ** (-0.5)
    cos_table, sin_table = rope_tables(length, head_dim)
    positions = jnp.arange(length, dtype=jnp.int32)
    segments = segment_ids[0]
    allowed = (positions[:, None] >= positions[None, :]) & (segments[:, None] == segments[None, :])
    hidden_float = hidden_in.astype(f32)
    attn_inverse = inverse_rms(hidden_float)
    normed_one = spread((hidden_float * attn_inverse * attn_gain).astype(bf16))
    qkv_flat = qkv_full.reshape(model_width, -1)
    qkv = (
        jnp.dot(normed_one, qkv_flat, preferred_element_type=f32).reshape(
            length, 3, local_heads, head_dim
        )
        + bias_full
    )
    query = rotate(qkv[:, 0], cos_table, sin_table).astype(bf16)
    keys = rotate(qkv[:, 1], cos_table, sin_table).astype(bf16)
    values = qkv[:, 2].astype(bf16)
    scores = masked_scores(query, keys, allowed, score_scale)
    row_peak = jnp.max(scores, axis=-1, keepdims=True)
    log_total = row_peak + jnp.log(jnp.sum(jnp.exp(scores - row_peak), axis=-1, keepdims=True))
    probs_b = jnp.exp(scores - log_total).astype(bf16)
    heads_out = (
        jnp.einsum("hqk,khd->qhd", probs_b, values, preferred_element_type=f32)
        .astype(bf16)
        .reshape(length, -1)
    )
    middle = hidden_float + head_total(jnp.dot(heads_out, out_full, preferred_element_type=f32))
    ffn_inverse = inverse_rms(middle)
    normed_two_own = (middle * ffn_inverse * ffn_gain).astype(bf16)
    normed_all = lax.all_gather(normed_two_own, every, axis=0, tiled=True)

    gate_w = jnp.concatenate([expert_up[:, 0], shared_up[:, 0]], axis=1)
    upper_w = jnp.concatenate([expert_up[:, 1], shared_up[:, 1]], axis=1)
    both_w = jnp.concatenate([gate_w, upper_w], axis=1)
    down_w = jnp.concatenate([expert_dn, shared_dn], axis=0)
    units = expert_width + shared_width
    gate_logit = jnp.sum(normed_all.astype(f32) * shared_gate_vec, axis=-1)
    gate_prob = jax.nn.sigmoid(gate_logit)
    scale = jnp.concatenate(
        [
            jnp.broadcast_to(expert_scale[:, None], (expert_scale.shape[0], expert_width)),
            jnp.broadcast_to(gate_prob[:, None], (expert_scale.shape[0], shared_width)),
        ],
        axis=1,
    )
    pre = jnp.dot(normed_all, both_w, preferred_element_type=f32)
    act, slope = silu_parts(pre[:, :units])
    upper = pre[:, units:]
    hidden = act * upper
    d_hidden = jnp.dot(grad_all, down_w.T, preferred_element_type=f32)
    agree = d_hidden * hidden
    route_part = jnp.sum(agree[:, :expert_width], axis=1)
    gate_part = jnp.sum(agree[:, expert_width:], axis=1)
    hidden_s = (hidden * scale).astype(bf16)
    d_scaled = d_hidden * scale
    d_both = jnp.concatenate(
        [(d_scaled * upper * slope).astype(bf16), (d_scaled * act).astype(bf16)], axis=1
    )
    d_normed_part = jnp.dot(d_both, both_w.T, preferred_element_type=f32).astype(bf16)
    lane = jnp.arange(128, dtype=jnp.int32)
    own_expert = lax.axis_index("fsdp")
    extra = jnp.where(lane == own_expert, route_part[:, None], 0.0) + jnp.where(
        lane == experts, gate_part[:, None], 0.0
    )
    d_sum = lax.psum_scatter(
        jnp.concatenate([d_normed_part, extra.astype(bf16)], axis=1),
        every,
        scatter_dimension=0,
        tiled=True,
    ).astype(f32)
    d_normed_two = d_sum[:, :model_width]
    token_part = jnp.dot(hidden_s, down_w, preferred_element_type=f32).astype(bf16)
    total = lax.psum_scatter(token_part, every, scatter_dimension=0, tiled=True).astype(f32)
    hidden_out = (middle + total).astype(bf16)
    own_start = tp_rank * own_rows
    ids_own = lax.dynamic_slice_in_dim(expert_ids, own_start, own_rows)
    picked = ids_own[:, :, None] == jnp.arange(experts, dtype=jnp.int32)
    route_grad = jnp.sum(
        jnp.where(picked, d_sum[:, None, model_width : model_width + experts], 0.0), axis=-1
    )
    gate_grad = d_sum[:, model_width + experts]
    g_down = jnp.dot(hidden_s.T, grad_all, preferred_element_type=f32)
    g_both = jnp.dot(normed_all.T, d_both, preferred_element_type=f32)
    g_expert_down = g_down[:expert_width][None]
    g_expert_gate_up = jnp.stack(
        [g_both[:, :expert_width], g_both[:, units : units + expert_width]], axis=1
    )[None]
    g_shared_gate_up = lax.all_to_all(
        jnp.stack([g_both[:, expert_width:units], g_both[:, units + expert_width :]], axis=1).astype(
            bf16
        ),
        "fsdp",
        split_axis=0,
        concat_axis=2,
        tiled=True,
    ).astype(f32)
    g_shared_down = lax.all_to_all(
        g_down[expert_width:].astype(bf16), "fsdp", split_axis=1, concat_axis=0, tiled=True
    ).astype(f32)

    own_gate = jax.nn.sigmoid(jnp.sum(normed_two_own.astype(f32) * shared_gate_vec, axis=-1))
    logit_grad = gate_grad * own_gate * (1.0 - own_gate)
    d_normed_two = d_normed_two + logit_grad[:, None] * shared_gate_vec
    g_gate_vec = jnp.sum(normed_two_own.astype(f32) * logit_grad[:, None], axis=0)
    hat_two = middle * ffn_inverse
    g_ffn_gain = jnp.sum(d_normed_two * hat_two, axis=0)
    middle_grad = out_grad.astype(f32) + norm_backward(d_normed_two, hat_two, ffn_inverse, ffn_gain)
    d_rows = spread(middle_grad.astype(bf16))
    g_out = jnp.dot(heads_out.T, d_rows, preferred_element_type=f32)
    d_heads = (
        jnp.dot(d_rows, out_full.T, preferred_element_type=f32)
        .astype(bf16)
        .reshape(length, local_heads, head_dim)
    )
    heads_three = heads_out.reshape(length, local_heads, head_dim)
    scores_again = masked_scores(query, keys, allowed, score_scale)
    probs_full = jnp.exp(scores_again - log_total)
    probs_again = probs_full.astype(bf16)
    d_values = jnp.einsum("hqk,qhd->khd", probs_again, d_heads, preferred_element_type=f32)
    d_probs = jnp.einsum("qhd,khd->hqk", d_heads, values, preferred_element_type=f32)
    delta = jnp.sum(d_heads.astype(f32) * heads_three.astype(f32), axis=-1)
    d_scores = (probs_full * (d_probs - delta.T[:, :, None])).astype(bf16)
    d_query = jnp.einsum("hqk,khd->qhd", d_scores, keys, preferred_element_type=f32) * score_scale
    d_keys = jnp.einsum("hqk,qhd->khd", d_scores, query, preferred_element_type=f32) * score_scale
    d_qkv = jnp.stack(
        [unrotate(d_query, cos_table, sin_table), unrotate(d_keys, cos_table, sin_table), d_values],
        axis=1,
    )
    g_bias = jnp.sum(d_qkv, axis=0)
    d_qkv_b = d_qkv.astype(bf16).reshape(length, -1)
    g_qkv = jnp.dot(normed_one.T, d_qkv_b, preferred_element_type=f32).reshape(qkv_full.shape)
    d_normed_one = head_total(jnp.dot(d_qkv_b, qkv_flat.T, preferred_element_type=f32))
    hat_one = hidden_float * attn_inverse
    g_attn_gain = jnp.sum(d_normed_one * hat_one, axis=0)
    hidden_grad = middle_grad + norm_backward(d_normed_one, hat_one, attn_inverse, attn_gain)
    g_qkv, g_bias, g_out = (
        lax.psum_scatter(g_qkv.astype(bf16), "fsdp", scatter_dimension=0, tiled=True).astype(f32),
        lax.psum_scatter(g_bias.astype(bf16), "fsdp", scatter_dimension=2, tiled=True).astype(f32),
        lax.psum_scatter(g_out.astype(bf16), "fsdp", scatter_dimension=1, tiled=True).astype(f32),
    )
    g_attn_gain, g_ffn_gain, g_gate_vec = (
        lax.psum_scatter(g_attn_gain, every, scatter_dimension=0, tiled=True),
        lax.psum_scatter(g_ffn_gain, every, scatter_dimension=0, tiled=True),
        lax.psum_scatter(g_gate_vec, every, scatter_dimension=0, tiled=True),
    )
    return (
        hidden_out,
        hidden_grad,
        route_grad,
        g_attn_gain,
        g_ffn_gain,
        g_qkv,
        g_bias,
        g_out,
        g_shared_gate_up,
        g_shared_down,
        g_gate_vec,
        g_expert_gate_up,
        g_expert_down,
    )


def on_device(*arrays):
    expert_ids = arrays[3]
    if 3 * expert_ids.shape[1] > lax.axis_size("fsdp"):
        return dense_plan(*arrays)
    return routed_plan(*arrays)


def solution(mesh):
    placed = (
        P(("fsdp", "tp"), None),
        P(("fsdp", "tp"), None),
        P("fsdp", None),
        P("fsdp", None),
        P("fsdp", None),
        P(),
        P(),
        P("fsdp", None, "tp", None),
        P(None, "tp", "fsdp"),
        P("tp", "fsdp"),
        P("fsdp", None, "tp"),
        P("tp", "fsdp"),
        P(),
        P("fsdp", None, None, "tp"),
        P("fsdp", "tp", None),
    )
    return jax.shard_map(
        on_device,
        mesh=mesh,
        in_specs=placed,
        out_specs=(
            P(("fsdp", "tp"), None),
            P(("fsdp", "tp"), None),
            P(("fsdp", "tp"), None),
            P(("fsdp", "tp")),
            P(("fsdp", "tp")),
            P("fsdp", None, "tp", None),
            P(None, "tp", "fsdp"),
            P("tp", "fsdp"),
            P("fsdp", None, "tp"),
            P("tp", "fsdp"),
            P(("fsdp", "tp")),
            P("fsdp", None, None, "tp"),
            P("fsdp", "tp", None),
        ),
        check_vma=False,
    )
```

```python
import functools

import jax
import jax.experimental.pallas as pl
import jax.experimental.pallas.tpu as pltpu
import jax.numpy as jnp
from jax import lax
from jax.sharding import PartitionSpec as P

epsilon = 1e-06


def rope_tables(length, head_dim):
    half_dim = head_dim // 2
    ratios = jnp.arange(half_dim, dtype=jnp.float32) * (2.0 / head_dim)
    frequency = jnp.exp(-jnp.log(10000.0) * ratios)
    angles = jnp.arange(length, dtype=jnp.float32)[:, None] * frequency[None, :]
    return (jnp.cos(angles)[:, None, :], jnp.sin(angles)[:, None, :])


def rotate(tensor, cos_table, sin_table):
    half_dim = tensor.shape[-1] // 2
    front_half = tensor[..., :half_dim]
    back_half = tensor[..., half_dim:]
    return jnp.concatenate(
        [
            front_half * cos_table - back_half * sin_table,
            back_half * cos_table + front_half * sin_table,
        ],
        axis=-1,
    )


def unrotate(tensor, cos_table, sin_table):
    half_dim = tensor.shape[-1] // 2
    front_half = tensor[..., :half_dim]
    back_half = tensor[..., half_dim:]
    return jnp.concatenate(
        [
            front_half * cos_table + back_half * sin_table,
            back_half * cos_table - front_half * sin_table,
        ],
        axis=-1,
    )


def silu_parts(gate_in):
    sigmoid_value = jax.nn.sigmoid(gate_in)
    return (gate_in * sigmoid_value, sigmoid_value * (1.0 + gate_in * (1.0 - sigmoid_value)))


def slot_table(route_ids, experts, capacity):
    flat_ids = route_ids.reshape(-1)
    onehot = (flat_ids[:, None] == jnp.arange(experts, dtype=jnp.int32)[None, :]).astype(jnp.int32)
    before = jnp.cumsum(onehot, axis=0, dtype=jnp.int32) - onehot
    ranks = jnp.sum(before * onehot, axis=1, dtype=jnp.int32)
    places = flat_ids * capacity + ranks
    filler = jnp.arange(flat_ids.shape[0], dtype=jnp.int32) + 1
    slot_rows = jnp.zeros((experts * capacity,), jnp.int32).at[places].set(filler)
    return (places.reshape(route_ids.shape), slot_rows.reshape(experts, capacity))


def inverse_rms(tensor):
    return lax.rsqrt(jnp.mean(tensor * tensor, axis=-1, keepdims=True) + epsilon)


def norm_backward(d_normed, hat_rows, inverse, gain_vec):
    d_hat = d_normed * gain_vec
    return inverse * (d_hat - hat_rows * jnp.mean(d_hat * hat_rows, axis=-1, keepdims=True))


def masked_scores(query, keys, allowed, score_scale):
    raw = jnp.einsum("qhd,khd->hqk", query, keys, preferred_element_type=jnp.float32) * score_scale
    return jnp.where(allowed[None], raw, -1e30)


def spread(rows):
    return lax.all_gather(rows, "tp", axis=0, tiled=True)


def head_total(partial_rows):
    return lax.psum_scatter(
        partial_rows.astype(jnp.bfloat16), "tp", scatter_dimension=0, tiled=True
    ).astype(jnp.float32)


def to_experts(buffer):
    return lax.all_to_all(buffer, "fsdp", split_axis=0, concat_axis=0, tiled=True)


def from_experts(buffer):
    return lax.all_to_all(buffer, "fsdp", split_axis=0, concat_axis=0, tiled=True)


def routed_plan(
    hidden_in,
    out_grad,
    segment_ids,
    expert_ids,
    route_weights,
    attn_gain,
    ffn_gain,
    qkv_weight,
    qkv_bias,
    out_weight,
    shared_gate_up,
    shared_down,
    shared_gate_vec,
    expert_gate_up,
    expert_down,
):
    tp_rank = lax.axis_index("tp")
    experts = lax.axis_size("fsdp")
    length = segment_ids.shape[1]
    top_count = expert_ids.shape[1]
    capacity = 3 * length * top_count // (2 * experts)
    own_rows = hidden_in.shape[0]
    model_width = hidden_in.shape[1]
    qkv_full, bias_full, out_full, shared_full, shared_down_full = (
        lax.all_gather(qkv_weight, "fsdp", axis=0, tiled=True),
        lax.all_gather(qkv_bias.astype(jnp.bfloat16), "fsdp", axis=2, tiled=True).astype(
            qkv_bias.dtype
        ),
        lax.all_gather(out_weight, "fsdp", axis=1, tiled=True),
        lax.all_gather(shared_gate_up, "fsdp", axis=0, tiled=True),
        lax.all_gather(shared_down, "fsdp", axis=1, tiled=True),
    )
    local_heads = qkv_full.shape[2]
    head_dim = qkv_full.shape[3]
    score_scale = head_dim ** (-0.5)
    cos_table, sin_table = rope_tables(length, head_dim)
    positions = jnp.arange(length, dtype=jnp.int32)
    segments = segment_ids[0]
    allowed = (positions[:, None] >= positions[None, :]) & (segments[:, None] == segments[None, :])
    hidden_float = hidden_in.astype(jnp.float32)
    attn_inverse = inverse_rms(hidden_float)
    normed_one = spread((hidden_float * attn_inverse * attn_gain).astype(jnp.bfloat16))
    qkv_flat = qkv_full.reshape(model_width, -1)
    qkv = (
        jnp.dot(normed_one, qkv_flat, preferred_element_type=jnp.float32).reshape(
            length, 3, local_heads, head_dim
        )
        + bias_full
    )
    query = rotate(qkv[:, 0], cos_table, sin_table).astype(jnp.bfloat16)
    keys = rotate(qkv[:, 1], cos_table, sin_table).astype(jnp.bfloat16)
    values = qkv[:, 2].astype(jnp.bfloat16)
    scores = masked_scores(query, keys, allowed, score_scale)
    row_peak = jnp.max(scores, axis=-1, keepdims=True)
    log_total = row_peak + jnp.log(jnp.sum(jnp.exp(scores - row_peak), axis=-1, keepdims=True))
    probs_b = jnp.exp(scores - log_total).astype(jnp.bfloat16)
    heads_out = (
        jnp.einsum("hqk,khd->qhd", probs_b, values, preferred_element_type=jnp.float32)
        .astype(jnp.bfloat16)
        .reshape(length, -1)
    )
    middle = hidden_float + head_total(
        jnp.dot(heads_out, out_full, preferred_element_type=jnp.float32)
    )
    ffn_inverse = inverse_rms(middle)
    normed_two_own = (middle * ffn_inverse * ffn_gain).astype(jnp.bfloat16)
    normed_two = spread(normed_two_own)
    gate_prob = jax.nn.sigmoid(jnp.sum(normed_two.astype(jnp.float32) * shared_gate_vec, axis=-1))
    shared_flat = shared_full.reshape(model_width, -1)
    shared_width = shared_full.shape[2]
    shared_pre = jnp.dot(normed_two, shared_flat, preferred_element_type=jnp.float32)
    shared_act, shared_slope = silu_parts(shared_pre[:, :shared_width])
    shared_upper = shared_pre[:, shared_width:]
    shared_hidden = (shared_act * shared_upper).astype(jnp.bfloat16)
    shared_part = jnp.dot(shared_hidden, shared_down_full, preferred_element_type=jnp.float32)
    places, slot_rows = slot_table(expert_ids, experts, capacity)
    filled = slot_rows > 0
    route_index = jnp.maximum(slot_rows - 1, 0)
    source_rows = route_index // top_count
    flat_weights = route_weights.reshape(-1)
    slot_weights = jnp.where(filled, flat_weights[route_index], 0.0)
    send_rows = jnp.where(filled[:, :, None], normed_two[source_rows], jnp.zeros((), jnp.bfloat16))
    arrived = to_experts(send_rows).reshape(-1, model_width)
    expert_flat = expert_gate_up[0].reshape(model_width, -1)
    expert_width = expert_gate_up.shape[3]
    down_local = expert_down[0]
    expert_pre = jnp.dot(arrived, expert_flat, preferred_element_type=jnp.float32)
    expert_act, expert_slope = silu_parts(expert_pre[:, :expert_width])
    expert_upper = expert_pre[:, expert_width:]
    expert_hidden = (expert_act * expert_upper).astype(jnp.bfloat16)
    expert_part = jnp.dot(expert_hidden, down_local, preferred_element_type=jnp.float32).astype(
        jnp.bfloat16
    )
    returned = from_experts(expert_part.reshape(experts, capacity, model_width)).reshape(
        experts * capacity, model_width
    )
    picked = returned[places].astype(jnp.float32)
    token_term = gate_prob[:, None] * shared_part + jnp.sum(
        route_weights[:, :, None] * picked, axis=1
    )
    own_extra = 0.0
    total = (
        lax.psum_scatter(
            token_term.astype(jnp.bfloat16), "tp", scatter_dimension=0, tiled=True
        ).astype(jnp.float32)
        + own_extra
    )
    hidden_out = (middle + total).astype(jnp.bfloat16)
    grad_rows = spread(out_grad)
    grad_float = grad_rows.astype(jnp.float32)
    gate_part = jnp.sum(grad_float * shared_part, axis=-1)
    scaled_grad = (gate_prob[:, None] * grad_float).astype(jnp.bfloat16)
    shared_d_hidden = jnp.dot(scaled_grad, shared_down_full.T, preferred_element_type=jnp.float32)
    shared_d_cat = jnp.concatenate(
        [
            (shared_d_hidden * shared_upper * shared_slope).astype(jnp.bfloat16),
            (shared_d_hidden * shared_act).astype(jnp.bfloat16),
        ],
        axis=1,
    )
    g_shared_down = jnp.dot(shared_hidden.T, scaled_grad, preferred_element_type=jnp.float32)
    g_shared_gate_up = jnp.dot(
        normed_two.T, shared_d_cat, preferred_element_type=jnp.float32
    ).reshape(shared_full.shape)
    d_normed_part = jnp.dot(shared_d_cat, shared_flat.T, preferred_element_type=jnp.float32)
    expert_grad_in = (slot_weights[:, :, None] * grad_float[source_rows]).astype(jnp.bfloat16)
    arrived_grad = to_experts(expert_grad_in).reshape(-1, model_width)
    back_act, back_slope, back_upper, back_hidden = (
        expert_act,
        expert_slope,
        expert_upper,
        expert_hidden,
    )
    expert_d_hidden = jnp.dot(arrived_grad, down_local.T, preferred_element_type=jnp.float32)
    expert_d_cat = jnp.concatenate(
        [
            (expert_d_hidden * back_upper * back_slope).astype(jnp.bfloat16),
            (expert_d_hidden * back_act).astype(jnp.bfloat16),
        ],
        axis=1,
    )
    g_expert_down = jnp.dot(back_hidden.T, arrived_grad, preferred_element_type=jnp.float32)[None]
    g_expert_gate_up = jnp.dot(arrived.T, expert_d_cat, preferred_element_type=jnp.float32).reshape(
        expert_gate_up.shape
    )
    expert_d_part = jnp.dot(expert_d_cat, expert_flat.T, preferred_element_type=jnp.float32).astype(
        jnp.bfloat16
    )
    route_part = jnp.sum(grad_float[:, None, :] * picked, axis=-1)
    returned_grad = from_experts(expert_d_part.reshape(experts, capacity, model_width)).reshape(
        experts * capacity, model_width
    )
    d_normed_part = d_normed_part + jnp.sum(returned_grad[places].astype(jnp.float32), axis=1)
    d_normed_two, route_grad, gate_grad = (
        lax.psum_scatter(
            d_normed_part.astype(jnp.bfloat16), "tp", scatter_dimension=0, tiled=True
        ).astype(jnp.float32),
        lax.psum_scatter(
            route_part.astype(jnp.bfloat16), "tp", scatter_dimension=0, tiled=True
        ).astype(jnp.float32),
        lax.psum_scatter(
            gate_part.astype(jnp.bfloat16), "tp", scatter_dimension=0, tiled=True
        ).astype(jnp.float32),
    )
    own_gate = lax.dynamic_slice_in_dim(gate_prob, tp_rank * own_rows, own_rows)
    logit_grad = gate_grad * own_gate * (1.0 - own_gate)
    d_normed_two = d_normed_two + logit_grad[:, None] * shared_gate_vec
    g_gate_vec = jnp.sum(normed_two_own.astype(jnp.float32) * logit_grad[:, None], axis=0)
    hat_two = middle * ffn_inverse
    g_ffn_gain = jnp.sum(d_normed_two * hat_two, axis=0)
    middle_grad = out_grad.astype(jnp.float32) + norm_backward(
        d_normed_two, hat_two, ffn_inverse, ffn_gain
    )
    d_rows = spread(middle_grad.astype(jnp.bfloat16))
    g_out = jnp.dot(heads_out.T, d_rows, preferred_element_type=jnp.float32)
    d_heads = (
        jnp.dot(d_rows, out_full.T, preferred_element_type=jnp.float32)
        .astype(jnp.bfloat16)
        .reshape(length, local_heads, head_dim)
    )
    heads_three = heads_out.reshape(length, local_heads, head_dim)
    scores_again = masked_scores(query, keys, allowed, score_scale)
    probs_full = jnp.exp(scores_again - log_total)
    probs_again = probs_full.astype(jnp.bfloat16)
    d_values = jnp.einsum("hqk,qhd->khd", probs_again, d_heads, preferred_element_type=jnp.float32)
    d_probs = jnp.einsum("qhd,khd->hqk", d_heads, values, preferred_element_type=jnp.float32)
    delta = jnp.sum(d_heads.astype(jnp.float32) * heads_three.astype(jnp.float32), axis=-1)
    d_scores = (probs_full * (d_probs - delta.T[:, :, None])).astype(jnp.bfloat16)
    d_query = (
        jnp.einsum("hqk,khd->qhd", d_scores, keys, preferred_element_type=jnp.float32) * score_scale
    )
    d_keys = (
        jnp.einsum("hqk,qhd->khd", d_scores, query, preferred_element_type=jnp.float32)
        * score_scale
    )
    d_qkv = jnp.stack(
        [unrotate(d_query, cos_table, sin_table), unrotate(d_keys, cos_table, sin_table), d_values],
        axis=1,
    )
    g_bias = jnp.sum(d_qkv, axis=0)
    d_qkv_b = d_qkv.astype(jnp.bfloat16).reshape(length, -1)
    g_qkv = jnp.dot(normed_one.T, d_qkv_b, preferred_element_type=jnp.float32).reshape(
        qkv_full.shape
    )
    d_normed_one = head_total(jnp.dot(d_qkv_b, qkv_flat.T, preferred_element_type=jnp.float32))
    hat_one = hidden_float * attn_inverse
    g_attn_gain = jnp.sum(d_normed_one * hat_one, axis=0)
    hidden_grad = middle_grad + norm_backward(d_normed_one, hat_one, attn_inverse, attn_gain)
    g_qkv, g_bias, g_out, g_shared_gate_up, g_shared_down = (
        lax.psum_scatter(
            g_qkv.astype(jnp.bfloat16), "fsdp", scatter_dimension=0, tiled=True
        ).astype(jnp.float32),
        lax.psum_scatter(
            g_bias.astype(jnp.bfloat16), "fsdp", scatter_dimension=2, tiled=True
        ).astype(jnp.float32),
        lax.psum_scatter(
            g_out.astype(jnp.bfloat16), "fsdp", scatter_dimension=1, tiled=True
        ).astype(jnp.float32),
        lax.psum_scatter(
            g_shared_gate_up.astype(jnp.bfloat16), "fsdp", scatter_dimension=0, tiled=True
        ).astype(jnp.float32),
        lax.psum_scatter(
            g_shared_down.astype(jnp.bfloat16), "fsdp", scatter_dimension=1, tiled=True
        ).astype(jnp.float32),
    )
    g_attn_gain, g_ffn_gain, g_gate_vec = (
        lax.psum_scatter(g_attn_gain, ("fsdp", "tp"), scatter_dimension=0, tiled=True),
        lax.psum_scatter(g_ffn_gain, ("fsdp", "tp"), scatter_dimension=0, tiled=True),
        lax.psum_scatter(g_gate_vec, ("fsdp", "tp"), scatter_dimension=0, tiled=True),
    )
    return (
        hidden_out,
        hidden_grad,
        route_grad,
        g_attn_gain,
        g_ffn_gain,
        g_qkv,
        g_bias,
        g_out,
        g_shared_gate_up,
        g_shared_down,
        g_gate_vec,
        g_expert_gate_up,
        g_expert_down,
    )


MESH = pl.DeviceIdType.MESH


def flipped(index, bit):
    return index + bit - 2 * bit * ((index // bit) % 2)


def place():
    me = lax.axis_index("fsdp")
    rank = lax.axis_index("tp")
    return me, rank


def greet(me, rank, tp):
    barrier = pltpu.get_barrier_semaphore()
    for bit in (1, 2, 4):
        pl.semaphore_signal(
            barrier, inc=1, device_id=(flipped(me, bit), rank), device_id_type=MESH
        )

    @pl.when(rank > 0)
    def _():
        pl.semaphore_signal(barrier, inc=1, device_id=(me, rank - 1), device_id_type=MESH)

    @pl.when(rank < tp - 1)
    def _():
        pl.semaphore_signal(barrier, inc=1, device_id=(me, rank + 1), device_id_type=MESH)

    left = (rank + tp - 1) // tp
    right = (2 * (tp - 1) - rank) // tp
    pl.semaphore_wait(barrier, 3 + left + right)


def gather_kernel(tp, own_ref, all_ref, local_sem, z_send, z_recv, p_send, p_recv):
    me, rank = place()
    greet(me, rank, tp)
    rows = own_ref.shape[0]
    half = rows // 2
    pack_rows = rows * tp

    def region(pack, block, start=0, count=None):
        count = rows if count is None else count
        return all_ref.at[pl.ds(pack * pack_rows + block * rows + start, count)]

    def along_z(block, right):
        way = 0 if right else 1
        ref = region(me, block)
        return pltpu.make_async_remote_copy(
            src_ref=ref,
            dst_ref=ref,
            send_sem=z_send.at[way, block],
            recv_sem=z_recv.at[way, block],
            device_id=(me, rank + 1 if right else rank - 1),
            device_id_type=MESH,
        )

    def across(bit, pack_bits, block, slot, start=0, count=None):
        pack = me
        for one in (2, 4):
            if pack_bits & one:
                pack = flipped(pack, one)
        ref = region(pack, block, start, count)
        return pltpu.make_async_remote_copy(
            src_ref=ref,
            dst_ref=ref,
            send_sem=p_send.at[slot, block],
            recv_sem=p_recv.at[slot, block],
            device_id=(flipped(me, bit), rank),
            device_id_type=MESH,
        )

    def own_x(block):
        return across(2, 0, block, 0)

    def own_y(block):
        return across(4, 0, block, 1)

    def own_core(block):
        return across(1, 0, block, 2)

    def x_to_y(block):
        return across(4, 2, block, 3, 0, half)

    def x_to_core(block):
        return across(1, 2, block, 4)

    def y_to_x(block):
        return across(2, 4, block, 5, half, half)

    def y_to_core(block):
        return across(1, 4, block, 6)

    def diag_to_core(block):
        return across(1, 6, block, 7)

    def start_plane(block):
        own_x(block).start()
        own_y(block).start()
        own_core(block).start()

    def forward(block):
        own_x(block).wait_recv()
        x_to_y(block).start()
        x_to_core(block).start()
        own_y(block).wait_recv()
        y_to_x(block).start()
        y_to_core(block).start()

    def finish(block):
        x_to_y(block).wait_recv()
        y_to_x(block).wait_recv()
        diag_to_core(block).start()

    def z_step(step):
        @pl.when(rank >= step)
        def _():
            block = rank - step
            along_z(block, True).wait_recv()

            @pl.when(rank < tp - 1)
            def _():
                along_z(block, True).start()

            start_plane(block)

        @pl.when(rank + step < tp)
        def _():
            block = rank + step
            along_z(block, False).wait_recv()

            @pl.when(rank > 0)
            def _():
                along_z(block, False).start()

            start_plane(block)

    mine = pltpu.make_async_copy(own_ref, region(me, rank), local_sem)
    mine.start()
    mine.wait()

    @pl.when(rank < tp - 1)
    def _():
        along_z(rank, True).start()

    @pl.when(rank > 0)
    def _():
        along_z(rank, False).start()

    start_plane(rank)
    order = [rank]
    for bit in (1, 2):
        order = order + [flipped(one, bit) for one in order]
    z_step(1)
    forward(order[0])
    z_step(2)
    forward(order[1])
    finish(order[0])
    z_step(3)
    forward(order[2])
    finish(order[1])
    forward(order[3])
    finish(order[2])
    finish(order[3])
    for block in order:
        own_core(block).wait_recv()
        x_to_core(block).wait_recv()
        y_to_core(block).wait_recv()
        diag_to_core(block).wait_recv()
    for block in order:
        own_x(block).wait_send()
        own_y(block).wait_send()
        own_core(block).wait_send()
        x_to_y(block).wait_send()
        x_to_core(block).wait_send()
        y_to_x(block).wait_send()
        y_to_core(block).wait_send()
        diag_to_core(block).wait_send()
    for block in range(tp):

        @pl.when((block <= rank) & (rank < tp - 1))
        def _():
            along_z(block, True).wait_send()

        @pl.when((block >= rank) & (rank > 0))
        def _():
            along_z(block, False).wait_send()


def gather_everywhere(own, fsdp, tp, collective_id):
    rows, width = own.shape
    return pl.pallas_call(
        functools.partial(gather_kernel, tp),
        out_shape=jax.ShapeDtypeStruct((fsdp * tp * rows, width), own.dtype),
        in_specs=[pl.BlockSpec(memory_space=pl.ANY)],
        out_specs=pl.BlockSpec(memory_space=pl.ANY),
        scratch_shapes=[
            pltpu.SemaphoreType.DMA,
            pltpu.SemaphoreType.DMA((2, tp)),
            pltpu.SemaphoreType.DMA((2, tp)),
            pltpu.SemaphoreType.DMA((8, tp)),
            pltpu.SemaphoreType.DMA((8, tp)),
        ],
        compiler_params=pltpu.CompilerParams(
            collective_id=collective_id, has_side_effects=True, vmem_limit_bytes=16 << 20
        ),
        name="gather_rows",
    )(own)


def scatter_kernel(tp, parts, *refs):
    ins = refs[:parts]
    outs = refs[parts : 2 * parts]
    buffers = refs[2 * parts : 7 * parts]
    mine, other, diag_in, last_in, z_in = (
        buffers[i * parts : (i + 1) * parts] for i in range(5)
    )
    l_sem, c_send, c_recv, p_send, p_recv, z_send, z_recv = refs[7 * parts :]
    me, rank = place()
    greet(me, rank, tp)
    f32 = jnp.float32
    blocks = [rank]
    for bit in (1, 2):
        blocks = blocks + [flipped(one, bit) for one in blocks]
    blocks = blocks[::-1]
    packs = [me, flipped(me, 2), flipped(me, 4), flipped(flipped(me, 2), 4)]
    every = range(parts)
    rows = [ref.shape[0] for ref in outs]
    low = [pl.ds(0, count // 2) for count in rows]
    high = [pl.ds(count // 2, count // 2) for count in rows]

    def region(i, pack, block):
        return ins[i].at[pl.ds((pack * tp + block) * rows[i], rows[i])]

    def local(k, j, i):
        return pltpu.make_async_copy(
            region(i, packs[k], blocks[j]), mine[i].at[k, j], l_sem.at[k, j, i]
        )

    def core(k, j, i):
        return pltpu.make_async_remote_copy(
            src_ref=region(i, flipped(packs[k], 1), blocks[j]),
            dst_ref=other[i].at[k, j],
            send_sem=c_send.at[k, j, i],
            recv_sem=c_recv.at[k, j, i],
            device_id=(flipped(me, 1), rank),
            device_id_type=MESH,
        )

    def across(bit, src, dst, slot, j, i):
        return pltpu.make_async_remote_copy(
            src_ref=src,
            dst_ref=dst,
            send_sem=p_send.at[slot, j, i],
            recv_sem=p_recv.at[slot, j, i],
            device_id=(flipped(me, bit), rank),
            device_id_type=MESH,
        )

    def diag_x(j, i):
        return across(2, mine[i].at[3, j, low[i]], diag_in[i].at[j, 0], 0, j, i)

    def diag_y(j, i):
        return across(4, mine[i].at[3, j, high[i]], diag_in[i].at[j, 1], 1, j, i)

    def direct_x(j, i):
        return across(2, mine[i].at[1, j, low[i]], last_in[i].at[j, 0, low[i]], 2, j, i)

    def direct_y(j, i):
        return across(4, mine[i].at[2, j, high[i]], last_in[i].at[j, 1, high[i]], 3, j, i)

    def summed_x(j, i):
        return across(2, mine[i].at[1, j, high[i]], last_in[i].at[j, 0, high[i]], 4, j, i)

    def summed_y(j, i):
        return across(4, mine[i].at[2, j, low[i]], last_in[i].at[j, 1, low[i]], 5, j, i)

    def along_z(j, right, i):
        way = 0 if right else 1
        block = blocks[j]
        return pltpu.make_async_remote_copy(
            src_ref=mine[i].at[0, j],
            dst_ref=z_in[i].at[way, block],
            send_sem=z_send.at[way, block, i],
            recv_sem=z_recv.at[way, block, i],
            device_id=(me, rank + 1 if right else rank - 1),
            device_id_type=MESH,
        )

    for j in range(tp):
        for k in (3, 2, 1, 0):
            for i in every:
                core(k, j, i).start()
                local(k, j, i).start()

    def add(ref, spot, one):
        ref[spot] = (ref[spot].astype(f32) + one.astype(f32)).astype(ref.dtype)

    def first(j):
        for k in (3, 2, 1, 0):
            for i in every:
                core(k, j, i).wait_recv()
                local(k, j, i).wait()
                add(mine[i], (k, j), other[i][k, j])
                if k == 3:
                    diag_x(j, i).start()
                    diag_y(j, i).start()
                if k == 2:
                    direct_y(j, i).start()
                if k == 1:
                    direct_x(j, i).start()

    def second(j):
        for i in every:
            diag_x(j, i).wait_recv()
            add(mine[i], (2, j, low[i]), diag_in[i][j, 0])
            summed_y(j, i).start()
            diag_y(j, i).wait_recv()
            add(mine[i], (1, j, high[i]), diag_in[i][j, 1])
            summed_x(j, i).start()

    def third(j):
        block = blocks[j]
        for i in every:
            direct_x(j, i).wait_recv()
            direct_y(j, i).wait_recv()
            summed_x(j, i).wait_recv()
            summed_y(j, i).wait_recv()
            total = (
                mine[i][0, j].astype(f32)
                + last_in[i][j, 0].astype(f32)
                + last_in[i][j, 1].astype(f32)
            )
            if j < tp - 1:
                mine[i][0, j] = total.astype(mine[i].dtype)
            else:
                outs[i][...] = total
        if j < tp - 1:

            @pl.when((block > rank) & (rank > 0))
            def _():
                for i in every:
                    along_z(j, True, i).wait_recv()
                    add(mine[i], (0, j), z_in[i][0, block])

            @pl.when((block < rank) & (rank < tp - 1))
            def _():
                for i in every:
                    along_z(j, False, i).wait_recv()
                    add(mine[i], (0, j), z_in[i][1, block])

            @pl.when(block > rank)
            def _():
                for i in every:
                    along_z(j, True, i).start()

            @pl.when(block < rank)
            def _():
                for i in every:
                    along_z(j, False, i).start()
        else:

            @pl.when(rank > 0)
            def _():
                for i in every:
                    along_z(j, True, i).wait_recv()
                    outs[i][...] += z_in[i][0, block].astype(f32)

            @pl.when(rank < tp - 1)
            def _():
                for i in every:
                    along_z(j, False, i).wait_recv()
                    outs[i][...] += z_in[i][1, block].astype(f32)

    first(0)
    first(1)
    second(0)
    first(2)
    second(1)
    third(0)
    first(3)
    second(2)
    third(1)
    second(3)
    third(2)
    third(3)
    for j in range(tp):
        for i in every:
            for k in range(4):
                core(k, j, i).wait_send()
            for copy in (diag_x, diag_y, direct_x, direct_y, summed_x, summed_y):
                copy(j, i).wait_send()
        block = blocks[j]
        if j < tp - 1:

            @pl.when(block > rank)
            def _():
                for i in every:
                    along_z(j, True, i).wait_send()

            @pl.when(block < rank)
            def _():
                for i in every:
                    along_z(j, False, i).wait_send()


def scatter_sum(arrays, fsdp, tp, collective_id):
    parts = len(arrays)
    shapes = [(one.shape[0] // (fsdp * tp), one.shape[1]) for one in arrays]
    kind = arrays[0].dtype
    scratch = [pltpu.VMEM((4, tp, rows, width), kind) for rows, width in shapes]
    scratch += [pltpu.VMEM((4, tp, rows, width), kind) for rows, width in shapes]
    scratch += [pltpu.VMEM((tp, 2, rows // 2, width), kind) for rows, width in shapes]
    scratch += [pltpu.VMEM((tp, 2, rows, width), kind) for rows, width in shapes]
    scratch += [pltpu.VMEM((2, tp, rows, width), kind) for rows, width in shapes]
    return pl.pallas_call(
        functools.partial(scatter_kernel, tp, parts),
        out_shape=[jax.ShapeDtypeStruct(shape, jnp.float32) for shape in shapes],
        in_specs=[pl.BlockSpec(memory_space=pl.ANY)] * parts,
        out_specs=[pl.BlockSpec(memory_space=pltpu.VMEM)] * parts,
        scratch_shapes=scratch
        + [
            pltpu.SemaphoreType.DMA((4, tp, parts)),
            pltpu.SemaphoreType.DMA((4, tp, parts)),
            pltpu.SemaphoreType.DMA((4, tp, parts)),
            pltpu.SemaphoreType.DMA((6, tp, parts)),
            pltpu.SemaphoreType.DMA((6, tp, parts)),
            pltpu.SemaphoreType.DMA((2, tp, parts)),
            pltpu.SemaphoreType.DMA((2, tp, parts)),
        ],
        compiler_params=pltpu.CompilerParams(
            collective_id=collective_id, has_side_effects=True, vmem_limit_bytes=48 << 20
        ),
        name="scatter_rows",
    )(*arrays)


def dense_plan(
    hidden_in,
    out_grad,
    segment_ids,
    expert_ids,
    route_weights,
    attn_gain,
    ffn_gain,
    qkv_weight,
    qkv_bias,
    out_weight,
    shared_gate_up,
    shared_down,
    shared_gate_vec,
    expert_gate_up,
    expert_down,
):
    every = ("fsdp", "tp")
    tp_rank = lax.axis_index("tp")
    experts = lax.axis_size("fsdp")
    packs = experts
    length = segment_ids.shape[1]
    own_rows = hidden_in.shape[0]
    model_width = hidden_in.shape[1]
    bf16 = jnp.bfloat16
    f32 = jnp.float32

    grad_all = lax.all_gather(out_grad, every, axis=0, tiled=True)
    qkv_full = lax.all_gather(qkv_weight, "fsdp", axis=0, tiled=True)
    bias_full = lax.all_gather(qkv_bias.astype(bf16), "fsdp", axis=2, tiled=True).astype(f32)
    out_full = lax.all_gather(out_weight, "fsdp", axis=1, tiled=True)
    shared_up = lax.all_to_all(shared_gate_up, "fsdp", split_axis=2, concat_axis=0, tiled=True)
    shared_dn = lax.all_to_all(shared_down, "fsdp", split_axis=0, concat_axis=1, tiled=True)
    expert_up = expert_gate_up[0]
    expert_dn = expert_down[0]
    expert_width = expert_up.shape[2]
    shared_width = shared_up.shape[2]

    chosen = expert_ids[:, :, None] == jnp.arange(experts, dtype=jnp.int32)
    table = jnp.sum(jnp.where(chosen, route_weights[:, :, None], 0.0), axis=1)
    expert_scale = lax.all_to_all(table.T, "fsdp", split_axis=0, concat_axis=0, tiled=True)
    expert_scale = expert_scale.reshape(-1)

    local_heads = qkv_full.shape[2]
    head_dim = qkv_full.shape[3]
    score_scale = head_dim ** (-0.5)
    cos_table, sin_table = rope_tables(length, head_dim)
    positions = jnp.arange(length, dtype=jnp.int32)
    segments = segment_ids[0]
    allowed = (positions[:, None] >= positions[None, :]) & (segments[:, None] == segments[None, :])
    hidden_float = hidden_in.astype(f32)
    attn_inverse = inverse_rms(hidden_float)
    normed_one = spread((hidden_float * attn_inverse * attn_gain).astype(bf16))
    qkv_flat = qkv_full.reshape(model_width, -1)
    qkv = (
        jnp.dot(normed_one, qkv_flat, preferred_element_type=f32).reshape(
            length, 3, local_heads, head_dim
        )
        + bias_full
    )
    query = rotate(qkv[:, 0], cos_table, sin_table).astype(bf16)
    keys = rotate(qkv[:, 1], cos_table, sin_table).astype(bf16)
    values = qkv[:, 2].astype(bf16)
    scores = masked_scores(query, keys, allowed, score_scale)
    row_peak = jnp.max(scores, axis=-1, keepdims=True)
    log_total = row_peak + jnp.log(jnp.sum(jnp.exp(scores - row_peak), axis=-1, keepdims=True))
    probs_b = jnp.exp(scores - log_total).astype(bf16)
    heads_out = (
        jnp.einsum("hqk,khd->qhd", probs_b, values, preferred_element_type=f32)
        .astype(bf16)
        .reshape(length, -1)
    )
    middle = hidden_float + head_total(jnp.dot(heads_out, out_full, preferred_element_type=f32))
    ffn_inverse = inverse_rms(middle)
    normed_two_own = (middle * ffn_inverse * ffn_gain).astype(bf16)
    normed_all = gather_everywhere(normed_two_own, experts, lax.axis_size("tp"), 1)

    gate_w = jnp.concatenate([expert_up[:, 0], shared_up[:, 0]], axis=1)
    upper_w = jnp.concatenate([expert_up[:, 1], shared_up[:, 1]], axis=1)
    both_w = jnp.concatenate([gate_w, upper_w], axis=1)
    down_w = jnp.concatenate([expert_dn, shared_dn], axis=0)
    units = expert_width + shared_width
    gate_logit = jnp.sum(normed_all.astype(f32) * shared_gate_vec, axis=-1)
    gate_prob = jax.nn.sigmoid(gate_logit)
    scale = jnp.concatenate(
        [
            jnp.broadcast_to(expert_scale[:, None], (expert_scale.shape[0], expert_width)),
            jnp.broadcast_to(gate_prob[:, None], (expert_scale.shape[0], shared_width)),
        ],
        axis=1,
    )
    pre = jnp.dot(normed_all, both_w, preferred_element_type=f32)
    act, slope = silu_parts(pre[:, :units])
    upper = pre[:, units:]
    hidden = act * upper
    d_hidden = jnp.dot(grad_all, down_w.T, preferred_element_type=f32)
    agree = d_hidden * hidden
    route_part = jnp.sum(agree[:, :expert_width], axis=1)
    gate_part = jnp.sum(agree[:, expert_width:], axis=1)
    hidden_s = (hidden * scale).astype(bf16)
    d_scaled = d_hidden * scale
    d_both = jnp.concatenate(
        [(d_scaled * upper * slope).astype(bf16), (d_scaled * act).astype(bf16)], axis=1
    )
    d_normed_part = jnp.dot(d_both, both_w.T, preferred_element_type=f32).astype(bf16)
    lines = jnp.arange(16, dtype=jnp.int32)[None, :, None]
    route_lines = route_part.reshape(-1, 1, own_rows)
    gate_lines = gate_part.reshape(-1, 1, own_rows)
    extra = jnp.where(lines == lax.axis_index("fsdp"), route_lines, 0.0) + jnp.where(
        lines == experts, gate_lines, 0.0
    )
    extra_high = extra.astype(bf16)
    extra_low = (extra - extra_high.astype(f32)).astype(bf16)
    extra = jnp.concatenate([extra_high, extra_low], axis=1).reshape(-1, own_rows)
    d_normed_two, extra_sum = scatter_sum([d_normed_part, extra], experts, lax.axis_size("tp"), 2)
    extra_sum = extra_sum[:16] + extra_sum[16:]
    token_part = jnp.dot(hidden_s, down_w, preferred_element_type=f32).astype(bf16)
    (total,) = scatter_sum([token_part], experts, lax.axis_size("tp"), 3)
    hidden_out = (middle + total).astype(bf16)
    own_start = tp_rank * own_rows
    ids_own = lax.dynamic_slice_in_dim(expert_ids, own_start, own_rows)
    picked = ids_own[:, :, None] == jnp.arange(experts, dtype=jnp.int32)
    route_grad = jnp.sum(jnp.where(picked, extra_sum[:experts].T[:, None, :], 0.0), axis=-1)
    gate_grad = extra_sum[experts]
    g_down = jnp.dot(hidden_s.T, grad_all, preferred_element_type=f32)
    g_both = jnp.dot(normed_all.T, d_both, preferred_element_type=f32)
    g_expert_down = g_down[:expert_width][None]
    g_expert_gate_up = jnp.stack(
        [g_both[:, :expert_width], g_both[:, units : units + expert_width]], axis=1
    )[None]
    g_shared_gate_up = lax.all_to_all(
        jnp.stack([g_both[:, expert_width:units], g_both[:, units + expert_width :]], axis=1).astype(
            bf16
        ),
        "fsdp",
        split_axis=0,
        concat_axis=2,
        tiled=True,
    ).astype(f32)
    g_shared_down = lax.all_to_all(
        g_down[expert_width:].astype(bf16), "fsdp", split_axis=1, concat_axis=0, tiled=True
    ).astype(f32)

    own_gate = jax.nn.sigmoid(jnp.sum(normed_two_own.astype(f32) * shared_gate_vec, axis=-1))
    logit_grad = gate_grad * own_gate * (1.0 - own_gate)
    d_normed_two = d_normed_two + logit_grad[:, None] * shared_gate_vec
    g_gate_vec = jnp.sum(normed_two_own.astype(f32) * logit_grad[:, None], axis=0)
    hat_two = middle * ffn_inverse
    g_ffn_gain = jnp.sum(d_normed_two * hat_two, axis=0)
    middle_grad = out_grad.astype(f32) + norm_backward(d_normed_two, hat_two, ffn_inverse, ffn_gain)
    d_rows = spread(middle_grad.astype(bf16))
    g_out = jnp.dot(heads_out.T, d_rows, preferred_element_type=f32)
    d_heads = (
        jnp.dot(d_rows, out_full.T, preferred_element_type=f32)
        .astype(bf16)
        .reshape(length, local_heads, head_dim)
    )
    heads_three = heads_out.reshape(length, local_heads, head_dim)
    scores_again = masked_scores(query, keys, allowed, score_scale)
    probs_full = jnp.exp(scores_again - log_total)
    probs_again = probs_full.astype(bf16)
    d_values = jnp.einsum("hqk,qhd->khd", probs_again, d_heads, preferred_element_type=f32)
    d_probs = jnp.einsum("qhd,khd->hqk", d_heads, values, preferred_element_type=f32)
    delta = jnp.sum(d_heads.astype(f32) * heads_three.astype(f32), axis=-1)
    d_scores = (probs_full * (d_probs - delta.T[:, :, None])).astype(bf16)
    d_query = jnp.einsum("hqk,khd->qhd", d_scores, keys, preferred_element_type=f32) * score_scale
    d_keys = jnp.einsum("hqk,qhd->khd", d_scores, query, preferred_element_type=f32) * score_scale
    d_qkv = jnp.stack(
        [unrotate(d_query, cos_table, sin_table), unrotate(d_keys, cos_table, sin_table), d_values],
        axis=1,
    )
    g_bias = jnp.sum(d_qkv, axis=0)
    d_qkv_b = d_qkv.astype(bf16).reshape(length, -1)
    g_qkv = jnp.dot(normed_one.T, d_qkv_b, preferred_element_type=f32).reshape(qkv_full.shape)
    d_normed_one = head_total(jnp.dot(d_qkv_b, qkv_flat.T, preferred_element_type=f32))
    hat_one = hidden_float * attn_inverse
    g_attn_gain = jnp.sum(d_normed_one * hat_one, axis=0)
    hidden_grad = middle_grad + norm_backward(d_normed_one, hat_one, attn_inverse, attn_gain)
    g_qkv, g_bias, g_out = (
        lax.psum_scatter(g_qkv.astype(bf16), "fsdp", scatter_dimension=0, tiled=True).astype(f32),
        lax.psum_scatter(g_bias.astype(bf16), "fsdp", scatter_dimension=2, tiled=True).astype(f32),
        lax.psum_scatter(g_out.astype(bf16), "fsdp", scatter_dimension=1, tiled=True).astype(f32),
    )
    g_attn_gain, g_ffn_gain, g_gate_vec = (
        lax.psum_scatter(g_attn_gain, every, scatter_dimension=0, tiled=True),
        lax.psum_scatter(g_ffn_gain, every, scatter_dimension=0, tiled=True),
        lax.psum_scatter(g_gate_vec, every, scatter_dimension=0, tiled=True),
    )
    return (
        hidden_out,
        hidden_grad,
        route_grad,
        g_attn_gain,
        g_ffn_gain,
        g_qkv,
        g_bias,
        g_out,
        g_shared_gate_up,
        g_shared_down,
        g_gate_vec,
        g_expert_gate_up,
        g_expert_down,
    )


def on_device(*arrays):
    if lax.axis_size("fsdp") == 8 and lax.axis_size("tp") == 4 and arrays[3].shape[1] >= 3:
        return dense_plan(*arrays)
    return routed_plan(*arrays)


def solution(mesh):
    placed = (
        P(("fsdp", "tp"), None),
        P(("fsdp", "tp"), None),
        P("fsdp", None),
        P("fsdp", None),
        P("fsdp", None),
        P(),
        P(),
        P("fsdp", None, "tp", None),
        P(None, "tp", "fsdp"),
        P("tp", "fsdp"),
        P("fsdp", None, "tp"),
        P("tp", "fsdp"),
        P(),
        P("fsdp", None, None, "tp"),
        P("fsdp", "tp", None),
    )
    return jax.shard_map(
        on_device,
        mesh=mesh,
        in_specs=placed,
        out_specs=(
            P(("fsdp", "tp"), None),
            P(("fsdp", "tp"), None),
            P(("fsdp", "tp"), None),
            P(("fsdp", "tp")),
            P(("fsdp", "tp")),
            P("fsdp", None, "tp", None),
            P(None, "tp", "fsdp"),
            P("tp", "fsdp"),
            P("fsdp", None, "tp"),
            P("tp", "fsdp"),
            P(("fsdp", "tp")),
            P("fsdp", None, None, "tp"),
            P("fsdp", "tp", None),
        ),
        check_vma=False,
    )
```

```python
import functools

import jax
import jax.experimental.pallas as pl
import jax.experimental.pallas.tpu as pltpu
import jax.numpy as jnp
from jax import lax
from jax.sharding import PartitionSpec as P

epsilon = 1e-06


def rope_tables(length, head_dim):
    half_dim = head_dim // 2
    ratios = jnp.arange(half_dim, dtype=jnp.float32) * (2.0 / head_dim)
    frequency = jnp.exp(-jnp.log(10000.0) * ratios)
    angles = jnp.arange(length, dtype=jnp.float32)[:, None] * frequency[None, :]
    return (jnp.cos(angles)[:, None, :], jnp.sin(angles)[:, None, :])


def rotate(tensor, cos_table, sin_table):
    half_dim = tensor.shape[-1] // 2
    front_half = tensor[..., :half_dim]
    back_half = tensor[..., half_dim:]
    return jnp.concatenate(
        [
            front_half * cos_table - back_half * sin_table,
            back_half * cos_table + front_half * sin_table,
        ],
        axis=-1,
    )


def unrotate(tensor, cos_table, sin_table):
    half_dim = tensor.shape[-1] // 2
    front_half = tensor[..., :half_dim]
    back_half = tensor[..., half_dim:]
    return jnp.concatenate(
        [
            front_half * cos_table + back_half * sin_table,
            back_half * cos_table - front_half * sin_table,
        ],
        axis=-1,
    )


def silu_parts(gate_in):
    sigmoid_value = jax.nn.sigmoid(gate_in)
    return (gate_in * sigmoid_value, sigmoid_value * (1.0 + gate_in * (1.0 - sigmoid_value)))


def slot_table(route_ids, experts, capacity):
    flat_ids = route_ids.reshape(-1)
    onehot = (flat_ids[:, None] == jnp.arange(experts, dtype=jnp.int32)[None, :]).astype(jnp.int32)
    before = jnp.cumsum(onehot, axis=0, dtype=jnp.int32) - onehot
    ranks = jnp.sum(before * onehot, axis=1, dtype=jnp.int32)
    places = flat_ids * capacity + ranks
    filler = jnp.arange(flat_ids.shape[0], dtype=jnp.int32) + 1
    slot_rows = jnp.zeros((experts * capacity,), jnp.int32).at[places].set(filler)
    return (places.reshape(route_ids.shape), slot_rows.reshape(experts, capacity))


def inverse_rms(tensor):
    return lax.rsqrt(jnp.mean(tensor * tensor, axis=-1, keepdims=True) + epsilon)


def norm_backward(d_normed, hat_rows, inverse, gain_vec):
    d_hat = d_normed * gain_vec
    return inverse * (d_hat - hat_rows * jnp.mean(d_hat * hat_rows, axis=-1, keepdims=True))


def masked_scores(query, keys, allowed, score_scale):
    raw = jnp.einsum("qhd,khd->hqk", query, keys, preferred_element_type=jnp.float32) * score_scale
    return jnp.where(allowed[None], raw, -1e30)


def spread(rows):
    return lax.all_gather(rows, "tp", axis=0, tiled=True)


def head_total(partial_rows):
    return lax.psum_scatter(
        partial_rows.astype(jnp.bfloat16), "tp", scatter_dimension=0, tiled=True
    ).astype(jnp.float32)


def to_experts(buffer):
    return lax.all_to_all(buffer, "fsdp", split_axis=0, concat_axis=0, tiled=True)


def from_experts(buffer):
    return lax.all_to_all(buffer, "fsdp", split_axis=0, concat_axis=0, tiled=True)


def routed_plan(
    hidden_in,
    out_grad,
    segment_ids,
    expert_ids,
    route_weights,
    attn_gain,
    ffn_gain,
    qkv_weight,
    qkv_bias,
    out_weight,
    shared_gate_up,
    shared_down,
    shared_gate_vec,
    expert_gate_up,
    expert_down,
):
    tp_rank = lax.axis_index("tp")
    experts = lax.axis_size("fsdp")
    length = segment_ids.shape[1]
    top_count = expert_ids.shape[1]
    capacity = 3 * length * top_count // (2 * experts)
    own_rows = hidden_in.shape[0]
    model_width = hidden_in.shape[1]
    qkv_full, bias_full, out_full, shared_full, shared_down_full = (
        lax.all_gather(qkv_weight, "fsdp", axis=0, tiled=True),
        lax.all_gather(qkv_bias.astype(jnp.bfloat16), "fsdp", axis=2, tiled=True).astype(
            qkv_bias.dtype
        ),
        lax.all_gather(out_weight, "fsdp", axis=1, tiled=True),
        lax.all_gather(shared_gate_up, "fsdp", axis=0, tiled=True),
        lax.all_gather(shared_down, "fsdp", axis=1, tiled=True),
    )
    local_heads = qkv_full.shape[2]
    head_dim = qkv_full.shape[3]
    score_scale = head_dim ** (-0.5)
    cos_table, sin_table = rope_tables(length, head_dim)
    positions = jnp.arange(length, dtype=jnp.int32)
    segments = segment_ids[0]
    allowed = (positions[:, None] >= positions[None, :]) & (segments[:, None] == segments[None, :])
    hidden_float = hidden_in.astype(jnp.float32)
    attn_inverse = inverse_rms(hidden_float)
    normed_one = spread((hidden_float * attn_inverse * attn_gain).astype(jnp.bfloat16))
    qkv_flat = qkv_full.reshape(model_width, -1)
    qkv = (
        jnp.dot(normed_one, qkv_flat, preferred_element_type=jnp.float32).reshape(
            length, 3, local_heads, head_dim
        )
        + bias_full
    )
    query = rotate(qkv[:, 0], cos_table, sin_table).astype(jnp.bfloat16)
    keys = rotate(qkv[:, 1], cos_table, sin_table).astype(jnp.bfloat16)
    values = qkv[:, 2].astype(jnp.bfloat16)
    scores = masked_scores(query, keys, allowed, score_scale)
    row_peak = jnp.max(scores, axis=-1, keepdims=True)
    log_total = row_peak + jnp.log(jnp.sum(jnp.exp(scores - row_peak), axis=-1, keepdims=True))
    probs_b = jnp.exp(scores - log_total).astype(jnp.bfloat16)
    heads_out = (
        jnp.einsum("hqk,khd->qhd", probs_b, values, preferred_element_type=jnp.float32)
        .astype(jnp.bfloat16)
        .reshape(length, -1)
    )
    middle = hidden_float + head_total(
        jnp.dot(heads_out, out_full, preferred_element_type=jnp.float32)
    )
    ffn_inverse = inverse_rms(middle)
    normed_two_own = (middle * ffn_inverse * ffn_gain).astype(jnp.bfloat16)
    normed_two = spread(normed_two_own)
    gate_prob = jax.nn.sigmoid(jnp.sum(normed_two.astype(jnp.float32) * shared_gate_vec, axis=-1))
    shared_flat = shared_full.reshape(model_width, -1)
    shared_width = shared_full.shape[2]
    shared_pre = jnp.dot(normed_two, shared_flat, preferred_element_type=jnp.float32)
    shared_act, shared_slope = silu_parts(shared_pre[:, :shared_width])
    shared_upper = shared_pre[:, shared_width:]
    shared_hidden = (shared_act * shared_upper).astype(jnp.bfloat16)
    shared_part = jnp.dot(shared_hidden, shared_down_full, preferred_element_type=jnp.float32)
    places, slot_rows = slot_table(expert_ids, experts, capacity)
    filled = slot_rows > 0
    route_index = jnp.maximum(slot_rows - 1, 0)
    source_rows = route_index // top_count
    flat_weights = route_weights.reshape(-1)
    slot_weights = jnp.where(filled, flat_weights[route_index], 0.0)
    send_rows = jnp.where(filled[:, :, None], normed_two[source_rows], jnp.zeros((), jnp.bfloat16))
    arrived = to_experts(send_rows).reshape(-1, model_width)
    expert_flat = expert_gate_up[0].reshape(model_width, -1)
    expert_width = expert_gate_up.shape[3]
    down_local = expert_down[0]
    expert_pre = jnp.dot(arrived, expert_flat, preferred_element_type=jnp.float32)
    expert_act, expert_slope = silu_parts(expert_pre[:, :expert_width])
    expert_upper = expert_pre[:, expert_width:]
    expert_hidden = (expert_act * expert_upper).astype(jnp.bfloat16)
    expert_part = jnp.dot(expert_hidden, down_local, preferred_element_type=jnp.float32).astype(
        jnp.bfloat16
    )
    returned = from_experts(expert_part.reshape(experts, capacity, model_width)).reshape(
        experts * capacity, model_width
    )
    picked = returned[places].astype(jnp.float32)
    token_term = gate_prob[:, None] * shared_part + jnp.sum(
        route_weights[:, :, None] * picked, axis=1
    )
    own_extra = 0.0
    total = (
        lax.psum_scatter(
            token_term.astype(jnp.bfloat16), "tp", scatter_dimension=0, tiled=True
        ).astype(jnp.float32)
        + own_extra
    )
    hidden_out = (middle + total).astype(jnp.bfloat16)
    grad_rows = spread(out_grad)
    grad_float = grad_rows.astype(jnp.float32)
    gate_part = jnp.sum(grad_float * shared_part, axis=-1)
    scaled_grad = (gate_prob[:, None] * grad_float).astype(jnp.bfloat16)
    shared_d_hidden = jnp.dot(scaled_grad, shared_down_full.T, preferred_element_type=jnp.float32)
    shared_d_cat = jnp.concatenate(
        [
            (shared_d_hidden * shared_upper * shared_slope).astype(jnp.bfloat16),
            (shared_d_hidden * shared_act).astype(jnp.bfloat16),
        ],
        axis=1,
    )
    g_shared_down = jnp.dot(shared_hidden.T, scaled_grad, preferred_element_type=jnp.float32)
    g_shared_gate_up = jnp.dot(
        normed_two.T, shared_d_cat, preferred_element_type=jnp.float32
    ).reshape(shared_full.shape)
    d_normed_part = jnp.dot(shared_d_cat, shared_flat.T, preferred_element_type=jnp.float32)
    expert_grad_in = (slot_weights[:, :, None] * grad_float[source_rows]).astype(jnp.bfloat16)
    arrived_grad = to_experts(expert_grad_in).reshape(-1, model_width)
    back_act, back_slope, back_upper, back_hidden = (
        expert_act,
        expert_slope,
        expert_upper,
        expert_hidden,
    )
    expert_d_hidden = jnp.dot(arrived_grad, down_local.T, preferred_element_type=jnp.float32)
    expert_d_cat = jnp.concatenate(
        [
            (expert_d_hidden * back_upper * back_slope).astype(jnp.bfloat16),
            (expert_d_hidden * back_act).astype(jnp.bfloat16),
        ],
        axis=1,
    )
    g_expert_down = jnp.dot(back_hidden.T, arrived_grad, preferred_element_type=jnp.float32)[None]
    g_expert_gate_up = jnp.dot(arrived.T, expert_d_cat, preferred_element_type=jnp.float32).reshape(
        expert_gate_up.shape
    )
    expert_d_part = jnp.dot(expert_d_cat, expert_flat.T, preferred_element_type=jnp.float32).astype(
        jnp.bfloat16
    )
    route_part = jnp.sum(grad_float[:, None, :] * picked, axis=-1)
    returned_grad = from_experts(expert_d_part.reshape(experts, capacity, model_width)).reshape(
        experts * capacity, model_width
    )
    d_normed_part = d_normed_part + jnp.sum(returned_grad[places].astype(jnp.float32), axis=1)
    d_normed_two, route_grad, gate_grad = (
        lax.psum_scatter(
            d_normed_part.astype(jnp.bfloat16), "tp", scatter_dimension=0, tiled=True
        ).astype(jnp.float32),
        lax.psum_scatter(
            route_part.astype(jnp.bfloat16), "tp", scatter_dimension=0, tiled=True
        ).astype(jnp.float32),
        lax.psum_scatter(
            gate_part.astype(jnp.bfloat16), "tp", scatter_dimension=0, tiled=True
        ).astype(jnp.float32),
    )
    own_gate = lax.dynamic_slice_in_dim(gate_prob, tp_rank * own_rows, own_rows)
    logit_grad = gate_grad * own_gate * (1.0 - own_gate)
    d_normed_two = d_normed_two + logit_grad[:, None] * shared_gate_vec
    g_gate_vec = jnp.sum(normed_two_own.astype(jnp.float32) * logit_grad[:, None], axis=0)
    hat_two = middle * ffn_inverse
    g_ffn_gain = jnp.sum(d_normed_two * hat_two, axis=0)
    middle_grad = out_grad.astype(jnp.float32) + norm_backward(
        d_normed_two, hat_two, ffn_inverse, ffn_gain
    )
    d_rows = spread(middle_grad.astype(jnp.bfloat16))
    g_out = jnp.dot(heads_out.T, d_rows, preferred_element_type=jnp.float32)
    d_heads = (
        jnp.dot(d_rows, out_full.T, preferred_element_type=jnp.float32)
        .astype(jnp.bfloat16)
        .reshape(length, local_heads, head_dim)
    )
    heads_three = heads_out.reshape(length, local_heads, head_dim)
    scores_again = masked_scores(query, keys, allowed, score_scale)
    probs_full = jnp.exp(scores_again - log_total)
    probs_again = probs_full.astype(jnp.bfloat16)
    d_values = jnp.einsum("hqk,qhd->khd", probs_again, d_heads, preferred_element_type=jnp.float32)
    d_probs = jnp.einsum("qhd,khd->hqk", d_heads, values, preferred_element_type=jnp.float32)
    delta = jnp.sum(d_heads.astype(jnp.float32) * heads_three.astype(jnp.float32), axis=-1)
    d_scores = (probs_full * (d_probs - delta.T[:, :, None])).astype(jnp.bfloat16)
    d_query = (
        jnp.einsum("hqk,khd->qhd", d_scores, keys, preferred_element_type=jnp.float32) * score_scale
    )
    d_keys = (
        jnp.einsum("hqk,qhd->khd", d_scores, query, preferred_element_type=jnp.float32)
        * score_scale
    )
    d_qkv = jnp.stack(
        [unrotate(d_query, cos_table, sin_table), unrotate(d_keys, cos_table, sin_table), d_values],
        axis=1,
    )
    g_bias = jnp.sum(d_qkv, axis=0)
    d_qkv_b = d_qkv.astype(jnp.bfloat16).reshape(length, -1)
    g_qkv = jnp.dot(normed_one.T, d_qkv_b, preferred_element_type=jnp.float32).reshape(
        qkv_full.shape
    )
    d_normed_one = head_total(jnp.dot(d_qkv_b, qkv_flat.T, preferred_element_type=jnp.float32))
    hat_one = hidden_float * attn_inverse
    g_attn_gain = jnp.sum(d_normed_one * hat_one, axis=0)
    hidden_grad = middle_grad + norm_backward(d_normed_one, hat_one, attn_inverse, attn_gain)
    g_qkv, g_bias, g_out, g_shared_gate_up, g_shared_down = (
        lax.psum_scatter(
            g_qkv.astype(jnp.bfloat16), "fsdp", scatter_dimension=0, tiled=True
        ).astype(jnp.float32),
        lax.psum_scatter(
            g_bias.astype(jnp.bfloat16), "fsdp", scatter_dimension=2, tiled=True
        ).astype(jnp.float32),
        lax.psum_scatter(
            g_out.astype(jnp.bfloat16), "fsdp", scatter_dimension=1, tiled=True
        ).astype(jnp.float32),
        lax.psum_scatter(
            g_shared_gate_up.astype(jnp.bfloat16), "fsdp", scatter_dimension=0, tiled=True
        ).astype(jnp.float32),
        lax.psum_scatter(
            g_shared_down.astype(jnp.bfloat16), "fsdp", scatter_dimension=1, tiled=True
        ).astype(jnp.float32),
    )
    g_attn_gain, g_ffn_gain, g_gate_vec = (
        lax.psum_scatter(g_attn_gain, ("fsdp", "tp"), scatter_dimension=0, tiled=True),
        lax.psum_scatter(g_ffn_gain, ("fsdp", "tp"), scatter_dimension=0, tiled=True),
        lax.psum_scatter(g_gate_vec, ("fsdp", "tp"), scatter_dimension=0, tiled=True),
    )
    return (
        hidden_out,
        hidden_grad,
        route_grad,
        g_attn_gain,
        g_ffn_gain,
        g_qkv,
        g_bias,
        g_out,
        g_shared_gate_up,
        g_shared_down,
        g_gate_vec,
        g_expert_gate_up,
        g_expert_down,
    )


MESH = pl.DeviceIdType.MESH


def flipped(index, bit):
    return index + bit - 2 * bit * ((index // bit) % 2)


def place():
    me = lax.axis_index("fsdp")
    rank = lax.axis_index("tp")
    return me, rank


def greet(me, rank, tp):
    barrier = pltpu.get_barrier_semaphore()
    for bit in (1, 2, 4):
        pl.semaphore_signal(
            barrier, inc=1, device_id=(flipped(me, bit), rank), device_id_type=MESH
        )

    @pl.when(rank > 0)
    def _():
        pl.semaphore_signal(barrier, inc=1, device_id=(me, rank - 1), device_id_type=MESH)

    @pl.when(rank < tp - 1)
    def _():
        pl.semaphore_signal(barrier, inc=1, device_id=(me, rank + 1), device_id_type=MESH)

    left = (rank + tp - 1) // tp
    right = (2 * (tp - 1) - rank) // tp
    pl.semaphore_wait(barrier, 3 + left + right)


def scatter_kernel(tp, parts, *refs):
    ins = refs[:parts]
    outs = refs[parts : 2 * parts]
    buffers = refs[2 * parts : 7 * parts]
    mine, other, diag_in, last_in, z_in = (
        buffers[i * parts : (i + 1) * parts] for i in range(5)
    )
    l_sem, c_send, c_recv, p_send, p_recv, z_send, z_recv = refs[7 * parts :]
    me, rank = place()
    greet(me, rank, tp)
    f32 = jnp.float32
    blocks = [rank]
    for bit in (1, 2):
        blocks = blocks + [flipped(one, bit) for one in blocks]
    blocks = blocks[::-1]
    packs = [me, flipped(me, 2), flipped(me, 4), flipped(flipped(me, 2), 4)]
    every = range(parts)
    rows = [ref.shape[0] for ref in outs]
    low = [pl.ds(0, count // 2) for count in rows]
    high = [pl.ds(count // 2, count // 2) for count in rows]

    def region(i, pack, block):
        return ins[i].at[pl.ds((pack * tp + block) * rows[i], rows[i])]

    def local(k, j, i):
        return pltpu.make_async_copy(
            region(i, packs[k], blocks[j]), mine[i].at[k, j], l_sem.at[k, j, i]
        )

    def core(k, j, i):
        return pltpu.make_async_remote_copy(
            src_ref=region(i, flipped(packs[k], 1), blocks[j]),
            dst_ref=other[i].at[k, j],
            send_sem=c_send.at[k, j, i],
            recv_sem=c_recv.at[k, j, i],
            device_id=(flipped(me, 1), rank),
            device_id_type=MESH,
        )

    def across(bit, src, dst, slot, j, i):
        return pltpu.make_async_remote_copy(
            src_ref=src,
            dst_ref=dst,
            send_sem=p_send.at[slot, j, i],
            recv_sem=p_recv.at[slot, j, i],
            device_id=(flipped(me, bit), rank),
            device_id_type=MESH,
        )

    def diag_x(j, i):
        return across(2, mine[i].at[3, j, low[i]], diag_in[i].at[j, 0], 0, j, i)

    def diag_y(j, i):
        return across(4, mine[i].at[3, j, high[i]], diag_in[i].at[j, 1], 1, j, i)

    def direct_x(j, i):
        return across(2, mine[i].at[1, j, low[i]], last_in[i].at[j, 0, low[i]], 2, j, i)

    def direct_y(j, i):
        return across(4, mine[i].at[2, j, high[i]], last_in[i].at[j, 1, high[i]], 3, j, i)

    def summed_x(j, i):
        return across(2, mine[i].at[1, j, high[i]], last_in[i].at[j, 0, high[i]], 4, j, i)

    def summed_y(j, i):
        return across(4, mine[i].at[2, j, low[i]], last_in[i].at[j, 1, low[i]], 5, j, i)

    def along_z(j, right, i):
        way = 0 if right else 1
        block = blocks[j]
        return pltpu.make_async_remote_copy(
            src_ref=mine[i].at[0, j],
            dst_ref=z_in[i].at[way, block],
            send_sem=z_send.at[way, block, i],
            recv_sem=z_recv.at[way, block, i],
            device_id=(me, rank + 1 if right else rank - 1),
            device_id_type=MESH,
        )

    for j in range(tp):
        for k in (3, 2, 1, 0):
            for i in every:
                core(k, j, i).start()
                local(k, j, i).start()

    def add(ref, spot, one):
        ref[spot] = (ref[spot].astype(f32) + one.astype(f32)).astype(ref.dtype)

    def first(j):
        for k in (3, 2, 1, 0):
            for i in every:
                core(k, j, i).wait_recv()
                local(k, j, i).wait()
                add(mine[i], (k, j), other[i][k, j])
                if k == 3:
                    diag_x(j, i).start()
                    diag_y(j, i).start()
                if k == 2:
                    direct_y(j, i).start()
                if k == 1:
                    direct_x(j, i).start()

    def second(j):
        for i in every:
            diag_x(j, i).wait_recv()
            add(mine[i], (2, j, low[i]), diag_in[i][j, 0])
            summed_y(j, i).start()
            diag_y(j, i).wait_recv()
            add(mine[i], (1, j, high[i]), diag_in[i][j, 1])
            summed_x(j, i).start()

    def third(j):
        block = blocks[j]
        for i in every:
            direct_x(j, i).wait_recv()
            direct_y(j, i).wait_recv()
            summed_x(j, i).wait_recv()
            summed_y(j, i).wait_recv()
            total = (
                mine[i][0, j].astype(f32)
                + last_in[i][j, 0].astype(f32)
                + last_in[i][j, 1].astype(f32)
            )
            if j < tp - 1:
                mine[i][0, j] = total.astype(mine[i].dtype)
            else:
                outs[i][...] = total
        if j < tp - 1:

            @pl.when((block > rank) & (rank > 0))
            def _():
                for i in every:
                    along_z(j, True, i).wait_recv()
                    add(mine[i], (0, j), z_in[i][0, block])

            @pl.when((block < rank) & (rank < tp - 1))
            def _():
                for i in every:
                    along_z(j, False, i).wait_recv()
                    add(mine[i], (0, j), z_in[i][1, block])

            @pl.when(block > rank)
            def _():
                for i in every:
                    along_z(j, True, i).start()

            @pl.when(block < rank)
            def _():
                for i in every:
                    along_z(j, False, i).start()
        else:

            @pl.when(rank > 0)
            def _():
                for i in every:
                    along_z(j, True, i).wait_recv()
                    outs[i][...] += z_in[i][0, block].astype(f32)

            @pl.when(rank < tp - 1)
            def _():
                for i in every:
                    along_z(j, False, i).wait_recv()
                    outs[i][...] += z_in[i][1, block].astype(f32)

    first(0)
    first(1)
    second(0)
    first(2)
    second(1)
    third(0)
    first(3)
    second(2)
    third(1)
    second(3)
    third(2)
    third(3)
    for j in range(tp):
        for i in every:
            for k in range(4):
                core(k, j, i).wait_send()
            for copy in (diag_x, diag_y, direct_x, direct_y, summed_x, summed_y):
                copy(j, i).wait_send()
        block = blocks[j]
        if j < tp - 1:

            @pl.when(block > rank)
            def _():
                for i in every:
                    along_z(j, True, i).wait_send()

            @pl.when(block < rank)
            def _():
                for i in every:
                    along_z(j, False, i).wait_send()


def scatter_sum(arrays, fsdp, tp, collective_id):
    parts = len(arrays)
    shapes = [(one.shape[0] // (fsdp * tp), one.shape[1]) for one in arrays]
    kind = arrays[0].dtype
    scratch = [pltpu.VMEM((4, tp, rows, width), kind) for rows, width in shapes]
    scratch += [pltpu.VMEM((4, tp, rows, width), kind) for rows, width in shapes]
    scratch += [pltpu.VMEM((tp, 2, rows // 2, width), kind) for rows, width in shapes]
    scratch += [pltpu.VMEM((tp, 2, rows, width), kind) for rows, width in shapes]
    scratch += [pltpu.VMEM((2, tp, rows, width), kind) for rows, width in shapes]
    return pl.pallas_call(
        functools.partial(scatter_kernel, tp, parts),
        out_shape=[jax.ShapeDtypeStruct(shape, jnp.float32) for shape in shapes],
        in_specs=[pl.BlockSpec(memory_space=pl.ANY)] * parts,
        out_specs=[pl.BlockSpec(memory_space=pltpu.VMEM)] * parts,
        scratch_shapes=scratch
        + [
            pltpu.SemaphoreType.DMA((4, tp, parts)),
            pltpu.SemaphoreType.DMA((4, tp, parts)),
            pltpu.SemaphoreType.DMA((4, tp, parts)),
            pltpu.SemaphoreType.DMA((6, tp, parts)),
            pltpu.SemaphoreType.DMA((6, tp, parts)),
            pltpu.SemaphoreType.DMA((2, tp, parts)),
            pltpu.SemaphoreType.DMA((2, tp, parts)),
        ],
        compiler_params=pltpu.CompilerParams(
            collective_id=collective_id, has_side_effects=True, vmem_limit_bytes=48 << 20
        ),
        name="scatter_rows",
    )(*arrays)


UNIT = 640
NT = (((1,), (1,)), ((), ()))


def ffn_kernel(tp, expert_width, shared_width, *refs):
    own_ref, grad_ref, both_ref, down_ref, scale_ref = refs[:5]
    all_ref, d_ref, hid_ref, y_ref, dsum_ref, esum_ref = refs[5:11]
    (
        g_buf, x_buf, dh_buf, d_buf, h_buf, stage, acc, diag_in, last_in, z_in,
        stage_e, acc_e, other_e, diag_e, last_e, z_in_e,
        local_sem, g_sem, x_sem, d_sem, h_sem, y_sem,
        az_send, az_recv, ap_send, ap_recv,
        c_send, c_recv, ce_send, ce_recv, p_send, p_recv, pe_send, pe_recv,
        z_send, z_recv, ze_send, ze_recv,
    ) = refs[11:]
    me, rank = place()
    greet(me, rank, tp)
    f32 = jnp.float32
    bf16 = jnp.bfloat16
    rows = own_ref.shape[0]
    pack_rows = rows * tp
    tile = pack_rows // 2
    near = rank // 2
    tokens = all_ref.shape[0]

    def region(pack, block, start=0, count=None):
        count = rows if count is None else count
        return all_ref.at[pl.ds(pack * pack_rows + block * rows + start, count)]

    def gather_z(block, right):
        way = 0 if right else 1
        ref = region(me, block)
        return pltpu.make_async_remote_copy(
            src_ref=ref,
            dst_ref=ref,
            send_sem=az_send.at[way, block],
            recv_sem=az_recv.at[way, block],
            device_id=(me, rank + 1 if right else rank - 1),
            device_id_type=MESH,
        )

    def gather(bit, pack_bits, block, slot, start=0, count=None):
        pack = me
        for one in (2, 4):
            if pack_bits & one:
                pack = flipped(pack, one)
        ref = region(pack, block, start, count)
        return pltpu.make_async_remote_copy(
            src_ref=ref,
            dst_ref=ref,
            send_sem=ap_send.at[slot, block],
            recv_sem=ap_recv.at[slot, block],
            device_id=(flipped(me, bit), rank),
            device_id_type=MESH,
        )

    def to_core(q, block):
        return gather(1, 2 * q, block, q)

    def own_x(block):
        return gather(2, 0, block, 4)

    def own_y(block):
        return gather(4, 0, block, 5)

    def x_to_y(block):
        return gather(4, 2, block, 6, 0, rows // 2)

    def y_to_x(block):
        return gather(2, 4, block, 7, rows // 2, rows // 2)

    def start_plane(block):
        own_x(block).start()
        own_y(block).start()
        to_core(0, block).start()

    def forward(block):
        own_x(block).wait_recv()
        x_to_y(block).start()
        to_core(1, block).start()
        own_y(block).wait_recv()
        y_to_x(block).start()
        to_core(2, block).start()

    def finish(block):
        x_to_y(block).wait_recv()
        y_to_x(block).wait_recv()
        to_core(3, block).start()

    def z_step(step):
        @pl.when(rank >= step)
        def _():
            block = rank - step
            gather_z(block, True).wait_recv()

            @pl.when(rank < tp - 1)
            def _():
                gather_z(block, True).start()

            start_plane(block)

        @pl.when(rank + step < tp)
        def _():
            block = rank + step
            gather_z(block, False).wait_recv()

            @pl.when(rank > 0)
            def _():
                gather_z(block, False).start()

            start_plane(block)

    order = [rank]
    for bit in (1, 2):
        order = order + [flipped(one, bit) for one in order]

    def control(i):
        steps = {
            0: [(forward, order[0])],
            1: [(z_step, 2), (forward, order[1])],
            2: [(z_step, 3)],
            3: [(finish, order[0])],
            4: [(finish, order[1])],
            5: [(forward, order[2])],
            7: [(forward, order[3])],
            8: [(finish, order[2])],
            11: [(finish, order[3])],
        }
        for at, todo in steps.items():

            @pl.when(i == at)
            def _():
                for act, what in todo:
                    act(what)

    def core(q, h):
        return pltpu.make_async_remote_copy(
            src_ref=stage.at[h],
            dst_ref=acc.at[q, h],
            send_sem=c_send.at[q, h],
            recv_sem=c_recv.at[q, h],
            device_id=(flipped(me, 1), rank),
            device_id_type=MESH,
        )

    def core_e(q):
        return pltpu.make_async_remote_copy(
            src_ref=stage_e.at[q],
            dst_ref=other_e.at[q],
            send_sem=ce_send.at[q],
            recv_sem=ce_recv.at[q],
            device_id=(flipped(me, 1), rank),
            device_id_type=MESH,
        )

    def across(bit, src, dst, slot, h):
        return pltpu.make_async_remote_copy(
            src_ref=src,
            dst_ref=dst,
            send_sem=p_send.at[slot, h],
            recv_sem=p_recv.at[slot, h],
            device_id=(flipped(me, bit), rank),
            device_id_type=MESH,
        )

    def diag_x(h):
        return across(2, acc.at[3, h, 0], diag_in.at[h, 0], 0, h)

    def diag_y(h):
        return across(4, acc.at[3, h, 1], diag_in.at[h, 1], 1, h)

    def direct_x(h):
        return across(2, acc.at[1, h, 0], last_in.at[h, 0, 0], 2, h)

    def direct_y(h):
        return across(4, acc.at[2, h, 1], last_in.at[h, 1, 1], 3, h)

    def summed_x(h):
        return across(2, acc.at[1, h, 1], last_in.at[h, 0, 1], 4, h)

    def summed_y(h):
        return across(4, acc.at[2, h, 0], last_in.at[h, 1, 0], 5, h)

    def across_e(bit, src, dst, slot):
        return pltpu.make_async_remote_copy(
            src_ref=src,
            dst_ref=dst,
            send_sem=pe_send.at[slot],
            recv_sem=pe_recv.at[slot],
            device_id=(flipped(me, bit), rank),
            device_id_type=MESH,
        )

    def diag_lines():
        return across_e(2, acc_e.at[3], diag_e, 0)

    def direct_lines():
        return across_e(2, acc_e.at[1], last_e.at[0], 1)

    def summed_lines():
        return across_e(4, acc_e.at[2], last_e.at[1], 2)

    blocks = order[::-1]

    def along_z(j, right):
        way = 0 if right else 1
        block = blocks[j]
        return pltpu.make_async_remote_copy(
            src_ref=acc.at[0, j // 2, block % 2],
            dst_ref=z_in.at[way, block],
            send_sem=z_send.at[way, block],
            recv_sem=z_recv.at[way, block],
            device_id=(me, rank + 1 if right else rank - 1),
            device_id_type=MESH,
        )

    def along_z_e(j, right):
        way = 0 if right else 1
        block = blocks[j]
        return pltpu.make_async_remote_copy(
            src_ref=acc_e.at[0, block],
            dst_ref=z_in_e.at[way, block],
            send_sem=ze_send.at[way, block],
            recv_sem=ze_recv.at[way, block],
            device_id=(me, rank + 1 if right else rank - 1),
            device_id_type=MESH,
        )

    def add(ref, spot, one):
        ref[spot] = (ref[spot].astype(f32) + one.astype(f32)).astype(ref.dtype)

    def second(h):
        diag_x(h).wait_recv()
        add(acc, (2, h, 0), diag_in[h, 0])
        summed_y(h).start()
        diag_y(h).wait_recv()
        add(acc, (1, h, 1), diag_in[h, 1])
        summed_x(h).start()

    def third(j):
        h = j // 2
        block = blocks[j]
        part = block % 2
        if j % 2 == 0:
            direct_x(h).wait_recv()
            direct_y(h).wait_recv()
            summed_x(h).wait_recv()
            summed_y(h).wait_recv()
        if j == 0:
            direct_lines().wait_recv()
            summed_lines().wait_recv()
        total = (
            acc[0, h, part].astype(f32)
            + last_in[h, 0, part].astype(f32)
            + last_in[h, 1, part].astype(f32)
        )
        lines = acc_e[0, block] + last_e[0, block] + last_e[1, block]
        if j < tp - 1:
            acc[0, h, part] = total.astype(bf16)
            acc_e[0, block] = lines

            @pl.when((block > rank) & (rank > 0))
            def _():
                along_z(j, True).wait_recv()
                along_z_e(j, True).wait_recv()
                add(acc, (0, h, part), z_in[0, block])
                add(acc_e, (0, block), z_in_e[0, block])

            @pl.when((block < rank) & (rank < tp - 1))
            def _():
                along_z(j, False).wait_recv()
                along_z_e(j, False).wait_recv()
                add(acc, (0, h, part), z_in[1, block])
                add(acc_e, (0, block), z_in_e[1, block])

            @pl.when(block > rank)
            def _():
                along_z(j, True).start()
                along_z_e(j, True).start()

            @pl.when(block < rank)
            def _():
                along_z(j, False).start()
                along_z_e(j, False).start()
        else:
            dsum_ref[...] = total
            esum_ref[...] = lines

            @pl.when(rank > 0)
            def _():
                along_z(j, True).wait_recv()
                along_z_e(j, True).wait_recv()
                dsum_ref[...] += z_in[0, block].astype(f32)
                esum_ref[...] += z_in_e[0, block]

            @pl.when(rank < tp - 1)
            def _():
                along_z(j, False).wait_recv()
                along_z_e(j, False).wait_recv()
                dsum_ref[...] += z_in[1, block].astype(f32)
                esum_ref[...] += z_in_e[1, block]

    def grad_load(n, slot):
        return pltpu.make_async_copy(
            grad_ref.at[pl.ds(n * pack_rows, pack_rows)], g_buf.at[slot], g_sem.at[slot]
        )

    def hidden_grads(first, last):
        def body(n, carry):
            slot = n % 2

            @pl.when(n + 1 < tokens // pack_rows)
            def _():
                grad_load(n + 1, 1 - slot).start()

            grad_load(n, slot).wait()
            dh_buf[pl.ds(n * pack_rows, pack_rows), :] = lax.dot_general(
                g_buf[slot], down_ref[...], NT, preferred_element_type=f32
            ).astype(bf16)
            return carry

        lax.fori_loop(first, last, body, 0)

    core_of, x_of, y_of = me % 2, (me // 2) % 2, me // 4

    def tile_of(i):
        t = i // 2
        o = i % 2
        s = t // 6
        q = (1 - s) * (t % 3) + 3 * s
        h = (1 - s) * (1 - t // 3) + s * (t - 6)
        pack = (
            4 * ((y_of + q // 2) % 2) + 2 * ((x_of + q % 2) % 2) + (core_of + 1 - o) % 2
        )
        half = h * near + (1 - h) * (1 - near)
        return q, o, h, pack, half

    def tile_rows(pack, half):
        return pl.ds(pl.multiple_of(pack * pack_rows + half * tile, tile), tile)

    def row_load(i):
        q, o, h, pack, half = tile_of(i)
        return pltpu.make_async_copy(
            all_ref.at[tile_rows(pack, half)], x_buf.at[i % 2], x_sem.at[i % 2]
        )

    def prefetch(i):
        q, o, h, pack, half = tile_of(i)

        @pl.when(o == 0)
        def _():
            for part in range(2):
                block = 2 * half + part
                ref = region(pack, block)
                pltpu.make_async_remote_copy(
                    src_ref=ref,
                    dst_ref=ref,
                    send_sem=ap_send.at[q, block],
                    recv_sem=ap_recv.at[q, block],
                    device_id=(flipped(me, 1), rank),
                    device_id_type=MESH,
                ).wait_recv()

        row_load(i).start()

    def d_store(i):
        q, o, h, pack, half = tile_of(i)
        return pltpu.make_async_copy(
            d_buf.at[i % 2], d_ref.at[tile_rows(pack, half)], d_sem.at[i % 2]
        )

    units = expert_width + shared_width

    def one_tile(i, carry):
        q, o, h, pack, half = tile_of(i)
        slot = i % 2
        at = tile_rows(pack, half)
        row_load(i).wait()

        @pl.when(i >= 2)
        def _():
            d_store(i - 2).wait()

        pre = jnp.dot(x_buf[slot], both_ref[...], preferred_element_type=f32)
        gate, upper = pre[:, :UNIT], pre[:, UNIT:]
        lane = lax.broadcasted_iota(jnp.int32, (1, UNIT), 1)
        logit = gate[:, units : units + 1] + gate[:, units + 1 : units + 2]
        gate_prob = 1.0 / (1.0 + jnp.exp(-logit))
        scale = jnp.where(
            lane < expert_width, scale_ref[at, :], jnp.where(lane < units, gate_prob, 0.0)
        )
        sigmoid = 1.0 / (1.0 + jnp.exp(-gate))
        act = gate * sigmoid
        slope = sigmoid * (1.0 + gate * (1.0 - sigmoid))
        hidden = act * upper
        d_hidden = dh_buf[at, :].astype(f32)
        line = lax.broadcasted_iota(jnp.int32, (16, UNIT), 0)
        unit = lax.broadcasted_iota(jnp.int32, (16, UNIT), 1)
        of_expert = (line == me) & (unit < expert_width)
        of_shared = (line == 8) & (unit >= expert_width)
        pick = jnp.where(of_expert | of_shared, 1.0, 0.0).astype(bf16)
        lines = lax.dot_general(
            pick, (d_hidden * hidden).astype(bf16), NT, preferred_element_type=f32
        )
        h_buf[at, :] = (hidden * scale).astype(bf16)
        d_scaled = d_hidden * scale
        d_buf[slot, :, :UNIT] = (d_scaled * upper * slope).astype(bf16)
        d_buf[slot, :, UNIT:] = (d_scaled * act).astype(bf16)
        control(i)

        @pl.when(i < 15)
        def _():
            prefetch(i + 1)

        d_rows = lax.dot_general(d_buf[slot], both_ref[...], NT, preferred_element_type=f32)
        d_store(i).start()

        @pl.when(o == 0)
        def _():
            @pl.when(q > 0)
            def _():
                core(q - 1, h).wait_send()

            for part in range(2):
                stage[h, part] = d_rows[part * rows : (part + 1) * rows].astype(bf16)
                stage_e[q, 2 * half + part] = lines[:, part * rows : (part + 1) * rows]
            core(q, h).start()

            @pl.when(((h == 0) & (q < 3)) | ((h == 1) & (q == 3)))
            def _():
                core_e(q).start()

        @pl.when(o == 1)
        def _():
            core(q, h).wait_recv()
            for part in range(2):
                add(acc, (q, h, part), d_rows[part * rows : (part + 1) * rows])
                acc_e[q, 2 * half + part] = lines[:, part * rows : (part + 1) * rows]

            @pl.when(((h == 0) & (q < 3)) | ((h == 1) & (q == 3)))
            def _():
                core_e(q).wait_recv()
                acc_e[q] = acc_e[q] + other_e[q]

                @pl.when(q == 1)
                def _():
                    direct_lines().start()

                @pl.when(q == 3)
                def _():
                    diag_lines().start()

            @pl.when(q == 1)
            def _():
                direct_x(h).start()

            @pl.when(q == 2)
            def _():
                direct_y(h).start()

            @pl.when(q == 3)
            def _():
                diag_x(h).start()
                diag_y(h).start()

        return carry

    def y_store(n, slot):
        return pltpu.make_async_copy(
            g_buf.at[slot], y_ref.at[pl.ds(n * pack_rows, pack_rows)], y_sem.at[slot]
        )

    def outputs(first, last):
        def body(n, carry):
            slot = n % 2

            @pl.when(n >= 2)
            def _():
                y_store(n - 2, slot).wait()

            g_buf[slot] = jnp.dot(
                h_buf[pl.ds(n * pack_rows, pack_rows), :],
                down_ref[...],
                preferred_element_type=f32,
            ).astype(bf16)
            y_store(n, slot).start()
            return carry

        lax.fori_loop(first, last, body, 0)

    grad_load(0, 0).start()
    mine = pltpu.make_async_copy(own_ref, region(me, rank), local_sem)
    mine.start()
    mine.wait()

    @pl.when(rank < tp - 1)
    def _():
        gather_z(rank, True).start()

    @pl.when(rank > 0)
    def _():
        gather_z(rank, False).start()

    start_plane(rank)
    packs = tokens // pack_rows
    hidden_grads(0, 5)
    z_step(1)
    hidden_grads(5, packs)
    prefetch(0)
    lax.fori_loop(0, 16, one_tile, 0)
    hidden_store = pltpu.make_async_copy(h_buf, hid_ref, h_sem)
    hidden_store.start()
    outputs(0, 4)
    second(0)
    outputs(4, 6)
    diag_lines().wait_recv()
    acc_e[2] = acc_e[2] + diag_e[...]
    summed_lines().start()
    second(1)
    outputs(6, packs)
    third(0)
    third(1)
    third(2)
    third(3)

    hidden_store.wait()
    for n in (packs - 2, packs - 1):
        y_store(n, n % 2).wait()
    for i in (14, 15):
        d_store(i).wait()
    core(3, 0).wait_send()
    core(3, 1).wait_send()
    for q in range(4):
        core_e(q).wait_send()
    for copy in (diag_lines, direct_lines, summed_lines):
        copy().wait_send()
    for h in range(2):
        for copy in (diag_x, diag_y, direct_x, direct_y, summed_x, summed_y):
            copy(h).wait_send()
    for block in order:
        for q in range(4):
            to_core(q, block).wait_send()
        for copy in (own_x, own_y, x_to_y, y_to_x):
            copy(block).wait_send()
    for j in range(tp - 1):
        block = blocks[j]

        @pl.when(block > rank)
        def _():
            along_z(j, True).wait_send()
            along_z_e(j, True).wait_send()

        @pl.when(block < rank)
        def _():
            along_z(j, False).wait_send()
            along_z_e(j, False).wait_send()

    for block in range(tp):

        @pl.when((block <= rank) & (rank < tp - 1))
        def _():
            gather_z(block, True).wait_send()

        @pl.when((block >= rank) & (rank > 0))
        def _():
            gather_z(block, False).wait_send()


def ffn(own, grad_all, both, down, scale, fsdp, tp, expert_width, shared_width, collective_id):
    rows, width = own.shape
    tokens = rows * fsdp * tp
    pack_rows = rows * tp
    tile = pack_rows // 2
    bf16 = jnp.bfloat16
    f32 = jnp.float32
    dma = pltpu.SemaphoreType.DMA
    anywhere = pl.BlockSpec(memory_space=pl.ANY)
    vmem = pl.BlockSpec(memory_space=pltpu.VMEM)
    return pl.pallas_call(
        functools.partial(ffn_kernel, tp, expert_width, shared_width),
        out_shape=[
            jax.ShapeDtypeStruct((tokens, width), bf16),
            jax.ShapeDtypeStruct((tokens, 2 * UNIT), bf16),
            jax.ShapeDtypeStruct((tokens, UNIT), bf16),
            jax.ShapeDtypeStruct((tokens, width), bf16),
            jax.ShapeDtypeStruct((rows, width), f32),
            jax.ShapeDtypeStruct((16, rows), f32),
        ],
        in_specs=[anywhere, anywhere, vmem, vmem, vmem],
        out_specs=[anywhere, anywhere, anywhere, anywhere, vmem, vmem],
        scratch_shapes=[
            pltpu.VMEM((2, pack_rows, width), bf16),
            pltpu.VMEM((2, tile, width), bf16),
            pltpu.VMEM((tokens, UNIT), bf16),
            pltpu.VMEM((2, tile, 2 * UNIT), bf16),
            pltpu.VMEM((tokens, UNIT), bf16),
            pltpu.VMEM((2, 2, rows, width), bf16),
            pltpu.VMEM((4, 2, 2, rows, width), bf16),
            pltpu.VMEM((2, 2, rows, width), bf16),
            pltpu.VMEM((2, 2, 2, rows, width), bf16),
            pltpu.VMEM((2, tp, rows, width), bf16),
            pltpu.VMEM((4, tp, 16, rows), f32),
            pltpu.VMEM((4, tp, 16, rows), f32),
            pltpu.VMEM((4, tp, 16, rows), f32),
            pltpu.VMEM((tp, 16, rows), f32),
            pltpu.VMEM((2, tp, 16, rows), f32),
            pltpu.VMEM((2, tp, 16, rows), f32),
            dma, dma((2,)), dma((2,)), dma((2,)), dma, dma((2,)),
            dma((2, tp)), dma((2, tp)), dma((8, tp)), dma((8, tp)),
            dma((4, 2)), dma((4, 2)), dma((4,)), dma((4,)),
            dma((6, 2)), dma((6, 2)), dma((3,)), dma((3,)),
            dma((2, tp)), dma((2, tp)), dma((2, tp)), dma((2, tp)),
        ],
        compiler_params=pltpu.CompilerParams(
            collective_id=collective_id, has_side_effects=True, vmem_limit_bytes=61 << 20
        ),
        name="ffn",
    )(own, grad_all, both, down, scale)


def dense_plan(
    hidden_in,
    out_grad,
    segment_ids,
    expert_ids,
    route_weights,
    attn_gain,
    ffn_gain,
    qkv_weight,
    qkv_bias,
    out_weight,
    shared_gate_up,
    shared_down,
    shared_gate_vec,
    expert_gate_up,
    expert_down,
):
    every = ("fsdp", "tp")
    tp_rank = lax.axis_index("tp")
    experts = lax.axis_size("fsdp")
    packs = experts
    length = segment_ids.shape[1]
    own_rows = hidden_in.shape[0]
    model_width = hidden_in.shape[1]
    bf16 = jnp.bfloat16
    f32 = jnp.float32

    grad_all = lax.all_gather(out_grad, every, axis=0, tiled=True)
    qkv_full = lax.all_gather(qkv_weight, "fsdp", axis=0, tiled=True)
    bias_full = lax.all_gather(qkv_bias.astype(bf16), "fsdp", axis=2, tiled=True).astype(f32)
    out_full = lax.all_gather(out_weight, "fsdp", axis=1, tiled=True)
    shared_up = lax.all_to_all(shared_gate_up, "fsdp", split_axis=2, concat_axis=0, tiled=True)
    shared_dn = lax.all_to_all(shared_down, "fsdp", split_axis=0, concat_axis=1, tiled=True)
    expert_up = expert_gate_up[0]
    expert_dn = expert_down[0]
    expert_width = expert_up.shape[2]
    shared_width = shared_up.shape[2]

    chosen = expert_ids[:, :, None] == jnp.arange(experts, dtype=jnp.int32)
    table = jnp.sum(jnp.where(chosen, route_weights[:, :, None], 0.0), axis=1)
    expert_scale = lax.all_to_all(table.T, "fsdp", split_axis=0, concat_axis=0, tiled=True)
    expert_scale = expert_scale.reshape(-1)

    local_heads = qkv_full.shape[2]
    head_dim = qkv_full.shape[3]
    score_scale = head_dim ** (-0.5)
    cos_table, sin_table = rope_tables(length, head_dim)
    positions = jnp.arange(length, dtype=jnp.int32)
    segments = segment_ids[0]
    allowed = (positions[:, None] >= positions[None, :]) & (segments[:, None] == segments[None, :])
    hidden_float = hidden_in.astype(f32)
    attn_inverse = inverse_rms(hidden_float)
    normed_one = spread((hidden_float * attn_inverse * attn_gain).astype(bf16))
    qkv_flat = qkv_full.reshape(model_width, -1)
    qkv = (
        jnp.dot(normed_one, qkv_flat, preferred_element_type=f32).reshape(
            length, 3, local_heads, head_dim
        )
        + bias_full
    )
    query = rotate(qkv[:, 0], cos_table, sin_table).astype(bf16)
    keys = rotate(qkv[:, 1], cos_table, sin_table).astype(bf16)
    values = qkv[:, 2].astype(bf16)
    scores = masked_scores(query, keys, allowed, score_scale)
    row_peak = jnp.max(scores, axis=-1, keepdims=True)
    log_total = row_peak + jnp.log(jnp.sum(jnp.exp(scores - row_peak), axis=-1, keepdims=True))
    probs_b = jnp.exp(scores - log_total).astype(bf16)
    heads_out = (
        jnp.einsum("hqk,khd->qhd", probs_b, values, preferred_element_type=f32)
        .astype(bf16)
        .reshape(length, -1)
    )
    middle = hidden_float + head_total(jnp.dot(heads_out, out_full, preferred_element_type=f32))
    ffn_inverse = inverse_rms(middle)
    normed_two_own = (middle * ffn_inverse * ffn_gain).astype(bf16)

    vec_high = shared_gate_vec.astype(bf16)
    vec_low = (shared_gate_vec - vec_high.astype(f32)).astype(bf16)
    units = expert_width + shared_width
    none = jnp.zeros((model_width, UNIT - units), bf16)
    both_w = jnp.concatenate(
        [
            expert_up[:, 0],
            shared_up[:, 0],
            vec_high[:, None],
            vec_low[:, None],
            none[:, 2:],
            expert_up[:, 1],
            shared_up[:, 1],
            none,
        ],
        axis=1,
    )
    down_w = jnp.concatenate([expert_dn, shared_dn, none.T], axis=0)
    normed_all, d_all, hidden_all, token_part, d_normed_two, extra_sum = ffn(
        normed_two_own,
        grad_all,
        both_w,
        down_w,
        expert_scale[:, None],
        experts,
        lax.axis_size("tp"),
        expert_width,
        shared_width,
        1,
    )
    (total,) = scatter_sum([token_part], experts, lax.axis_size("tp"), 3)
    hidden_out = (middle + total).astype(bf16)
    own_start = tp_rank * own_rows
    ids_own = lax.dynamic_slice_in_dim(expert_ids, own_start, own_rows)
    picked = ids_own[:, :, None] == jnp.arange(experts, dtype=jnp.int32)
    route_grad = jnp.sum(jnp.where(picked, extra_sum[:experts].T[:, None, :], 0.0), axis=-1)
    gate_grad = extra_sum[experts]
    g_down = jnp.dot(hidden_all.T, grad_all, preferred_element_type=f32)
    g_both = jnp.dot(normed_all.T, d_all, preferred_element_type=f32)
    g_expert_down = g_down[:expert_width][None]
    g_expert_gate_up = jnp.stack(
        [g_both[:, :expert_width], g_both[:, UNIT : UNIT + expert_width]], axis=1
    )[None]
    g_shared_gate_up = lax.all_to_all(
        jnp.stack(
            [g_both[:, expert_width:units], g_both[:, UNIT + expert_width : UNIT + units]], axis=1
        ).astype(bf16),
        "fsdp",
        split_axis=0,
        concat_axis=2,
        tiled=True,
    ).astype(f32)
    g_shared_down = lax.all_to_all(
        g_down[expert_width:units].astype(bf16), "fsdp", split_axis=1, concat_axis=0, tiled=True
    ).astype(f32)

    own_gate = jax.nn.sigmoid(jnp.sum(normed_two_own.astype(f32) * shared_gate_vec, axis=-1))
    logit_grad = gate_grad * own_gate * (1.0 - own_gate)
    d_normed_two = d_normed_two + logit_grad[:, None] * shared_gate_vec
    g_gate_vec = jnp.sum(normed_two_own.astype(f32) * logit_grad[:, None], axis=0)
    hat_two = middle * ffn_inverse
    g_ffn_gain = jnp.sum(d_normed_two * hat_two, axis=0)
    middle_grad = out_grad.astype(f32) + norm_backward(d_normed_two, hat_two, ffn_inverse, ffn_gain)
    d_rows = spread(middle_grad.astype(bf16))
    g_out = jnp.dot(heads_out.T, d_rows, preferred_element_type=f32)
    d_heads = (
        jnp.dot(d_rows, out_full.T, preferred_element_type=f32)
        .astype(bf16)
        .reshape(length, local_heads, head_dim)
    )
    heads_three = heads_out.reshape(length, local_heads, head_dim)
    scores_again = masked_scores(query, keys, allowed, score_scale)
    probs_full = jnp.exp(scores_again - log_total)
    probs_again = probs_full.astype(bf16)
    d_values = jnp.einsum("hqk,qhd->khd", probs_again, d_heads, preferred_element_type=f32)
    d_probs = jnp.einsum("qhd,khd->hqk", d_heads, values, preferred_element_type=f32)
    delta = jnp.sum(d_heads.astype(f32) * heads_three.astype(f32), axis=-1)
    d_scores = (probs_full * (d_probs - delta.T[:, :, None])).astype(bf16)
    d_query = jnp.einsum("hqk,khd->qhd", d_scores, keys, preferred_element_type=f32) * score_scale
    d_keys = jnp.einsum("hqk,qhd->khd", d_scores, query, preferred_element_type=f32) * score_scale
    d_qkv = jnp.stack(
        [unrotate(d_query, cos_table, sin_table), unrotate(d_keys, cos_table, sin_table), d_values],
        axis=1,
    )
    g_bias = jnp.sum(d_qkv, axis=0)
    d_qkv_b = d_qkv.astype(bf16).reshape(length, -1)
    g_qkv = jnp.dot(normed_one.T, d_qkv_b, preferred_element_type=f32).reshape(qkv_full.shape)
    d_normed_one = head_total(jnp.dot(d_qkv_b, qkv_flat.T, preferred_element_type=f32))
    hat_one = hidden_float * attn_inverse
    g_attn_gain = jnp.sum(d_normed_one * hat_one, axis=0)
    hidden_grad = middle_grad + norm_backward(d_normed_one, hat_one, attn_inverse, attn_gain)
    g_qkv, g_bias, g_out = (
        lax.psum_scatter(g_qkv.astype(bf16), "fsdp", scatter_dimension=0, tiled=True).astype(f32),
        lax.psum_scatter(g_bias.astype(bf16), "fsdp", scatter_dimension=2, tiled=True).astype(f32),
        lax.psum_scatter(g_out.astype(bf16), "fsdp", scatter_dimension=1, tiled=True).astype(f32),
    )
    g_attn_gain, g_ffn_gain, g_gate_vec = (
        lax.psum_scatter(g_attn_gain, every, scatter_dimension=0, tiled=True),
        lax.psum_scatter(g_ffn_gain, every, scatter_dimension=0, tiled=True),
        lax.psum_scatter(g_gate_vec, every, scatter_dimension=0, tiled=True),
    )
    return (
        hidden_out,
        hidden_grad,
        route_grad,
        g_attn_gain,
        g_ffn_gain,
        g_qkv,
        g_bias,
        g_out,
        g_shared_gate_up,
        g_shared_down,
        g_gate_vec,
        g_expert_gate_up,
        g_expert_down,
    )


def on_device(*arrays):
    if lax.axis_size("fsdp") == 8 and lax.axis_size("tp") == 4 and arrays[3].shape[1] >= 3:
        return dense_plan(*arrays)
    return routed_plan(*arrays)


def solution(mesh):
    placed = (
        P(("fsdp", "tp"), None),
        P(("fsdp", "tp"), None),
        P("fsdp", None),
        P("fsdp", None),
        P("fsdp", None),
        P(),
        P(),
        P("fsdp", None, "tp", None),
        P(None, "tp", "fsdp"),
        P("tp", "fsdp"),
        P("fsdp", None, "tp"),
        P("tp", "fsdp"),
        P(),
        P("fsdp", None, None, "tp"),
        P("fsdp", "tp", None),
    )
    return jax.shard_map(
        on_device,
        mesh=mesh,
        in_specs=placed,
        out_specs=(
            P(("fsdp", "tp"), None),
            P(("fsdp", "tp"), None),
            P(("fsdp", "tp"), None),
            P(("fsdp", "tp")),
            P(("fsdp", "tp")),
            P("fsdp", None, "tp", None),
            P(None, "tp", "fsdp"),
            P("tp", "fsdp"),
            P("fsdp", None, "tp"),
            P("tp", "fsdp"),
            P(("fsdp", "tp")),
            P("fsdp", None, None, "tp"),
            P("fsdp", "tp", None),
        ),
        check_vma=False,
    )
```

```python
import functools

import jax
import jax.experimental.pallas as pl
import jax.experimental.pallas.tpu as pltpu
import jax.numpy as jnp
from jax import lax
from jax.sharding import PartitionSpec as P

epsilon = 1e-06


def rope_tables(length, head_dim):
    half_dim = head_dim // 2
    ratios = jnp.arange(half_dim, dtype=jnp.float32) * (2.0 / head_dim)
    frequency = jnp.exp(-jnp.log(10000.0) * ratios)
    angles = jnp.arange(length, dtype=jnp.float32)[:, None] * frequency[None, :]
    return (jnp.cos(angles)[:, None, :], jnp.sin(angles)[:, None, :])


def rotate(tensor, cos_table, sin_table):
    half_dim = tensor.shape[-1] // 2
    front_half = tensor[..., :half_dim]
    back_half = tensor[..., half_dim:]
    return jnp.concatenate(
        [
            front_half * cos_table - back_half * sin_table,
            back_half * cos_table + front_half * sin_table,
        ],
        axis=-1,
    )


def unrotate(tensor, cos_table, sin_table):
    half_dim = tensor.shape[-1] // 2
    front_half = tensor[..., :half_dim]
    back_half = tensor[..., half_dim:]
    return jnp.concatenate(
        [
            front_half * cos_table + back_half * sin_table,
            back_half * cos_table - front_half * sin_table,
        ],
        axis=-1,
    )


def silu_parts(gate_in):
    sigmoid_value = jax.nn.sigmoid(gate_in)
    return (gate_in * sigmoid_value, sigmoid_value * (1.0 + gate_in * (1.0 - sigmoid_value)))


def slot_table(route_ids, experts, capacity):
    flat_ids = route_ids.reshape(-1)
    onehot = (flat_ids[:, None] == jnp.arange(experts, dtype=jnp.int32)[None, :]).astype(jnp.int32)
    before = jnp.cumsum(onehot, axis=0, dtype=jnp.int32) - onehot
    ranks = jnp.sum(before * onehot, axis=1, dtype=jnp.int32)
    places = flat_ids * capacity + ranks
    filler = jnp.arange(flat_ids.shape[0], dtype=jnp.int32) + 1
    slot_rows = jnp.zeros((experts * capacity,), jnp.int32).at[places].set(filler)
    return (places.reshape(route_ids.shape), slot_rows.reshape(experts, capacity))


def inverse_rms(tensor):
    return lax.rsqrt(jnp.mean(tensor * tensor, axis=-1, keepdims=True) + epsilon)


def norm_backward(d_normed, hat_rows, inverse, gain_vec):
    d_hat = d_normed * gain_vec
    return inverse * (d_hat - hat_rows * jnp.mean(d_hat * hat_rows, axis=-1, keepdims=True))


def masked_scores(query, keys, allowed, score_scale):
    raw = jnp.einsum("qhd,khd->hqk", query, keys, preferred_element_type=jnp.float32) * score_scale
    return jnp.where(allowed[None], raw, -1e30)


def spread(rows):
    return lax.all_gather(rows, "tp", axis=0, tiled=True)


def head_total(partial_rows):
    return lax.psum_scatter(
        partial_rows.astype(jnp.bfloat16), "tp", scatter_dimension=0, tiled=True
    ).astype(jnp.float32)


def to_experts(buffer):
    return lax.all_to_all(buffer, "fsdp", split_axis=0, concat_axis=0, tiled=True)


def from_experts(buffer):
    return lax.all_to_all(buffer, "fsdp", split_axis=0, concat_axis=0, tiled=True)


def routed_plan(
    hidden_in,
    out_grad,
    segment_ids,
    expert_ids,
    route_weights,
    attn_gain,
    ffn_gain,
    qkv_weight,
    qkv_bias,
    out_weight,
    shared_gate_up,
    shared_down,
    shared_gate_vec,
    expert_gate_up,
    expert_down,
):
    tp_rank = lax.axis_index("tp")
    experts = lax.axis_size("fsdp")
    length = segment_ids.shape[1]
    top_count = expert_ids.shape[1]
    capacity = 3 * length * top_count // (2 * experts)
    own_rows = hidden_in.shape[0]
    model_width = hidden_in.shape[1]
    qkv_full, bias_full, out_full, shared_full, shared_down_full = (
        lax.all_gather(qkv_weight, "fsdp", axis=0, tiled=True),
        lax.all_gather(qkv_bias.astype(jnp.bfloat16), "fsdp", axis=2, tiled=True).astype(
            qkv_bias.dtype
        ),
        lax.all_gather(out_weight, "fsdp", axis=1, tiled=True),
        lax.all_gather(shared_gate_up, "fsdp", axis=0, tiled=True),
        lax.all_gather(shared_down, "fsdp", axis=1, tiled=True),
    )
    local_heads = qkv_full.shape[2]
    head_dim = qkv_full.shape[3]
    score_scale = head_dim ** (-0.5)
    cos_table, sin_table = rope_tables(length, head_dim)
    positions = jnp.arange(length, dtype=jnp.int32)
    segments = segment_ids[0]
    allowed = (positions[:, None] >= positions[None, :]) & (segments[:, None] == segments[None, :])
    hidden_float = hidden_in.astype(jnp.float32)
    attn_inverse = inverse_rms(hidden_float)
    normed_one = spread((hidden_float * attn_inverse * attn_gain).astype(jnp.bfloat16))
    qkv_flat = qkv_full.reshape(model_width, -1)
    qkv = (
        jnp.dot(normed_one, qkv_flat, preferred_element_type=jnp.float32).reshape(
            length, 3, local_heads, head_dim
        )
        + bias_full
    )
    query = rotate(qkv[:, 0], cos_table, sin_table).astype(jnp.bfloat16)
    keys = rotate(qkv[:, 1], cos_table, sin_table).astype(jnp.bfloat16)
    values = qkv[:, 2].astype(jnp.bfloat16)
    scores = masked_scores(query, keys, allowed, score_scale)
    row_peak = jnp.max(scores, axis=-1, keepdims=True)
    log_total = row_peak + jnp.log(jnp.sum(jnp.exp(scores - row_peak), axis=-1, keepdims=True))
    probs_b = jnp.exp(scores - log_total).astype(jnp.bfloat16)
    heads_out = (
        jnp.einsum("hqk,khd->qhd", probs_b, values, preferred_element_type=jnp.float32)
        .astype(jnp.bfloat16)
        .reshape(length, -1)
    )
    middle = hidden_float + head_total(
        jnp.dot(heads_out, out_full, preferred_element_type=jnp.float32)
    )
    ffn_inverse = inverse_rms(middle)
    normed_two_own = (middle * ffn_inverse * ffn_gain).astype(jnp.bfloat16)
    normed_two = spread(normed_two_own)
    gate_prob = jax.nn.sigmoid(jnp.sum(normed_two.astype(jnp.float32) * shared_gate_vec, axis=-1))
    shared_flat = shared_full.reshape(model_width, -1)
    shared_width = shared_full.shape[2]
    shared_pre = jnp.dot(normed_two, shared_flat, preferred_element_type=jnp.float32)
    shared_act, shared_slope = silu_parts(shared_pre[:, :shared_width])
    shared_upper = shared_pre[:, shared_width:]
    shared_hidden = (shared_act * shared_upper).astype(jnp.bfloat16)
    shared_part = jnp.dot(shared_hidden, shared_down_full, preferred_element_type=jnp.float32)
    places, slot_rows = slot_table(expert_ids, experts, capacity)
    filled = slot_rows > 0
    route_index = jnp.maximum(slot_rows - 1, 0)
    source_rows = route_index // top_count
    flat_weights = route_weights.reshape(-1)
    slot_weights = jnp.where(filled, flat_weights[route_index], 0.0)
    send_rows = jnp.where(filled[:, :, None], normed_two[source_rows], jnp.zeros((), jnp.bfloat16))
    arrived = to_experts(send_rows).reshape(-1, model_width)
    expert_flat = expert_gate_up[0].reshape(model_width, -1)
    expert_width = expert_gate_up.shape[3]
    down_local = expert_down[0]
    expert_pre = jnp.dot(arrived, expert_flat, preferred_element_type=jnp.float32)
    expert_act, expert_slope = silu_parts(expert_pre[:, :expert_width])
    expert_upper = expert_pre[:, expert_width:]
    expert_hidden = (expert_act * expert_upper).astype(jnp.bfloat16)
    expert_part = jnp.dot(expert_hidden, down_local, preferred_element_type=jnp.float32).astype(
        jnp.bfloat16
    )
    returned = from_experts(expert_part.reshape(experts, capacity, model_width)).reshape(
        experts * capacity, model_width
    )
    picked = returned[places].astype(jnp.float32)
    token_term = gate_prob[:, None] * shared_part + jnp.sum(
        route_weights[:, :, None] * picked, axis=1
    )
    own_extra = 0.0
    total = (
        lax.psum_scatter(
            token_term.astype(jnp.bfloat16), "tp", scatter_dimension=0, tiled=True
        ).astype(jnp.float32)
        + own_extra
    )
    hidden_out = (middle + total).astype(jnp.bfloat16)
    grad_rows = spread(out_grad)
    grad_float = grad_rows.astype(jnp.float32)
    gate_part = jnp.sum(grad_float * shared_part, axis=-1)
    scaled_grad = (gate_prob[:, None] * grad_float).astype(jnp.bfloat16)
    shared_d_hidden = jnp.dot(scaled_grad, shared_down_full.T, preferred_element_type=jnp.float32)
    shared_d_cat = jnp.concatenate(
        [
            (shared_d_hidden * shared_upper * shared_slope).astype(jnp.bfloat16),
            (shared_d_hidden * shared_act).astype(jnp.bfloat16),
        ],
        axis=1,
    )
    g_shared_down = jnp.dot(shared_hidden.T, scaled_grad, preferred_element_type=jnp.float32)
    g_shared_gate_up = jnp.dot(
        normed_two.T, shared_d_cat, preferred_element_type=jnp.float32
    ).reshape(shared_full.shape)
    d_normed_part = jnp.dot(shared_d_cat, shared_flat.T, preferred_element_type=jnp.float32)
    expert_grad_in = (slot_weights[:, :, None] * grad_float[source_rows]).astype(jnp.bfloat16)
    arrived_grad = to_experts(expert_grad_in).reshape(-1, model_width)
    back_act, back_slope, back_upper, back_hidden = (
        expert_act,
        expert_slope,
        expert_upper,
        expert_hidden,
    )
    expert_d_hidden = jnp.dot(arrived_grad, down_local.T, preferred_element_type=jnp.float32)
    expert_d_cat = jnp.concatenate(
        [
            (expert_d_hidden * back_upper * back_slope).astype(jnp.bfloat16),
            (expert_d_hidden * back_act).astype(jnp.bfloat16),
        ],
        axis=1,
    )
    g_expert_down = jnp.dot(back_hidden.T, arrived_grad, preferred_element_type=jnp.float32)[None]
    g_expert_gate_up = jnp.dot(arrived.T, expert_d_cat, preferred_element_type=jnp.float32).reshape(
        expert_gate_up.shape
    )
    expert_d_part = jnp.dot(expert_d_cat, expert_flat.T, preferred_element_type=jnp.float32).astype(
        jnp.bfloat16
    )
    route_part = jnp.sum(grad_float[:, None, :] * picked, axis=-1)
    returned_grad = from_experts(expert_d_part.reshape(experts, capacity, model_width)).reshape(
        experts * capacity, model_width
    )
    d_normed_part = d_normed_part + jnp.sum(returned_grad[places].astype(jnp.float32), axis=1)
    d_normed_two, route_grad, gate_grad = (
        lax.psum_scatter(
            d_normed_part.astype(jnp.bfloat16), "tp", scatter_dimension=0, tiled=True
        ).astype(jnp.float32),
        lax.psum_scatter(
            route_part.astype(jnp.bfloat16), "tp", scatter_dimension=0, tiled=True
        ).astype(jnp.float32),
        lax.psum_scatter(
            gate_part.astype(jnp.bfloat16), "tp", scatter_dimension=0, tiled=True
        ).astype(jnp.float32),
    )
    own_gate = lax.dynamic_slice_in_dim(gate_prob, tp_rank * own_rows, own_rows)
    logit_grad = gate_grad * own_gate * (1.0 - own_gate)
    d_normed_two = d_normed_two + logit_grad[:, None] * shared_gate_vec
    g_gate_vec = jnp.sum(normed_two_own.astype(jnp.float32) * logit_grad[:, None], axis=0)
    hat_two = middle * ffn_inverse
    g_ffn_gain = jnp.sum(d_normed_two * hat_two, axis=0)
    middle_grad = out_grad.astype(jnp.float32) + norm_backward(
        d_normed_two, hat_two, ffn_inverse, ffn_gain
    )
    d_rows = spread(middle_grad.astype(jnp.bfloat16))
    g_out = jnp.dot(heads_out.T, d_rows, preferred_element_type=jnp.float32)
    d_heads = (
        jnp.dot(d_rows, out_full.T, preferred_element_type=jnp.float32)
        .astype(jnp.bfloat16)
        .reshape(length, local_heads, head_dim)
    )
    heads_three = heads_out.reshape(length, local_heads, head_dim)
    scores_again = masked_scores(query, keys, allowed, score_scale)
    probs_full = jnp.exp(scores_again - log_total)
    probs_again = probs_full.astype(jnp.bfloat16)
    d_values = jnp.einsum("hqk,qhd->khd", probs_again, d_heads, preferred_element_type=jnp.float32)
    d_probs = jnp.einsum("qhd,khd->hqk", d_heads, values, preferred_element_type=jnp.float32)
    delta = jnp.sum(d_heads.astype(jnp.float32) * heads_three.astype(jnp.float32), axis=-1)
    d_scores = (probs_full * (d_probs - delta.T[:, :, None])).astype(jnp.bfloat16)
    d_query = (
        jnp.einsum("hqk,khd->qhd", d_scores, keys, preferred_element_type=jnp.float32) * score_scale
    )
    d_keys = (
        jnp.einsum("hqk,qhd->khd", d_scores, query, preferred_element_type=jnp.float32)
        * score_scale
    )
    d_qkv = jnp.stack(
        [unrotate(d_query, cos_table, sin_table), unrotate(d_keys, cos_table, sin_table), d_values],
        axis=1,
    )
    g_bias = jnp.sum(d_qkv, axis=0)
    d_qkv_b = d_qkv.astype(jnp.bfloat16).reshape(length, -1)
    g_qkv = jnp.dot(normed_one.T, d_qkv_b, preferred_element_type=jnp.float32).reshape(
        qkv_full.shape
    )
    d_normed_one = head_total(jnp.dot(d_qkv_b, qkv_flat.T, preferred_element_type=jnp.float32))
    hat_one = hidden_float * attn_inverse
    g_attn_gain = jnp.sum(d_normed_one * hat_one, axis=0)
    hidden_grad = middle_grad + norm_backward(d_normed_one, hat_one, attn_inverse, attn_gain)
    g_qkv, g_bias, g_out, g_shared_gate_up, g_shared_down = (
        lax.psum_scatter(
            g_qkv.astype(jnp.bfloat16), "fsdp", scatter_dimension=0, tiled=True
        ).astype(jnp.float32),
        lax.psum_scatter(
            g_bias.astype(jnp.bfloat16), "fsdp", scatter_dimension=2, tiled=True
        ).astype(jnp.float32),
        lax.psum_scatter(
            g_out.astype(jnp.bfloat16), "fsdp", scatter_dimension=1, tiled=True
        ).astype(jnp.float32),
        lax.psum_scatter(
            g_shared_gate_up.astype(jnp.bfloat16), "fsdp", scatter_dimension=0, tiled=True
        ).astype(jnp.float32),
        lax.psum_scatter(
            g_shared_down.astype(jnp.bfloat16), "fsdp", scatter_dimension=1, tiled=True
        ).astype(jnp.float32),
    )
    g_attn_gain, g_ffn_gain, g_gate_vec = (
        lax.psum_scatter(g_attn_gain, ("fsdp", "tp"), scatter_dimension=0, tiled=True),
        lax.psum_scatter(g_ffn_gain, ("fsdp", "tp"), scatter_dimension=0, tiled=True),
        lax.psum_scatter(g_gate_vec, ("fsdp", "tp"), scatter_dimension=0, tiled=True),
    )
    return (
        hidden_out,
        hidden_grad,
        route_grad,
        g_attn_gain,
        g_ffn_gain,
        g_qkv,
        g_bias,
        g_out,
        g_shared_gate_up,
        g_shared_down,
        g_gate_vec,
        g_expert_gate_up,
        g_expert_down,
    )


MESH = pl.DeviceIdType.MESH


def flipped(index, bit):
    return index + bit - 2 * bit * ((index // bit) % 2)


def place():
    me = lax.axis_index("fsdp")
    rank = lax.axis_index("tp")
    return me, rank


def greet(me, rank, tp):
    barrier = pltpu.get_barrier_semaphore()
    for bit in (1, 2, 4):
        pl.semaphore_signal(
            barrier, inc=1, device_id=(flipped(me, bit), rank), device_id_type=MESH
        )

    @pl.when(rank > 0)
    def _():
        pl.semaphore_signal(barrier, inc=1, device_id=(me, rank - 1), device_id_type=MESH)

    @pl.when(rank < tp - 1)
    def _():
        pl.semaphore_signal(barrier, inc=1, device_id=(me, rank + 1), device_id_type=MESH)

    left = (rank + tp - 1) // tp
    right = (2 * (tp - 1) - rank) // tp
    pl.semaphore_wait(barrier, 3 + left + right)


def scatter_kernel(tp, parts, *refs):
    ins = refs[:parts]
    outs = refs[parts : 2 * parts]
    buffers = refs[2 * parts : 7 * parts]
    mine, other, diag_in, last_in, z_in = (
        buffers[i * parts : (i + 1) * parts] for i in range(5)
    )
    l_sem, c_send, c_recv, p_send, p_recv, z_send, z_recv = refs[7 * parts :]
    me, rank = place()
    greet(me, rank, tp)
    f32 = jnp.float32
    blocks = [rank]
    for bit in (1, 2):
        blocks = blocks + [flipped(one, bit) for one in blocks]
    blocks = blocks[::-1]
    packs = [me, flipped(me, 2), flipped(me, 4), flipped(flipped(me, 2), 4)]
    every = range(parts)
    rows = [ref.shape[0] for ref in outs]
    low = [pl.ds(0, count // 2) for count in rows]
    high = [pl.ds(count // 2, count // 2) for count in rows]

    def region(i, pack, block):
        return ins[i].at[pl.ds((pack * tp + block) * rows[i], rows[i])]

    def local(k, j, i):
        return pltpu.make_async_copy(
            region(i, packs[k], blocks[j]), mine[i].at[k, j], l_sem.at[k, j, i]
        )

    def core(k, j, i):
        return pltpu.make_async_remote_copy(
            src_ref=region(i, flipped(packs[k], 1), blocks[j]),
            dst_ref=other[i].at[k, j],
            send_sem=c_send.at[k, j, i],
            recv_sem=c_recv.at[k, j, i],
            device_id=(flipped(me, 1), rank),
            device_id_type=MESH,
        )

    def across(bit, src, dst, slot, j, i):
        return pltpu.make_async_remote_copy(
            src_ref=src,
            dst_ref=dst,
            send_sem=p_send.at[slot, j, i],
            recv_sem=p_recv.at[slot, j, i],
            device_id=(flipped(me, bit), rank),
            device_id_type=MESH,
        )

    def diag_x(j, i):
        return across(2, mine[i].at[3, j, low[i]], diag_in[i].at[j, 0], 0, j, i)

    def diag_y(j, i):
        return across(4, mine[i].at[3, j, high[i]], diag_in[i].at[j, 1], 1, j, i)

    def direct_x(j, i):
        return across(2, mine[i].at[1, j, low[i]], last_in[i].at[j, 0, low[i]], 2, j, i)

    def direct_y(j, i):
        return across(4, mine[i].at[2, j, high[i]], last_in[i].at[j, 1, high[i]], 3, j, i)

    def summed_x(j, i):
        return across(2, mine[i].at[1, j, high[i]], last_in[i].at[j, 0, high[i]], 4, j, i)

    def summed_y(j, i):
        return across(4, mine[i].at[2, j, low[i]], last_in[i].at[j, 1, low[i]], 5, j, i)

    def along_z(j, right, i):
        way = 0 if right else 1
        block = blocks[j]
        return pltpu.make_async_remote_copy(
            src_ref=mine[i].at[0, j],
            dst_ref=z_in[i].at[way, block],
            send_sem=z_send.at[way, block, i],
            recv_sem=z_recv.at[way, block, i],
            device_id=(me, rank + 1 if right else rank - 1),
            device_id_type=MESH,
        )

    for j in range(tp):
        for k in (3, 2, 1, 0):
            for i in every:
                core(k, j, i).start()
                local(k, j, i).start()

    def add(ref, spot, one):
        ref[spot] = (ref[spot].astype(f32) + one.astype(f32)).astype(ref.dtype)

    def first(j):
        for k in (3, 2, 1, 0):
            for i in every:
                core(k, j, i).wait_recv()
                local(k, j, i).wait()
                add(mine[i], (k, j), other[i][k, j])
                if k == 3:
                    diag_x(j, i).start()
                    diag_y(j, i).start()
                if k == 2:
                    direct_y(j, i).start()
                if k == 1:
                    direct_x(j, i).start()

    def second(j):
        for i in every:
            diag_x(j, i).wait_recv()
            add(mine[i], (2, j, low[i]), diag_in[i][j, 0])
            summed_y(j, i).start()
            diag_y(j, i).wait_recv()
            add(mine[i], (1, j, high[i]), diag_in[i][j, 1])
            summed_x(j, i).start()

    def third(j):
        block = blocks[j]
        for i in every:
            direct_x(j, i).wait_recv()
            direct_y(j, i).wait_recv()
            summed_x(j, i).wait_recv()
            summed_y(j, i).wait_recv()
            total = (
                mine[i][0, j].astype(f32)
                + last_in[i][j, 0].astype(f32)
                + last_in[i][j, 1].astype(f32)
            )
            if j < tp - 1:
                mine[i][0, j] = total.astype(mine[i].dtype)
            else:
                outs[i][...] = total
        if j < tp - 1:

            @pl.when((block > rank) & (rank > 0))
            def _():
                for i in every:
                    along_z(j, True, i).wait_recv()
                    add(mine[i], (0, j), z_in[i][0, block])

            @pl.when((block < rank) & (rank < tp - 1))
            def _():
                for i in every:
                    along_z(j, False, i).wait_recv()
                    add(mine[i], (0, j), z_in[i][1, block])

            @pl.when(block > rank)
            def _():
                for i in every:
                    along_z(j, True, i).start()

            @pl.when(block < rank)
            def _():
                for i in every:
                    along_z(j, False, i).start()
        else:

            @pl.when(rank > 0)
            def _():
                for i in every:
                    along_z(j, True, i).wait_recv()
                    outs[i][...] += z_in[i][0, block].astype(f32)

            @pl.when(rank < tp - 1)
            def _():
                for i in every:
                    along_z(j, False, i).wait_recv()
                    outs[i][...] += z_in[i][1, block].astype(f32)

    first(0)
    first(1)
    second(0)
    first(2)
    second(1)
    third(0)
    first(3)
    second(2)
    third(1)
    second(3)
    third(2)
    third(3)
    for j in range(tp):
        for i in every:
            for k in range(4):
                core(k, j, i).wait_send()
            for copy in (diag_x, diag_y, direct_x, direct_y, summed_x, summed_y):
                copy(j, i).wait_send()
        block = blocks[j]
        if j < tp - 1:

            @pl.when(block > rank)
            def _():
                for i in every:
                    along_z(j, True, i).wait_send()

            @pl.when(block < rank)
            def _():
                for i in every:
                    along_z(j, False, i).wait_send()


def scatter_sum(arrays, fsdp, tp, collective_id):
    parts = len(arrays)
    shapes = [(one.shape[0] // (fsdp * tp), one.shape[1]) for one in arrays]
    kind = arrays[0].dtype
    scratch = [pltpu.VMEM((4, tp, rows, width), kind) for rows, width in shapes]
    scratch += [pltpu.VMEM((4, tp, rows, width), kind) for rows, width in shapes]
    scratch += [pltpu.VMEM((tp, 2, rows // 2, width), kind) for rows, width in shapes]
    scratch += [pltpu.VMEM((tp, 2, rows, width), kind) for rows, width in shapes]
    scratch += [pltpu.VMEM((2, tp, rows, width), kind) for rows, width in shapes]
    return pl.pallas_call(
        functools.partial(scatter_kernel, tp, parts),
        out_shape=[jax.ShapeDtypeStruct(shape, jnp.float32) for shape in shapes],
        in_specs=[pl.BlockSpec(memory_space=pl.ANY)] * parts,
        out_specs=[pl.BlockSpec(memory_space=pltpu.VMEM)] * parts,
        scratch_shapes=scratch
        + [
            pltpu.SemaphoreType.DMA((4, tp, parts)),
            pltpu.SemaphoreType.DMA((4, tp, parts)),
            pltpu.SemaphoreType.DMA((4, tp, parts)),
            pltpu.SemaphoreType.DMA((6, tp, parts)),
            pltpu.SemaphoreType.DMA((6, tp, parts)),
            pltpu.SemaphoreType.DMA((2, tp, parts)),
            pltpu.SemaphoreType.DMA((2, tp, parts)),
        ],
        compiler_params=pltpu.CompilerParams(
            collective_id=collective_id, has_side_effects=True, vmem_limit_bytes=48 << 20
        ),
        name="scatter_rows",
    )(*arrays)


def prologue_kernel(tp, halved, *refs):
    parts = len(halved)
    own_ref, pieces = refs[0], refs[1 : 1 + parts]
    rows_ref, fulls = refs[1 + parts], refs[2 + parts : 2 + 2 * parts]
    l_sem, z_send, z_recv, p_send, p_recv = refs[2 + 2 * parts :]
    me, rank = place()
    greet(me, rank, tp)
    rows = own_ref.shape[0]

    def along_z(block, right):
        way = 0 if right else 1
        spot = rows_ref.at[pl.ds(block * rows, rows)]
        return pltpu.make_async_remote_copy(
            src_ref=spot,
            dst_ref=spot,
            send_sem=z_send.at[way, block],
            recv_sem=z_recv.at[way, block],
            device_id=(me, rank + 1 if right else rank - 1),
            device_id_type=MESH,
        )

    def region(i, owner_bits, start=0, count=None):
        owner = me
        for one in (2, 4):
            if owner_bits & one:
                owner = flipped(owner, one)
        size = pieces[i].shape[0]
        count = size if count is None else count
        return fulls[i].at[pl.ds(owner * size + start, count)]

    def across(i, bit, owner_bits, slot, start=0, count=None):
        spot = region(i, owner_bits, start, count)
        return pltpu.make_async_remote_copy(
            src_ref=pieces[i] if owner_bits == 0 else spot,
            dst_ref=spot,
            send_sem=p_send.at[slot, i],
            recv_sem=p_recv.at[slot, i],
            device_id=(flipped(me, bit), rank),
            device_id_type=MESH,
        )

    def to_core(q, i):
        return across(i, 1, 2 * q, q)

    def own_x(i):
        return across(i, 2, 0, 4)

    def own_y(i):
        return across(i, 4, 0, 5)

    def x_to_y(i):
        size = pieces[i].shape[0]
        return across(i, 4, 2, 6, 0, size // 2 if halved[i] else size)

    def y_to_x(i):
        size = pieces[i].shape[0]
        return across(i, 2, 4, 7, size // 2, size // 2)

    def local(i):
        return pltpu.make_async_copy(pieces[i], region(i, 0), l_sem.at[i])

    def forward(i):
        own_x(i).wait_recv()
        x_to_y(i).start()
        to_core(1, i).start()
        own_y(i).wait_recv()
        if halved[i]:
            y_to_x(i).start()
        to_core(2, i).start()

    def finish(i):
        x_to_y(i).wait_recv()
        if halved[i]:
            y_to_x(i).wait_recv()
        to_core(3, i).start()

    def z_step(step):
        @pl.when(rank >= step)
        def _():
            along_z(rank - step, True).wait_recv()

            @pl.when(rank < tp - 1)
            def _():
                along_z(rank - step, True).start()

        @pl.when(rank + step < tp)
        def _():
            along_z(rank + step, False).wait_recv()

            @pl.when(rank > 0)
            def _():
                along_z(rank + step, False).start()

    for i in range(parts):
        own_x(i).start()
        own_y(i).start()
        to_core(0, i).start()
    mine = pltpu.make_async_copy(own_ref, rows_ref.at[pl.ds(rank * rows, rows)], l_sem.at[parts])
    mine.start()
    for i in range(parts):
        local(i).start()
    mine.wait()

    @pl.when(rank < tp - 1)
    def _():
        along_z(rank, True).start()

    @pl.when(rank > 0)
    def _():
        along_z(rank, False).start()

    z_step(1)
    forward(0)
    z_step(2)
    for i in range(1, parts):
        forward(i)
    finish(0)
    z_step(3)
    for i in range(1, parts):
        finish(i)
    for i in range(parts):
        local(i).wait()
        for q in range(4):
            to_core(q, i).wait_recv()
    for i in range(parts):
        for q in range(4):
            to_core(q, i).wait_send()
        own_x(i).wait_send()
        own_y(i).wait_send()
        x_to_y(i).wait_send()
        if halved[i]:
            y_to_x(i).wait_send()
    for block in range(tp):

        @pl.when((block <= rank) & (rank < tp - 1))
        def _():
            along_z(block, True).wait_send()

        @pl.when((block >= rank) & (rank > 0))
        def _():
            along_z(block, False).wait_send()


def prologue(own, pieces, fsdp, tp, collective_id):
    parts = len(pieces)
    halved = [one.shape[0] >= 32 for one in pieces]
    dma = pltpu.SemaphoreType.DMA
    anywhere = pl.BlockSpec(memory_space=pl.ANY)
    shapes = [(own.shape[0] * tp, own.shape[1])]
    shapes += [(one.shape[0] * fsdp, one.shape[1]) for one in pieces]
    return pl.pallas_call(
        functools.partial(prologue_kernel, tp, halved),
        out_shape=[
            jax.ShapeDtypeStruct(shape, one.dtype) for shape, one in zip(shapes, [own] + pieces)
        ],
        in_specs=[anywhere] * (1 + parts),
        out_specs=[anywhere] * (1 + parts),
        scratch_shapes=[
            dma((parts + 1,)),
            dma((2, tp)),
            dma((2, tp)),
            dma((8, parts)),
            dma((8, parts)),
        ],
        compiler_params=pltpu.CompilerParams(
            collective_id=collective_id, has_side_effects=True, vmem_limit_bytes=16 << 20
        ),
        name="prologue",
    )(own, *pieces)


UNIT = 640
SHARED = 384
NT = (((1,), (1,)), ((), ()))


def ffn_kernel(tp, expert_width, shared_width, *refs):
    part_ref, hidden_ref, gain_ref, grad_ref, both_ref, down_ref, scale_ref = refs[:7]
    middle_ref, all_ref, d_ref, hid_ref, y_ref, dsum_ref, esum_ref = refs[7:14]
    (
        n_buf, g_buf, x_buf, dh_buf, d_buf, stage, acc, diag_in, last_in, z_in,
        stage_e, acc_e, other_e, diag_e, last_e, z_in_e,
        local_sem, g_sem, x_sem, d_sem, h_sem, y_sem,
        az_send, az_recv, ap_send, ap_recv,
        c_send, c_recv, ce_send, ce_recv, p_send, p_recv, pe_send, pe_recv,
        z_send, z_recv, ze_send, ze_recv, f_sem, f_send, f_recv,
    ) = refs[14:]
    me, rank = place()
    greet(me, rank, tp)
    f32 = jnp.float32
    bf16 = jnp.bfloat16
    rows = hidden_ref.shape[0]
    pack_rows = rows * tp
    tile = pack_rows // 2
    near = rank // 2
    tokens = all_ref.shape[0]

    def region(pack, block, start=0, count=None):
        count = rows if count is None else count
        return all_ref.at[pl.ds(pack * pack_rows + block * rows + start, count)]

    def gather_z(block, right):
        way = 0 if right else 1
        ref = region(me, block)
        return pltpu.make_async_remote_copy(
            src_ref=ref,
            dst_ref=ref,
            send_sem=az_send.at[way, block],
            recv_sem=az_recv.at[way, block],
            device_id=(me, rank + 1 if right else rank - 1),
            device_id_type=MESH,
        )

    def gather(bit, pack_bits, block, slot, start=0, count=None):
        pack = me
        for one in (2, 4):
            if pack_bits & one:
                pack = flipped(pack, one)
        ref = region(pack, block, start, count)
        return pltpu.make_async_remote_copy(
            src_ref=ref,
            dst_ref=ref,
            send_sem=ap_send.at[slot, block],
            recv_sem=ap_recv.at[slot, block],
            device_id=(flipped(me, bit), rank),
            device_id_type=MESH,
        )

    def to_core(q, block):
        return gather(1, 2 * q, block, q)

    def own_x(block):
        return gather(2, 0, block, 4)

    def own_y(block):
        return gather(4, 0, block, 5)

    def x_to_y(block):
        return gather(4, 2, block, 6, 0, rows // 2)

    def y_to_x(block):
        return gather(2, 4, block, 7, rows // 2, rows // 2)

    def start_plane(block):
        own_x(block).start()
        own_y(block).start()
        to_core(0, block).start()

    def forward(block):
        own_x(block).wait_recv()
        x_to_y(block).start()
        to_core(1, block).start()
        own_y(block).wait_recv()
        y_to_x(block).start()
        to_core(2, block).start()

    def finish(block):
        x_to_y(block).wait_recv()
        y_to_x(block).wait_recv()
        to_core(3, block).start()

    def z_step(step):
        @pl.when(rank >= step)
        def _():
            block = rank - step
            gather_z(block, True).wait_recv()

            @pl.when(rank < tp - 1)
            def _():
                gather_z(block, True).start()

            start_plane(block)

        @pl.when(rank + step < tp)
        def _():
            block = rank + step
            gather_z(block, False).wait_recv()

            @pl.when(rank > 0)
            def _():
                gather_z(block, False).start()

            start_plane(block)

    order = [rank]
    for bit in (1, 2):
        order = order + [flipped(one, bit) for one in order]

    def control(i):
        steps = {
            0: [(forward, order[0])],
            1: [(z_step, 2), (forward, order[1])],
            2: [(z_step, 3)],
            3: [(finish, order[0])],
            4: [(finish, order[1])],
            5: [(forward, order[2])],
            7: [(forward, order[3])],
            8: [(finish, order[2])],
            11: [(finish, order[3])],
        }
        for at, todo in steps.items():

            @pl.when(i == at)
            def _():
                for act, what in todo:
                    act(what)

    def core(q, h):
        return pltpu.make_async_remote_copy(
            src_ref=stage.at[h],
            dst_ref=acc.at[q, h],
            send_sem=c_send.at[q, h],
            recv_sem=c_recv.at[q, h],
            device_id=(flipped(me, 1), rank),
            device_id_type=MESH,
        )

    def core_e(q):
        return pltpu.make_async_remote_copy(
            src_ref=stage_e.at[q],
            dst_ref=other_e.at[q],
            send_sem=ce_send.at[q],
            recv_sem=ce_recv.at[q],
            device_id=(flipped(me, 1), rank),
            device_id_type=MESH,
        )

    def across(bit, src, dst, slot, h):
        return pltpu.make_async_remote_copy(
            src_ref=src,
            dst_ref=dst,
            send_sem=p_send.at[slot, h],
            recv_sem=p_recv.at[slot, h],
            device_id=(flipped(me, bit), rank),
            device_id_type=MESH,
        )

    def diag_x(h):
        return across(2, acc.at[3, h, 0], diag_in.at[h, 0], 0, h)

    def diag_y(h):
        return across(4, acc.at[3, h, 1], diag_in.at[h, 1], 1, h)

    def direct_x(h):
        return across(2, acc.at[1, h, 0], last_in.at[h, 0, 0], 2, h)

    def direct_y(h):
        return across(4, acc.at[2, h, 1], last_in.at[h, 1, 1], 3, h)

    def summed_x(h):
        return across(2, acc.at[1, h, 1], last_in.at[h, 0, 1], 4, h)

    def summed_y(h):
        return across(4, acc.at[2, h, 0], last_in.at[h, 1, 0], 5, h)

    def across_e(bit, src, dst, slot):
        return pltpu.make_async_remote_copy(
            src_ref=src,
            dst_ref=dst,
            send_sem=pe_send.at[slot],
            recv_sem=pe_recv.at[slot],
            device_id=(flipped(me, bit), rank),
            device_id_type=MESH,
        )

    def diag_lines():
        return across_e(2, acc_e.at[3], diag_e, 0)

    def direct_lines():
        return across_e(2, acc_e.at[1], last_e.at[0], 1)

    def summed_lines():
        return across_e(4, acc_e.at[2], last_e.at[1], 2)

    blocks = [3 * (1 - near), 2 - near, flipped(rank, 1), rank]

    def along_z(j, right):
        way = 0 if right else 1
        block = blocks[j]
        return pltpu.make_async_remote_copy(
            src_ref=acc.at[0, j // 2, block % 2],
            dst_ref=z_in.at[way, block],
            send_sem=z_send.at[way, block],
            recv_sem=z_recv.at[way, block],
            device_id=(me, rank + 1 if right else rank - 1),
            device_id_type=MESH,
        )

    def along_z_e(j, right):
        way = 0 if right else 1
        block = blocks[j]
        return pltpu.make_async_remote_copy(
            src_ref=acc_e.at[0, block],
            dst_ref=z_in_e.at[way, block],
            send_sem=ze_send.at[way, block],
            recv_sem=ze_recv.at[way, block],
            device_id=(me, rank + 1 if right else rank - 1),
            device_id_type=MESH,
        )

    def add(ref, spot, one):
        ref[spot] = (ref[spot].astype(f32) + one.astype(f32)).astype(ref.dtype)

    def second(h):
        diag_x(h).wait_recv()
        add(acc, (2, h, 0), diag_in[h, 0])
        summed_y(h).start()
        diag_y(h).wait_recv()
        add(acc, (1, h, 1), diag_in[h, 1])
        summed_x(h).start()

    def third(j):
        h = j // 2
        block = blocks[j]
        part = block % 2
        if j % 2 == 0:
            direct_x(h).wait_recv()
            direct_y(h).wait_recv()
            summed_x(h).wait_recv()
            summed_y(h).wait_recv()
        if j == 0:
            direct_lines().wait_recv()
            summed_lines().wait_recv()
        total = (
            acc[0, h, part].astype(f32)
            + last_in[h, 0, part].astype(f32)
            + last_in[h, 1, part].astype(f32)
        )
        lines = acc_e[0, block] + last_e[0, block] + last_e[1, block]
        if j < tp - 1:
            acc[0, h, part] = total.astype(bf16)
            acc_e[0, block] = lines

            @pl.when((block > rank) & (rank > 0))
            def _():
                along_z(j, True).wait_recv()
                along_z_e(j, True).wait_recv()
                add(acc, (0, h, part), z_in[0, block])
                add(acc_e, (0, block), z_in_e[0, block])

            @pl.when((block < rank) & (rank < tp - 1))
            def _():
                along_z(j, False).wait_recv()
                along_z_e(j, False).wait_recv()
                add(acc, (0, h, part), z_in[1, block])
                add(acc_e, (0, block), z_in_e[1, block])

            @pl.when(block > rank)
            def _():
                along_z(j, True).start()
                along_z_e(j, True).start()

            @pl.when(block < rank)
            def _():
                along_z(j, False).start()
                along_z_e(j, False).start()
        else:
            dsum_ref[...] = total
            esum_ref[...] = lines

            @pl.when(rank > 0)
            def _():
                along_z(j, True).wait_recv()
                along_z_e(j, True).wait_recv()
                dsum_ref[...] += z_in[0, block].astype(f32)
                esum_ref[...] += z_in_e[0, block]

            @pl.when(rank < tp - 1)
            def _():
                along_z(j, False).wait_recv()
                along_z_e(j, False).wait_recv()
                dsum_ref[...] += z_in[1, block].astype(f32)
                esum_ref[...] += z_in_e[1, block]

    def front_load(block):
        return pltpu.make_async_copy(
            part_ref.at[pl.ds(block * rows, rows)],
            x_buf.at[block // 2, pl.ds(block % 2 * rows, rows)],
            f_sem.at[block],
        )

    def front_z(j, right):
        way = 0 if right else 1
        block = blocks[j]
        return pltpu.make_async_remote_copy(
            src_ref=x_buf.at[block // 2, pl.ds(block % 2 * rows, rows)],
            dst_ref=z_in.at[way, block],
            send_sem=f_send.at[way, block],
            recv_sem=f_recv.at[way, block],
            device_id=(me, rank + 1 if right else rank - 1),
            device_id_type=MESH,
        )

    def front(j):
        block = blocks[j]
        spot = (block // 2, pl.ds(pl.multiple_of(block % 2 * rows, rows), rows))
        front_load(block).wait()
        if j < tp - 1:

            @pl.when((block > rank) & (rank > 0))
            def _():
                front_z(j, True).wait_recv()
                add(x_buf, spot, z_in[0, block])

            @pl.when((block < rank) & (rank < tp - 1))
            def _():
                front_z(j, False).wait_recv()
                add(x_buf, spot, z_in[1, block])

            @pl.when(block > rank)
            def _():
                front_z(j, True).start()

            @pl.when(block < rank)
            def _():
                front_z(j, False).start()
        else:
            middle_ref[...] = hidden_ref[...].astype(f32) + x_buf[spot].astype(f32)

            @pl.when(rank > 0)
            def _():
                front_z(j, True).wait_recv()
                middle_ref[...] += z_in[0, block].astype(f32)

            @pl.when(rank < tp - 1)
            def _():
                front_z(j, False).wait_recv()
                middle_ref[...] += z_in[1, block].astype(f32)

            middle = middle_ref[...]
            mean = jnp.mean(middle * middle, axis=-1, keepdims=True)
            normed = middle * lax.rsqrt(mean + epsilon) * gain_ref[...]
            n_buf[...] = normed.astype(bf16)

    def grad_load(n, slot):
        return pltpu.make_async_copy(
            grad_ref.at[pl.ds(n * pack_rows, pack_rows)], g_buf.at[slot], g_sem.at[slot]
        )

    def hidden_grads(first, last):
        def body(n, carry):
            slot = n % 2

            @pl.when(n + 1 < tokens // pack_rows)
            def _():
                grad_load(n + 1, 1 - slot).start()

            grad_load(n, slot).wait()
            dh_buf[pl.ds(n * pack_rows, pack_rows), :] = lax.dot_general(
                g_buf[slot], down_ref[...], NT, preferred_element_type=f32
            ).astype(bf16)
            return carry

        lax.fori_loop(first, last, body, 0)

    core_of, x_of, y_of = me % 2, (me // 2) % 2, me // 4

    def tile_of(i):
        t = i // 2
        o = i % 2
        s = t // 6
        q = (1 - s) * (t % 3) + 3 * s
        h = (1 - s) * (1 - t // 3) + s * (t - 6)
        pack = (
            4 * ((y_of + q // 2) % 2) + 2 * ((x_of + q % 2) % 2) + (core_of + 1 - o) % 2
        )
        half = h * near + (1 - h) * (1 - near)
        return q, o, h, pack, half

    def tile_rows(pack, half):
        return pl.ds(pl.multiple_of(pack * pack_rows + half * tile, tile), tile)

    def row_load(i):
        q, o, h, pack, half = tile_of(i)
        return pltpu.make_async_copy(
            all_ref.at[tile_rows(pack, half)], x_buf.at[i % 2], x_sem.at[i % 2]
        )

    def prefetch(i):
        q, o, h, pack, half = tile_of(i)

        @pl.when(o == 0)
        def _():
            for part in range(2):
                block = 2 * half + part
                ref = region(pack, block)
                pltpu.make_async_remote_copy(
                    src_ref=ref,
                    dst_ref=ref,
                    send_sem=ap_send.at[q, block],
                    recv_sem=ap_recv.at[q, block],
                    device_id=(flipped(me, 1), rank),
                    device_id_type=MESH,
                ).wait_recv()

        row_load(i).start()

    def d_store(i):
        q, o, h, pack, half = tile_of(i)
        return pltpu.make_async_copy(
            d_buf.at[i % 2], d_ref.at[tile_rows(pack, half)], d_sem.at[i % 2]
        )

    units = SHARED + shared_width

    def one_tile(i, carry):
        q, o, h, pack, half = tile_of(i)
        slot = i % 2
        at = tile_rows(pack, half)
        row_load(i).wait()

        @pl.when(i >= 2)
        def _():
            d_store(i - 2).wait()

        pre = jnp.dot(x_buf[slot], both_ref[...], preferred_element_type=f32)
        gate, upper = pre[:, :UNIT], pre[:, UNIT:]
        lane = lax.broadcasted_iota(jnp.int32, (1, UNIT), 1)
        logit = gate[:, units : units + 1] + gate[:, units + 1 : units + 2]
        gate_prob = 1.0 / (1.0 + jnp.exp(-logit))
        scale = jnp.where(
            lane < expert_width, scale_ref[at, :1], jnp.where(lane < units, gate_prob, 0.0)
        )
        sigmoid = 1.0 / (1.0 + jnp.exp(-gate))
        act = gate * sigmoid
        slope = sigmoid * (1.0 + gate * (1.0 - sigmoid))
        hidden = act * upper
        d_hidden = dh_buf[at, :].astype(f32)
        line = lax.broadcasted_iota(jnp.int32, (16, UNIT), 0)
        unit = lax.broadcasted_iota(jnp.int32, (16, UNIT), 1)
        of_expert = (line == me) & (unit < expert_width)
        of_shared = (line == 8) & (unit >= SHARED)
        pick = jnp.where(of_expert | of_shared, 1.0, 0.0).astype(bf16)
        lines = lax.dot_general(
            pick, (d_hidden * hidden).astype(bf16), NT, preferred_element_type=f32
        )
        dh_buf[at, :] = (hidden * scale).astype(bf16)
        d_scaled = d_hidden * scale
        d_buf[slot, :, :UNIT] = (d_scaled * upper * slope).astype(bf16)
        d_buf[slot, :, UNIT:] = (d_scaled * act).astype(bf16)
        control(i)

        @pl.when(i < 15)
        def _():
            prefetch(i + 1)

        d_rows = lax.dot_general(d_buf[slot], both_ref[...], NT, preferred_element_type=f32)
        d_store(i).start()

        @pl.when(o == 0)
        def _():
            @pl.when(q > 0)
            def _():
                core(q - 1, h).wait_send()

            for part in range(2):
                stage[h, part] = d_rows[part * rows : (part + 1) * rows].astype(bf16)
                stage_e[q, 2 * half + part] = lines[:, part * rows : (part + 1) * rows]
            core(q, h).start()

            @pl.when(((h == 0) & (q < 3)) | ((h == 1) & (q == 3)))
            def _():
                core_e(q).start()

        @pl.when(o == 1)
        def _():
            core(q, h).wait_recv()
            for part in range(2):
                add(acc, (q, h, part), d_rows[part * rows : (part + 1) * rows])
                acc_e[q, 2 * half + part] = lines[:, part * rows : (part + 1) * rows]

            @pl.when(((h == 0) & (q < 3)) | ((h == 1) & (q == 3)))
            def _():
                core_e(q).wait_recv()
                acc_e[q] = acc_e[q] + other_e[q]

                @pl.when(q == 1)
                def _():
                    direct_lines().start()

                @pl.when(q == 3)
                def _():
                    diag_lines().start()

            @pl.when(q == 1)
            def _():
                direct_x(h).start()

            @pl.when(q == 2)
            def _():
                direct_y(h).start()

            @pl.when(q == 3)
            def _():
                diag_x(h).start()
                diag_y(h).start()

        return carry

    def y_store(n, slot):
        return pltpu.make_async_copy(
            g_buf.at[slot], y_ref.at[pl.ds(n * pack_rows, pack_rows)], y_sem.at[slot]
        )

    def outputs(first, last):
        def body(n, carry):
            slot = n % 2

            @pl.when(n >= 2)
            def _():
                y_store(n - 2, slot).wait()

            g_buf[slot] = jnp.dot(
                dh_buf[pl.ds(n * pack_rows, pack_rows), :],
                down_ref[...],
                preferred_element_type=f32,
            ).astype(bf16)
            y_store(n, slot).start()
            return carry

        lax.fori_loop(first, last, body, 0)

    grad_load(0, 0).start()
    packs = tokens // pack_rows
    for block in blocks:
        front_load(block).start()
    front(0)
    hidden_grads(0, 3)
    front(1)
    hidden_grads(3, 6)
    front(2)
    hidden_grads(6, packs)
    front(3)
    mine = pltpu.make_async_copy(n_buf, region(me, rank), local_sem)
    mine.start()
    mine.wait()

    @pl.when(rank < tp - 1)
    def _():
        gather_z(rank, True).start()

    @pl.when(rank > 0)
    def _():
        gather_z(rank, False).start()

    start_plane(rank)
    for j in range(tp - 1):
        block = blocks[j]

        @pl.when(block > rank)
        def _():
            front_z(j, True).wait_send()

        @pl.when(block < rank)
        def _():
            front_z(j, False).wait_send()

    z_step(1)
    prefetch(0)
    lax.fori_loop(0, 16, one_tile, 0)
    hidden_store = pltpu.make_async_copy(dh_buf, hid_ref, h_sem)
    hidden_store.start()
    outputs(0, 4)
    second(0)
    outputs(4, 6)
    diag_lines().wait_recv()
    acc_e[2] = acc_e[2] + diag_e[...]
    summed_lines().start()
    second(1)
    outputs(6, packs)
    third(0)
    third(1)
    third(2)
    third(3)

    hidden_store.wait()
    for n in (packs - 2, packs - 1):
        y_store(n, n % 2).wait()
    for i in (14, 15):
        d_store(i).wait()
    core(3, 0).wait_send()
    core(3, 1).wait_send()
    for q in range(4):
        core_e(q).wait_send()
    for copy in (diag_lines, direct_lines, summed_lines):
        copy().wait_send()
    for h in range(2):
        for copy in (diag_x, diag_y, direct_x, direct_y, summed_x, summed_y):
            copy(h).wait_send()
    for block in order:
        for q in range(4):
            to_core(q, block).wait_send()
        for copy in (own_x, own_y, x_to_y, y_to_x):
            copy(block).wait_send()
    for j in range(tp - 1):
        block = blocks[j]

        @pl.when(block > rank)
        def _():
            along_z(j, True).wait_send()
            along_z_e(j, True).wait_send()

        @pl.when(block < rank)
        def _():
            along_z(j, False).wait_send()
            along_z_e(j, False).wait_send()

    for block in range(tp):

        @pl.when((block <= rank) & (rank < tp - 1))
        def _():
            gather_z(block, True).wait_send()

        @pl.when((block >= rank) & (rank > 0))
        def _():
            gather_z(block, False).wait_send()


def ffn(
    part, hidden, gain, grad_all, both, down, scale, fsdp, tp, expert_width, shared_width, collective_id
):
    rows, width = hidden.shape
    tokens = rows * fsdp * tp
    pack_rows = rows * tp
    tile = pack_rows // 2
    bf16 = jnp.bfloat16
    f32 = jnp.float32
    dma = pltpu.SemaphoreType.DMA
    anywhere = pl.BlockSpec(memory_space=pl.ANY)
    vmem = pl.BlockSpec(memory_space=pltpu.VMEM)
    return pl.pallas_call(
        functools.partial(ffn_kernel, tp, expert_width, shared_width),
        out_shape=[
            jax.ShapeDtypeStruct((rows, width), f32),
            jax.ShapeDtypeStruct((tokens, width), bf16),
            jax.ShapeDtypeStruct((tokens, 2 * UNIT), bf16),
            jax.ShapeDtypeStruct((tokens, UNIT), bf16),
            jax.ShapeDtypeStruct((tokens, width), bf16),
            jax.ShapeDtypeStruct((rows, width), f32),
            jax.ShapeDtypeStruct((16, rows), f32),
        ],
        in_specs=[anywhere, vmem, vmem, anywhere, vmem, vmem, vmem],
        out_specs=[vmem, anywhere, anywhere, anywhere, anywhere, vmem, vmem],
        scratch_shapes=[
            pltpu.VMEM((rows, width), bf16),
            pltpu.VMEM((2, pack_rows, width), bf16),
            pltpu.VMEM((2, tile, width), bf16),
            pltpu.VMEM((tokens, UNIT), bf16),
            pltpu.VMEM((2, tile, 2 * UNIT), bf16),
            pltpu.VMEM((2, 2, rows, width), bf16),
            pltpu.VMEM((4, 2, 2, rows, width), bf16),
            pltpu.VMEM((2, 2, rows, width), bf16),
            pltpu.VMEM((2, 2, 2, rows, width), bf16),
            pltpu.VMEM((2, tp, rows, width), bf16),
            pltpu.VMEM((4, tp, 16, rows), f32),
            pltpu.VMEM((4, tp, 16, rows), f32),
            pltpu.VMEM((4, tp, 16, rows), f32),
            pltpu.VMEM((tp, 16, rows), f32),
            pltpu.VMEM((2, tp, 16, rows), f32),
            pltpu.VMEM((2, tp, 16, rows), f32),
            dma, dma((2,)), dma((2,)), dma((2,)), dma, dma((2,)),
            dma((2, tp)), dma((2, tp)), dma((8, tp)), dma((8, tp)),
            dma((4, 2)), dma((4, 2)), dma((4,)), dma((4,)),
            dma((6, 2)), dma((6, 2)), dma((3,)), dma((3,)),
            dma((2, tp)), dma((2, tp)), dma((2, tp)), dma((2, tp)),
            dma((tp,)), dma((2, tp)), dma((2, tp)),
        ],
        compiler_params=pltpu.CompilerParams(
            collective_id=collective_id, has_side_effects=True, vmem_limit_bytes=61 << 20
        ),
        name="ffn",
    )(part, hidden, gain, grad_all, both, down, scale)


def dense_plan(
    hidden_in,
    out_grad,
    segment_ids,
    expert_ids,
    route_weights,
    attn_gain,
    ffn_gain,
    qkv_weight,
    qkv_bias,
    out_weight,
    shared_gate_up,
    shared_down,
    shared_gate_vec,
    expert_gate_up,
    expert_down,
):
    every = ("fsdp", "tp")
    tp_rank = lax.axis_index("tp")
    experts = lax.axis_size("fsdp")
    packs = experts
    length = segment_ids.shape[1]
    own_rows = hidden_in.shape[0]
    model_width = hidden_in.shape[1]
    bf16 = jnp.bfloat16
    f32 = jnp.float32

    grad_all = lax.all_gather(out_grad, every, axis=0, tiled=True)
    shared_up = lax.all_to_all(shared_gate_up, "fsdp", split_axis=2, concat_axis=0, tiled=True)
    shared_dn = lax.all_to_all(shared_down, "fsdp", split_axis=0, concat_axis=1, tiled=True)
    expert_up = expert_gate_up[0]
    expert_dn = expert_down[0]
    expert_width = expert_up.shape[2]
    shared_width = shared_up.shape[2]

    chosen = expert_ids[:, :, None] == jnp.arange(experts, dtype=jnp.int32)
    table = jnp.sum(jnp.where(chosen, route_weights[:, :, None], 0.0), axis=1)
    local_heads = qkv_weight.shape[2]
    head_dim = qkv_weight.shape[3]
    score_scale = head_dim ** (-0.5)
    cos_table, sin_table = rope_tables(length, head_dim)
    positions = jnp.arange(length, dtype=jnp.int32)
    segments = segment_ids[0]
    allowed = (positions[:, None] >= positions[None, :]) & (segments[:, None] == segments[None, :])
    hidden_float = hidden_in.astype(f32)
    attn_inverse = inverse_rms(hidden_float)
    bias_rows = 3 * local_heads
    bias_columns = qkv_bias.shape[2]
    bias_piece = jnp.pad(
        qkv_bias.reshape(bias_rows, bias_columns), ((0, 16 - bias_rows), (0, 128 - bias_columns))
    )
    normed_one, qkv_flat, out_pieces, tables, bias_pieces = prologue(
        (hidden_float * attn_inverse * attn_gain).astype(bf16),
        [qkv_weight.reshape(-1, 3 * local_heads * head_dim), out_weight, table.T, bias_piece],
        experts,
        lax.axis_size("tp"),
        4,
    )
    out_full = out_pieces.reshape(experts, local_heads * head_dim, -1)
    out_full = out_full.transpose(1, 0, 2).reshape(local_heads * head_dim, model_width)
    expert_scale = lax.dynamic_index_in_dim(
        tables.reshape(packs, experts, length), lax.axis_index("fsdp"), axis=1, keepdims=False
    ).reshape(-1)
    bias_full = bias_pieces.reshape(experts, 16, 128)[:, :bias_rows, :bias_columns]
    bias_full = bias_full.transpose(1, 0, 2).reshape(3, local_heads, head_dim)
    qkv = (
        jnp.dot(normed_one, qkv_flat, preferred_element_type=f32).reshape(
            length, 3, local_heads, head_dim
        )
        + bias_full
    )
    query = rotate(qkv[:, 0], cos_table, sin_table).astype(bf16)
    keys = rotate(qkv[:, 1], cos_table, sin_table).astype(bf16)
    values = qkv[:, 2].astype(bf16)
    scores = masked_scores(query, keys, allowed, score_scale)
    row_peak = jnp.max(scores, axis=-1, keepdims=True)
    log_total = row_peak + jnp.log(jnp.sum(jnp.exp(scores - row_peak), axis=-1, keepdims=True))
    probs_b = jnp.exp(scores - log_total).astype(bf16)
    heads_out = (
        jnp.einsum("hqk,khd->qhd", probs_b, values, preferred_element_type=f32)
        .astype(bf16)
        .reshape(length, -1)
    )
    vec_high = shared_gate_vec.astype(bf16)
    vec_low = (shared_gate_vec - vec_high.astype(f32)).astype(bf16)
    gap = jnp.zeros((model_width, SHARED - expert_width), bf16)
    rest = jnp.zeros((model_width, UNIT - SHARED - shared_width), bf16)
    both_w = jnp.concatenate(
        [
            expert_up[:, 0],
            gap,
            shared_up[:, 0],
            vec_high[:, None],
            vec_low[:, None],
            rest[:, 2:],
            expert_up[:, 1],
            gap,
            shared_up[:, 1],
            rest,
        ],
        axis=1,
    )
    down_w = jnp.concatenate([expert_dn, gap.T, shared_dn, rest.T], axis=0)
    middle, normed_all, d_all, hidden_all, token_part, d_normed_two, extra_sum = ffn(
        jnp.dot(heads_out, out_full, preferred_element_type=f32).astype(bf16),
        hidden_in,
        ffn_gain[None],
        grad_all,
        both_w,
        down_w,
        jnp.broadcast_to(expert_scale[:, None], (expert_scale.shape[0], 128)),
        experts,
        lax.axis_size("tp"),
        expert_width,
        shared_width,
        1,
    )
    ffn_inverse = inverse_rms(middle)
    normed_two_own = (middle * ffn_inverse * ffn_gain).astype(bf16)
    (total,) = scatter_sum([token_part], experts, lax.axis_size("tp"), 3)
    hidden_out = (middle + total).astype(bf16)
    own_start = tp_rank * own_rows
    ids_own = lax.dynamic_slice_in_dim(expert_ids, own_start, own_rows)
    picked = ids_own[:, :, None] == jnp.arange(experts, dtype=jnp.int32)
    route_grad = jnp.sum(jnp.where(picked, extra_sum[:experts].T[:, None, :], 0.0), axis=-1)
    gate_grad = extra_sum[experts]
    units = SHARED + shared_width
    g_down = jnp.dot(hidden_all.T, grad_all, preferred_element_type=f32)
    g_both = jnp.dot(normed_all.T, d_all, preferred_element_type=f32)
    g_expert_down = g_down[:expert_width][None]
    g_expert_gate_up = jnp.stack(
        [g_both[:, :expert_width], g_both[:, UNIT : UNIT + expert_width]], axis=1
    )[None]
    g_shared_gate_up = lax.all_to_all(
        jnp.stack(
            [g_both[:, SHARED:units], g_both[:, UNIT + SHARED : UNIT + units]], axis=1
        ).astype(bf16),
        "fsdp",
        split_axis=0,
        concat_axis=2,
        tiled=True,
    ).astype(f32)
    g_shared_down = lax.all_to_all(
        g_down[SHARED:units].astype(bf16), "fsdp", split_axis=1, concat_axis=0, tiled=True
    ).astype(f32)

    own_gate = jax.nn.sigmoid(jnp.sum(normed_two_own.astype(f32) * shared_gate_vec, axis=-1))
    logit_grad = gate_grad * own_gate * (1.0 - own_gate)
    d_normed_two = d_normed_two + logit_grad[:, None] * shared_gate_vec
    g_gate_vec = jnp.sum(normed_two_own.astype(f32) * logit_grad[:, None], axis=0)
    hat_two = middle * ffn_inverse
    g_ffn_gain = jnp.sum(d_normed_two * hat_two, axis=0)
    middle_grad = out_grad.astype(f32) + norm_backward(d_normed_two, hat_two, ffn_inverse, ffn_gain)
    d_rows = spread(middle_grad.astype(bf16))
    g_out = jnp.dot(heads_out.T, d_rows, preferred_element_type=f32)
    d_heads = (
        jnp.dot(d_rows, out_full.T, preferred_element_type=f32)
        .astype(bf16)
        .reshape(length, local_heads, head_dim)
    )
    heads_three = heads_out.reshape(length, local_heads, head_dim)
    scores_again = masked_scores(query, keys, allowed, score_scale)
    probs_full = jnp.exp(scores_again - log_total)
    probs_again = probs_full.astype(bf16)
    d_values = jnp.einsum("hqk,qhd->khd", probs_again, d_heads, preferred_element_type=f32)
    d_probs = jnp.einsum("qhd,khd->hqk", d_heads, values, preferred_element_type=f32)
    delta = jnp.sum(d_heads.astype(f32) * heads_three.astype(f32), axis=-1)
    d_scores = (probs_full * (d_probs - delta.T[:, :, None])).astype(bf16)
    d_query = jnp.einsum("hqk,khd->qhd", d_scores, keys, preferred_element_type=f32) * score_scale
    d_keys = jnp.einsum("hqk,qhd->khd", d_scores, query, preferred_element_type=f32) * score_scale
    d_qkv = jnp.stack(
        [unrotate(d_query, cos_table, sin_table), unrotate(d_keys, cos_table, sin_table), d_values],
        axis=1,
    )
    g_bias = jnp.sum(d_qkv, axis=0)
    d_qkv_b = d_qkv.astype(bf16).reshape(length, -1)
    g_qkv = jnp.dot(normed_one.T, d_qkv_b, preferred_element_type=f32).reshape(model_width, 3, local_heads, head_dim)
    d_normed_one = head_total(jnp.dot(d_qkv_b, qkv_flat.T, preferred_element_type=f32))
    hat_one = hidden_float * attn_inverse
    g_attn_gain = jnp.sum(d_normed_one * hat_one, axis=0)
    hidden_grad = middle_grad + norm_backward(d_normed_one, hat_one, attn_inverse, attn_gain)
    g_qkv, g_bias, g_out = (
        lax.psum_scatter(g_qkv.astype(bf16), "fsdp", scatter_dimension=0, tiled=True).astype(f32),
        lax.psum_scatter(g_bias.astype(bf16), "fsdp", scatter_dimension=2, tiled=True).astype(f32),
        lax.psum_scatter(g_out.astype(bf16), "fsdp", scatter_dimension=1, tiled=True).astype(f32),
    )
    g_attn_gain, g_ffn_gain, g_gate_vec = (
        lax.psum_scatter(g_attn_gain, every, scatter_dimension=0, tiled=True),
        lax.psum_scatter(g_ffn_gain, every, scatter_dimension=0, tiled=True),
        lax.psum_scatter(g_gate_vec, every, scatter_dimension=0, tiled=True),
    )
    return (
        hidden_out,
        hidden_grad,
        route_grad,
        g_attn_gain,
        g_ffn_gain,
        g_qkv,
        g_bias,
        g_out,
        g_shared_gate_up,
        g_shared_down,
        g_gate_vec,
        g_expert_gate_up,
        g_expert_down,
    )


def on_device(*arrays):
    if lax.axis_size("fsdp") == 8 and lax.axis_size("tp") == 4 and arrays[3].shape[1] >= 3:
        return dense_plan(*arrays)
    return routed_plan(*arrays)


def solution(mesh):
    placed = (
        P(("fsdp", "tp"), None),
        P(("fsdp", "tp"), None),
        P("fsdp", None),
        P("fsdp", None),
        P("fsdp", None),
        P(),
        P(),
        P("fsdp", None, "tp", None),
        P(None, "tp", "fsdp"),
        P("tp", "fsdp"),
        P("fsdp", None, "tp"),
        P("tp", "fsdp"),
        P(),
        P("fsdp", None, None, "tp"),
        P("fsdp", "tp", None),
    )
    return jax.shard_map(
        on_device,
        mesh=mesh,
        in_specs=placed,
        out_specs=(
            P(("fsdp", "tp"), None),
            P(("fsdp", "tp"), None),
            P(("fsdp", "tp"), None),
            P(("fsdp", "tp")),
            P(("fsdp", "tp")),
            P("fsdp", None, "tp", None),
            P(None, "tp", "fsdp"),
            P("tp", "fsdp"),
            P("fsdp", None, "tp"),
            P("tp", "fsdp"),
            P(("fsdp", "tp")),
            P("fsdp", None, None, "tp"),
            P("fsdp", "tp", None),
        ),
        check_vma=False,
    )
```

```python
import functools

import jax
import jax.experimental.pallas as pl
import jax.experimental.pallas.tpu as pltpu
import jax.numpy as jnp
from jax import lax
from jax.sharding import PartitionSpec as P

epsilon = 1e-06


def rope_tables(length, head_dim):
    half_dim = head_dim // 2
    ratios = jnp.arange(half_dim, dtype=jnp.float32) * (2.0 / head_dim)
    frequency = jnp.exp(-jnp.log(10000.0) * ratios)
    angles = jnp.arange(length, dtype=jnp.float32)[:, None] * frequency[None, :]
    return (jnp.cos(angles)[:, None, :], jnp.sin(angles)[:, None, :])


def rotate(tensor, cos_table, sin_table):
    half_dim = tensor.shape[-1] // 2
    front_half = tensor[..., :half_dim]
    back_half = tensor[..., half_dim:]
    return jnp.concatenate(
        [
            front_half * cos_table - back_half * sin_table,
            back_half * cos_table + front_half * sin_table,
        ],
        axis=-1,
    )


def unrotate(tensor, cos_table, sin_table):
    half_dim = tensor.shape[-1] // 2
    front_half = tensor[..., :half_dim]
    back_half = tensor[..., half_dim:]
    return jnp.concatenate(
        [
            front_half * cos_table + back_half * sin_table,
            back_half * cos_table - front_half * sin_table,
        ],
        axis=-1,
    )


def silu_parts(gate_in):
    sigmoid_value = jax.nn.sigmoid(gate_in)
    return (gate_in * sigmoid_value, sigmoid_value * (1.0 + gate_in * (1.0 - sigmoid_value)))


def slot_table(route_ids, experts, capacity):
    flat_ids = route_ids.reshape(-1)
    onehot = (flat_ids[:, None] == jnp.arange(experts, dtype=jnp.int32)[None, :]).astype(jnp.int32)
    before = jnp.cumsum(onehot, axis=0, dtype=jnp.int32) - onehot
    ranks = jnp.sum(before * onehot, axis=1, dtype=jnp.int32)
    places = flat_ids * capacity + ranks
    filler = jnp.arange(flat_ids.shape[0], dtype=jnp.int32) + 1
    slot_rows = jnp.zeros((experts * capacity,), jnp.int32).at[places].set(filler)
    return (places.reshape(route_ids.shape), slot_rows.reshape(experts, capacity))


def inverse_rms(tensor):
    return lax.rsqrt(jnp.mean(tensor * tensor, axis=-1, keepdims=True) + epsilon)


def norm_backward(d_normed, hat_rows, inverse, gain_vec):
    d_hat = d_normed * gain_vec
    return inverse * (d_hat - hat_rows * jnp.mean(d_hat * hat_rows, axis=-1, keepdims=True))


def masked_scores(query, keys, allowed, score_scale):
    raw = jnp.einsum("qhd,khd->hqk", query, keys, preferred_element_type=jnp.float32) * score_scale
    return jnp.where(allowed[None], raw, -1e30)


def spread(rows):
    return lax.all_gather(rows, "tp", axis=0, tiled=True)


def head_total(partial_rows):
    return lax.psum_scatter(
        partial_rows.astype(jnp.bfloat16), "tp", scatter_dimension=0, tiled=True
    ).astype(jnp.float32)


def to_experts(buffer):
    return lax.all_to_all(buffer, "fsdp", split_axis=0, concat_axis=0, tiled=True)


def from_experts(buffer):
    return lax.all_to_all(buffer, "fsdp", split_axis=0, concat_axis=0, tiled=True)


def routed_plan(
    hidden_in,
    out_grad,
    segment_ids,
    expert_ids,
    route_weights,
    attn_gain,
    ffn_gain,
    qkv_weight,
    qkv_bias,
    out_weight,
    shared_gate_up,
    shared_down,
    shared_gate_vec,
    expert_gate_up,
    expert_down,
):
    tp_rank = lax.axis_index("tp")
    experts = lax.axis_size("fsdp")
    length = segment_ids.shape[1]
    top_count = expert_ids.shape[1]
    capacity = 3 * length * top_count // (2 * experts)
    own_rows = hidden_in.shape[0]
    model_width = hidden_in.shape[1]
    qkv_full, bias_full, out_full, shared_full, shared_down_full = (
        lax.all_gather(qkv_weight, "fsdp", axis=0, tiled=True),
        lax.all_gather(qkv_bias.astype(jnp.bfloat16), "fsdp", axis=2, tiled=True).astype(
            qkv_bias.dtype
        ),
        lax.all_gather(out_weight, "fsdp", axis=1, tiled=True),
        lax.all_gather(shared_gate_up, "fsdp", axis=0, tiled=True),
        lax.all_gather(shared_down, "fsdp", axis=1, tiled=True),
    )
    local_heads = qkv_full.shape[2]
    head_dim = qkv_full.shape[3]
    score_scale = head_dim ** (-0.5)
    cos_table, sin_table = rope_tables(length, head_dim)
    positions = jnp.arange(length, dtype=jnp.int32)
    segments = segment_ids[0]
    allowed = (positions[:, None] >= positions[None, :]) & (segments[:, None] == segments[None, :])
    hidden_float = hidden_in.astype(jnp.float32)
    attn_inverse = inverse_rms(hidden_float)
    normed_one = spread((hidden_float * attn_inverse * attn_gain).astype(jnp.bfloat16))
    qkv_flat = qkv_full.reshape(model_width, -1)
    qkv = (
        jnp.dot(normed_one, qkv_flat, preferred_element_type=jnp.float32).reshape(
            length, 3, local_heads, head_dim
        )
        + bias_full
    )
    query = rotate(qkv[:, 0], cos_table, sin_table).astype(jnp.bfloat16)
    keys = rotate(qkv[:, 1], cos_table, sin_table).astype(jnp.bfloat16)
    values = qkv[:, 2].astype(jnp.bfloat16)
    scores = masked_scores(query, keys, allowed, score_scale)
    row_peak = jnp.max(scores, axis=-1, keepdims=True)
    log_total = row_peak + jnp.log(jnp.sum(jnp.exp(scores - row_peak), axis=-1, keepdims=True))
    probs_b = jnp.exp(scores - log_total).astype(jnp.bfloat16)
    heads_out = (
        jnp.einsum("hqk,khd->qhd", probs_b, values, preferred_element_type=jnp.float32)
        .astype(jnp.bfloat16)
        .reshape(length, -1)
    )
    middle = hidden_float + head_total(
        jnp.dot(heads_out, out_full, preferred_element_type=jnp.float32)
    )
    ffn_inverse = inverse_rms(middle)
    normed_two_own = (middle * ffn_inverse * ffn_gain).astype(jnp.bfloat16)
    normed_two = spread(normed_two_own)
    gate_prob = jax.nn.sigmoid(jnp.sum(normed_two.astype(jnp.float32) * shared_gate_vec, axis=-1))
    shared_flat = shared_full.reshape(model_width, -1)
    shared_width = shared_full.shape[2]
    shared_pre = jnp.dot(normed_two, shared_flat, preferred_element_type=jnp.float32)
    shared_act, shared_slope = silu_parts(shared_pre[:, :shared_width])
    shared_upper = shared_pre[:, shared_width:]
    shared_hidden = (shared_act * shared_upper).astype(jnp.bfloat16)
    shared_part = jnp.dot(shared_hidden, shared_down_full, preferred_element_type=jnp.float32)
    places, slot_rows = slot_table(expert_ids, experts, capacity)
    filled = slot_rows > 0
    route_index = jnp.maximum(slot_rows - 1, 0)
    source_rows = route_index // top_count
    flat_weights = route_weights.reshape(-1)
    slot_weights = jnp.where(filled, flat_weights[route_index], 0.0)
    send_rows = jnp.where(filled[:, :, None], normed_two[source_rows], jnp.zeros((), jnp.bfloat16))
    arrived = to_experts(send_rows).reshape(-1, model_width)
    expert_flat = expert_gate_up[0].reshape(model_width, -1)
    expert_width = expert_gate_up.shape[3]
    down_local = expert_down[0]
    expert_pre = jnp.dot(arrived, expert_flat, preferred_element_type=jnp.float32)
    expert_act, expert_slope = silu_parts(expert_pre[:, :expert_width])
    expert_upper = expert_pre[:, expert_width:]
    expert_hidden = (expert_act * expert_upper).astype(jnp.bfloat16)
    expert_part = jnp.dot(expert_hidden, down_local, preferred_element_type=jnp.float32).astype(
        jnp.bfloat16
    )
    returned = from_experts(expert_part.reshape(experts, capacity, model_width)).reshape(
        experts * capacity, model_width
    )
    picked = returned[places].astype(jnp.float32)
    token_term = gate_prob[:, None] * shared_part + jnp.sum(
        route_weights[:, :, None] * picked, axis=1
    )
    own_extra = 0.0
    total = (
        lax.psum_scatter(
            token_term.astype(jnp.bfloat16), "tp", scatter_dimension=0, tiled=True
        ).astype(jnp.float32)
        + own_extra
    )
    hidden_out = (middle + total).astype(jnp.bfloat16)
    grad_rows = spread(out_grad)
    grad_float = grad_rows.astype(jnp.float32)
    gate_part = jnp.sum(grad_float * shared_part, axis=-1)
    scaled_grad = (gate_prob[:, None] * grad_float).astype(jnp.bfloat16)
    shared_d_hidden = jnp.dot(scaled_grad, shared_down_full.T, preferred_element_type=jnp.float32)
    shared_d_cat = jnp.concatenate(
        [
            (shared_d_hidden * shared_upper * shared_slope).astype(jnp.bfloat16),
            (shared_d_hidden * shared_act).astype(jnp.bfloat16),
        ],
        axis=1,
    )
    g_shared_down = jnp.dot(shared_hidden.T, scaled_grad, preferred_element_type=jnp.float32)
    g_shared_gate_up = jnp.dot(
        normed_two.T, shared_d_cat, preferred_element_type=jnp.float32
    ).reshape(shared_full.shape)
    d_normed_part = jnp.dot(shared_d_cat, shared_flat.T, preferred_element_type=jnp.float32)
    expert_grad_in = (slot_weights[:, :, None] * grad_float[source_rows]).astype(jnp.bfloat16)
    arrived_grad = to_experts(expert_grad_in).reshape(-1, model_width)
    back_act, back_slope, back_upper, back_hidden = (
        expert_act,
        expert_slope,
        expert_upper,
        expert_hidden,
    )
    expert_d_hidden = jnp.dot(arrived_grad, down_local.T, preferred_element_type=jnp.float32)
    expert_d_cat = jnp.concatenate(
        [
            (expert_d_hidden * back_upper * back_slope).astype(jnp.bfloat16),
            (expert_d_hidden * back_act).astype(jnp.bfloat16),
        ],
        axis=1,
    )
    g_expert_down = jnp.dot(back_hidden.T, arrived_grad, preferred_element_type=jnp.float32)[None]
    g_expert_gate_up = jnp.dot(arrived.T, expert_d_cat, preferred_element_type=jnp.float32).reshape(
        expert_gate_up.shape
    )
    expert_d_part = jnp.dot(expert_d_cat, expert_flat.T, preferred_element_type=jnp.float32).astype(
        jnp.bfloat16
    )
    route_part = jnp.sum(grad_float[:, None, :] * picked, axis=-1)
    returned_grad = from_experts(expert_d_part.reshape(experts, capacity, model_width)).reshape(
        experts * capacity, model_width
    )
    d_normed_part = d_normed_part + jnp.sum(returned_grad[places].astype(jnp.float32), axis=1)
    d_normed_two, route_grad, gate_grad = (
        lax.psum_scatter(
            d_normed_part.astype(jnp.bfloat16), "tp", scatter_dimension=0, tiled=True
        ).astype(jnp.float32),
        lax.psum_scatter(
            route_part.astype(jnp.bfloat16), "tp", scatter_dimension=0, tiled=True
        ).astype(jnp.float32),
        lax.psum_scatter(
            gate_part.astype(jnp.bfloat16), "tp", scatter_dimension=0, tiled=True
        ).astype(jnp.float32),
    )
    own_gate = lax.dynamic_slice_in_dim(gate_prob, tp_rank * own_rows, own_rows)
    logit_grad = gate_grad * own_gate * (1.0 - own_gate)
    d_normed_two = d_normed_two + logit_grad[:, None] * shared_gate_vec
    g_gate_vec = jnp.sum(normed_two_own.astype(jnp.float32) * logit_grad[:, None], axis=0)
    hat_two = middle * ffn_inverse
    g_ffn_gain = jnp.sum(d_normed_two * hat_two, axis=0)
    middle_grad = out_grad.astype(jnp.float32) + norm_backward(
        d_normed_two, hat_two, ffn_inverse, ffn_gain
    )
    d_rows = spread(middle_grad.astype(jnp.bfloat16))
    g_out = jnp.dot(heads_out.T, d_rows, preferred_element_type=jnp.float32)
    d_heads = (
        jnp.dot(d_rows, out_full.T, preferred_element_type=jnp.float32)
        .astype(jnp.bfloat16)
        .reshape(length, local_heads, head_dim)
    )
    heads_three = heads_out.reshape(length, local_heads, head_dim)
    scores_again = masked_scores(query, keys, allowed, score_scale)
    probs_full = jnp.exp(scores_again - log_total)
    probs_again = probs_full.astype(jnp.bfloat16)
    d_values = jnp.einsum("hqk,qhd->khd", probs_again, d_heads, preferred_element_type=jnp.float32)
    d_probs = jnp.einsum("qhd,khd->hqk", d_heads, values, preferred_element_type=jnp.float32)
    delta = jnp.sum(d_heads.astype(jnp.float32) * heads_three.astype(jnp.float32), axis=-1)
    d_scores = (probs_full * (d_probs - delta.T[:, :, None])).astype(jnp.bfloat16)
    d_query = (
        jnp.einsum("hqk,khd->qhd", d_scores, keys, preferred_element_type=jnp.float32) * score_scale
    )
    d_keys = (
        jnp.einsum("hqk,qhd->khd", d_scores, query, preferred_element_type=jnp.float32)
        * score_scale
    )
    d_qkv = jnp.stack(
        [unrotate(d_query, cos_table, sin_table), unrotate(d_keys, cos_table, sin_table), d_values],
        axis=1,
    )
    g_bias = jnp.sum(d_qkv, axis=0)
    d_qkv_b = d_qkv.astype(jnp.bfloat16).reshape(length, -1)
    g_qkv = jnp.dot(normed_one.T, d_qkv_b, preferred_element_type=jnp.float32).reshape(
        qkv_full.shape
    )
    d_normed_one = head_total(jnp.dot(d_qkv_b, qkv_flat.T, preferred_element_type=jnp.float32))
    hat_one = hidden_float * attn_inverse
    g_attn_gain = jnp.sum(d_normed_one * hat_one, axis=0)
    hidden_grad = middle_grad + norm_backward(d_normed_one, hat_one, attn_inverse, attn_gain)
    g_qkv, g_bias, g_out, g_shared_gate_up, g_shared_down = (
        lax.psum_scatter(
            g_qkv.astype(jnp.bfloat16), "fsdp", scatter_dimension=0, tiled=True
        ).astype(jnp.float32),
        lax.psum_scatter(
            g_bias.astype(jnp.bfloat16), "fsdp", scatter_dimension=2, tiled=True
        ).astype(jnp.float32),
        lax.psum_scatter(
            g_out.astype(jnp.bfloat16), "fsdp", scatter_dimension=1, tiled=True
        ).astype(jnp.float32),
        lax.psum_scatter(
            g_shared_gate_up.astype(jnp.bfloat16), "fsdp", scatter_dimension=0, tiled=True
        ).astype(jnp.float32),
        lax.psum_scatter(
            g_shared_down.astype(jnp.bfloat16), "fsdp", scatter_dimension=1, tiled=True
        ).astype(jnp.float32),
    )
    g_attn_gain, g_ffn_gain, g_gate_vec = (
        lax.psum_scatter(g_attn_gain, ("fsdp", "tp"), scatter_dimension=0, tiled=True),
        lax.psum_scatter(g_ffn_gain, ("fsdp", "tp"), scatter_dimension=0, tiled=True),
        lax.psum_scatter(g_gate_vec, ("fsdp", "tp"), scatter_dimension=0, tiled=True),
    )
    return (
        hidden_out,
        hidden_grad,
        route_grad,
        g_attn_gain,
        g_ffn_gain,
        g_qkv,
        g_bias,
        g_out,
        g_shared_gate_up,
        g_shared_down,
        g_gate_vec,
        g_expert_gate_up,
        g_expert_down,
    )


MESH = pl.DeviceIdType.MESH


def flipped(index, bit):
    return index + bit - 2 * bit * ((index // bit) % 2)


def place():
    me = lax.axis_index("fsdp")
    rank = lax.axis_index("tp")
    return me, rank


def greet(me, rank, tp):
    barrier = pltpu.get_barrier_semaphore()
    for bit in (1, 2, 4):
        pl.semaphore_signal(
            barrier, inc=1, device_id=(flipped(me, bit), rank), device_id_type=MESH
        )

    @pl.when(rank > 0)
    def _():
        pl.semaphore_signal(barrier, inc=1, device_id=(me, rank - 1), device_id_type=MESH)

    @pl.when(rank < tp - 1)
    def _():
        pl.semaphore_signal(barrier, inc=1, device_id=(me, rank + 1), device_id_type=MESH)

    left = (rank + tp - 1) // tp
    right = (2 * (tp - 1) - rank) // tp
    pl.semaphore_wait(barrier, 3 + left + right)


def prologue_kernel(tp, halved, *refs):
    parts = len(halved)
    own_ref, pieces = refs[0], refs[1 : 1 + parts]
    rows_ref, fulls = refs[1 + parts], refs[2 + parts : 2 + 2 * parts]
    l_sem, z_send, z_recv, p_send, p_recv = refs[2 + 2 * parts :]
    me, rank = place()
    greet(me, rank, tp)
    rows = own_ref.shape[0]

    def along_z(block, right):
        way = 0 if right else 1
        spot = rows_ref.at[pl.ds(block * rows, rows)]
        return pltpu.make_async_remote_copy(
            src_ref=spot,
            dst_ref=spot,
            send_sem=z_send.at[way, block],
            recv_sem=z_recv.at[way, block],
            device_id=(me, rank + 1 if right else rank - 1),
            device_id_type=MESH,
        )

    def region(i, owner_bits, start=0, count=None):
        owner = me
        for one in (2, 4):
            if owner_bits & one:
                owner = flipped(owner, one)
        size = pieces[i].shape[0]
        count = size if count is None else count
        return fulls[i].at[pl.ds(owner * size + start, count)]

    def across(i, bit, owner_bits, slot, start=0, count=None):
        spot = region(i, owner_bits, start, count)
        return pltpu.make_async_remote_copy(
            src_ref=pieces[i] if owner_bits == 0 else spot,
            dst_ref=spot,
            send_sem=p_send.at[slot, i],
            recv_sem=p_recv.at[slot, i],
            device_id=(flipped(me, bit), rank),
            device_id_type=MESH,
        )

    def to_core(q, i):
        return across(i, 1, 2 * q, q)

    def own_x(i):
        return across(i, 2, 0, 4)

    def own_y(i):
        return across(i, 4, 0, 5)

    def x_to_y(i):
        size = pieces[i].shape[0]
        return across(i, 4, 2, 6, 0, size // 2 if halved[i] else size)

    def y_to_x(i):
        size = pieces[i].shape[0]
        return across(i, 2, 4, 7, size // 2, size // 2)

    def local(i):
        return pltpu.make_async_copy(pieces[i], region(i, 0), l_sem.at[i])

    def forward(i):
        own_x(i).wait_recv()
        x_to_y(i).start()
        to_core(1, i).start()
        own_y(i).wait_recv()
        if halved[i]:
            y_to_x(i).start()
        to_core(2, i).start()

    def finish(i):
        x_to_y(i).wait_recv()
        if halved[i]:
            y_to_x(i).wait_recv()
        to_core(3, i).start()

    def z_step(step):
        @pl.when(rank >= step)
        def _():
            along_z(rank - step, True).wait_recv()

            @pl.when(rank < tp - 1)
            def _():
                along_z(rank - step, True).start()

        @pl.when(rank + step < tp)
        def _():
            along_z(rank + step, False).wait_recv()

            @pl.when(rank > 0)
            def _():
                along_z(rank + step, False).start()

    for i in range(parts):
        own_x(i).start()
        own_y(i).start()
        to_core(0, i).start()
    mine = pltpu.make_async_copy(own_ref, rows_ref.at[pl.ds(rank * rows, rows)], l_sem.at[parts])
    mine.start()
    for i in range(parts):
        local(i).start()
    mine.wait()

    @pl.when(rank < tp - 1)
    def _():
        along_z(rank, True).start()

    @pl.when(rank > 0)
    def _():
        along_z(rank, False).start()

    z_step(1)
    forward(0)
    z_step(2)
    for i in range(1, parts):
        forward(i)
    finish(0)
    z_step(3)
    for i in range(1, parts):
        finish(i)
    for i in range(parts):
        local(i).wait()
        for q in range(4):
            to_core(q, i).wait_recv()
    for i in range(parts):
        for q in range(4):
            to_core(q, i).wait_send()
        own_x(i).wait_send()
        own_y(i).wait_send()
        x_to_y(i).wait_send()
        if halved[i]:
            y_to_x(i).wait_send()
    for block in range(tp):

        @pl.when((block <= rank) & (rank < tp - 1))
        def _():
            along_z(block, True).wait_send()

        @pl.when((block >= rank) & (rank > 0))
        def _():
            along_z(block, False).wait_send()


def prologue(own, pieces, fsdp, tp, collective_id):
    parts = len(pieces)
    halved = [one.shape[0] >= 32 for one in pieces]
    dma = pltpu.SemaphoreType.DMA
    anywhere = pl.BlockSpec(memory_space=pl.ANY)
    shapes = [(own.shape[0] * tp, own.shape[1])]
    shapes += [(one.shape[0] * fsdp, one.shape[1]) for one in pieces]
    return pl.pallas_call(
        functools.partial(prologue_kernel, tp, halved),
        out_shape=[
            jax.ShapeDtypeStruct(shape, one.dtype) for shape, one in zip(shapes, [own] + pieces)
        ],
        in_specs=[anywhere] * (1 + parts),
        out_specs=[anywhere] * (1 + parts),
        scratch_shapes=[
            dma((parts + 1,)),
            dma((2, tp)),
            dma((2, tp)),
            dma((8, parts)),
            dma((8, parts)),
        ],
        compiler_params=pltpu.CompilerParams(
            collective_id=collective_id, has_side_effects=True, vmem_limit_bytes=16 << 20
        ),
        name="prologue",
    )(own, *pieces)


UNIT = 640
SHARED = 384
NT = (((1,), (1,)), ((), ()))


def ffn_kernel(tp, expert_width, shared_width, *refs):
    part_ref, hidden_ref, gain_ref, grad_ref, both_ref, down_ref, scale_ref = refs[:7]
    middle_ref, all_ref, d_ref, hid_ref, y_ref, dsum_ref, esum_ref = refs[7:14]
    (
        n_buf, g_buf, x_buf, dh_buf, d_buf, stage, acc, diag_in, last_in, z_in,
        stage_e, acc_e, other_e, diag_e, last_e, z_in_e,
        local_sem, g_sem, x_sem, d_sem, h_sem, y_sem,
        az_send, az_recv, ap_send, ap_recv,
        c_send, c_recv, ce_send, ce_recv, p_send, p_recv, pe_send, pe_recv,
        z_send, z_recv, ze_send, ze_recv, f_sem, f_send, f_recv,
    ) = refs[14:]
    me, rank = place()
    greet(me, rank, tp)
    f32 = jnp.float32
    bf16 = jnp.bfloat16
    rows = hidden_ref.shape[0]
    pack_rows = rows * tp
    tile = pack_rows // 2
    near = rank // 2
    tokens = all_ref.shape[0]

    def region(pack, block, start=0, count=None):
        count = rows if count is None else count
        return all_ref.at[pl.ds(pack * pack_rows + block * rows + start, count)]

    def gather_z(block, right):
        way = 0 if right else 1
        ref = region(me, block)
        return pltpu.make_async_remote_copy(
            src_ref=ref,
            dst_ref=ref,
            send_sem=az_send.at[way, block],
            recv_sem=az_recv.at[way, block],
            device_id=(me, rank + 1 if right else rank - 1),
            device_id_type=MESH,
        )

    def gather(bit, pack_bits, block, slot, start=0, count=None):
        pack = me
        for one in (2, 4):
            if pack_bits & one:
                pack = flipped(pack, one)
        ref = region(pack, block, start, count)
        return pltpu.make_async_remote_copy(
            src_ref=ref,
            dst_ref=ref,
            send_sem=ap_send.at[slot, block],
            recv_sem=ap_recv.at[slot, block],
            device_id=(flipped(me, bit), rank),
            device_id_type=MESH,
        )

    def to_core(q, block):
        return gather(1, 2 * q, block, q)

    def own_x(block):
        return gather(2, 0, block, 4)

    def own_y(block):
        return gather(4, 0, block, 5)

    def x_to_y(block):
        return gather(4, 2, block, 6, 0, rows // 2)

    def y_to_x(block):
        return gather(2, 4, block, 7, rows // 2, rows // 2)

    def start_plane(block):
        own_x(block).start()
        own_y(block).start()
        to_core(0, block).start()

    def forward(block):
        own_x(block).wait_recv()
        x_to_y(block).start()
        to_core(1, block).start()
        own_y(block).wait_recv()
        y_to_x(block).start()
        to_core(2, block).start()

    def finish(block):
        x_to_y(block).wait_recv()
        y_to_x(block).wait_recv()
        to_core(3, block).start()

    def z_step(step):
        @pl.when(rank >= step)
        def _():
            block = rank - step
            gather_z(block, True).wait_recv()

            @pl.when(rank < tp - 1)
            def _():
                gather_z(block, True).start()

            start_plane(block)

        @pl.when(rank + step < tp)
        def _():
            block = rank + step
            gather_z(block, False).wait_recv()

            @pl.when(rank > 0)
            def _():
                gather_z(block, False).start()

            start_plane(block)

    order = [rank]
    for bit in (1, 2):
        order = order + [flipped(one, bit) for one in order]

    def control(i):
        steps = {
            0: [(forward, order[0])],
            1: [(z_step, 2), (forward, order[1])],
            2: [(z_step, 3)],
            3: [(finish, order[0])],
            4: [(finish, order[1])],
            5: [(forward, order[2])],
            7: [(forward, order[3])],
            8: [(finish, order[2])],
            11: [(finish, order[3])],
        }
        for at, todo in steps.items():

            @pl.when(i == at)
            def _():
                for act, what in todo:
                    act(what)

    def core(q, h):
        return pltpu.make_async_remote_copy(
            src_ref=stage.at[h],
            dst_ref=acc.at[q, h],
            send_sem=c_send.at[q, h],
            recv_sem=c_recv.at[q, h],
            device_id=(flipped(me, 1), rank),
            device_id_type=MESH,
        )

    def core_e(q):
        return pltpu.make_async_remote_copy(
            src_ref=stage_e.at[q],
            dst_ref=other_e.at[q],
            send_sem=ce_send.at[q],
            recv_sem=ce_recv.at[q],
            device_id=(flipped(me, 1), rank),
            device_id_type=MESH,
        )

    def across(bit, src, dst, slot, h):
        return pltpu.make_async_remote_copy(
            src_ref=src,
            dst_ref=dst,
            send_sem=p_send.at[slot, h],
            recv_sem=p_recv.at[slot, h],
            device_id=(flipped(me, bit), rank),
            device_id_type=MESH,
        )

    def diag_x(h):
        return across(2, acc.at[3, h, 0], diag_in.at[h, 0], 0, h)

    def diag_y(h):
        return across(4, acc.at[3, h, 1], diag_in.at[h, 1], 1, h)

    def direct_x(h):
        return across(2, acc.at[1, h, 0], last_in.at[h, 0, 0], 2, h)

    def direct_y(h):
        return across(4, acc.at[2, h, 1], last_in.at[h, 1, 1], 3, h)

    def summed_x(h):
        return across(2, acc.at[1, h, 1], last_in.at[h, 0, 1], 4, h)

    def summed_y(h):
        return across(4, acc.at[2, h, 0], last_in.at[h, 1, 0], 5, h)

    def across_e(bit, src, dst, slot):
        return pltpu.make_async_remote_copy(
            src_ref=src,
            dst_ref=dst,
            send_sem=pe_send.at[slot],
            recv_sem=pe_recv.at[slot],
            device_id=(flipped(me, bit), rank),
            device_id_type=MESH,
        )

    def diag_lines():
        return across_e(2, acc_e.at[3], diag_e, 0)

    def direct_lines():
        return across_e(2, acc_e.at[1], last_e.at[0], 1)

    def summed_lines():
        return across_e(4, acc_e.at[2], last_e.at[1], 2)

    blocks = [3 * (1 - near), 2 - near, flipped(rank, 1), rank]

    def along_z(j, right):
        way = 0 if right else 1
        block = blocks[j]
        return pltpu.make_async_remote_copy(
            src_ref=acc.at[0, j // 2, block % 2],
            dst_ref=z_in.at[way, block],
            send_sem=z_send.at[way, block],
            recv_sem=z_recv.at[way, block],
            device_id=(me, rank + 1 if right else rank - 1),
            device_id_type=MESH,
        )

    def along_z_e(j, right):
        way = 0 if right else 1
        block = blocks[j]
        return pltpu.make_async_remote_copy(
            src_ref=acc_e.at[0, block],
            dst_ref=z_in_e.at[way, block],
            send_sem=ze_send.at[way, block],
            recv_sem=ze_recv.at[way, block],
            device_id=(me, rank + 1 if right else rank - 1),
            device_id_type=MESH,
        )

    def add(ref, spot, one):
        ref[spot] = (ref[spot].astype(f32) + one.astype(f32)).astype(ref.dtype)

    def second(h):
        diag_x(h).wait_recv()
        add(acc, (2, h, 0), diag_in[h, 0])
        summed_y(h).start()
        diag_y(h).wait_recv()
        add(acc, (1, h, 1), diag_in[h, 1])
        summed_x(h).start()

    def third(j):
        h = j // 2
        block = blocks[j]
        part = block % 2
        if j % 2 == 0:
            direct_x(h).wait_recv()
            direct_y(h).wait_recv()
            summed_x(h).wait_recv()
            summed_y(h).wait_recv()
        if j == 0:
            direct_lines().wait_recv()
            summed_lines().wait_recv()
        total = (
            acc[0, h, part].astype(f32)
            + last_in[h, 0, part].astype(f32)
            + last_in[h, 1, part].astype(f32)
        )
        lines = acc_e[0, block] + last_e[0, block] + last_e[1, block]
        if j < tp - 1:
            acc[0, h, part] = total.astype(bf16)
            acc_e[0, block] = lines

            @pl.when((block > rank) & (rank > 0))
            def _():
                along_z(j, True).wait_recv()
                along_z_e(j, True).wait_recv()
                add(acc, (0, h, part), z_in[0, block])
                add(acc_e, (0, block), z_in_e[0, block])

            @pl.when((block < rank) & (rank < tp - 1))
            def _():
                along_z(j, False).wait_recv()
                along_z_e(j, False).wait_recv()
                add(acc, (0, h, part), z_in[1, block])
                add(acc_e, (0, block), z_in_e[1, block])

            @pl.when(block > rank)
            def _():
                along_z(j, True).start()
                along_z_e(j, True).start()

            @pl.when(block < rank)
            def _():
                along_z(j, False).start()
                along_z_e(j, False).start()
        else:
            dsum_ref[...] = total
            esum_ref[...] = lines

            @pl.when(rank > 0)
            def _():
                along_z(j, True).wait_recv()
                along_z_e(j, True).wait_recv()
                dsum_ref[...] += z_in[0, block].astype(f32)
                esum_ref[...] += z_in_e[0, block]

            @pl.when(rank < tp - 1)
            def _():
                along_z(j, False).wait_recv()
                along_z_e(j, False).wait_recv()
                dsum_ref[...] += z_in[1, block].astype(f32)
                esum_ref[...] += z_in_e[1, block]

    def front_load(block):
        return pltpu.make_async_copy(
            part_ref.at[pl.ds(block * rows, rows)],
            x_buf.at[block // 2, pl.ds(block % 2 * rows, rows)],
            f_sem.at[block],
        )

    def front_z(j, right):
        way = 0 if right else 1
        block = blocks[j]
        return pltpu.make_async_remote_copy(
            src_ref=x_buf.at[block // 2, pl.ds(block % 2 * rows, rows)],
            dst_ref=z_in.at[way, block],
            send_sem=f_send.at[way, block],
            recv_sem=f_recv.at[way, block],
            device_id=(me, rank + 1 if right else rank - 1),
            device_id_type=MESH,
        )

    def front(j):
        block = blocks[j]
        spot = (block // 2, pl.ds(pl.multiple_of(block % 2 * rows, rows), rows))
        front_load(block).wait()
        if j < tp - 1:

            @pl.when((block > rank) & (rank > 0))
            def _():
                front_z(j, True).wait_recv()
                add(x_buf, spot, z_in[0, block])

            @pl.when((block < rank) & (rank < tp - 1))
            def _():
                front_z(j, False).wait_recv()
                add(x_buf, spot, z_in[1, block])

            @pl.when(block > rank)
            def _():
                front_z(j, True).start()

            @pl.when(block < rank)
            def _():
                front_z(j, False).start()
        else:
            middle_ref[...] = hidden_ref[...].astype(f32) + x_buf[spot].astype(f32)

            @pl.when(rank > 0)
            def _():
                front_z(j, True).wait_recv()
                middle_ref[...] += z_in[0, block].astype(f32)

            @pl.when(rank < tp - 1)
            def _():
                front_z(j, False).wait_recv()
                middle_ref[...] += z_in[1, block].astype(f32)

            middle = middle_ref[...]
            mean = jnp.mean(middle * middle, axis=-1, keepdims=True)
            normed = middle * lax.rsqrt(mean + epsilon) * gain_ref[...]
            n_buf[...] = normed.astype(bf16)

    def grad_load(n, slot):
        return pltpu.make_async_copy(
            grad_ref.at[pl.ds(n * pack_rows, pack_rows)], g_buf.at[slot], g_sem.at[slot]
        )

    def hidden_grads(first, last):
        def body(n, carry):
            slot = n % 2

            @pl.when(n + 1 < tokens // pack_rows)
            def _():
                grad_load(n + 1, 1 - slot).start()

            grad_load(n, slot).wait()
            dh_buf[pl.ds(n * pack_rows, pack_rows), :] = lax.dot_general(
                g_buf[slot], down_ref[...], NT, preferred_element_type=f32
            ).astype(bf16)
            return carry

        lax.fori_loop(first, last, body, 0)

    core_of, x_of, y_of = me % 2, (me // 2) % 2, me // 4

    def tile_of(i):
        t = i // 2
        o = i % 2
        s = t // 6
        q = (1 - s) * (t % 3) + 3 * s
        h = (1 - s) * (1 - t // 3) + s * (t - 6)
        pack = (
            4 * ((y_of + q // 2) % 2) + 2 * ((x_of + q % 2) % 2) + (core_of + 1 - o) % 2
        )
        half = h * near + (1 - h) * (1 - near)
        return q, o, h, pack, half

    def tile_rows(pack, half):
        return pl.ds(pl.multiple_of(pack * pack_rows + half * tile, tile), tile)

    def row_load(i):
        q, o, h, pack, half = tile_of(i)
        return pltpu.make_async_copy(
            all_ref.at[tile_rows(pack, half)], x_buf.at[i % 2], x_sem.at[i % 2]
        )

    def prefetch(i):
        q, o, h, pack, half = tile_of(i)

        @pl.when(o == 0)
        def _():
            for part in range(2):
                block = 2 * half + part
                ref = region(pack, block)
                pltpu.make_async_remote_copy(
                    src_ref=ref,
                    dst_ref=ref,
                    send_sem=ap_send.at[q, block],
                    recv_sem=ap_recv.at[q, block],
                    device_id=(flipped(me, 1), rank),
                    device_id_type=MESH,
                ).wait_recv()

        row_load(i).start()

    def d_store(i):
        q, o, h, pack, half = tile_of(i)
        return pltpu.make_async_copy(
            d_buf.at[i % 2], d_ref.at[tile_rows(pack, half)], d_sem.at[i % 2]
        )

    units = SHARED + shared_width

    def one_tile(i, carry):
        q, o, h, pack, half = tile_of(i)
        slot = i % 2
        at = tile_rows(pack, half)
        row_load(i).wait()

        @pl.when(i >= 2)
        def _():
            d_store(i - 2).wait()

        pre = jnp.dot(x_buf[slot], both_ref[...], preferred_element_type=f32)
        gate, upper = pre[:, :UNIT], pre[:, UNIT:]
        lane = lax.broadcasted_iota(jnp.int32, (1, UNIT), 1)
        logit = gate[:, units : units + 1] + gate[:, units + 1 : units + 2]
        gate_prob = 1.0 / (1.0 + jnp.exp(-logit))
        scale = jnp.where(
            lane < expert_width, scale_ref[at, :1], jnp.where(lane < units, gate_prob, 0.0)
        )
        sigmoid = 1.0 / (1.0 + jnp.exp(-gate))
        act = gate * sigmoid
        slope = sigmoid * (1.0 + gate * (1.0 - sigmoid))
        hidden = act * upper
        d_hidden = dh_buf[at, :].astype(f32)
        line = lax.broadcasted_iota(jnp.int32, (16, UNIT), 0)
        unit = lax.broadcasted_iota(jnp.int32, (16, UNIT), 1)
        of_expert = (line == me) & (unit < expert_width)
        of_shared = (line == 8) & (unit >= SHARED)
        pick = jnp.where(of_expert | of_shared, 1.0, 0.0).astype(bf16)
        lines = lax.dot_general(
            pick, (d_hidden * hidden).astype(bf16), NT, preferred_element_type=f32
        )
        dh_buf[at, :] = (hidden * scale).astype(bf16)
        d_scaled = d_hidden * scale
        d_buf[slot, :, :UNIT] = (d_scaled * upper * slope).astype(bf16)
        d_buf[slot, :, UNIT:] = (d_scaled * act).astype(bf16)
        control(i)

        @pl.when(i < 15)
        def _():
            prefetch(i + 1)

        d_rows = lax.dot_general(d_buf[slot], both_ref[...], NT, preferred_element_type=f32)
        d_store(i).start()

        @pl.when(o == 0)
        def _():
            @pl.when(q > 0)
            def _():
                core(q - 1, h).wait_send()

            for part in range(2):
                stage[h, part] = d_rows[part * rows : (part + 1) * rows].astype(bf16)
                stage_e[q, 2 * half + part] = lines[:, part * rows : (part + 1) * rows]
            core(q, h).start()

            @pl.when(((h == 0) & (q < 3)) | ((h == 1) & (q == 3)))
            def _():
                core_e(q).start()

        @pl.when(o == 1)
        def _():
            core(q, h).wait_recv()
            for part in range(2):
                add(acc, (q, h, part), d_rows[part * rows : (part + 1) * rows])
                acc_e[q, 2 * half + part] = lines[:, part * rows : (part + 1) * rows]

            @pl.when(((h == 0) & (q < 3)) | ((h == 1) & (q == 3)))
            def _():
                core_e(q).wait_recv()
                acc_e[q] = acc_e[q] + other_e[q]

                @pl.when(q == 1)
                def _():
                    direct_lines().start()

                @pl.when(q == 3)
                def _():
                    diag_lines().start()

            @pl.when(q == 1)
            def _():
                direct_x(h).start()

            @pl.when(q == 2)
            def _():
                direct_y(h).start()

            @pl.when(q == 3)
            def _():
                diag_x(h).start()
                diag_y(h).start()

        return carry

    def y_store(n, slot):
        return pltpu.make_async_copy(
            g_buf.at[slot], y_ref.at[pl.ds(n * pack_rows, pack_rows)], y_sem.at[slot]
        )

    def outputs(first, last):
        def body(n, carry):
            slot = n % 2

            @pl.when(n >= 2)
            def _():
                y_store(n - 2, slot).wait()

            g_buf[slot] = jnp.dot(
                dh_buf[pl.ds(n * pack_rows, pack_rows), :],
                down_ref[...],
                preferred_element_type=f32,
            ).astype(bf16)
            y_store(n, slot).start()
            return carry

        lax.fori_loop(first, last, body, 0)

    grad_load(0, 0).start()
    packs = tokens // pack_rows
    for block in blocks:
        front_load(block).start()
    front(0)
    hidden_grads(0, 3)
    front(1)
    hidden_grads(3, 6)
    front(2)
    hidden_grads(6, packs)
    front(3)
    mine = pltpu.make_async_copy(n_buf, region(me, rank), local_sem)
    mine.start()
    mine.wait()

    @pl.when(rank < tp - 1)
    def _():
        gather_z(rank, True).start()

    @pl.when(rank > 0)
    def _():
        gather_z(rank, False).start()

    start_plane(rank)
    for j in range(tp - 1):
        block = blocks[j]

        @pl.when(block > rank)
        def _():
            front_z(j, True).wait_send()

        @pl.when(block < rank)
        def _():
            front_z(j, False).wait_send()

    z_step(1)
    prefetch(0)
    lax.fori_loop(0, 16, one_tile, 0)
    hidden_store = pltpu.make_async_copy(dh_buf, hid_ref, h_sem)
    hidden_store.start()
    outputs(0, 4)
    second(0)
    outputs(4, 6)
    diag_lines().wait_recv()
    acc_e[2] = acc_e[2] + diag_e[...]
    summed_lines().start()
    second(1)
    outputs(6, packs)
    third(0)
    third(1)
    third(2)
    third(3)

    hidden_store.wait()
    for n in (packs - 2, packs - 1):
        y_store(n, n % 2).wait()
    for i in (14, 15):
        d_store(i).wait()
    core(3, 0).wait_send()
    core(3, 1).wait_send()
    for q in range(4):
        core_e(q).wait_send()
    for copy in (diag_lines, direct_lines, summed_lines):
        copy().wait_send()
    for h in range(2):
        for copy in (diag_x, diag_y, direct_x, direct_y, summed_x, summed_y):
            copy(h).wait_send()
    for block in order:
        for q in range(4):
            to_core(q, block).wait_send()
        for copy in (own_x, own_y, x_to_y, y_to_x):
            copy(block).wait_send()
    for j in range(tp - 1):
        block = blocks[j]

        @pl.when(block > rank)
        def _():
            along_z(j, True).wait_send()
            along_z_e(j, True).wait_send()

        @pl.when(block < rank)
        def _():
            along_z(j, False).wait_send()
            along_z_e(j, False).wait_send()

    for block in range(tp):

        @pl.when((block <= rank) & (rank < tp - 1))
        def _():
            gather_z(block, True).wait_send()

        @pl.when((block >= rank) & (rank > 0))
        def _():
            gather_z(block, False).wait_send()


def ffn(
    part, hidden, gain, grad_all, both, down, scale, fsdp, tp, expert_width, shared_width, collective_id
):
    rows, width = hidden.shape
    tokens = rows * fsdp * tp
    pack_rows = rows * tp
    tile = pack_rows // 2
    bf16 = jnp.bfloat16
    f32 = jnp.float32
    dma = pltpu.SemaphoreType.DMA
    anywhere = pl.BlockSpec(memory_space=pl.ANY)
    vmem = pl.BlockSpec(memory_space=pltpu.VMEM)
    return pl.pallas_call(
        functools.partial(ffn_kernel, tp, expert_width, shared_width),
        out_shape=[
            jax.ShapeDtypeStruct((rows, width), f32),
            jax.ShapeDtypeStruct((tokens, width), bf16),
            jax.ShapeDtypeStruct((tokens, 2 * UNIT), bf16),
            jax.ShapeDtypeStruct((tokens, UNIT), bf16),
            jax.ShapeDtypeStruct((tokens, width), bf16),
            jax.ShapeDtypeStruct((rows, width), f32),
            jax.ShapeDtypeStruct((16, rows), f32),
        ],
        in_specs=[anywhere, vmem, vmem, anywhere, vmem, vmem, vmem],
        out_specs=[vmem, anywhere, anywhere, anywhere, anywhere, vmem, vmem],
        scratch_shapes=[
            pltpu.VMEM((rows, width), bf16),
            pltpu.VMEM((2, pack_rows, width), bf16),
            pltpu.VMEM((2, tile, width), bf16),
            pltpu.VMEM((tokens, UNIT), bf16),
            pltpu.VMEM((2, tile, 2 * UNIT), bf16),
            pltpu.VMEM((2, 2, rows, width), bf16),
            pltpu.VMEM((4, 2, 2, rows, width), bf16),
            pltpu.VMEM((2, 2, rows, width), bf16),
            pltpu.VMEM((2, 2, 2, rows, width), bf16),
            pltpu.VMEM((2, tp, rows, width), bf16),
            pltpu.VMEM((4, tp, 16, rows), f32),
            pltpu.VMEM((4, tp, 16, rows), f32),
            pltpu.VMEM((4, tp, 16, rows), f32),
            pltpu.VMEM((tp, 16, rows), f32),
            pltpu.VMEM((2, tp, 16, rows), f32),
            pltpu.VMEM((2, tp, 16, rows), f32),
            dma, dma((2,)), dma((2,)), dma((2,)), dma, dma((2,)),
            dma((2, tp)), dma((2, tp)), dma((8, tp)), dma((8, tp)),
            dma((4, 2)), dma((4, 2)), dma((4,)), dma((4,)),
            dma((6, 2)), dma((6, 2)), dma((3,)), dma((3,)),
            dma((2, tp)), dma((2, tp)), dma((2, tp)), dma((2, tp)),
            dma((tp,)), dma((2, tp)), dma((2, tp)),
        ],
        compiler_params=pltpu.CompilerParams(
            collective_id=collective_id, has_side_effects=True, vmem_limit_bytes=61 << 20
        ),
        name="ffn",
    )(part, hidden, gain, grad_all, both, down, scale)


TN = (((0,), (0,)), ((), ()))


def outputs_kernel(tp, expert_width, shared_width, *refs):
    y_ref, own_ref, x_ref, d_ref, h_ref, g_ref = refs[:6]
    total_ref, rows_ref, ge_ref, gs_ref, de_ref, ds_ref = refs[6:12]
    (
        mine, other, diag_in, last_in, z_in, d_buf, h_buf, col_buf, ge_buf, gs_buf, de_buf, ds_buf,
        l_sem, c_send, c_recv, p_send, p_recv, z_send, z_recv, a_sem, a_send, a_recv,
        w_sem, col_sem, out_sem,
    ) = refs[12:]
    me, rank = place()
    greet(me, rank, tp)
    f32 = jnp.float32
    bf16 = jnp.bfloat16
    rows = total_ref.shape[0]
    half = rows // 2
    near = rank // 2
    blocks = [3 * (1 - near), 2 - near, flipped(rank, 1), rank]
    packs = [me, flipped(me, 2), flipped(me, 4), flipped(flipped(me, 2), 4)]
    low, high = pl.ds(0, half), pl.ds(half, half)

    def gather_z(block, right):
        way = 0 if right else 1
        spot = rows_ref.at[pl.ds(block * rows, rows)]
        return pltpu.make_async_remote_copy(
            src_ref=spot,
            dst_ref=spot,
            send_sem=a_send.at[way, block],
            recv_sem=a_recv.at[way, block],
            device_id=(me, rank + 1 if right else rank - 1),
            device_id_type=MESH,
        )

    def gather_step(step):
        @pl.when(rank >= step)
        def _():
            gather_z(rank - step, True).wait_recv()

            @pl.when(rank < tp - 1)
            def _():
                gather_z(rank - step, True).start()

        @pl.when(rank + step < tp)
        def _():
            gather_z(rank + step, False).wait_recv()

            @pl.when(rank > 0)
            def _():
                gather_z(rank + step, False).start()

    def region(pack, block):
        return y_ref.at[pl.ds((pack * tp + block) * rows, rows)]

    def local(k, j):
        return pltpu.make_async_copy(region(packs[k], blocks[j]), mine.at[k, j], l_sem.at[k, j])

    def core(k, j):
        return pltpu.make_async_remote_copy(
            src_ref=region(flipped(packs[k], 1), blocks[j]),
            dst_ref=other.at[k, j],
            send_sem=c_send.at[k, j],
            recv_sem=c_recv.at[k, j],
            device_id=(flipped(me, 1), rank),
            device_id_type=MESH,
        )

    def across(bit, src, dst, slot, j):
        return pltpu.make_async_remote_copy(
            src_ref=src,
            dst_ref=dst,
            send_sem=p_send.at[slot, j],
            recv_sem=p_recv.at[slot, j],
            device_id=(flipped(me, bit), rank),
            device_id_type=MESH,
        )

    def diag_x(j):
        return across(2, mine.at[3, j, low], diag_in.at[j, 0], 0, j)

    def diag_y(j):
        return across(4, mine.at[3, j, high], diag_in.at[j, 1], 1, j)

    def direct_x(j):
        return across(2, mine.at[1, j, low], last_in.at[j, 0, low], 2, j)

    def direct_y(j):
        return across(4, mine.at[2, j, high], last_in.at[j, 1, high], 3, j)

    def summed_x(j):
        return across(2, mine.at[1, j, high], last_in.at[j, 0, high], 4, j)

    def summed_y(j):
        return across(4, mine.at[2, j, low], last_in.at[j, 1, low], 5, j)

    def along_z(j, right):
        way = 0 if right else 1
        block = blocks[j]
        return pltpu.make_async_remote_copy(
            src_ref=mine.at[0, j],
            dst_ref=z_in.at[way, block],
            send_sem=z_send.at[way, block],
            recv_sem=z_recv.at[way, block],
            device_id=(me, rank + 1 if right else rank - 1),
            device_id_type=MESH,
        )

    def add(ref, spot, one):
        ref[spot] = (ref[spot].astype(f32) + one.astype(f32)).astype(ref.dtype)

    def first(j):
        for k in (3, 2, 1, 0):
            core(k, j).wait_recv()
            local(k, j).wait()
            add(mine, (k, j), other[k, j])
            if k == 3:
                diag_x(j).start()
                diag_y(j).start()
            if k == 2:
                direct_y(j).start()
            if k == 1:
                direct_x(j).start()

    def second(j):
        diag_x(j).wait_recv()
        add(mine, (2, j, low), diag_in[j, 0])
        summed_y(j).start()
        diag_y(j).wait_recv()
        add(mine, (1, j, high), diag_in[j, 1])
        summed_x(j).start()

    def third(j):
        block = blocks[j]
        direct_x(j).wait_recv()
        direct_y(j).wait_recv()
        summed_x(j).wait_recv()
        summed_y(j).wait_recv()
        total = mine[0, j].astype(f32) + last_in[j, 0].astype(f32) + last_in[j, 1].astype(f32)
        if j < tp - 1:
            mine[0, j] = total.astype(bf16)

            @pl.when((block > rank) & (rank > 0))
            def _():
                along_z(j, True).wait_recv()
                add(mine, (0, j), z_in[0, block])

            @pl.when((block < rank) & (rank < tp - 1))
            def _():
                along_z(j, False).wait_recv()
                add(mine, (0, j), z_in[1, block])

            @pl.when(block > rank)
            def _():
                along_z(j, True).start()

            @pl.when(block < rank)
            def _():
                along_z(j, False).start()
        else:
            total_ref[...] = total

            @pl.when(rank > 0)
            def _():
                along_z(j, True).wait_recv()
                total_ref[...] += z_in[0, block].astype(f32)

            @pl.when(rank < tp - 1)
            def _():
                along_z(j, False).wait_recv()
                total_ref[...] += z_in[1, block].astype(f32)

    span = col_buf.shape[2]
    steps = x_ref.shape[1] // span
    units = SHARED + shared_width

    def columns(n, slot, of_x):
        ref = x_ref if of_x else g_ref
        return pltpu.make_async_copy(
            ref.at[:, pl.ds(pl.multiple_of(n * span, span), span)],
            col_buf.at[slot],
            col_sem.at[slot],
        )

    def up_stores(n, slot):
        at = pl.ds(pl.multiple_of(n * span, span), span)
        return (
            pltpu.make_async_copy(ge_buf.at[slot], ge_ref.at[:, at], out_sem.at[0, slot]),
            pltpu.make_async_copy(gs_buf.at[slot], gs_ref.at[:, at], out_sem.at[1, slot]),
        )

    def down_stores(n, slot):
        at = pl.ds(pl.multiple_of(n * span, span), span)
        return (
            pltpu.make_async_copy(de_buf.at[slot], de_ref.at[:, at], out_sem.at[2, slot]),
            pltpu.make_async_copy(ds_buf.at[slot], ds_ref.at[n], out_sem.at[3, slot]),
        )

    def up_step(n, carry):
        slot = n % 2

        @pl.when(n + 1 < steps)
        def _():
            columns(n + 1, 1 - slot, True).start()

        @pl.when(n + 1 == steps)
        def _():
            columns(0, 1 - slot, False).start()

        columns(n, slot, True).wait()

        @pl.when(n >= 2)
        def _():
            for copy in up_stores(n - 2, slot):
                copy.wait()

        grads = lax.dot_general(col_buf[slot], d_buf[...], TN, preferred_element_type=f32)
        for part in range(2):
            base = part * UNIT
            ge_buf[slot, part] = grads[:, base : base + expert_width]
            gs_buf[slot, part] = grads[:, base + SHARED : base + units].astype(bf16)
        for copy in up_stores(n, slot):
            copy.start()
        return carry

    def down_step(n, carry):
        slot = n % 2

        @pl.when(n + 1 < steps)
        def _():
            columns(n + 1, 1 - slot, False).start()

        columns(n, slot, False).wait()

        @pl.when(n >= 2)
        def _():
            for copy in down_stores(n - 2, slot):
                copy.wait()

        grads = lax.dot_general(h_buf[...], col_buf[slot], TN, preferred_element_type=f32)
        de_buf[slot] = grads[:expert_width]
        ds_buf[slot] = grads[SHARED:units].astype(bf16)
        for copy in down_stores(n, slot):
            copy.start()
        return carry

    load_d = pltpu.make_async_copy(d_ref, d_buf, w_sem.at[0])
    load_h = pltpu.make_async_copy(h_ref, h_buf, w_sem.at[1])
    own = pltpu.make_async_copy(own_ref, rows_ref.at[pl.ds(rank * rows, rows)], a_sem)
    own.start()
    for j in range(tp):
        for k in (3, 2, 1, 0):
            core(k, j).start()
            local(k, j).start()
    load_d.start()
    columns(0, 0, True).start()
    load_h.start()
    own.wait()

    @pl.when(rank < tp - 1)
    def _():
        gather_z(rank, True).start()

    @pl.when(rank > 0)
    def _():
        gather_z(rank, False).start()

    first(0)
    first(1)
    load_d.wait()
    lax.fori_loop(0, 2, up_step, 0)
    second(0)
    gather_step(1)
    first(2)
    lax.fori_loop(2, 4, up_step, 0)
    second(1)
    first(3)
    lax.fori_loop(4, 6, up_step, 0)
    gather_step(2)
    third(0)
    second(2)
    lax.fori_loop(6, 8, up_step, 0)
    gather_step(3)
    third(1)
    second(3)
    load_h.wait()
    lax.fori_loop(0, steps, down_step, 0)
    third(2)
    third(3)

    for n in (steps - 2, steps - 1):
        for copy in up_stores(n, n % 2) + down_stores(n, n % 2):
            copy.wait()
    for j in range(tp):
        for k in range(4):
            core(k, j).wait_send()
        for copy in (diag_x, diag_y, direct_x, direct_y, summed_x, summed_y):
            copy(j).wait_send()
        block = blocks[j]
        if j < tp - 1:

            @pl.when(block > rank)
            def _():
                along_z(j, True).wait_send()

            @pl.when(block < rank)
            def _():
                along_z(j, False).wait_send()

    for block in range(tp):

        @pl.when((block <= rank) & (rank < tp - 1))
        def _():
            gather_z(block, True).wait_send()

        @pl.when((block >= rank) & (rank > 0))
        def _():
            gather_z(block, False).wait_send()


def outputs(y, own, x, d, h, g, fsdp, tp, expert_width, shared_width, collective_id):
    rows, width = own.shape
    tokens = y.shape[0]
    span = width // fsdp
    bf16 = jnp.bfloat16
    f32 = jnp.float32
    dma = pltpu.SemaphoreType.DMA
    anywhere = pl.BlockSpec(memory_space=pl.ANY)
    return pl.pallas_call(
        functools.partial(outputs_kernel, tp, expert_width, shared_width),
        out_shape=[
            jax.ShapeDtypeStruct((rows, width), f32),
            jax.ShapeDtypeStruct((rows * tp, width), bf16),
            jax.ShapeDtypeStruct((2, width, expert_width), f32),
            jax.ShapeDtypeStruct((2, width, shared_width), bf16),
            jax.ShapeDtypeStruct((expert_width, width), f32),
            jax.ShapeDtypeStruct((fsdp, shared_width, span), bf16),
        ],
        in_specs=[anywhere] * 6,
        out_specs=[pl.BlockSpec(memory_space=pltpu.VMEM)] + [anywhere] * 5,
        scratch_shapes=[
            pltpu.VMEM((4, tp, rows, width), bf16),
            pltpu.VMEM((4, tp, rows, width), bf16),
            pltpu.VMEM((tp, 2, rows // 2, width), bf16),
            pltpu.VMEM((tp, 2, rows, width), bf16),
            pltpu.VMEM((2, tp, rows, width), bf16),
            pltpu.VMEM((tokens, 2 * UNIT), bf16),
            pltpu.VMEM((tokens, UNIT), bf16),
            pltpu.VMEM((2, tokens, span), bf16),
            pltpu.VMEM((2, 2, span, expert_width), f32),
            pltpu.VMEM((2, 2, span, shared_width), bf16),
            pltpu.VMEM((2, expert_width, span), f32),
            pltpu.VMEM((2, shared_width, span), bf16),
            dma((4, tp)), dma((4, tp)), dma((4, tp)), dma((6, tp)), dma((6, tp)),
            dma((2, tp)), dma((2, tp)), dma, dma((2, tp)), dma((2, tp)),
            dma((2,)), dma((2,)), dma((4, 2)),
        ],
        compiler_params=pltpu.CompilerParams(
            collective_id=collective_id, has_side_effects=True, vmem_limit_bytes=60 << 20
        ),
        name="outputs",
    )(y, own, x, d, h, g)


def epilogue_kernel(fsdp, tp, parts, *refs):
    ins, refs = refs[:parts], refs[parts:]
    gs_ref, ds_ref, dn_ref, hidden_ref, grad_ref, gain_ref, sums_ref = refs[:7]
    refs = refs[7:]
    outs, refs = refs[:parts], refs[parts:]
    gs_out, ds_out, hidden_grad_ref, gains_ref = refs[:4]
    refs = refs[4:]
    mine, other, diag_in, last_in = (refs[i * parts : (i + 1) * parts] for i in range(4))
    (
        gs_in, ds_in, dn_buf, z_in, v_send, v_in, w_send, w_in,
        l_sem, c_send, c_recv, p_send, p_recv, s_sem, s_send, s_recv,
        f_sem, f_send, f_recv, v_ssem, v_rsem, w_ssem, w_rsem,
    ) = refs[4 * parts :]
    me, rank = place()
    f32 = jnp.float32
    bf16 = jnp.bfloat16
    rows, width = hidden_ref.shape
    near = rank // 2
    blocks = [3 * (1 - near), 2 - near, flipped(rank, 1), rank]
    packs = [me, flipped(me, 2), flipped(me, 4), flipped(flipped(me, 2), 4)]
    every = range(parts)
    chunks = outs[0].shape[0]
    sizes = [ref.shape[1] for ref in outs]
    low = [pl.ds(0, size // 2) for size in sizes]
    high = [pl.ds(size // 2, size // 2) for size in sizes]

    def plane(bits):
        peer = me
        for one in (1, 2, 4):
            if bits & one:
                peer = flipped(peer, one)
        return peer

    def line(bits):
        peer = rank
        for one in (1, 2):
            if bits & one:
                peer = flipped(peer, one)
        return peer

    barrier = pltpu.get_barrier_semaphore()
    for bits in range(1, fsdp):
        pl.semaphore_signal(
            barrier, inc=1, device_id=(plane(bits), rank), device_id_type=MESH
        )
    for bits in range(1, tp):
        pl.semaphore_signal(barrier, inc=1, device_id=(me, line(bits)), device_id_type=MESH)
    pl.semaphore_wait(barrier, fsdp - 1 + tp - 1)

    def add(ref, spot, one):
        ref[spot] = (ref[spot].astype(f32) + one.astype(f32)).astype(ref.dtype)

    def region(i, pack, j):
        return ins[i].at[pl.ds((pack * chunks + j) * sizes[i], sizes[i])]

    def local(k, j, i):
        return pltpu.make_async_copy(region(i, packs[k], j), mine[i].at[k, j], l_sem.at[k, j, i])

    def core(k, j, i):
        return pltpu.make_async_remote_copy(
            src_ref=region(i, flipped(packs[k], 1), j),
            dst_ref=other[i].at[k, j],
            send_sem=c_send.at[k, j, i],
            recv_sem=c_recv.at[k, j, i],
            device_id=(flipped(me, 1), rank),
            device_id_type=MESH,
        )

    def across(bit, src, dst, slot, j, i):
        return pltpu.make_async_remote_copy(
            src_ref=src,
            dst_ref=dst,
            send_sem=p_send.at[slot, j, i],
            recv_sem=p_recv.at[slot, j, i],
            device_id=(flipped(me, bit), rank),
            device_id_type=MESH,
        )

    def diag_x(j, i):
        return across(2, mine[i].at[3, j, low[i]], diag_in[i].at[j, 0], 0, j, i)

    def diag_y(j, i):
        return across(4, mine[i].at[3, j, high[i]], diag_in[i].at[j, 1], 1, j, i)

    def direct_x(j, i):
        return across(2, mine[i].at[1, j, low[i]], last_in[i].at[j, 0, low[i]], 2, j, i)

    def direct_y(j, i):
        return across(4, mine[i].at[2, j, high[i]], last_in[i].at[j, 1, high[i]], 3, j, i)

    def summed_x(j, i):
        return across(2, mine[i].at[1, j, high[i]], last_in[i].at[j, 0, high[i]], 4, j, i)

    def summed_y(j, i):
        return across(4, mine[i].at[2, j, low[i]], last_in[i].at[j, 1, low[i]], 5, j, i)

    def first(j):
        for i in every:
            for k in (3, 2, 1, 0):
                core(k, j, i).wait_recv()
                local(k, j, i).wait()
                add(mine[i], (k, j), other[i][k, j])
                if k == 3:
                    diag_x(j, i).start()
                    diag_y(j, i).start()
                if k == 2:
                    direct_y(j, i).start()
                if k == 1:
                    direct_x(j, i).start()

    def second(j):
        for i in every:
            diag_x(j, i).wait_recv()
            add(mine[i], (2, j, low[i]), diag_in[i][j, 0])
            summed_y(j, i).start()
            diag_y(j, i).wait_recv()
            add(mine[i], (1, j, high[i]), diag_in[i][j, 1])
            summed_x(j, i).start()

    def third(j):
        for i in every:
            direct_x(j, i).wait_recv()
            direct_y(j, i).wait_recv()
            summed_x(j, i).wait_recv()
            summed_y(j, i).wait_recv()
            outs[i][j] = (
                mine[i][0, j].astype(f32)
                + last_in[i][j, 0].astype(f32)
                + last_in[i][j, 1].astype(f32)
            )

    span = ds_ref.shape[2]

    def shared_up(bits):
        at = pl.ds(pl.multiple_of(plane(bits) * span, span), span)
        return pltpu.make_async_remote_copy(
            src_ref=gs_ref.at[:, at],
            dst_ref=gs_in.at[me],
            send_sem=s_send.at[0, bits],
            recv_sem=s_recv.at[0, bits],
            device_id=(plane(bits), rank),
            device_id_type=MESH,
        )

    def shared_down(bits):
        return pltpu.make_async_remote_copy(
            src_ref=ds_ref.at[plane(bits)],
            dst_ref=ds_in.at[me],
            send_sem=s_send.at[1, bits],
            recv_sem=s_recv.at[1, bits],
            device_id=(plane(bits), rank),
            device_id_type=MESH,
        )

    own_up = pltpu.make_async_copy(
        gs_ref.at[:, pl.ds(pl.multiple_of(me * span, span), span)], gs_in.at[me], s_sem.at[0]
    )
    own_down = pltpu.make_async_copy(ds_ref.at[me], ds_in.at[me], s_sem.at[1])

    def front_load(block):
        return pltpu.make_async_copy(
            dn_ref.at[pl.ds(block * rows, rows)], dn_buf.at[block], f_sem.at[block]
        )

    def front_z(j, right):
        way = 0 if right else 1
        block = blocks[j]
        return pltpu.make_async_remote_copy(
            src_ref=dn_buf.at[block],
            dst_ref=z_in.at[way, block],
            send_sem=f_send.at[way, block],
            recv_sem=f_recv.at[way, block],
            device_id=(me, rank + 1 if right else rank - 1),
            device_id_type=MESH,
        )

    def front(j):
        block = blocks[j]
        front_load(block).wait()
        if j < tp - 1:

            @pl.when((block > rank) & (rank > 0))
            def _():
                front_z(j, True).wait_recv()
                add(dn_buf, (block,), z_in[0, block])

            @pl.when((block < rank) & (rank < tp - 1))
            def _():
                front_z(j, False).wait_recv()
                add(dn_buf, (block,), z_in[1, block])

            @pl.when(block > rank)
            def _():
                front_z(j, True).start()

            @pl.when(block < rank)
            def _():
                front_z(j, False).start()
        else:
            hidden_grad_ref[...] = dn_buf[block].astype(f32)

            @pl.when(rank > 0)
            def _():
                front_z(j, True).wait_recv()
                hidden_grad_ref[...] += z_in[0, block].astype(f32)

            @pl.when(rank < tp - 1)
            def _():
                front_z(j, False).wait_recv()
                hidden_grad_ref[...] += z_in[1, block].astype(f32)

    share = width // fsdp
    part = share // tp

    def gains_plane(bits):
        return pltpu.make_async_remote_copy(
            src_ref=v_send.at[plane(bits)],
            dst_ref=v_in.at[me],
            send_sem=v_ssem.at[bits],
            recv_sem=v_rsem.at[bits],
            device_id=(plane(bits), rank),
            device_id_type=MESH,
        )

    def gains_line(bits):
        return pltpu.make_async_remote_copy(
            src_ref=w_send.at[line(bits)],
            dst_ref=w_in.at[rank],
            send_sem=w_ssem.at[bits],
            recv_sem=w_rsem.at[bits],
            device_id=(me, line(bits)),
            device_id_type=MESH,
        )

    for block in blocks:
        front_load(block).start()
    for j in range(chunks):
        for i in every:
            for k in (3, 2, 1, 0):
                core(k, j, i).start()
                local(k, j, i).start()
    front(0)
    first(0)
    for bits in (6, 7, 2, 3, 4, 5, 1):
        shared_up(bits).start()
        shared_down(bits).start()
    own_up.start()
    own_down.start()
    first(1)
    second(0)
    front(1)
    second(1)
    front(2)
    front(3)
    d_normed = hidden_grad_ref[...]
    hidden = hidden_ref[...].astype(f32)
    inverse = lax.rsqrt(jnp.mean(hidden * hidden, axis=-1, keepdims=True) + epsilon)
    hat = hidden * inverse
    v_send[...] = jnp.zeros_like(v_send)
    attn_gain = jnp.sum(d_normed * hat, axis=0, keepdims=True)
    for owner in range(fsdp):
        at = slice(owner * share, (owner + 1) * share)
        v_send[owner, 0:1] = attn_gain[:, at]
        v_send[owner, 1:3] = sums_ref[:, at]
    for bits in range(1, fsdp):
        gains_plane(bits).start()
    d_hat = d_normed * gain_ref[...]
    mean = jnp.mean(d_hat * hat, axis=-1, keepdims=True)
    hidden_grad_ref[...] = grad_ref[...] + inverse * (d_hat - hat * mean)
    third(0)
    total = v_send[me]
    for bits in range(1, fsdp):
        gains_plane(bits).wait_recv()
        total = total + v_in[plane(bits)]
    w_send[...] = jnp.zeros_like(w_send)
    for owner in range(tp):
        w_send[owner, :, :part] = total[:, owner * part : (owner + 1) * part]
    for bits in range(1, tp):
        gains_line(bits).start()
    third(1)
    own_up.wait()
    own_down.wait()
    for bits in range(1, fsdp):
        shared_up(bits).wait_recv()
        shared_down(bits).wait_recv()
    units = gs_in.shape[3]
    for owner in range(fsdp):
        at = slice(owner * units, (owner + 1) * units)
        gs_out[:, :, at] = gs_in[owner].astype(f32)
        ds_out[at] = ds_in[owner].astype(f32)
    total = w_send[rank]
    for bits in range(1, tp):
        gains_line(bits).wait_recv()
        total = total + w_in[line(bits)]
    gains_ref[...] = total

    for j in range(chunks):
        for i in every:
            for k in range(4):
                core(k, j, i).wait_send()
            for copy in (diag_x, diag_y, direct_x, direct_y, summed_x, summed_y):
                copy(j, i).wait_send()
    for bits in range(1, fsdp):
        shared_up(bits).wait_send()
        shared_down(bits).wait_send()
        gains_plane(bits).wait_send()
    for bits in range(1, tp):
        gains_line(bits).wait_send()
    for j in range(tp - 1):
        block = blocks[j]

        @pl.when(block > rank)
        def _():
            front_z(j, True).wait_send()

        @pl.when(block < rank)
        def _():
            front_z(j, False).wait_send()


def epilogue(arrays, shared_up, shared_down, dn, hidden, grad, gain, sums, fsdp, tp, collective_id):
    chunks = 2
    parts = len(arrays)
    rows, width = hidden.shape
    units = shared_up.shape[2]
    span = shared_down.shape[2]
    f32 = jnp.float32
    shapes = [(one.shape[0] // (fsdp * chunks), one.shape[1], one.dtype) for one in arrays]
    scratch = [pltpu.VMEM((4, chunks, size, w), kind) for size, w, kind in shapes]
    scratch += [pltpu.VMEM((4, chunks, size, w), kind) for size, w, kind in shapes]
    scratch += [pltpu.VMEM((chunks, 2, size // 2, w), kind) for size, w, kind in shapes]
    scratch += [pltpu.VMEM((chunks, 2, size, w), kind) for size, w, kind in shapes]
    dma = pltpu.SemaphoreType.DMA
    anywhere = pl.BlockSpec(memory_space=pl.ANY)
    vmem = pl.BlockSpec(memory_space=pltpu.VMEM)
    out_shape = [jax.ShapeDtypeStruct((chunks, size, w), f32) for size, w, _ in shapes]
    out_shape += [
        jax.ShapeDtypeStruct((2, span, fsdp * units), f32),
        jax.ShapeDtypeStruct((fsdp * units, span), f32),
        jax.ShapeDtypeStruct((rows, width), f32),
        jax.ShapeDtypeStruct((8, 128), f32),
    ]
    return pl.pallas_call(
        functools.partial(epilogue_kernel, fsdp, tp, parts),
        out_shape=out_shape,
        in_specs=[anywhere] * (parts + 3) + [vmem] * 4,
        out_specs=[vmem] * len(out_shape),
        scratch_shapes=scratch
        + [
            pltpu.VMEM((fsdp, 2, span, units), shared_up.dtype),
            pltpu.VMEM((fsdp, units, span), shared_down.dtype),
            pltpu.VMEM((tp, rows, width), dn.dtype),
            pltpu.VMEM((2, tp, rows, width), dn.dtype),
            pltpu.VMEM((fsdp, 8, width // fsdp), f32),
            pltpu.VMEM((fsdp, 8, width // fsdp), f32),
            pltpu.VMEM((tp, 8, 128), f32),
            pltpu.VMEM((tp, 8, 128), f32),
            dma((4, chunks, parts)), dma((4, chunks, parts)), dma((4, chunks, parts)),
            dma((6, chunks, parts)), dma((6, chunks, parts)),
            dma((2,)), dma((2, fsdp)), dma((2, fsdp)),
            dma((tp,)), dma((2, tp)), dma((2, tp)),
            dma((fsdp,)), dma((fsdp,)), dma((tp,)), dma((tp,)),
        ],
        compiler_params=pltpu.CompilerParams(
            collective_id=collective_id, has_side_effects=True, vmem_limit_bytes=48 << 20
        ),
        name="epilogue",
    )(*arrays, shared_up, shared_down, dn, hidden, grad, gain, sums)


def dense_plan(
    hidden_in,
    out_grad,
    segment_ids,
    expert_ids,
    route_weights,
    attn_gain,
    ffn_gain,
    qkv_weight,
    qkv_bias,
    out_weight,
    shared_gate_up,
    shared_down,
    shared_gate_vec,
    expert_gate_up,
    expert_down,
):
    every = ("fsdp", "tp")
    tp_rank = lax.axis_index("tp")
    experts = lax.axis_size("fsdp")
    packs = experts
    length = segment_ids.shape[1]
    own_rows = hidden_in.shape[0]
    model_width = hidden_in.shape[1]
    bf16 = jnp.bfloat16
    f32 = jnp.float32

    grad_all = lax.all_gather(out_grad, every, axis=0, tiled=True)
    shared_up = lax.all_to_all(shared_gate_up, "fsdp", split_axis=2, concat_axis=0, tiled=True)
    shared_dn = lax.all_to_all(shared_down, "fsdp", split_axis=0, concat_axis=1, tiled=True)
    expert_up = expert_gate_up[0]
    expert_dn = expert_down[0]
    expert_width = expert_up.shape[2]
    shared_width = shared_up.shape[2]

    chosen = expert_ids[:, :, None] == jnp.arange(experts, dtype=jnp.int32)
    table = jnp.sum(jnp.where(chosen, route_weights[:, :, None], 0.0), axis=1)
    local_heads = qkv_weight.shape[2]
    head_dim = qkv_weight.shape[3]
    score_scale = head_dim ** (-0.5)
    cos_table, sin_table = rope_tables(length, head_dim)
    positions = jnp.arange(length, dtype=jnp.int32)
    segments = segment_ids[0]
    allowed = (positions[:, None] >= positions[None, :]) & (segments[:, None] == segments[None, :])
    hidden_float = hidden_in.astype(f32)
    attn_inverse = inverse_rms(hidden_float)
    bias_rows = 3 * local_heads
    bias_columns = qkv_bias.shape[2]
    bias_piece = jnp.pad(
        qkv_bias.reshape(bias_rows, bias_columns), ((0, 16 - bias_rows), (0, 128 - bias_columns))
    )
    normed_one, qkv_flat, out_pieces, tables, bias_pieces = prologue(
        (hidden_float * attn_inverse * attn_gain).astype(bf16),
        [qkv_weight.reshape(-1, 3 * local_heads * head_dim), out_weight, table.T, bias_piece],
        experts,
        lax.axis_size("tp"),
        4,
    )
    out_full = out_pieces.reshape(experts, local_heads * head_dim, -1)
    out_full = out_full.transpose(1, 0, 2).reshape(local_heads * head_dim, model_width)
    expert_scale = lax.dynamic_index_in_dim(
        tables.reshape(packs, experts, length), lax.axis_index("fsdp"), axis=1, keepdims=False
    ).reshape(-1)
    bias_full = bias_pieces.reshape(experts, 16, 128)[:, :bias_rows, :bias_columns]
    bias_full = bias_full.transpose(1, 0, 2).reshape(3, local_heads, head_dim)
    qkv = (
        jnp.dot(normed_one, qkv_flat, preferred_element_type=f32).reshape(
            length, 3, local_heads, head_dim
        )
        + bias_full
    )
    query = rotate(qkv[:, 0], cos_table, sin_table).astype(bf16)
    keys = rotate(qkv[:, 1], cos_table, sin_table).astype(bf16)
    values = qkv[:, 2].astype(bf16)
    scores = masked_scores(query, keys, allowed, score_scale)
    row_peak = jnp.max(scores, axis=-1, keepdims=True)
    log_total = row_peak + jnp.log(jnp.sum(jnp.exp(scores - row_peak), axis=-1, keepdims=True))
    probs_b = jnp.exp(scores - log_total).astype(bf16)
    heads_out = (
        jnp.einsum("hqk,khd->qhd", probs_b, values, preferred_element_type=f32)
        .astype(bf16)
        .reshape(length, -1)
    )
    vec_high = shared_gate_vec.astype(bf16)
    vec_low = (shared_gate_vec - vec_high.astype(f32)).astype(bf16)
    gap = jnp.zeros((model_width, SHARED - expert_width), bf16)
    rest = jnp.zeros((model_width, UNIT - SHARED - shared_width), bf16)
    both_w = jnp.concatenate(
        [
            expert_up[:, 0],
            gap,
            shared_up[:, 0],
            vec_high[:, None],
            vec_low[:, None],
            rest[:, 2:],
            expert_up[:, 1],
            gap,
            shared_up[:, 1],
            rest,
        ],
        axis=1,
    )
    down_w = jnp.concatenate([expert_dn, gap.T, shared_dn, rest.T], axis=0)
    middle, normed_all, d_all, hidden_all, token_part, d_normed_two, extra_sum = ffn(
        jnp.dot(heads_out, out_full, preferred_element_type=f32).astype(bf16),
        hidden_in,
        ffn_gain[None],
        grad_all,
        both_w,
        down_w,
        jnp.broadcast_to(expert_scale[:, None], (expert_scale.shape[0], 128)),
        experts,
        lax.axis_size("tp"),
        expert_width,
        shared_width,
        1,
    )
    ffn_inverse = inverse_rms(middle)
    normed_two_own = (middle * ffn_inverse * ffn_gain).astype(bf16)
    own_start = tp_rank * own_rows
    ids_own = lax.dynamic_slice_in_dim(expert_ids, own_start, own_rows)
    picked = ids_own[:, :, None] == jnp.arange(experts, dtype=jnp.int32)
    route_grad = jnp.sum(jnp.where(picked, extra_sum[:experts].T[:, None, :], 0.0), axis=-1)
    gate_grad = extra_sum[experts]
    own_gate = jax.nn.sigmoid(jnp.sum(normed_two_own.astype(f32) * shared_gate_vec, axis=-1))
    logit_grad = gate_grad * own_gate * (1.0 - own_gate)
    d_normed_two = d_normed_two + logit_grad[:, None] * shared_gate_vec
    g_gate_vec = jnp.sum(normed_two_own.astype(f32) * logit_grad[:, None], axis=0)
    hat_two = middle * ffn_inverse
    g_ffn_gain = jnp.sum(d_normed_two * hat_two, axis=0)
    middle_grad = out_grad.astype(f32) + norm_backward(d_normed_two, hat_two, ffn_inverse, ffn_gain)
    total, d_rows, g_expert_up, g_shared_up, g_expert_down, g_shared_down = outputs(
        token_part,
        middle_grad.astype(bf16),
        normed_all,
        d_all,
        hidden_all,
        grad_all,
        experts,
        lax.axis_size("tp"),
        expert_width,
        shared_width,
        2,
    )
    hidden_out = (middle + total).astype(bf16)
    g_out = jnp.einsum(
        "tk,tfn->fkn",
        heads_out,
        d_rows.reshape(length, experts, -1),
        preferred_element_type=f32,
    ).astype(bf16)
    d_heads = (
        jnp.dot(d_rows, out_full.T, preferred_element_type=f32)
        .astype(bf16)
        .reshape(length, local_heads, head_dim)
    )
    heads_three = heads_out.reshape(length, local_heads, head_dim)
    scores_again = masked_scores(query, keys, allowed, score_scale)
    probs_full = jnp.exp(scores_again - log_total)
    probs_again = probs_full.astype(bf16)
    d_values = jnp.einsum("hqk,qhd->khd", probs_again, d_heads, preferred_element_type=f32)
    d_probs = jnp.einsum("qhd,khd->hqk", d_heads, values, preferred_element_type=f32)
    delta = jnp.sum(d_heads.astype(f32) * heads_three.astype(f32), axis=-1)
    d_scores = (probs_full * (d_probs - delta.T[:, :, None])).astype(bf16)
    d_query = jnp.einsum("hqk,khd->qhd", d_scores, keys, preferred_element_type=f32) * score_scale
    d_keys = jnp.einsum("hqk,qhd->khd", d_scores, query, preferred_element_type=f32) * score_scale
    d_qkv = jnp.stack(
        [unrotate(d_query, cos_table, sin_table), unrotate(d_keys, cos_table, sin_table), d_values],
        axis=1,
    )
    g_bias = jnp.sum(d_qkv, axis=0).reshape(bias_rows, experts, bias_columns).transpose(1, 0, 2)
    g_bias = jnp.pad(g_bias, ((0, 0), (0, 32 - bias_rows), (0, 128 - bias_columns)))
    d_qkv_b = d_qkv.astype(bf16).reshape(length, -1)
    g_qkv = jnp.dot(normed_one.T, d_qkv_b, preferred_element_type=f32).astype(bf16)
    d_normed_one = jnp.dot(d_qkv_b, qkv_flat.T, preferred_element_type=f32).astype(bf16)
    g_qkv, g_out, g_bias, g_shared_up, g_shared_down, hidden_grad, gains = epilogue(
        [g_qkv, g_out.reshape(-1, g_out.shape[2]), g_bias.reshape(-1, 128)],
        g_shared_up,
        g_shared_down,
        d_normed_one,
        hidden_in,
        middle_grad,
        attn_gain[None],
        jnp.stack([g_ffn_gain, g_gate_vec]),
        experts,
        lax.axis_size("tp"),
        3,
    )
    share = model_width // (experts * lax.axis_size("tp"))
    g_bias = g_bias.reshape(32, 128)[:bias_rows, :bias_columns]
    return (
        hidden_out,
        hidden_grad,
        route_grad,
        gains[0, :share],
        gains[1, :share],
        g_qkv.reshape(-1, 3, local_heads, head_dim),
        g_bias.reshape(qkv_bias.shape),
        g_out.reshape(out_weight.shape),
        g_shared_up.transpose(1, 0, 2),
        g_shared_down,
        gains[2, :share],
        g_expert_up.transpose(1, 0, 2)[None],
        g_expert_down[None],
    )


def on_device(*arrays):
    if lax.axis_size("fsdp") == 8 and lax.axis_size("tp") == 4 and arrays[3].shape[1] >= 3:
        return dense_plan(*arrays)
    return routed_plan(*arrays)


def solution(mesh):
    placed = (
        P(("fsdp", "tp"), None),
        P(("fsdp", "tp"), None),
        P("fsdp", None),
        P("fsdp", None),
        P("fsdp", None),
        P(),
        P(),
        P("fsdp", None, "tp", None),
        P(None, "tp", "fsdp"),
        P("tp", "fsdp"),
        P("fsdp", None, "tp"),
        P("tp", "fsdp"),
        P(),
        P("fsdp", None, None, "tp"),
        P("fsdp", "tp", None),
    )
    return jax.shard_map(
        on_device,
        mesh=mesh,
        in_specs=placed,
        out_specs=(
            P(("fsdp", "tp"), None),
            P(("fsdp", "tp"), None),
            P(("fsdp", "tp"), None),
            P(("fsdp", "tp")),
            P(("fsdp", "tp")),
            P("fsdp", None, "tp", None),
            P(None, "tp", "fsdp"),
            P("tp", "fsdp"),
            P("fsdp", None, "tp"),
            P("tp", "fsdp"),
            P(("fsdp", "tp")),
            P("fsdp", None, None, "tp"),
            P("fsdp", "tp", None),
        ),
        check_vma=False,
    )
```

```python
import functools

import jax
import jax.experimental.pallas as pl
import jax.experimental.pallas.tpu as pltpu
import jax.numpy as jnp
from jax import lax
from jax.sharding import PartitionSpec as P

epsilon = 1e-06


def rope_tables(length, head_dim):
    half_dim = head_dim // 2
    ratios = jnp.arange(half_dim, dtype=jnp.float32) * (2.0 / head_dim)
    frequency = jnp.exp(-jnp.log(10000.0) * ratios)
    angles = jnp.arange(length, dtype=jnp.float32)[:, None] * frequency[None, :]
    return (jnp.cos(angles)[:, None, :], jnp.sin(angles)[:, None, :])


def rotate(tensor, cos_table, sin_table):
    half_dim = tensor.shape[-1] // 2
    front_half = tensor[..., :half_dim]
    back_half = tensor[..., half_dim:]
    return jnp.concatenate(
        [
            front_half * cos_table - back_half * sin_table,
            back_half * cos_table + front_half * sin_table,
        ],
        axis=-1,
    )


def unrotate(tensor, cos_table, sin_table):
    half_dim = tensor.shape[-1] // 2
    front_half = tensor[..., :half_dim]
    back_half = tensor[..., half_dim:]
    return jnp.concatenate(
        [
            front_half * cos_table + back_half * sin_table,
            back_half * cos_table - front_half * sin_table,
        ],
        axis=-1,
    )


def silu_parts(gate_in):
    sigmoid_value = jax.nn.sigmoid(gate_in)
    return (gate_in * sigmoid_value, sigmoid_value * (1.0 + gate_in * (1.0 - sigmoid_value)))


def slot_table(route_ids, experts, capacity):
    flat_ids = route_ids.reshape(-1)
    onehot = (flat_ids[:, None] == jnp.arange(experts, dtype=jnp.int32)[None, :]).astype(jnp.int32)
    before = jnp.cumsum(onehot, axis=0, dtype=jnp.int32) - onehot
    ranks = jnp.sum(before * onehot, axis=1, dtype=jnp.int32)
    places = flat_ids * capacity + ranks
    filler = jnp.arange(flat_ids.shape[0], dtype=jnp.int32) + 1
    slot_rows = jnp.zeros((experts * capacity,), jnp.int32).at[places].set(filler)
    return (places.reshape(route_ids.shape), slot_rows.reshape(experts, capacity))


def inverse_rms(tensor):
    return lax.rsqrt(jnp.mean(tensor * tensor, axis=-1, keepdims=True) + epsilon)


def norm_backward(d_normed, hat_rows, inverse, gain_vec):
    d_hat = d_normed * gain_vec
    return inverse * (d_hat - hat_rows * jnp.mean(d_hat * hat_rows, axis=-1, keepdims=True))


def masked_scores(query, keys, allowed, score_scale):
    raw = jnp.einsum("qhd,khd->hqk", query, keys, preferred_element_type=jnp.float32) * score_scale
    return jnp.where(allowed[None], raw, -1e30)


def spread(rows):
    return lax.all_gather(rows, "tp", axis=0, tiled=True)


def head_total(partial_rows):
    return lax.psum_scatter(
        partial_rows.astype(jnp.bfloat16), "tp", scatter_dimension=0, tiled=True
    ).astype(jnp.float32)


def to_experts(buffer):
    return lax.all_to_all(buffer, "fsdp", split_axis=0, concat_axis=0, tiled=True)


def from_experts(buffer):
    return lax.all_to_all(buffer, "fsdp", split_axis=0, concat_axis=0, tiled=True)


def routed_plan(
    hidden_in,
    out_grad,
    segment_ids,
    expert_ids,
    route_weights,
    attn_gain,
    ffn_gain,
    qkv_weight,
    qkv_bias,
    out_weight,
    shared_gate_up,
    shared_down,
    shared_gate_vec,
    expert_gate_up,
    expert_down,
):
    tp_rank = lax.axis_index("tp")
    experts = lax.axis_size("fsdp")
    length = segment_ids.shape[1]
    top_count = expert_ids.shape[1]
    capacity = 3 * length * top_count // (2 * experts)
    own_rows = hidden_in.shape[0]
    model_width = hidden_in.shape[1]
    qkv_full, bias_full, out_full, shared_full, shared_down_full = (
        lax.all_gather(qkv_weight, "fsdp", axis=0, tiled=True),
        lax.all_gather(qkv_bias.astype(jnp.bfloat16), "fsdp", axis=2, tiled=True).astype(
            qkv_bias.dtype
        ),
        lax.all_gather(out_weight, "fsdp", axis=1, tiled=True),
        lax.all_gather(shared_gate_up, "fsdp", axis=0, tiled=True),
        lax.all_gather(shared_down, "fsdp", axis=1, tiled=True),
    )
    local_heads = qkv_full.shape[2]
    head_dim = qkv_full.shape[3]
    score_scale = head_dim ** (-0.5)
    cos_table, sin_table = rope_tables(length, head_dim)
    positions = jnp.arange(length, dtype=jnp.int32)
    segments = segment_ids[0]
    allowed = (positions[:, None] >= positions[None, :]) & (segments[:, None] == segments[None, :])
    hidden_float = hidden_in.astype(jnp.float32)
    attn_inverse = inverse_rms(hidden_float)
    normed_one = spread((hidden_float * attn_inverse * attn_gain).astype(jnp.bfloat16))
    qkv_flat = qkv_full.reshape(model_width, -1)
    qkv = (
        jnp.dot(normed_one, qkv_flat, preferred_element_type=jnp.float32).reshape(
            length, 3, local_heads, head_dim
        )
        + bias_full
    )
    query = rotate(qkv[:, 0], cos_table, sin_table).astype(jnp.bfloat16)
    keys = rotate(qkv[:, 1], cos_table, sin_table).astype(jnp.bfloat16)
    values = qkv[:, 2].astype(jnp.bfloat16)
    scores = masked_scores(query, keys, allowed, score_scale)
    row_peak = jnp.max(scores, axis=-1, keepdims=True)
    log_total = row_peak + jnp.log(jnp.sum(jnp.exp(scores - row_peak), axis=-1, keepdims=True))
    probs_b = jnp.exp(scores - log_total).astype(jnp.bfloat16)
    heads_out = (
        jnp.einsum("hqk,khd->qhd", probs_b, values, preferred_element_type=jnp.float32)
        .astype(jnp.bfloat16)
        .reshape(length, -1)
    )
    middle = hidden_float + head_total(
        jnp.dot(heads_out, out_full, preferred_element_type=jnp.float32)
    )
    ffn_inverse = inverse_rms(middle)
    normed_two_own = (middle * ffn_inverse * ffn_gain).astype(jnp.bfloat16)
    normed_two = spread(normed_two_own)
    gate_prob = jax.nn.sigmoid(jnp.sum(normed_two.astype(jnp.float32) * shared_gate_vec, axis=-1))
    shared_flat = shared_full.reshape(model_width, -1)
    shared_width = shared_full.shape[2]
    shared_pre = jnp.dot(normed_two, shared_flat, preferred_element_type=jnp.float32)
    shared_act, shared_slope = silu_parts(shared_pre[:, :shared_width])
    shared_upper = shared_pre[:, shared_width:]
    shared_hidden = (shared_act * shared_upper).astype(jnp.bfloat16)
    shared_part = jnp.dot(shared_hidden, shared_down_full, preferred_element_type=jnp.float32)
    places, slot_rows = slot_table(expert_ids, experts, capacity)
    filled = slot_rows > 0
    route_index = jnp.maximum(slot_rows - 1, 0)
    source_rows = route_index // top_count
    flat_weights = route_weights.reshape(-1)
    slot_weights = jnp.where(filled, flat_weights[route_index], 0.0)
    send_rows = jnp.where(filled[:, :, None], normed_two[source_rows], jnp.zeros((), jnp.bfloat16))
    arrived = to_experts(send_rows).reshape(-1, model_width)
    expert_flat = expert_gate_up[0].reshape(model_width, -1)
    expert_width = expert_gate_up.shape[3]
    down_local = expert_down[0]
    expert_pre = jnp.dot(arrived, expert_flat, preferred_element_type=jnp.float32)
    expert_act, expert_slope = silu_parts(expert_pre[:, :expert_width])
    expert_upper = expert_pre[:, expert_width:]
    expert_hidden = (expert_act * expert_upper).astype(jnp.bfloat16)
    expert_part = jnp.dot(expert_hidden, down_local, preferred_element_type=jnp.float32).astype(
        jnp.bfloat16
    )
    returned = from_experts(expert_part.reshape(experts, capacity, model_width)).reshape(
        experts * capacity, model_width
    )
    picked = returned[places].astype(jnp.float32)
    token_term = gate_prob[:, None] * shared_part + jnp.sum(
        route_weights[:, :, None] * picked, axis=1
    )
    own_extra = 0.0
    total = (
        lax.psum_scatter(
            token_term.astype(jnp.bfloat16), "tp", scatter_dimension=0, tiled=True
        ).astype(jnp.float32)
        + own_extra
    )
    hidden_out = (middle + total).astype(jnp.bfloat16)
    grad_rows = spread(out_grad)
    grad_float = grad_rows.astype(jnp.float32)
    gate_part = jnp.sum(grad_float * shared_part, axis=-1)
    scaled_grad = (gate_prob[:, None] * grad_float).astype(jnp.bfloat16)
    shared_d_hidden = jnp.dot(scaled_grad, shared_down_full.T, preferred_element_type=jnp.float32)
    shared_d_cat = jnp.concatenate(
        [
            (shared_d_hidden * shared_upper * shared_slope).astype(jnp.bfloat16),
            (shared_d_hidden * shared_act).astype(jnp.bfloat16),
        ],
        axis=1,
    )
    g_shared_down = jnp.dot(shared_hidden.T, scaled_grad, preferred_element_type=jnp.float32)
    g_shared_gate_up = jnp.dot(
        normed_two.T, shared_d_cat, preferred_element_type=jnp.float32
    ).reshape(shared_full.shape)
    d_normed_part = jnp.dot(shared_d_cat, shared_flat.T, preferred_element_type=jnp.float32)
    expert_grad_in = (slot_weights[:, :, None] * grad_float[source_rows]).astype(jnp.bfloat16)
    arrived_grad = to_experts(expert_grad_in).reshape(-1, model_width)
    back_act, back_slope, back_upper, back_hidden = (
        expert_act,
        expert_slope,
        expert_upper,
        expert_hidden,
    )
    expert_d_hidden = jnp.dot(arrived_grad, down_local.T, preferred_element_type=jnp.float32)
    expert_d_cat = jnp.concatenate(
        [
            (expert_d_hidden * back_upper * back_slope).astype(jnp.bfloat16),
            (expert_d_hidden * back_act).astype(jnp.bfloat16),
        ],
        axis=1,
    )
    g_expert_down = jnp.dot(back_hidden.T, arrived_grad, preferred_element_type=jnp.float32)[None]
    g_expert_gate_up = jnp.dot(arrived.T, expert_d_cat, preferred_element_type=jnp.float32).reshape(
        expert_gate_up.shape
    )
    expert_d_part = jnp.dot(expert_d_cat, expert_flat.T, preferred_element_type=jnp.float32).astype(
        jnp.bfloat16
    )
    route_part = jnp.sum(grad_float[:, None, :] * picked, axis=-1)
    returned_grad = from_experts(expert_d_part.reshape(experts, capacity, model_width)).reshape(
        experts * capacity, model_width
    )
    d_normed_part = d_normed_part + jnp.sum(returned_grad[places].astype(jnp.float32), axis=1)
    d_normed_two, route_grad, gate_grad = (
        lax.psum_scatter(
            d_normed_part.astype(jnp.bfloat16), "tp", scatter_dimension=0, tiled=True
        ).astype(jnp.float32),
        lax.psum_scatter(
            route_part.astype(jnp.bfloat16), "tp", scatter_dimension=0, tiled=True
        ).astype(jnp.float32),
        lax.psum_scatter(
            gate_part.astype(jnp.bfloat16), "tp", scatter_dimension=0, tiled=True
        ).astype(jnp.float32),
    )
    own_gate = lax.dynamic_slice_in_dim(gate_prob, tp_rank * own_rows, own_rows)
    logit_grad = gate_grad * own_gate * (1.0 - own_gate)
    d_normed_two = d_normed_two + logit_grad[:, None] * shared_gate_vec
    g_gate_vec = jnp.sum(normed_two_own.astype(jnp.float32) * logit_grad[:, None], axis=0)
    hat_two = middle * ffn_inverse
    g_ffn_gain = jnp.sum(d_normed_two * hat_two, axis=0)
    middle_grad = out_grad.astype(jnp.float32) + norm_backward(
        d_normed_two, hat_two, ffn_inverse, ffn_gain
    )
    d_rows = spread(middle_grad.astype(jnp.bfloat16))
    g_out = jnp.dot(heads_out.T, d_rows, preferred_element_type=jnp.float32)
    d_heads = (
        jnp.dot(d_rows, out_full.T, preferred_element_type=jnp.float32)
        .astype(jnp.bfloat16)
        .reshape(length, local_heads, head_dim)
    )
    heads_three = heads_out.reshape(length, local_heads, head_dim)
    scores_again = masked_scores(query, keys, allowed, score_scale)
    probs_full = jnp.exp(scores_again - log_total)
    probs_again = probs_full.astype(jnp.bfloat16)
    d_values = jnp.einsum("hqk,qhd->khd", probs_again, d_heads, preferred_element_type=jnp.float32)
    d_probs = jnp.einsum("qhd,khd->hqk", d_heads, values, preferred_element_type=jnp.float32)
    delta = jnp.sum(d_heads.astype(jnp.float32) * heads_three.astype(jnp.float32), axis=-1)
    d_scores = (probs_full * (d_probs - delta.T[:, :, None])).astype(jnp.bfloat16)
    d_query = (
        jnp.einsum("hqk,khd->qhd", d_scores, keys, preferred_element_type=jnp.float32) * score_scale
    )
    d_keys = (
        jnp.einsum("hqk,qhd->khd", d_scores, query, preferred_element_type=jnp.float32)
        * score_scale
    )
    d_qkv = jnp.stack(
        [unrotate(d_query, cos_table, sin_table), unrotate(d_keys, cos_table, sin_table), d_values],
        axis=1,
    )
    g_bias = jnp.sum(d_qkv, axis=0)
    d_qkv_b = d_qkv.astype(jnp.bfloat16).reshape(length, -1)
    g_qkv = jnp.dot(normed_one.T, d_qkv_b, preferred_element_type=jnp.float32).reshape(
        qkv_full.shape
    )
    d_normed_one = head_total(jnp.dot(d_qkv_b, qkv_flat.T, preferred_element_type=jnp.float32))
    hat_one = hidden_float * attn_inverse
    g_attn_gain = jnp.sum(d_normed_one * hat_one, axis=0)
    hidden_grad = middle_grad + norm_backward(d_normed_one, hat_one, attn_inverse, attn_gain)
    g_qkv, g_bias, g_out, g_shared_gate_up, g_shared_down = (
        lax.psum_scatter(
            g_qkv.astype(jnp.bfloat16), "fsdp", scatter_dimension=0, tiled=True
        ).astype(jnp.float32),
        lax.psum_scatter(
            g_bias.astype(jnp.bfloat16), "fsdp", scatter_dimension=2, tiled=True
        ).astype(jnp.float32),
        lax.psum_scatter(
            g_out.astype(jnp.bfloat16), "fsdp", scatter_dimension=1, tiled=True
        ).astype(jnp.float32),
        lax.psum_scatter(
            g_shared_gate_up.astype(jnp.bfloat16), "fsdp", scatter_dimension=0, tiled=True
        ).astype(jnp.float32),
        lax.psum_scatter(
            g_shared_down.astype(jnp.bfloat16), "fsdp", scatter_dimension=1, tiled=True
        ).astype(jnp.float32),
    )
    g_attn_gain, g_ffn_gain, g_gate_vec = (
        lax.psum_scatter(g_attn_gain, ("fsdp", "tp"), scatter_dimension=0, tiled=True),
        lax.psum_scatter(g_ffn_gain, ("fsdp", "tp"), scatter_dimension=0, tiled=True),
        lax.psum_scatter(g_gate_vec, ("fsdp", "tp"), scatter_dimension=0, tiled=True),
    )
    return (
        hidden_out,
        hidden_grad,
        route_grad,
        g_attn_gain,
        g_ffn_gain,
        g_qkv,
        g_bias,
        g_out,
        g_shared_gate_up,
        g_shared_down,
        g_gate_vec,
        g_expert_gate_up,
        g_expert_down,
    )


MESH = pl.DeviceIdType.MESH


def flipped(index, bit):
    return index + bit - 2 * bit * ((index // bit) % 2)


def place():
    me = lax.axis_index("fsdp")
    rank = lax.axis_index("tp")
    return me, rank


def greet(me, rank, tp):
    barrier = pltpu.get_barrier_semaphore()
    for bit in (1, 2, 4):
        pl.semaphore_signal(
            barrier, inc=1, device_id=(flipped(me, bit), rank), device_id_type=MESH
        )

    @pl.when(rank > 0)
    def _():
        pl.semaphore_signal(barrier, inc=1, device_id=(me, rank - 1), device_id_type=MESH)

    @pl.when(rank < tp - 1)
    def _():
        pl.semaphore_signal(barrier, inc=1, device_id=(me, rank + 1), device_id_type=MESH)

    left = (rank + tp - 1) // tp
    right = (2 * (tp - 1) - rank) // tp
    pl.semaphore_wait(barrier, 3 + left + right)


UNIT = 640
SHARED = 384
NT = (((1,), (1,)), ((), ()))


def ffn_kernel(tp, expert_width, shared_width, *refs):
    part_ref, hidden_ref, gain_ref, vec_ref, scale_ref, grad_ref = refs[:6]
    expert_up, shared_up, expert_down, shared_down = refs[6:10]
    middle_ref, all_ref, grads_ref, d_ref, hid_ref, y_ref, dsum_ref, esum_ref = refs[10:18]
    (
        x_all, g_buf, dh_buf, d_buf, stage, acc, diag_in, last_in, z_in, both_buf, down_buf,
        eu_buf, su_buf, stage_e, acc_e, other_e, diag_e, last_e, z_in_e,
        local_sem, w_sem, dn_sem, g_sem, x_sem, d_sem, h_sem, y_sem, f_sem, f_send, f_recv,
        az_send, az_recv, ap_send, ap_recv, gp_send, gp_recv,
        c_send, c_recv, ce_send, ce_recv, p_send, p_recv, pe_send, pe_recv,
        z_send, z_recv, ze_send, ze_recv,
    ) = refs[18:]
    me, rank = place()
    greet(me, rank, tp)
    f32 = jnp.float32
    bf16 = jnp.bfloat16
    subs, rows, width = hidden_ref.shape
    tile = tp * rows
    pack_rows = subs * tile
    packs = x_all.shape[0]
    near = rank // 2
    order = [rank]
    for bit in (1, 2):
        order = order + [flipped(one, bit) for one in order]
    blocks = [3 * (1 - near), 2 - near, flipped(rank, 1), rank]
    core_of, x_of, y_of = me % 2, (me // 2) % 2, me // 4

    def pack_of(bits):
        return (
            4 * ((y_of + bits // 4) % 2)
            + 2 * ((x_of + (bits // 2) % 2) % 2)
            + (core_of + bits % 2) % 2
        )

    def add(ref, spot, one):
        ref[spot] = (ref[spot].astype(f32) + one.astype(f32)).astype(ref.dtype)

    def remote(src, dst, send, recv, bit):
        return pltpu.make_async_remote_copy(
            src_ref=src,
            dst_ref=dst,
            send_sem=send,
            recv_sem=recv,
            device_id=(flipped(me, bit), rank),
            device_id_type=MESH,
        )

    def remote_z(src, dst, send, recv, right):
        return pltpu.make_async_remote_copy(
            src_ref=src,
            dst_ref=dst,
            send_sem=send,
            recv_sem=recv,
            device_id=(me, rank + 1 if right else rank - 1),
            device_id_type=MESH,
        )

    def gather_z(block, sub, right):
        way = 0 if right else 1
        ref = x_all.at[me, block, sub]
        return remote_z(
            ref, ref, az_send.at[way, block, sub], az_recv.at[way, block, sub], right
        )

    def gather(bit, pack_bits, block, sub, slot, start=0, count=None):
        count = rows if count is None else count
        ref = x_all.at[pack_of(pack_bits), block, sub, pl.ds(start, count)]
        return remote(ref, ref, ap_send.at[slot, block, sub], ap_recv.at[slot, block, sub], bit)

    def to_core(q, block, sub):
        return gather(1, 2 * q, block, sub, q)

    def own_x(block, sub):
        return gather(2, 0, block, sub, 4)

    def own_y(block, sub):
        return gather(4, 0, block, sub, 5)

    def x_to_y(block, sub):
        return gather(4, 2, block, sub, 6, 0, rows // 2)

    def y_to_x(block, sub):
        return gather(2, 4, block, sub, 7, rows // 2, rows // 2)

    def start_plane(block, sub):
        own_x(block, sub).start()
        own_y(block, sub).start()
        to_core(0, block, sub).start()

    def start_rows(sub):
        @pl.when(rank < tp - 1)
        def _():
            gather_z(rank, sub, True).start()

        @pl.when(rank > 0)
        def _():
            gather_z(rank, sub, False).start()

        start_plane(rank, sub)

    def forward(place_in, sub):
        block = order[place_in]
        own_x(block, sub).wait_recv()
        x_to_y(block, sub).start()
        to_core(1, block, sub).start()
        own_y(block, sub).wait_recv()
        y_to_x(block, sub).start()
        to_core(2, block, sub).start()

    def finish(place_in, sub):
        block = order[place_in]
        x_to_y(block, sub).wait_recv()
        y_to_x(block, sub).wait_recv()
        to_core(3, block, sub).start()

    def z_step(step, sub):
        @pl.when(rank >= step)
        def _():
            block = rank - step
            gather_z(block, sub, True).wait_recv()

            @pl.when(rank < tp - 1)
            def _():
                gather_z(block, sub, True).start()

            start_plane(block, sub)

        @pl.when(rank + step < tp)
        def _():
            block = rank + step
            gather_z(block, sub, False).wait_recv()

            @pl.when(rank > 0)
            def _():
                gather_z(block, sub, False).start()

            start_plane(block, sub)

    def control(i):
        steps = {
            0: [(z_step, 1, 1), (finish, 1, 0)],
            1: [(forward, 3, 0)],
            2: [(forward, 0, 1), (finish, 2, 0)],
            3: [(z_step, 2, 1)],
            4: [(finish, 3, 0), (forward, 1, 1)],
            5: [(z_step, 3, 1)],
            6: [(finish, 0, 1)],
            7: [(forward, 2, 1)],
            8: [(finish, 1, 1)],
            9: [(forward, 3, 1)],
            10: [(finish, 2, 1)],
            11: [(finish, 3, 1)],
        }
        for at, todo in steps.items():

            @pl.when(i == at)
            def _():
                for act, what, sub in todo:
                    act(what, sub)

    def grad_region(pack, c, start=0, count=None):
        count = tile if count is None else count
        return grads_ref.at[pl.ds(pack * pack_rows + c * tile + start, count)]

    def grads(bit, pack_bits, c, slot, start=0, count=None):
        dst = grad_region(pack_of(pack_bits), c, start, count)
        src = grad_ref.at[pl.ds(c * tile, tile)] if pack_bits == 0 else dst
        return remote(src, dst, gp_send.at[slot, c], gp_recv.at[slot, c], bit)

    def grad_core(q, c):
        return grads(1, 2 * q, c, q)

    def grad_x(c):
        return grads(2, 0, c, 4)

    def grad_y(c):
        return grads(4, 0, c, 5)

    def grad_x_to_y(c):
        return grads(4, 2, c, 6, 0, tile // 2)

    def grad_y_to_x(c):
        return grads(2, 4, c, 7, tile // 2, tile // 2)

    def grad_forward(c):
        grad_x(c).wait_recv()
        grad_x_to_y(c).start()
        grad_core(1, c).start()
        grad_y(c).wait_recv()
        grad_y_to_x(c).start()
        grad_core(2, c).start()

    def grad_finish(c):
        grad_x_to_y(c).wait_recv()
        grad_y_to_x(c).wait_recv()
        grad_core(3, c).start()

    def core(q, s):
        return remote(stage.at[s], acc.at[q, s], c_send.at[q, s], c_recv.at[q, s], 1)

    def core_e(q):
        return remote(stage_e.at[q], other_e.at[q], ce_send.at[q], ce_recv.at[q], 1)

    low, high = pl.ds(0, tp // 2), pl.ds(tp // 2, tp // 2)

    def across(bit, src, dst, slot, s):
        return remote(src, dst, p_send.at[slot, s], p_recv.at[slot, s], bit)

    def diag_x(s):
        return across(2, acc.at[3, s, low], diag_in.at[s, 0], 0, s)

    def diag_y(s):
        return across(4, acc.at[3, s, high], diag_in.at[s, 1], 1, s)

    def direct_x(s):
        return across(2, acc.at[1, s, low], last_in.at[s, 0, low], 2, s)

    def direct_y(s):
        return across(4, acc.at[2, s, high], last_in.at[s, 1, high], 3, s)

    def summed_x(s):
        return across(2, acc.at[1, s, high], last_in.at[s, 0, high], 4, s)

    def summed_y(s):
        return across(4, acc.at[2, s, low], last_in.at[s, 1, low], 5, s)

    def diag_lines():
        return remote(acc_e.at[3], diag_e, pe_send.at[0], pe_recv.at[0], 2)

    def direct_lines():
        return remote(acc_e.at[1], last_e.at[0], pe_send.at[1], pe_recv.at[1], 2)

    def summed_lines():
        return remote(acc_e.at[2], last_e.at[1], pe_send.at[2], pe_recv.at[2], 4)

    def along_z(j, s, right):
        way = 0 if right else 1
        block = blocks[j]
        return remote_z(
            acc.at[0, s, block],
            z_in.at[way, block, s],
            z_send.at[way, block, s],
            z_recv.at[way, block, s],
            right,
        )

    def lines_z(right):
        way = 0 if right else 1
        return remote_z(
            acc_e.at[1 + way], z_in_e.at[way], ze_send.at[way], ze_recv.at[way], right
        )

    def second(s):
        diag_x(s).wait_recv()
        add(acc, (2, s, low), diag_in[s, 0])
        summed_y(s).start()
        diag_y(s).wait_recv()
        add(acc, (1, s, high), diag_in[s, 1])
        summed_x(s).start()

    def third(j, s):
        block = blocks[j]
        if j == 0:
            direct_x(s).wait_recv()
            direct_y(s).wait_recv()
            summed_x(s).wait_recv()
            summed_y(s).wait_recv()
        total = (
            acc[0, s, block].astype(f32)
            + last_in[s, 0, block].astype(f32)
            + last_in[s, 1, block].astype(f32)
        )
        if j < tp - 1:
            acc[0, s, block] = total.astype(bf16)

            @pl.when((block > rank) & (rank > 0))
            def _():
                along_z(j, s, True).wait_recv()
                add(acc, (0, s, block), z_in[0, block, s])

            @pl.when((block < rank) & (rank < tp - 1))
            def _():
                along_z(j, s, False).wait_recv()
                add(acc, (0, s, block), z_in[1, block, s])

            @pl.when(block > rank)
            def _():
                along_z(j, s, True).start()

            @pl.when(block < rank)
            def _():
                along_z(j, s, False).start()
        else:
            dsum_ref[s] = total

            @pl.when(rank > 0)
            def _():
                along_z(j, s, True).wait_recv()
                dsum_ref[s] += z_in[0, block, s].astype(f32)

            @pl.when(rank < tp - 1)
            def _():
                along_z(j, s, False).wait_recv()
                dsum_ref[s] += z_in[1, block, s].astype(f32)

    def sum_lines():
        direct_lines().wait_recv()
        summed_lines().wait_recv()
        direct_lines().wait_send()
        summed_lines().wait_send()
        own = acc_e[0] + last_e[0] + last_e[1]
        esum_ref[...] = own
        acc_e[1] = own
        acc_e[2] = own

        @pl.when(rank > 0)
        def _():
            lines_z(True).wait_recv()
            esum_ref[...] += z_in_e[0]
            acc_e[1] = own + z_in_e[0]

        @pl.when(rank < tp - 1)
        def _():
            lines_z(True).start()
            lines_z(False).wait_recv()
            esum_ref[...] += z_in_e[1]
            acc_e[2] = own + z_in_e[1]

        @pl.when(rank > 0)
        def _():
            lines_z(False).start()

    def front_load(block, s):
        return pltpu.make_async_copy(
            part_ref.at[block, s], stage.at[s, block], f_sem.at[block, s]
        )

    def front_z(j, s, right):
        way = 0 if right else 1
        block = blocks[j]
        return remote_z(
            stage.at[s, block],
            z_in.at[way, block, s],
            f_send.at[way, block, s],
            f_recv.at[way, block, s],
            right,
        )

    def front(j, s):
        block = blocks[j]
        front_load(block, s).wait()
        if j < tp - 1:

            @pl.when((block > rank) & (rank > 0))
            def _():
                front_z(j, s, True).wait_recv()
                add(stage, (s, block), z_in[0, block, s])

            @pl.when((block < rank) & (rank < tp - 1))
            def _():
                front_z(j, s, False).wait_recv()
                add(stage, (s, block), z_in[1, block, s])

            @pl.when(block > rank)
            def _():
                front_z(j, s, True).start()

            @pl.when(block < rank)
            def _():
                front_z(j, s, False).start()
        else:
            middle_ref[s] = hidden_ref[s].astype(f32) + stage[s, block].astype(f32)

            @pl.when(rank > 0)
            def _():
                front_z(j, s, True).wait_recv()
                middle_ref[s] += z_in[0, block, s].astype(f32)

            @pl.when(rank < tp - 1)
            def _():
                front_z(j, s, False).wait_recv()
                middle_ref[s] += z_in[1, block, s].astype(f32)

            middle = middle_ref[s]
            mean = jnp.mean(middle * middle, axis=-1, keepdims=True)
            normed = middle * lax.rsqrt(mean + epsilon) * gain_ref[...]
            x_all[me, rank, s] = normed.astype(bf16)
            start_rows(s)

    cut = eu_buf.shape[1]
    cuts = width // cut
    units = SHARED + shared_width

    def weight_loads(part, n, slot):
        at = pl.ds(pl.multiple_of(n * cut, cut), cut)
        return (
            pltpu.make_async_copy(expert_up.at[part, at], eu_buf.at[slot], w_sem.at[0, slot]),
            pltpu.make_async_copy(shared_up.at[part, at], su_buf.at[slot], w_sem.at[1, slot]),
        )

    def lay_out(part):
        base = part * UNIT

        def body(n, carry):
            slot = n % 2

            @pl.when(n + 1 < cuts)
            def _():
                for copy in weight_loads(part, n + 1, 1 - slot):
                    copy.start()

            for copy in weight_loads(part, n, slot):
                copy.wait()
            at = pl.ds(pl.multiple_of(n * cut, cut), cut)
            both_buf[at, base : base + UNIT] = jnp.zeros((cut, UNIT), bf16)
            both_buf[at, base : base + expert_width] = eu_buf[slot]
            both_buf[at, base + SHARED : base + units] = su_buf[slot]
            return carry

        for copy in weight_loads(part, 0, 0):
            copy.start()
        lax.fori_loop(0, cuts, body, 0)

    down_loads = (
        pltpu.make_async_copy(expert_down, down_buf.at[pl.ds(0, expert_width)], dn_sem.at[0]),
        pltpu.make_async_copy(shared_down, down_buf.at[pl.ds(SHARED, shared_width)], dn_sem.at[1]),
    )

    def hidden_grads(count, task, own=False):
        def load(n, slot):
            pack_bits, c = task(n)
            src = grad_ref.at[pl.ds(c * tile, tile)] if own else grad_region(pack_of(pack_bits), c)
            return pltpu.make_async_copy(src, g_buf.at[slot], g_sem.at[slot])

        def body(n, carry):
            slot = n % 2

            @pl.when(n + 1 < count)
            def _():
                load(n + 1, 1 - slot).start()

            load(n, slot).wait()
            pack_bits, c = task(n)
            d_hidden = lax.dot_general(
                g_buf[slot], down_buf[...], NT, preferred_element_type=f32
            ).astype(bf16)
            dh_buf[pack_of(pack_bits), pl.ds(2 * c, 2)] = d_hidden.reshape(2, subs, rows, UNIT)
            return carry

        load(0, 0).start()
        lax.fori_loop(0, count, body, 0)
        if own:
            for c in range(2):
                own_store(c).start()
            for c in range(2):
                own_store(c).wait()

    def own_store(c):
        return pltpu.make_async_copy(g_buf.at[c], grad_region(me, c), local_sem.at[c])

    def tile_of(i):
        s = i // 8
        q = order_of(s, i // 2 % 4)
        o = i % 2
        return q, o, s, pack_of(2 * q + 1 - o)

    def order_of(s, r):
        return r + s * (r // 2) * (1 - 2 * (r % 2))

    def d_store(i):
        q, o, s, pack = tile_of(i)
        return pltpu.make_async_copy(d_buf.at[i % 2], d_ref.at[pack, :, s], d_sem.at[i % 2])

    def x_store(i):
        q, o, s, pack = tile_of(i)
        return pltpu.make_async_copy(x_all.at[pack, :, s], all_ref.at[pack, :, s], x_sem.at[i % 2])

    def one_tile(i, carry):
        q, o, s, pack = tile_of(i)
        slot = i % 2

        @pl.when(o == 0)
        def _():
            for block in range(tp):
                ref = x_all.at[pack, block, s]
                remote(
                    ref, ref, ap_send.at[q, block, s], ap_recv.at[q, block, s], 1
                ).wait_recv()

        @pl.when(i >= 2)
        def _():
            d_store(i - 2).wait()
            x_store(i - 2).wait()

        x_store(i).start()
        x = x_all[pack, :, s].reshape(tile, width)
        pre = jnp.dot(x, both_buf[...], preferred_element_type=f32)
        gate, upper = pre[:, :UNIT], pre[:, UNIT:]
        lane = lax.broadcasted_iota(jnp.int32, (1, UNIT), 1)
        logit = jnp.sum(x.astype(f32) * vec_ref[...], axis=-1, keepdims=True)
        gate_prob = 1.0 / (1.0 + jnp.exp(-logit))
        own_scale = jnp.broadcast_to(scale_ref[pack, s], (128, tile)).T[:, :1]
        scale = jnp.where(lane < SHARED, own_scale, gate_prob)
        sigmoid = 1.0 / (1.0 + jnp.exp(-gate))
        act = gate * sigmoid
        slope = sigmoid * (1.0 + gate * (1.0 - sigmoid))
        hidden = act * upper
        d_hidden = dh_buf[pack, :, s].reshape(tile, UNIT).astype(f32)
        line = lax.broadcasted_iota(jnp.int32, (16, UNIT), 0)
        unit = lax.broadcasted_iota(jnp.int32, (16, UNIT), 1)
        of_expert = (line == me) & (unit < SHARED)
        of_shared = (line == 8) & (unit >= SHARED)
        pick = jnp.where(of_expert | of_shared, 1.0, 0.0).astype(bf16)
        lines = lax.dot_general(
            pick, (d_hidden * hidden).astype(bf16), NT, preferred_element_type=f32
        )
        dh_buf[pack, :, s] = (hidden * scale).astype(bf16).reshape(tp, rows, UNIT)
        d_scaled = d_hidden * scale
        d_gate = (d_scaled * upper * slope).astype(bf16)
        d_upper = (d_scaled * act).astype(bf16)
        d_buf[slot, :, :, :UNIT] = d_gate.reshape(tp, rows, UNIT)
        d_buf[slot, :, :, UNIT:] = d_upper.reshape(tp, rows, UNIT)
        control(i)
        d_both = d_buf[slot].reshape(tile, 2 * UNIT)
        d_rows = lax.dot_general(d_both, both_buf[...], NT, preferred_element_type=f32)
        d_rows = d_rows.reshape(tp, rows, width)
        d_store(i).start()

        @pl.when(o == 0)
        def _():
            @pl.when(i % 8 >= 2)
            def _():
                core(order_of(s, i // 2 % 4 - 1), s).wait_send()

            stage[s] = d_rows.astype(bf16)
            stage_e[q, s] = lines
            core(q, s).start()

            @pl.when(s == 1)
            def _():
                core_e(q).start()

        @pl.when(o == 1)
        def _():
            core(q, s).wait_recv()
            add(acc, (q, s), d_rows)
            acc_e[q, s] = lines

            @pl.when(s == 1)
            def _():
                core_e(q).wait_recv()
                acc_e[q] = acc_e[q] + other_e[q]

                @pl.when(q == 1)
                def _():
                    direct_lines().start()

                @pl.when(q == 3)
                def _():
                    diag_lines().start()

            @pl.when(q == 1)
            def _():
                direct_x(s).start()

            @pl.when(q == 2)
            def _():
                direct_y(s).start()

            @pl.when(q == 3)
            def _():
                diag_x(s).start()
                diag_y(s).start()

            @pl.when(i == 11)
            def _():
                second(0)

        return carry

    def y_store(n, slot):
        return pltpu.make_async_copy(
            g_buf.at[slot], y_ref.at[pl.ds(n * tile, tile)], y_sem.at[slot]
        )

    def outputs(first, last):
        def body(n, carry):
            slot = n % 2

            @pl.when(n >= 2)
            def _():
                y_store(n - 2, slot).wait()

            hidden = dh_buf[n // 2, pl.ds(n % 2 * 2, 2)].reshape(tile, UNIT)
            g_buf[slot] = jnp.dot(hidden, down_buf[...], preferred_element_type=f32).astype(bf16)
            y_store(n, slot).start()
            return carry

        lax.fori_loop(first, last, body, 0)

    for c in range(2):
        grad_x(c).start()
        grad_y(c).start()
        grad_core(0, c).start()
    for s in range(subs):
        for block in blocks:
            front_load(block, s).start()
    down_buf[...] = jnp.zeros_like(down_buf)
    for copy in down_loads:
        copy.start()
    front(0, 0)
    lay_out(0)
    front(1, 0)
    lay_out(1)
    front(0, 1)
    front(2, 0)
    for copy in down_loads:
        copy.wait()
    front(3, 0)
    hidden_grads(2, lambda n: (0 * n, n), own=True)
    for c in range(2):
        grad_core(0, c).wait_recv()
    hidden_grads(2, lambda n: (0 * n + 1, n))
    grad_forward(0)
    front(1, 1)
    z_step(1, 0)
    for q in (1, 2):
        grad_core(q, 0).wait_recv()
    hidden_grads(4, lambda n: (2 + n, 0 * n))
    front(2, 1)
    z_step(2, 0)
    front(3, 1)
    z_step(3, 0)
    grad_forward(1)
    for q in (1, 2):
        grad_core(q, 1).wait_recv()
    hidden_grads(4, lambda n: (2 + n, 0 * n + 1))
    for s in range(subs):
        for j in range(tp - 1):
            block = blocks[j]

            @pl.when(block > rank)
            def _():
                front_z(j, s, True).wait_send()

            @pl.when(block < rank)
            def _():
                front_z(j, s, False).wait_send()

    forward(0, 0)
    grad_finish(0)
    forward(1, 0)
    grad_finish(1)
    for c in range(2):
        grad_core(3, c).wait_recv()
    hidden_grads(4, lambda n: (6 + n // 2, n % 2))
    finish(0, 0)
    forward(2, 0)
    lax.fori_loop(0, 16, one_tile, 0)
    hidden_store = pltpu.make_async_copy(dh_buf, hid_ref, h_sem)
    hidden_store.start()
    diag_lines().wait_recv()
    acc_e[2] = acc_e[2] + diag_e[...]
    summed_lines().start()
    outputs(0, 2)
    third(0, 0)
    outputs(2, 4)
    second(1)
    third(1, 0)
    outputs(4, 6)
    third(2, 0)
    outputs(6, 8)
    third(3, 0)
    sum_lines()
    outputs(8, 16)
    for j in range(tp):
        third(j, 1)

    hidden_store.wait()
    for n in (14, 15):
        y_store(n, n % 2).wait()
        d_store(n).wait()
        x_store(n).wait()
    core(3, 0).wait_send()
    core(2, 1).wait_send()
    diag_lines().wait_send()
    for q in range(4):
        core_e(q).wait_send()
    for c in range(2):
        for q in range(4):
            grad_core(q, c).wait_send()
        for copy in (grad_x, grad_y, grad_x_to_y, grad_y_to_x):
            copy(c).wait_send()
    for s in range(subs):
        for copy in (diag_x, diag_y, direct_x, direct_y, summed_x, summed_y):
            copy(s).wait_send()
        for block in range(tp):
            for q in range(4):
                to_core(q, block, s).wait_send()
            for copy in (own_x, own_y, x_to_y, y_to_x):
                copy(block, s).wait_send()

            @pl.when((block <= rank) & (rank < tp - 1))
            def _():
                gather_z(block, s, True).wait_send()

            @pl.when((block >= rank) & (rank > 0))
            def _():
                gather_z(block, s, False).wait_send()

        for j in range(tp - 1):
            block = blocks[j]

            @pl.when(block > rank)
            def _():
                along_z(j, s, True).wait_send()

            @pl.when(block < rank)
            def _():
                along_z(j, s, False).wait_send()

    @pl.when(rank < tp - 1)
    def _():
        lines_z(True).wait_send()

    @pl.when(rank > 0)
    def _():
        lines_z(False).wait_send()


def ffn(
    part, hidden, gain, vec, scale, grad, expert_up, shared_up, expert_down, shared_down,
    fsdp, tp, collective_id,
):
    own, width = hidden.shape
    subs = 2
    rows = own // subs
    tile = tp * rows
    tokens = fsdp * tp * own
    expert_width, shared_width = expert_down.shape[0], shared_down.shape[0]
    bf16 = jnp.bfloat16
    f32 = jnp.float32
    dma = pltpu.SemaphoreType.DMA
    anywhere = pl.BlockSpec(memory_space=pl.ANY)
    vmem = pl.BlockSpec(memory_space=pltpu.VMEM)
    all_rows = (fsdp, tp, subs, rows)
    lines = (subs, 16, tile)
    return pl.pallas_call(
        functools.partial(ffn_kernel, tp, expert_width, shared_width),
        out_shape=[
            jax.ShapeDtypeStruct((subs, rows, width), f32),
            jax.ShapeDtypeStruct(all_rows + (width,), bf16),
            jax.ShapeDtypeStruct((tokens, width), bf16),
            jax.ShapeDtypeStruct(all_rows + (2 * UNIT,), bf16),
            jax.ShapeDtypeStruct(all_rows + (UNIT,), bf16),
            jax.ShapeDtypeStruct((tokens, width), bf16),
            jax.ShapeDtypeStruct((subs, rows, width), f32),
            jax.ShapeDtypeStruct(lines, f32),
        ],
        in_specs=[anywhere] + [vmem] * 4 + [anywhere] * 5,
        out_specs=[vmem] + [anywhere] * 5 + [vmem] * 2,
        scratch_shapes=[
            pltpu.VMEM(all_rows + (width,), bf16),
            pltpu.VMEM((2, tile, width), bf16),
            pltpu.VMEM(all_rows + (UNIT,), bf16),
            pltpu.VMEM((2, tp, rows, 2 * UNIT), bf16),
            pltpu.VMEM((subs, tp, rows, width), bf16),
            pltpu.VMEM((4, subs, tp, rows, width), bf16),
            pltpu.VMEM((subs, 2, tp // 2, rows, width), bf16),
            pltpu.VMEM((subs, 2, tp, rows, width), bf16),
            pltpu.VMEM((2, tp, subs, rows, width), bf16),
            pltpu.VMEM((width, 2 * UNIT), bf16),
            pltpu.VMEM((UNIT, width), bf16),
            pltpu.VMEM((2, width // 8, expert_width), bf16),
            pltpu.VMEM((2, width // 8, shared_width), bf16),
            pltpu.VMEM((4,) + lines, f32),
            pltpu.VMEM((4,) + lines, f32),
            pltpu.VMEM((4,) + lines, f32),
            pltpu.VMEM(lines, f32),
            pltpu.VMEM((2,) + lines, f32),
            pltpu.VMEM((2,) + lines, f32),
            dma((2,)), dma((2, 2)), dma((2,)), dma((2,)), dma((2,)), dma((2,)), dma, dma((2,)),
            dma((tp, subs)), dma((2, tp, subs)), dma((2, tp, subs)),
            dma((2, tp, subs)), dma((2, tp, subs)), dma((8, tp, subs)), dma((8, tp, subs)),
            dma((8, 2)), dma((8, 2)),
            dma((4, subs)), dma((4, subs)), dma((4,)), dma((4,)),
            dma((6, subs)), dma((6, subs)), dma((3,)), dma((3,)),
            dma((2, tp, subs)), dma((2, tp, subs)), dma((2,)), dma((2,)),
        ],
        compiler_params=pltpu.CompilerParams(
            collective_id=collective_id, has_side_effects=True, vmem_limit_bytes=63 << 20
        ),
        name="ffn",
    )(
        part.reshape(tp, subs, rows, width), hidden.reshape(subs, rows, width), gain, vec,
        scale, grad, expert_up, shared_up, expert_down, shared_down,
    )


TN = (((0,), (0,)), ((), ()))
SUB = 2


def outputs_kernel(tp, expert_width, shared_width, *refs):
    y_ref, own_ref, x_ref, d_ref, h_ref, g_ref = refs[:6]
    total_ref, rows_ref, ge_ref, gs_ref, de_ref, ds_ref = refs[6:12]
    (
        mine, other, diag_in, last_in, z_in, d_buf, h_buf, col_buf, ge_buf, gs_buf, de_buf, ds_buf,
        l_sem, c_send, c_recv, p_send, p_recv, z_send, z_recv, a_sem, a_send, a_recv,
        w_sem, col_sem, out_sem,
    ) = refs[12:]
    me, rank = place()
    greet(me, rank, tp)
    f32 = jnp.float32
    bf16 = jnp.bfloat16
    rows = total_ref.shape[0]
    cut = rows // SUB
    half = cut // 2
    near = rank // 2
    blocks = [3 * (1 - near), 2 - near, flipped(rank, 1), rank]
    pieces = range(tp * SUB)
    packs = [me, flipped(me, 2), flipped(me, 4), flipped(flipped(me, 2), 4)]
    low, high = pl.ds(0, half), pl.ds(half, half)

    def gather_z(block, right):
        way = 0 if right else 1
        spot = rows_ref.at[pl.ds(block * rows, rows)]
        return pltpu.make_async_remote_copy(
            src_ref=spot,
            dst_ref=spot,
            send_sem=a_send.at[way, block],
            recv_sem=a_recv.at[way, block],
            device_id=(me, rank + 1 if right else rank - 1),
            device_id_type=MESH,
        )

    def gather_step(step):
        @pl.when(rank >= step)
        def _():
            gather_z(rank - step, True).wait_recv()

            @pl.when(rank < tp - 1)
            def _():
                gather_z(rank - step, True).start()

        @pl.when(rank + step < tp)
        def _():
            gather_z(rank + step, False).wait_recv()

            @pl.when(rank > 0)
            def _():
                gather_z(rank + step, False).start()

    def spot_of(j):
        return blocks[j // SUB] * SUB + j % SUB

    def region(pack, j):
        return y_ref.at[pl.ds((pack * tp * SUB + spot_of(j)) * cut, cut)]

    def local(k, j):
        return pltpu.make_async_copy(region(packs[k], j), mine.at[k, j], l_sem.at[k, j])

    def core(k, j):
        return pltpu.make_async_remote_copy(
            src_ref=region(flipped(packs[k], 1), j),
            dst_ref=other.at[k, j],
            send_sem=c_send.at[k, j],
            recv_sem=c_recv.at[k, j],
            device_id=(flipped(me, 1), rank),
            device_id_type=MESH,
        )

    def across(bit, src, dst, slot, j):
        return pltpu.make_async_remote_copy(
            src_ref=src,
            dst_ref=dst,
            send_sem=p_send.at[slot, j],
            recv_sem=p_recv.at[slot, j],
            device_id=(flipped(me, bit), rank),
            device_id_type=MESH,
        )

    def diag_x(j):
        return across(2, mine.at[3, j, low], diag_in.at[j, 0], 0, j)

    def diag_y(j):
        return across(4, mine.at[3, j, high], diag_in.at[j, 1], 1, j)

    def direct_x(j):
        return across(2, mine.at[1, j, low], last_in.at[j, 0, low], 2, j)

    def direct_y(j):
        return across(4, mine.at[2, j, high], last_in.at[j, 1, high], 3, j)

    def summed_x(j):
        return across(2, mine.at[1, j, high], last_in.at[j, 0, high], 4, j)

    def summed_y(j):
        return across(4, mine.at[2, j, low], last_in.at[j, 1, low], 5, j)

    def along_z(j, right):
        way = 0 if right else 1
        spot = spot_of(j)
        return pltpu.make_async_remote_copy(
            src_ref=mine.at[0, j],
            dst_ref=z_in.at[way, spot],
            send_sem=z_send.at[way, spot],
            recv_sem=z_recv.at[way, spot],
            device_id=(me, rank + 1 if right else rank - 1),
            device_id_type=MESH,
        )

    def add(ref, spot, one):
        ref[spot] = (ref[spot].astype(f32) + one.astype(f32)).astype(ref.dtype)

    def first(j):
        for k in (3, 2, 1, 0):
            core(k, j).wait_recv()
            local(k, j).wait()
            add(mine, (k, j), other[k, j])
            if k == 3:
                diag_x(j).start()
                diag_y(j).start()
            if k == 2:
                direct_y(j).start()
            if k == 1:
                direct_x(j).start()

    def second(j):
        diag_x(j).wait_recv()
        add(mine, (2, j, low), diag_in[j, 0])
        summed_y(j).start()
        diag_y(j).wait_recv()
        add(mine, (1, j, high), diag_in[j, 1])
        summed_x(j).start()

    def third(j):
        block = blocks[j // SUB]
        spot = spot_of(j)
        direct_x(j).wait_recv()
        direct_y(j).wait_recv()
        summed_x(j).wait_recv()
        summed_y(j).wait_recv()
        total = mine[0, j].astype(f32) + last_in[j, 0].astype(f32) + last_in[j, 1].astype(f32)
        if j < (tp - 1) * SUB:
            mine[0, j] = total.astype(bf16)

            @pl.when((block > rank) & (rank > 0))
            def _():
                along_z(j, True).wait_recv()
                add(mine, (0, j), z_in[0, spot])

            @pl.when((block < rank) & (rank < tp - 1))
            def _():
                along_z(j, False).wait_recv()
                add(mine, (0, j), z_in[1, spot])

            @pl.when(block > rank)
            def _():
                along_z(j, True).start()

            @pl.when(block < rank)
            def _():
                along_z(j, False).start()
        else:
            own_rows = pl.ds(j % SUB * cut, cut)
            total_ref[own_rows] = total

            @pl.when(rank > 0)
            def _():
                along_z(j, True).wait_recv()
                total_ref[own_rows] += z_in[0, spot].astype(f32)

            @pl.when(rank < tp - 1)
            def _():
                along_z(j, False).wait_recv()
                total_ref[own_rows] += z_in[1, spot].astype(f32)

    span = col_buf.shape[2]
    steps = x_ref.shape[1] // span
    units = SHARED + shared_width

    def columns(n, slot, of_x):
        ref = x_ref if of_x else g_ref
        return pltpu.make_async_copy(
            ref.at[:, pl.ds(pl.multiple_of(n * span, span), span)],
            col_buf.at[slot],
            col_sem.at[slot],
        )

    def up_stores(n, slot):
        at = pl.ds(pl.multiple_of(n * span, span), span)
        return (
            pltpu.make_async_copy(ge_buf.at[slot], ge_ref.at[:, at], out_sem.at[0, slot]),
            pltpu.make_async_copy(gs_buf.at[slot], gs_ref.at[:, at], out_sem.at[1, slot]),
        )

    def down_stores(n, slot):
        at = pl.ds(pl.multiple_of(n * span, span), span)
        return (
            pltpu.make_async_copy(de_buf.at[slot], de_ref.at[:, at], out_sem.at[2, slot]),
            pltpu.make_async_copy(ds_buf.at[slot], ds_ref.at[n], out_sem.at[3, slot]),
        )

    def up_step(n, carry):
        slot = n % 2

        @pl.when(n + 1 < steps)
        def _():
            columns(n + 1, 1 - slot, True).start()

        @pl.when(n + 1 == steps)
        def _():
            columns(0, 1 - slot, False).start()

        columns(n, slot, True).wait()

        @pl.when(n >= 2)
        def _():
            for copy in up_stores(n - 2, slot):
                copy.wait()

        grads = lax.dot_general(col_buf[slot], d_buf[...], TN, preferred_element_type=f32)
        for part in range(2):
            base = part * UNIT
            ge_buf[slot, part] = grads[:, base : base + expert_width]
            gs_buf[slot, part] = grads[:, base + SHARED : base + units].astype(bf16)
        for copy in up_stores(n, slot):
            copy.start()
        return carry

    def down_step(n, carry):
        slot = n % 2

        @pl.when(n + 1 < steps)
        def _():
            columns(n + 1, 1 - slot, False).start()

        columns(n, slot, False).wait()

        @pl.when(n >= 2)
        def _():
            for copy in down_stores(n - 2, slot):
                copy.wait()

        grads = lax.dot_general(h_buf[...], col_buf[slot], TN, preferred_element_type=f32)
        de_buf[slot] = grads[:expert_width]
        ds_buf[slot] = grads[SHARED:units].astype(bf16)
        for copy in down_stores(n, slot):
            copy.start()
        return carry

    load_d = pltpu.make_async_copy(d_ref, d_buf, w_sem.at[0])
    load_h = pltpu.make_async_copy(h_ref, h_buf, w_sem.at[1])
    own = pltpu.make_async_copy(own_ref, rows_ref.at[pl.ds(rank * rows, rows)], a_sem)
    own.start()
    for j in pieces:
        for k in (3, 2, 1, 0):
            core(k, j).start()
            local(k, j).start()
    load_d.start()
    columns(0, 0, True).start()
    load_h.start()
    own.wait()

    @pl.when(rank < tp - 1)
    def _():
        gather_z(rank, True).start()

    @pl.when(rank > 0)
    def _():
        gather_z(rank, False).start()

    first(0)
    first(1)
    load_d.wait()
    load_h.wait()
    for j in pieces:
        if j < len(pieces) // 2:
            lax.fori_loop(2 * j, 2 * j + 2, up_step, 0)
        else:
            later = j - len(pieces) // 2
            lax.fori_loop(2 * later, 2 * later + 2, down_step, 0)
        second(j)
        if j + 2 < len(pieces):
            first(j + 2)
        if j in (1, 3, 5):
            gather_step((j + 1) // 2)
        if j >= 2:
            third(j - 2)
    third(len(pieces) - 2)
    third(len(pieces) - 1)

    for n in (steps - 2, steps - 1):
        for copy in up_stores(n, n % 2) + down_stores(n, n % 2):
            copy.wait()
    for j in pieces:
        for k in range(4):
            core(k, j).wait_send()
        for copy in (diag_x, diag_y, direct_x, direct_y, summed_x, summed_y):
            copy(j).wait_send()
        block = blocks[j // SUB]
        if j < (tp - 1) * SUB:

            @pl.when(block > rank)
            def _():
                along_z(j, True).wait_send()

            @pl.when(block < rank)
            def _():
                along_z(j, False).wait_send()

    for block in range(tp):

        @pl.when((block <= rank) & (rank < tp - 1))
        def _():
            gather_z(block, True).wait_send()

        @pl.when((block >= rank) & (rank > 0))
        def _():
            gather_z(block, False).wait_send()


def outputs(y, own, x, d, h, g, fsdp, tp, expert_width, shared_width, collective_id):
    rows, width = own.shape
    tokens = y.shape[0]
    span = width // fsdp
    cut = rows // SUB
    bf16 = jnp.bfloat16
    f32 = jnp.float32
    dma = pltpu.SemaphoreType.DMA
    anywhere = pl.BlockSpec(memory_space=pl.ANY)
    return pl.pallas_call(
        functools.partial(outputs_kernel, tp, expert_width, shared_width),
        out_shape=[
            jax.ShapeDtypeStruct((rows, width), f32),
            jax.ShapeDtypeStruct((rows * tp, width), bf16),
            jax.ShapeDtypeStruct((2, width, expert_width), f32),
            jax.ShapeDtypeStruct((2, width, shared_width), bf16),
            jax.ShapeDtypeStruct((expert_width, width), f32),
            jax.ShapeDtypeStruct((fsdp, shared_width, span), bf16),
        ],
        in_specs=[anywhere, pl.BlockSpec(memory_space=pltpu.VMEM)] + [anywhere] * 4,
        out_specs=[pl.BlockSpec(memory_space=pltpu.VMEM)] + [anywhere] * 5,
        scratch_shapes=[
            pltpu.VMEM((4, tp * SUB, cut, width), bf16),
            pltpu.VMEM((4, tp * SUB, cut, width), bf16),
            pltpu.VMEM((tp * SUB, 2, cut // 2, width), bf16),
            pltpu.VMEM((tp * SUB, 2, cut, width), bf16),
            pltpu.VMEM((2, tp * SUB, cut, width), bf16),
            pltpu.VMEM((tokens, 2 * UNIT), bf16),
            pltpu.VMEM((tokens, UNIT), bf16),
            pltpu.VMEM((2, tokens, span), bf16),
            pltpu.VMEM((2, 2, span, expert_width), f32),
            pltpu.VMEM((2, 2, span, shared_width), bf16),
            pltpu.VMEM((2, expert_width, span), f32),
            pltpu.VMEM((2, shared_width, span), bf16),
            dma((4, tp * SUB)), dma((4, tp * SUB)), dma((4, tp * SUB)),
            dma((6, tp * SUB)), dma((6, tp * SUB)),
            dma((2, tp * SUB)), dma((2, tp * SUB)), dma, dma((2, tp)), dma((2, tp)),
            dma((2,)), dma((2,)), dma((4, 2)),
        ],
        compiler_params=pltpu.CompilerParams(
            collective_id=collective_id, has_side_effects=True, vmem_limit_bytes=60 << 20
        ),
        name="outputs",
    )(y, own, x, d, h, g)


def epilogue_kernel(fsdp, tp, parts, *refs):
    ins, refs = refs[:parts], refs[parts:]
    gs_ref, ds_ref, dn_ref, hidden_ref, grad_ref, gain_ref, sums_ref = refs[:7]
    refs = refs[7:]
    outs, refs = refs[:parts], refs[parts:]
    gs_out, ds_out, hidden_grad_ref, gains_ref = refs[:4]
    refs = refs[4:]
    mine, other, diag_in, last_in = (refs[i * parts : (i + 1) * parts] for i in range(4))
    (
        gs_in, ds_in, dn_buf, z_in, v_send, v_in, w_send, w_in,
        l_sem, c_send, c_recv, p_send, p_recv, s_sem, s_send, s_recv,
        f_sem, f_send, f_recv, v_ssem, v_rsem, w_ssem, w_rsem,
    ) = refs[4 * parts :]
    me, rank = place()
    f32 = jnp.float32
    bf16 = jnp.bfloat16
    rows, width = hidden_ref.shape
    near = rank // 2
    blocks = [3 * (1 - near), 2 - near, flipped(rank, 1), rank]
    packs = [me, flipped(me, 2), flipped(me, 4), flipped(flipped(me, 2), 4)]
    every = range(parts)
    chunks = outs[0].shape[0]
    sizes = [ref.shape[1] for ref in outs]
    low = [pl.ds(0, size // 2) for size in sizes]
    high = [pl.ds(size // 2, size // 2) for size in sizes]

    def plane(bits):
        peer = me
        for one in (1, 2, 4):
            if bits & one:
                peer = flipped(peer, one)
        return peer

    def line(bits):
        peer = rank
        for one in (1, 2):
            if bits & one:
                peer = flipped(peer, one)
        return peer

    barrier = pltpu.get_barrier_semaphore()
    for bits in range(1, fsdp):
        pl.semaphore_signal(
            barrier, inc=1, device_id=(plane(bits), rank), device_id_type=MESH
        )
    for bits in range(1, tp):
        pl.semaphore_signal(barrier, inc=1, device_id=(me, line(bits)), device_id_type=MESH)
    pl.semaphore_wait(barrier, fsdp - 1 + tp - 1)

    def add(ref, spot, one):
        ref[spot] = (ref[spot].astype(f32) + one.astype(f32)).astype(ref.dtype)

    def region(i, pack, j):
        return ins[i].at[pl.ds((pack * chunks + j) * sizes[i], sizes[i])]

    def local(k, j, i):
        return pltpu.make_async_copy(region(i, packs[k], j), mine[i].at[k, j], l_sem.at[k, j, i])

    def core(k, j, i):
        return pltpu.make_async_remote_copy(
            src_ref=region(i, flipped(packs[k], 1), j),
            dst_ref=other[i].at[k, j],
            send_sem=c_send.at[k, j, i],
            recv_sem=c_recv.at[k, j, i],
            device_id=(flipped(me, 1), rank),
            device_id_type=MESH,
        )

    def across(bit, src, dst, slot, j, i):
        return pltpu.make_async_remote_copy(
            src_ref=src,
            dst_ref=dst,
            send_sem=p_send.at[slot, j, i],
            recv_sem=p_recv.at[slot, j, i],
            device_id=(flipped(me, bit), rank),
            device_id_type=MESH,
        )

    def diag_x(j, i):
        return across(2, mine[i].at[3, j, low[i]], diag_in[i].at[j, 0], 0, j, i)

    def diag_y(j, i):
        return across(4, mine[i].at[3, j, high[i]], diag_in[i].at[j, 1], 1, j, i)

    def direct_x(j, i):
        return across(2, mine[i].at[1, j, low[i]], last_in[i].at[j, 0, low[i]], 2, j, i)

    def direct_y(j, i):
        return across(4, mine[i].at[2, j, high[i]], last_in[i].at[j, 1, high[i]], 3, j, i)

    def summed_x(j, i):
        return across(2, mine[i].at[1, j, high[i]], last_in[i].at[j, 0, high[i]], 4, j, i)

    def summed_y(j, i):
        return across(4, mine[i].at[2, j, low[i]], last_in[i].at[j, 1, low[i]], 5, j, i)

    def first(j):
        for i in every:
            for k in (3, 2, 1, 0):
                core(k, j, i).wait_recv()
                local(k, j, i).wait()
                add(mine[i], (k, j), other[i][k, j])
                if k == 3:
                    diag_x(j, i).start()
                    diag_y(j, i).start()
                if k == 2:
                    direct_y(j, i).start()
                if k == 1:
                    direct_x(j, i).start()

    def second(j):
        for i in every:
            diag_x(j, i).wait_recv()
            add(mine[i], (2, j, low[i]), diag_in[i][j, 0])
            summed_y(j, i).start()
            diag_y(j, i).wait_recv()
            add(mine[i], (1, j, high[i]), diag_in[i][j, 1])
            summed_x(j, i).start()

    def third(j):
        for i in every:
            direct_x(j, i).wait_recv()
            direct_y(j, i).wait_recv()
            summed_x(j, i).wait_recv()
            summed_y(j, i).wait_recv()
            outs[i][j] = (
                mine[i][0, j].astype(f32)
                + last_in[i][j, 0].astype(f32)
                + last_in[i][j, 1].astype(f32)
            )

    span = ds_ref.shape[2]

    def shared_up(bits):
        at = pl.ds(pl.multiple_of(plane(bits) * span, span), span)
        return pltpu.make_async_remote_copy(
            src_ref=gs_ref.at[:, at],
            dst_ref=gs_in.at[me],
            send_sem=s_send.at[0, bits],
            recv_sem=s_recv.at[0, bits],
            device_id=(plane(bits), rank),
            device_id_type=MESH,
        )

    def shared_down(bits):
        return pltpu.make_async_remote_copy(
            src_ref=ds_ref.at[plane(bits)],
            dst_ref=ds_in.at[me],
            send_sem=s_send.at[1, bits],
            recv_sem=s_recv.at[1, bits],
            device_id=(plane(bits), rank),
            device_id_type=MESH,
        )

    own_up = pltpu.make_async_copy(
        gs_ref.at[:, pl.ds(pl.multiple_of(me * span, span), span)], gs_in.at[me], s_sem.at[0]
    )
    own_down = pltpu.make_async_copy(ds_ref.at[me], ds_in.at[me], s_sem.at[1])

    def front_load(block):
        return pltpu.make_async_copy(
            dn_ref.at[pl.ds(block * rows, rows)], dn_buf.at[block], f_sem.at[block]
        )

    def front_z(j, right):
        way = 0 if right else 1
        block = blocks[j]
        return pltpu.make_async_remote_copy(
            src_ref=dn_buf.at[block],
            dst_ref=z_in.at[way, block],
            send_sem=f_send.at[way, block],
            recv_sem=f_recv.at[way, block],
            device_id=(me, rank + 1 if right else rank - 1),
            device_id_type=MESH,
        )

    def front(j):
        block = blocks[j]
        front_load(block).wait()
        if j < tp - 1:

            @pl.when((block > rank) & (rank > 0))
            def _():
                front_z(j, True).wait_recv()
                add(dn_buf, (block,), z_in[0, block])

            @pl.when((block < rank) & (rank < tp - 1))
            def _():
                front_z(j, False).wait_recv()
                add(dn_buf, (block,), z_in[1, block])

            @pl.when(block > rank)
            def _():
                front_z(j, True).start()

            @pl.when(block < rank)
            def _():
                front_z(j, False).start()
        else:
            hidden_grad_ref[...] = dn_buf[block].astype(f32)

            @pl.when(rank > 0)
            def _():
                front_z(j, True).wait_recv()
                hidden_grad_ref[...] += z_in[0, block].astype(f32)

            @pl.when(rank < tp - 1)
            def _():
                front_z(j, False).wait_recv()
                hidden_grad_ref[...] += z_in[1, block].astype(f32)

    share = width // fsdp
    part = share // tp

    def gains_plane(bits):
        return pltpu.make_async_remote_copy(
            src_ref=v_send.at[plane(bits)],
            dst_ref=v_in.at[me],
            send_sem=v_ssem.at[bits],
            recv_sem=v_rsem.at[bits],
            device_id=(plane(bits), rank),
            device_id_type=MESH,
        )

    def gains_line(bits):
        return pltpu.make_async_remote_copy(
            src_ref=w_send.at[line(bits)],
            dst_ref=w_in.at[rank],
            send_sem=w_ssem.at[bits],
            recv_sem=w_rsem.at[bits],
            device_id=(me, line(bits)),
            device_id_type=MESH,
        )

    for block in blocks:
        front_load(block).start()
    for j in range(chunks):
        for i in every:
            for k in (3, 2, 1, 0):
                core(k, j, i).start()
                local(k, j, i).start()
    ends = (rank == 0) | (rank == tp - 1)

    @pl.when(ends)
    def _():
        front(0)
        front(1)

    for bits in (6, 7, 2, 4, 3, 5, 1):
        shared_up(bits).start()
        shared_down(bits).start()
    own_up.start()
    own_down.start()
    first(0)
    first(1)

    @pl.when(jnp.logical_not(ends))
    def _():
        front(0)

    second(0)

    @pl.when(jnp.logical_not(ends))
    def _():
        front(1)

    second(1)
    front(2)
    front(3)
    d_normed = hidden_grad_ref[...]
    hidden = hidden_ref[...].astype(f32)
    inverse = lax.rsqrt(jnp.mean(hidden * hidden, axis=-1, keepdims=True) + epsilon)
    hat = hidden * inverse
    v_send[...] = jnp.zeros_like(v_send)
    attn_gain = jnp.sum(d_normed * hat, axis=0, keepdims=True)
    for owner in range(fsdp):
        at = slice(owner * share, (owner + 1) * share)
        v_send[owner, 0:1] = attn_gain[:, at]
        v_send[owner, 1:3] = sums_ref[:, at]
    for bits in range(1, fsdp):
        gains_plane(bits).start()
    d_hat = d_normed * gain_ref[...]
    mean = jnp.mean(d_hat * hat, axis=-1, keepdims=True)
    hidden_grad_ref[...] = grad_ref[...] + inverse * (d_hat - hat * mean)
    third(0)
    total = v_send[me]
    for bits in range(1, fsdp):
        gains_plane(bits).wait_recv()
        total = total + v_in[plane(bits)]
    w_send[...] = jnp.zeros_like(w_send)
    for owner in range(tp):
        w_send[owner, :, :part] = total[:, owner * part : (owner + 1) * part]
    for bits in range(1, tp):
        gains_line(bits).start()
    third(1)
    own_up.wait()
    own_down.wait()
    for bits in range(1, fsdp):
        shared_up(bits).wait_recv()
        shared_down(bits).wait_recv()
    units = gs_in.shape[3]
    for owner in range(fsdp):
        at = slice(owner * units, (owner + 1) * units)
        gs_out[:, :, at] = gs_in[owner].astype(f32)
        ds_out[at] = ds_in[owner].astype(f32)
    total = w_send[rank]
    for bits in range(1, tp):
        gains_line(bits).wait_recv()
        total = total + w_in[line(bits)]
    gains_ref[...] = total

    for j in range(chunks):
        for i in every:
            for k in range(4):
                core(k, j, i).wait_send()
            for copy in (diag_x, diag_y, direct_x, direct_y, summed_x, summed_y):
                copy(j, i).wait_send()
    for bits in range(1, fsdp):
        shared_up(bits).wait_send()
        shared_down(bits).wait_send()
        gains_plane(bits).wait_send()
    for bits in range(1, tp):
        gains_line(bits).wait_send()
    for j in range(tp - 1):
        block = blocks[j]

        @pl.when(block > rank)
        def _():
            front_z(j, True).wait_send()

        @pl.when(block < rank)
        def _():
            front_z(j, False).wait_send()


def epilogue(arrays, shared_up, shared_down, dn, hidden, grad, gain, sums, fsdp, tp, collective_id):
    chunks = 2
    parts = len(arrays)
    rows, width = hidden.shape
    units = shared_up.shape[2]
    span = shared_down.shape[2]
    f32 = jnp.float32
    shapes = [(one.shape[0] // (fsdp * chunks), one.shape[1], one.dtype) for one in arrays]
    scratch = [pltpu.VMEM((4, chunks, size, w), kind) for size, w, kind in shapes]
    scratch += [pltpu.VMEM((4, chunks, size, w), kind) for size, w, kind in shapes]
    scratch += [pltpu.VMEM((chunks, 2, size // 2, w), kind) for size, w, kind in shapes]
    scratch += [pltpu.VMEM((chunks, 2, size, w), kind) for size, w, kind in shapes]
    dma = pltpu.SemaphoreType.DMA
    anywhere = pl.BlockSpec(memory_space=pl.ANY)
    vmem = pl.BlockSpec(memory_space=pltpu.VMEM)
    out_shape = [jax.ShapeDtypeStruct((chunks, size, w), f32) for size, w, _ in shapes]
    out_shape += [
        jax.ShapeDtypeStruct((2, span, fsdp * units), f32),
        jax.ShapeDtypeStruct((fsdp * units, span), f32),
        jax.ShapeDtypeStruct((rows, width), f32),
        jax.ShapeDtypeStruct((8, 128), f32),
    ]
    return pl.pallas_call(
        functools.partial(epilogue_kernel, fsdp, tp, parts),
        out_shape=out_shape,
        in_specs=[anywhere] * (parts + 3) + [vmem] * 4,
        out_specs=[vmem] * len(out_shape),
        scratch_shapes=scratch
        + [
            pltpu.VMEM((fsdp, 2, span, units), shared_up.dtype),
            pltpu.VMEM((fsdp, units, span), shared_down.dtype),
            pltpu.VMEM((tp, rows, width), dn.dtype),
            pltpu.VMEM((2, tp, rows, width), dn.dtype),
            pltpu.VMEM((fsdp, 8, width // fsdp), f32),
            pltpu.VMEM((fsdp, 8, width // fsdp), f32),
            pltpu.VMEM((tp, 8, 128), f32),
            pltpu.VMEM((tp, 8, 128), f32),
            dma((4, chunks, parts)), dma((4, chunks, parts)), dma((4, chunks, parts)),
            dma((6, chunks, parts)), dma((6, chunks, parts)),
            dma((2,)), dma((2, fsdp)), dma((2, fsdp)),
            dma((tp,)), dma((2, tp)), dma((2, tp)),
            dma((fsdp,)), dma((fsdp,)), dma((tp,)), dma((tp,)),
        ],
        compiler_params=pltpu.CompilerParams(
            collective_id=collective_id, has_side_effects=True, vmem_limit_bytes=48 << 20
        ),
        name="epilogue",
    )(*arrays, shared_up, shared_down, dn, hidden, grad, gain, sums)

def plane_peer(me, bits):
    for one in (1, 2, 4):
        if bits & one:
            me = flipped(me, one)
    return me


def attend_kernel(tp, heads, halved, *refs):
    parts = len(halved)
    hidden_ref, gain_ref, grad_ref, seg_row_ref, seg_col_ref, cos_ref, sin_ref = refs[:7]
    up_ref, down_ref = refs[7:9]
    pieces, refs = refs[9 : 9 + parts], refs[9 + parts :]
    rows_out, grads_ref, q_ref, k_ref, v_ref, lt_ref, heads_ref, part_ref = refs[:8]
    up_out, down_out = refs[8:10]
    fulls_out, refs = refs[10 : 10 + parts], refs[10 + parts :]
    rows_ref, fulls, refs = refs[0], refs[1 : 1 + parts], refs[1 + parts :]
    (
        up_buf, down_buf, l_sem, e_sem, z_send, z_recv, g_send, g_recv, p_send, p_recv, s_sem, s_send, s_recv,
    ) = refs
    me, rank = place()
    f32 = jnp.float32
    bf16 = jnp.bfloat16
    rows, width = hidden_ref.shape
    length = rows * tp

    barrier = pltpu.get_barrier_semaphore()
    for bits in range(1, 8):
        pl.semaphore_signal(
            barrier, inc=1, device_id=(plane_peer(me, bits), rank), device_id_type=MESH
        )

    @pl.when(rank > 0)
    def _():
        pl.semaphore_signal(barrier, inc=1, device_id=(me, rank - 1), device_id_type=MESH)

    @pl.when(rank < tp - 1)
    def _():
        pl.semaphore_signal(barrier, inc=1, device_id=(me, rank + 1), device_id_type=MESH)

    left = (rank + tp - 1) // tp
    right = (2 * (tp - 1) - rank) // tp
    pl.semaphore_wait(barrier, 7 + left + right)

    def along_z(ref, sends, recvs, block, to_right):
        way = 0 if to_right else 1
        spot = ref.at[pl.ds(block * rows, rows)]
        return pltpu.make_async_remote_copy(
            src_ref=spot,
            dst_ref=spot,
            send_sem=sends.at[way, block],
            recv_sem=recvs.at[way, block],
            device_id=(me, rank + 1 if to_right else rank - 1),
            device_id_type=MESH,
        )

    def row_z(block, to_right):
        return along_z(rows_ref, z_send, z_recv, block, to_right)

    def grad_z(block, to_right):
        return along_z(grads_ref, g_send, g_recv, block, to_right)

    def z_start(copy):
        @pl.when(rank < tp - 1)
        def _():
            copy(rank, True).start()

        @pl.when(rank > 0)
        def _():
            copy(rank, False).start()

    def z_step(copy, step):
        @pl.when(rank >= step)
        def _():
            copy(rank - step, True).wait_recv()

            @pl.when(rank < tp - 1)
            def _():
                copy(rank - step, True).start()

        @pl.when(rank + step < tp)
        def _():
            copy(rank + step, False).wait_recv()

            @pl.when(rank > 0)
            def _():
                copy(rank + step, False).start()

    def z_end(copy):
        for block in range(tp):

            @pl.when((block <= rank) & (rank < tp - 1))
            def _():
                copy(block, True).wait_send()

            @pl.when((block >= rank) & (rank > 0))
            def _():
                copy(block, False).wait_send()

    def region(i, owner_bits, start=0, count=None):
        size = pieces[i].shape[0]
        count = size if count is None else count
        return fulls[i].at[pl.ds(plane_peer(me, owner_bits) * size + start, count)]

    def across(i, bit, owner_bits, slot, start=0, count=None):
        spot = region(i, owner_bits, start, count)
        return pltpu.make_async_remote_copy(
            src_ref=pieces[i] if owner_bits == 0 else spot,
            dst_ref=spot,
            send_sem=p_send.at[slot, i],
            recv_sem=p_recv.at[slot, i],
            device_id=(flipped(me, bit), rank),
            device_id_type=MESH,
        )

    def to_core(q, i):
        return across(i, 1, 2 * q, q)

    def own_x(i):
        return across(i, 2, 0, 4)

    def own_y(i):
        return across(i, 4, 0, 5)

    def x_to_y(i):
        size = pieces[i].shape[0]
        return across(i, 4, 2, 6, 0, size // 2 if halved[i] else size)

    def y_to_x(i):
        size = pieces[i].shape[0]
        return across(i, 2, 4, 7, size // 2, size // 2)

    def local(i):
        return pltpu.make_async_copy(pieces[i], region(i, 0), l_sem.at[i])

    def export(i):
        return pltpu.make_async_copy(fulls[i], fulls_out[i], e_sem.at[i])

    def forward(i):
        own_x(i).wait_recv()
        x_to_y(i).start()
        to_core(1, i).start()
        own_y(i).wait_recv()
        if halved[i]:
            y_to_x(i).start()
        to_core(2, i).start()

    def finish(i):
        x_to_y(i).wait_recv()
        if halved[i]:
            y_to_x(i).wait_recv()
        to_core(3, i).start()

    def arrived(i):
        local(i).wait()
        for q in range(4):
            to_core(q, i).wait_recv()
        export(i).start()

    up_rows = up_ref.shape[2]
    span = down_ref.shape[2]

    def shared_up(bits):
        return pltpu.make_async_remote_copy(
            src_ref=up_ref.at[plane_peer(me, bits)],
            dst_ref=up_out.at[:, pl.ds(pl.multiple_of(me * up_rows, up_rows), up_rows)],
            send_sem=s_send.at[0, bits],
            recv_sem=s_recv.at[0, bits],
            device_id=(plane_peer(me, bits), rank),
            device_id_type=MESH,
        )

    def shared_down(bits):
        return pltpu.make_async_remote_copy(
            src_ref=down_ref.at[plane_peer(me, bits)],
            dst_ref=down_out.at[:, pl.ds(pl.multiple_of(me * span, span), span)],
            send_sem=s_send.at[1, bits],
            recv_sem=s_recv.at[1, bits],
            device_id=(plane_peer(me, bits), rank),
            device_id_type=MESH,
        )

    own_loads = (
        pltpu.make_async_copy(up_ref.at[me], up_buf, s_sem.at[0]),
        pltpu.make_async_copy(down_ref.at[me], down_buf, s_sem.at[1]),
    )
    own_stores = (
        pltpu.make_async_copy(
            up_buf,
            up_out.at[:, pl.ds(pl.multiple_of(me * up_rows, up_rows), up_rows)],
            s_sem.at[0],
        ),
        pltpu.make_async_copy(
            down_buf, down_out.at[:, pl.ds(pl.multiple_of(me * span, span), span)], s_sem.at[1]
        ),
    )

    def project(which):
        at = slice(which * heads * 128, (which + 1) * heads * 128)
        return jnp.dot(rows_ref[...], fulls[0][:, at], preferred_element_type=f32)

    def bias(which, head):
        line = which * heads + head
        size = pieces[3].shape[0]
        share = 128 // 8
        return jnp.concatenate(
            [fulls[3][owner * size + line : owner * size + line + 1, :share] for owner in range(8)],
            axis=1,
        )

    def rotated(columns):
        return columns * cos_ref[...] + pltpu.roll(columns, 64, 1) * sin_ref[...]

    def make_heads():
        for which, ref in ((0, q_ref), (1, k_ref), (2, v_ref)):
            all_heads = project(which)
            for head in range(heads):
                at = slice(head * 128, (head + 1) * 128)
                one = all_heads[:, at] + bias(which, head)
                if which < 2:
                    one = rotated(one)
                ref[:, at] = one.astype(bf16)

    def attend(head):
        at = slice(head * 128, (head + 1) * 128)
        scores = lax.dot_general(q_ref[:, at], k_ref[:, at], NT, preferred_element_type=f32)
        line = lax.broadcasted_iota(jnp.int32, (length, length), 0)
        column = lax.broadcasted_iota(jnp.int32, (length, length), 1)
        allowed = (line >= column) & (seg_col_ref[...] == seg_row_ref[...])
        scores = jnp.where(allowed, scores * 128 ** (-0.5), -1e30)
        peak = jnp.max(scores, axis=-1, keepdims=True)
        log_total = peak + jnp.log(jnp.sum(jnp.exp(scores - peak), axis=-1, keepdims=True))
        probs = jnp.exp(scores - log_total).astype(bf16)
        lane = lax.broadcasted_iota(jnp.int32, (length, 128), 1)
        before = jnp.zeros((length, 128), f32) if head == 0 else lt_ref[...]
        lt_ref[...] = jnp.where(lane == head, log_total, before)
        heads_ref[:, at] = jnp.dot(probs, v_ref[:, at], preferred_element_type=f32).astype(bf16)

    def project_out():
        size = pieces[1].shape[0]
        share = width // 8
        for owner in range(8):
            part_ref[:, owner * share : (owner + 1) * share] = jnp.dot(
                heads_ref[...],
                fulls[1][owner * size : (owner + 1) * size, :],
                preferred_element_type=f32,
            ).astype(bf16)

    for i in range(parts):
        own_x(i).start()
        own_y(i).start()
        to_core(0, i).start()
    hidden = hidden_ref[...].astype(f32)
    inverse = lax.rsqrt(jnp.mean(hidden * hidden, axis=-1, keepdims=True) + epsilon)
    own_rows = pl.ds(pl.multiple_of(rank * rows, rows), rows)
    rows_ref[own_rows, :] = (hidden * inverse * gain_ref[...]).astype(bf16)
    z_start(row_z)
    own_grad = pltpu.make_async_copy(grad_ref, grads_ref.at[own_rows], l_sem.at[parts])
    own_grad.start()
    for i in range(parts):
        local(i).start()
    for copy in own_loads:
        copy.start()
    z_step(row_z, 1)
    forward(0)
    for load, store in zip(own_loads, own_stores):
        load.wait()
        store.start()
    z_step(row_z, 2)
    own_grad.wait()
    z_start(grad_z)
    for i in range(1, parts):
        forward(i)
    for bits in (6, 7, 2, 4, 3, 5, 1):
        shared_up(bits).start()
        shared_down(bits).start()
    finish(0)
    z_step(row_z, 3)
    rows_export = pltpu.make_async_copy(rows_ref, rows_out, e_sem.at[parts])
    rows_export.start()
    for i in range(1, parts):
        finish(i)
    z_step(grad_z, 1)
    for i in range(parts):
        arrived(i)
    make_heads()
    z_step(grad_z, 2)
    for head in range(heads):
        attend(head)
    project_out()
    z_step(grad_z, 3)

    rows_export.wait()
    for store in own_stores:
        store.wait()
    for i in range(parts):
        export(i).wait()
        for q in range(4):
            to_core(q, i).wait_send()
        own_x(i).wait_send()
        own_y(i).wait_send()
        x_to_y(i).wait_send()
        if halved[i]:
            y_to_x(i).wait_send()
    for bits in range(1, 8):
        for copy in (shared_up, shared_down):
            copy(bits).wait_recv()
            copy(bits).wait_send()
    z_end(row_z)
    z_end(grad_z)


def attend_pack(
    hidden, gain, grad, segments, cos, sin, shared_up, shared_down, pieces, fsdp, tp, heads, number
):
    rows, width = hidden.shape
    length = rows * tp
    parts = len(pieces)
    halved = [one.shape[0] >= 32 for one in pieces]
    bf16 = jnp.bfloat16
    f32 = jnp.float32
    dma = pltpu.SemaphoreType.DMA
    anywhere = pl.BlockSpec(memory_space=pl.ANY)
    vmem = pl.BlockSpec(memory_space=pltpu.VMEM)
    fulls = [(one.shape[0] * fsdp, one.shape[1]) for one in pieces]
    of_heads = jax.ShapeDtypeStruct((length, heads * 128), bf16)
    return pl.pallas_call(
        functools.partial(attend_kernel, tp, heads, halved),
        out_shape=[
            jax.ShapeDtypeStruct((length, width), bf16),
            jax.ShapeDtypeStruct((length, width), bf16),
            of_heads,
            of_heads,
            of_heads,
            jax.ShapeDtypeStruct((length, 128), f32),
            of_heads,
            jax.ShapeDtypeStruct((length, width), bf16),
            jax.ShapeDtypeStruct(
                (2, shared_up.shape[2] * fsdp, shared_up.shape[3]), shared_up.dtype
            ),
            jax.ShapeDtypeStruct((shared_down.shape[1], width), shared_down.dtype),
        ]
        + [jax.ShapeDtypeStruct(shape, one.dtype) for shape, one in zip(fulls, pieces)],
        in_specs=[vmem] * 7 + [anywhere] * (2 + parts),
        out_specs=[anywhere, anywhere] + [vmem] * 6 + [anywhere] * (2 + parts),
        scratch_shapes=[pltpu.VMEM((length, width), bf16)]
        + [pltpu.VMEM(shape, one.dtype) for shape, one in zip(fulls, pieces)]
        + [
            pltpu.VMEM(shared_up.shape[1:], shared_up.dtype),
            pltpu.VMEM(shared_down.shape[1:], shared_down.dtype),
            dma((parts + 1,)), dma((parts + 1,)),
            dma((2, tp)), dma((2, tp)), dma((2, tp)), dma((2, tp)),
            dma((8, parts)), dma((8, parts)), dma((2,)), dma((2, 8)), dma((2, 8)),
        ],
        compiler_params=pltpu.CompilerParams(
            collective_id=number, has_side_effects=True, vmem_limit_bytes=48 << 20
        ),
        name="attend",
    )(
        hidden, gain, grad, segments.reshape(1, -1), segments.reshape(-1, 1), cos, sin,
        shared_up, shared_down, *pieces,
    )


def dense_plan(
    hidden_in,
    out_grad,
    segment_ids,
    expert_ids,
    route_weights,
    attn_gain,
    ffn_gain,
    qkv_weight,
    qkv_bias,
    out_weight,
    shared_gate_up,
    shared_down,
    shared_gate_vec,
    expert_gate_up,
    expert_down,
):
    every = ("fsdp", "tp")
    tp_rank = lax.axis_index("tp")
    experts = lax.axis_size("fsdp")
    packs = experts
    length = segment_ids.shape[1]
    own_rows = hidden_in.shape[0]
    own_units = shared_gate_up.shape[0]
    model_width = hidden_in.shape[1]
    bf16 = jnp.bfloat16
    f32 = jnp.float32

    expert_up = expert_gate_up[0]
    expert_dn = expert_down[0]
    expert_width = expert_up.shape[2]
    shared_width = shared_gate_up.shape[2] // experts

    chosen = expert_ids[:, :, None] == jnp.arange(experts, dtype=jnp.int32)
    table = jnp.sum(jnp.where(chosen, route_weights[:, :, None], 0.0), axis=1)
    local_heads = qkv_weight.shape[2]
    head_dim = qkv_weight.shape[3]
    score_scale = head_dim ** (-0.5)
    cos_table, sin_table = rope_tables(length, head_dim)
    positions = jnp.arange(length, dtype=jnp.int32)
    segments = segment_ids[0]
    allowed = (positions[:, None] >= positions[None, :]) & (segments[:, None] == segments[None, :])
    hidden_float = hidden_in.astype(f32)
    attn_inverse = inverse_rms(hidden_float)
    bias_rows = 3 * local_heads
    bias_columns = qkv_bias.shape[2]
    bias_piece = jnp.pad(
        qkv_bias.reshape(bias_rows, bias_columns), ((0, 16 - bias_rows), (0, 128 - bias_columns))
    )
    heads_width = local_heads * head_dim
    up_pieces = shared_gate_up.reshape(own_units, 2, experts, shared_width).transpose(2, 1, 0, 3)
    cos_two = jnp.concatenate([cos_table[:, 0], cos_table[:, 0]], axis=1)
    sin_two = jnp.concatenate([-sin_table[:, 0], sin_table[:, 0]], axis=1)
    (
        normed_one,
        grad_pack,
        query,
        keys,
        values,
        log_total,
        heads_out,
        projected,
        shared_up,
        shared_dn,
        qkv_flat,
        out_pieces,
        tables,
        bias_pieces,
    ) = attend_pack(
        hidden_in,
        attn_gain[None],
        out_grad,
        segments,
        cos_two,
        sin_two,
        up_pieces,
        shared_down.reshape(experts, shared_width, -1),
        [qkv_weight.reshape(-1, 3 * heads_width), out_weight, table.T, bias_piece],
        experts,
        lax.axis_size("tp"),
        local_heads,
        4,
    )
    query, keys, values = (
        one.reshape(length, local_heads, head_dim) for one in (query, keys, values)
    )
    log_total = log_total[:, :local_heads].T[:, :, None]
    out_full = out_pieces.reshape(experts, heads_width, -1)
    out_full = out_full.transpose(1, 0, 2).reshape(heads_width, model_width)
    expert_scale = lax.dynamic_index_in_dim(
        tables.reshape(packs, experts, length), lax.axis_index("fsdp"), axis=1, keepdims=False
    ).reshape(-1)
    scales = expert_scale.reshape(packs, lax.axis_size("tp"), 2, own_rows // 2)
    scales = scales.transpose(0, 2, 1, 3).reshape(packs, 2, 1, length // 2)
    middle, normed_all, grad_all, d_all, hidden_all, token_part, d_normed_two, lines = ffn(
        projected,
        hidden_in,
        ffn_gain[None],
        shared_gate_vec[None],
        scales,
        grad_pack,
        expert_up.transpose(1, 0, 2),
        shared_up,
        expert_dn,
        shared_dn,
        experts,
        lax.axis_size("tp"),
        1,
    )
    tokens = token_part.shape[0]
    middle = middle.reshape(own_rows, model_width)
    normed_all = normed_all.reshape(tokens, model_width)
    d_all = d_all.reshape(tokens, -1)
    hidden_all = hidden_all.reshape(tokens, -1)
    d_normed_two = d_normed_two.reshape(own_rows, model_width)
    lines = lax.dynamic_slice_in_dim(lines, tp_rank * (own_rows // 2), own_rows // 2, axis=2)
    extra_sum = lines.transpose(1, 0, 2).reshape(16, own_rows)
    ffn_inverse = inverse_rms(middle)
    normed_two_own = (middle * ffn_inverse * ffn_gain).astype(bf16)
    own_start = tp_rank * own_rows
    ids_own = lax.dynamic_slice_in_dim(expert_ids, own_start, own_rows)
    picked = ids_own[:, :, None] == jnp.arange(experts, dtype=jnp.int32)
    route_grad = jnp.sum(jnp.where(picked, extra_sum[:experts].T[:, None, :], 0.0), axis=-1)
    gate_grad = extra_sum[experts]
    own_gate = jax.nn.sigmoid(jnp.sum(normed_two_own.astype(f32) * shared_gate_vec, axis=-1))
    logit_grad = gate_grad * own_gate * (1.0 - own_gate)
    d_normed_two = d_normed_two + logit_grad[:, None] * shared_gate_vec
    g_gate_vec = jnp.sum(normed_two_own.astype(f32) * logit_grad[:, None], axis=0)
    hat_two = middle * ffn_inverse
    g_ffn_gain = jnp.sum(d_normed_two * hat_two, axis=0)
    middle_grad = out_grad.astype(f32) + norm_backward(d_normed_two, hat_two, ffn_inverse, ffn_gain)
    total, d_rows, g_expert_up, g_shared_up, g_expert_down, g_shared_down = outputs(
        token_part,
        middle_grad.astype(bf16),
        normed_all,
        d_all,
        hidden_all,
        grad_all,
        experts,
        lax.axis_size("tp"),
        expert_width,
        shared_width,
        2,
    )
    hidden_out = (middle + total).astype(bf16)
    g_out = jnp.dot(d_rows.T, heads_out, preferred_element_type=f32).astype(bf16)
    d_heads = (
        jnp.dot(d_rows, out_full.T, preferred_element_type=f32)
        .astype(bf16)
        .reshape(length, local_heads, head_dim)
    )
    heads_three = heads_out.reshape(length, local_heads, head_dim)
    scores_again = masked_scores(query, keys, allowed, score_scale)
    probs_full = jnp.exp(scores_again - log_total)
    probs_again = probs_full.astype(bf16)
    d_values = jnp.einsum("hqk,qhd->khd", probs_again, d_heads, preferred_element_type=f32)
    d_probs = jnp.einsum("qhd,khd->hqk", d_heads, values, preferred_element_type=f32)
    delta = jnp.sum(d_heads.astype(f32) * heads_three.astype(f32), axis=-1)
    d_scores = (probs_full * (d_probs - delta.T[:, :, None])).astype(bf16)
    d_query = jnp.einsum("hqk,khd->qhd", d_scores, keys, preferred_element_type=f32) * score_scale
    d_keys = jnp.einsum("hqk,qhd->khd", d_scores, query, preferred_element_type=f32) * score_scale
    d_qkv = jnp.stack(
        [unrotate(d_query, cos_table, sin_table), unrotate(d_keys, cos_table, sin_table), d_values],
        axis=1,
    )
    g_bias = jnp.sum(d_qkv, axis=0).reshape(bias_rows, experts, bias_columns).transpose(1, 0, 2)
    g_bias = jnp.pad(g_bias, ((0, 0), (0, 32 - bias_rows), (0, 128 - bias_columns)))
    d_qkv_b = d_qkv.astype(bf16).reshape(length, -1)
    g_qkv = jnp.dot(normed_one.T, d_qkv_b, preferred_element_type=f32).astype(bf16)
    d_normed_one = jnp.dot(d_qkv_b, qkv_flat.T, preferred_element_type=f32).astype(bf16)
    g_qkv, g_out, g_bias, g_shared_up, g_shared_down, hidden_grad, gains = epilogue(
        [g_qkv, g_out, g_bias.reshape(-1, 128)],
        g_shared_up,
        g_shared_down,
        d_normed_one,
        hidden_in,
        middle_grad,
        attn_gain[None],
        jnp.stack([g_ffn_gain, g_gate_vec]),
        experts,
        lax.axis_size("tp"),
        3,
    )
    share = model_width // (experts * lax.axis_size("tp"))
    g_bias = g_bias.reshape(32, 128)[:bias_rows, :bias_columns]
    return (
        hidden_out,
        hidden_grad,
        route_grad,
        gains[0, :share],
        gains[1, :share],
        g_qkv.reshape(-1, 3, local_heads, head_dim),
        g_bias.reshape(qkv_bias.shape),
        g_out.reshape(out_weight.shape[::-1]).T,
        g_shared_up.transpose(1, 0, 2),
        g_shared_down,
        gains[2, :share],
        g_expert_up.transpose(1, 0, 2)[None],
        g_expert_down[None],
    )


def on_device(*arrays):
    if lax.axis_size("fsdp") == 8 and lax.axis_size("tp") == 4 and arrays[3].shape[1] >= 3:
        return dense_plan(*arrays)
    return routed_plan(*arrays)


def solution(mesh):
    placed = (
        P(("fsdp", "tp"), None),
        P(("fsdp", "tp"), None),
        P("fsdp", None),
        P("fsdp", None),
        P("fsdp", None),
        P(),
        P(),
        P("fsdp", None, "tp", None),
        P(None, "tp", "fsdp"),
        P("tp", "fsdp"),
        P("fsdp", None, "tp"),
        P("tp", "fsdp"),
        P(),
        P("fsdp", None, None, "tp"),
        P("fsdp", "tp", None),
    )
    return jax.shard_map(
        on_device,
        mesh=mesh,
        in_specs=placed,
        out_specs=(
            P(("fsdp", "tp"), None),
            P(("fsdp", "tp"), None),
            P(("fsdp", "tp"), None),
            P(("fsdp", "tp")),
            P(("fsdp", "tp")),
            P("fsdp", None, "tp", None),
            P(None, "tp", "fsdp"),
            P("tp", "fsdp"),
            P("fsdp", None, "tp"),
            P("tp", "fsdp"),
            P(("fsdp", "tp")),
            P("fsdp", None, None, "tp"),
            P("fsdp", "tp", None),
        ),
        check_vma=False,
    )
```

```python
import functools

import jax
import jax.experimental.pallas as pl
import jax.experimental.pallas.tpu as pltpu
import jax.numpy as jnp
from jax import lax
from jax.sharding import PartitionSpec as P

epsilon = 1e-06


def rope_tables(length, head_dim):
    half_dim = head_dim // 2
    ratios = jnp.arange(half_dim, dtype=jnp.float32) * (2.0 / head_dim)
    frequency = jnp.exp(-jnp.log(10000.0) * ratios)
    angles = jnp.arange(length, dtype=jnp.float32)[:, None] * frequency[None, :]
    return (jnp.cos(angles)[:, None, :], jnp.sin(angles)[:, None, :])


def rotate(tensor, cos_table, sin_table):
    half_dim = tensor.shape[-1] // 2
    front_half = tensor[..., :half_dim]
    back_half = tensor[..., half_dim:]
    return jnp.concatenate(
        [
            front_half * cos_table - back_half * sin_table,
            back_half * cos_table + front_half * sin_table,
        ],
        axis=-1,
    )


def unrotate(tensor, cos_table, sin_table):
    half_dim = tensor.shape[-1] // 2
    front_half = tensor[..., :half_dim]
    back_half = tensor[..., half_dim:]
    return jnp.concatenate(
        [
            front_half * cos_table + back_half * sin_table,
            back_half * cos_table - front_half * sin_table,
        ],
        axis=-1,
    )


def silu_parts(gate_in):
    sigmoid_value = jax.nn.sigmoid(gate_in)
    return (gate_in * sigmoid_value, sigmoid_value * (1.0 + gate_in * (1.0 - sigmoid_value)))


def slot_table(route_ids, experts, capacity):
    flat_ids = route_ids.reshape(-1)
    onehot = (flat_ids[:, None] == jnp.arange(experts, dtype=jnp.int32)[None, :]).astype(jnp.int32)
    before = jnp.cumsum(onehot, axis=0, dtype=jnp.int32) - onehot
    ranks = jnp.sum(before * onehot, axis=1, dtype=jnp.int32)
    places = flat_ids * capacity + ranks
    filler = jnp.arange(flat_ids.shape[0], dtype=jnp.int32) + 1
    slot_rows = jnp.zeros((experts * capacity,), jnp.int32).at[places].set(filler)
    return (places.reshape(route_ids.shape), slot_rows.reshape(experts, capacity))


def inverse_rms(tensor):
    return lax.rsqrt(jnp.mean(tensor * tensor, axis=-1, keepdims=True) + epsilon)


def norm_backward(d_normed, hat_rows, inverse, gain_vec):
    d_hat = d_normed * gain_vec
    return inverse * (d_hat - hat_rows * jnp.mean(d_hat * hat_rows, axis=-1, keepdims=True))


def masked_scores(query, keys, allowed, score_scale):
    raw = jnp.einsum("qhd,khd->hqk", query, keys, preferred_element_type=jnp.float32) * score_scale
    return jnp.where(allowed[None], raw, -1e30)


def spread(rows):
    return lax.all_gather(rows, "tp", axis=0, tiled=True)


def head_total(partial_rows):
    return lax.psum_scatter(
        partial_rows.astype(jnp.bfloat16), "tp", scatter_dimension=0, tiled=True
    ).astype(jnp.float32)


def to_experts(buffer):
    return lax.all_to_all(buffer, "fsdp", split_axis=0, concat_axis=0, tiled=True)


def from_experts(buffer):
    return lax.all_to_all(buffer, "fsdp", split_axis=0, concat_axis=0, tiled=True)


def routed_plan(
    hidden_in,
    out_grad,
    segment_ids,
    expert_ids,
    route_weights,
    attn_gain,
    ffn_gain,
    qkv_weight,
    qkv_bias,
    out_weight,
    shared_gate_up,
    shared_down,
    shared_gate_vec,
    expert_gate_up,
    expert_down,
):
    tp_rank = lax.axis_index("tp")
    experts = lax.axis_size("fsdp")
    length = segment_ids.shape[1]
    top_count = expert_ids.shape[1]
    capacity = 3 * length * top_count // (2 * experts)
    own_rows = hidden_in.shape[0]
    model_width = hidden_in.shape[1]
    qkv_full, bias_full, out_full, shared_full, shared_down_full = (
        lax.all_gather(qkv_weight, "fsdp", axis=0, tiled=True),
        lax.all_gather(qkv_bias.astype(jnp.bfloat16), "fsdp", axis=2, tiled=True).astype(
            qkv_bias.dtype
        ),
        lax.all_gather(out_weight, "fsdp", axis=1, tiled=True),
        lax.all_gather(shared_gate_up, "fsdp", axis=0, tiled=True),
        lax.all_gather(shared_down, "fsdp", axis=1, tiled=True),
    )
    local_heads = qkv_full.shape[2]
    head_dim = qkv_full.shape[3]
    score_scale = head_dim ** (-0.5)
    cos_table, sin_table = rope_tables(length, head_dim)
    positions = jnp.arange(length, dtype=jnp.int32)
    segments = segment_ids[0]
    allowed = (positions[:, None] >= positions[None, :]) & (segments[:, None] == segments[None, :])
    hidden_float = hidden_in.astype(jnp.float32)
    attn_inverse = inverse_rms(hidden_float)
    normed_one = spread((hidden_float * attn_inverse * attn_gain).astype(jnp.bfloat16))
    qkv_flat = qkv_full.reshape(model_width, -1)
    qkv = (
        jnp.dot(normed_one, qkv_flat, preferred_element_type=jnp.float32).reshape(
            length, 3, local_heads, head_dim
        )
        + bias_full
    )
    query = rotate(qkv[:, 0], cos_table, sin_table).astype(jnp.bfloat16)
    keys = rotate(qkv[:, 1], cos_table, sin_table).astype(jnp.bfloat16)
    values = qkv[:, 2].astype(jnp.bfloat16)
    scores = masked_scores(query, keys, allowed, score_scale)
    row_peak = jnp.max(scores, axis=-1, keepdims=True)
    log_total = row_peak + jnp.log(jnp.sum(jnp.exp(scores - row_peak), axis=-1, keepdims=True))
    probs_b = jnp.exp(scores - log_total).astype(jnp.bfloat16)
    heads_out = (
        jnp.einsum("hqk,khd->qhd", probs_b, values, preferred_element_type=jnp.float32)
        .astype(jnp.bfloat16)
        .reshape(length, -1)
    )
    middle = hidden_float + head_total(
        jnp.dot(heads_out, out_full, preferred_element_type=jnp.float32)
    )
    ffn_inverse = inverse_rms(middle)
    normed_two_own = (middle * ffn_inverse * ffn_gain).astype(jnp.bfloat16)
    normed_two = spread(normed_two_own)
    gate_prob = jax.nn.sigmoid(jnp.sum(normed_two.astype(jnp.float32) * shared_gate_vec, axis=-1))
    shared_flat = shared_full.reshape(model_width, -1)
    shared_width = shared_full.shape[2]
    shared_pre = jnp.dot(normed_two, shared_flat, preferred_element_type=jnp.float32)
    shared_act, shared_slope = silu_parts(shared_pre[:, :shared_width])
    shared_upper = shared_pre[:, shared_width:]
    shared_hidden = (shared_act * shared_upper).astype(jnp.bfloat16)
    shared_part = jnp.dot(shared_hidden, shared_down_full, preferred_element_type=jnp.float32)
    places, slot_rows = slot_table(expert_ids, experts, capacity)
    filled = slot_rows > 0
    route_index = jnp.maximum(slot_rows - 1, 0)
    source_rows = route_index // top_count
    flat_weights = route_weights.reshape(-1)
    slot_weights = jnp.where(filled, flat_weights[route_index], 0.0)
    send_rows = jnp.where(filled[:, :, None], normed_two[source_rows], jnp.zeros((), jnp.bfloat16))
    arrived = to_experts(send_rows).reshape(-1, model_width)
    expert_flat = expert_gate_up[0].reshape(model_width, -1)
    expert_width = expert_gate_up.shape[3]
    down_local = expert_down[0]
    expert_pre = jnp.dot(arrived, expert_flat, preferred_element_type=jnp.float32)
    expert_act, expert_slope = silu_parts(expert_pre[:, :expert_width])
    expert_upper = expert_pre[:, expert_width:]
    expert_hidden = (expert_act * expert_upper).astype(jnp.bfloat16)
    expert_part = jnp.dot(expert_hidden, down_local, preferred_element_type=jnp.float32).astype(
        jnp.bfloat16
    )
    returned = from_experts(expert_part.reshape(experts, capacity, model_width)).reshape(
        experts * capacity, model_width
    )
    picked = returned[places].astype(jnp.float32)
    token_term = gate_prob[:, None] * shared_part + jnp.sum(
        route_weights[:, :, None] * picked, axis=1
    )
    own_extra = 0.0
    total = (
        lax.psum_scatter(
            token_term.astype(jnp.bfloat16), "tp", scatter_dimension=0, tiled=True
        ).astype(jnp.float32)
        + own_extra
    )
    hidden_out = (middle + total).astype(jnp.bfloat16)
    grad_rows = spread(out_grad)
    grad_float = grad_rows.astype(jnp.float32)
    gate_part = jnp.sum(grad_float * shared_part, axis=-1)
    scaled_grad = (gate_prob[:, None] * grad_float).astype(jnp.bfloat16)
    shared_d_hidden = jnp.dot(scaled_grad, shared_down_full.T, preferred_element_type=jnp.float32)
    shared_d_cat = jnp.concatenate(
        [
            (shared_d_hidden * shared_upper * shared_slope).astype(jnp.bfloat16),
            (shared_d_hidden * shared_act).astype(jnp.bfloat16),
        ],
        axis=1,
    )
    g_shared_down = jnp.dot(shared_hidden.T, scaled_grad, preferred_element_type=jnp.float32)
    g_shared_gate_up = jnp.dot(
        normed_two.T, shared_d_cat, preferred_element_type=jnp.float32
    ).reshape(shared_full.shape)
    d_normed_part = jnp.dot(shared_d_cat, shared_flat.T, preferred_element_type=jnp.float32)
    expert_grad_in = (slot_weights[:, :, None] * grad_float[source_rows]).astype(jnp.bfloat16)
    arrived_grad = to_experts(expert_grad_in).reshape(-1, model_width)
    back_act, back_slope, back_upper, back_hidden = (
        expert_act,
        expert_slope,
        expert_upper,
        expert_hidden,
    )
    expert_d_hidden = jnp.dot(arrived_grad, down_local.T, preferred_element_type=jnp.float32)
    expert_d_cat = jnp.concatenate(
        [
            (expert_d_hidden * back_upper * back_slope).astype(jnp.bfloat16),
            (expert_d_hidden * back_act).astype(jnp.bfloat16),
        ],
        axis=1,
    )
    g_expert_down = jnp.dot(back_hidden.T, arrived_grad, preferred_element_type=jnp.float32)[None]
    g_expert_gate_up = jnp.dot(arrived.T, expert_d_cat, preferred_element_type=jnp.float32).reshape(
        expert_gate_up.shape
    )
    expert_d_part = jnp.dot(expert_d_cat, expert_flat.T, preferred_element_type=jnp.float32).astype(
        jnp.bfloat16
    )
    route_part = jnp.sum(grad_float[:, None, :] * picked, axis=-1)
    returned_grad = from_experts(expert_d_part.reshape(experts, capacity, model_width)).reshape(
        experts * capacity, model_width
    )
    d_normed_part = d_normed_part + jnp.sum(returned_grad[places].astype(jnp.float32), axis=1)
    d_normed_two, route_grad, gate_grad = (
        lax.psum_scatter(
            d_normed_part.astype(jnp.bfloat16), "tp", scatter_dimension=0, tiled=True
        ).astype(jnp.float32),
        lax.psum_scatter(
            route_part.astype(jnp.bfloat16), "tp", scatter_dimension=0, tiled=True
        ).astype(jnp.float32),
        lax.psum_scatter(
            gate_part.astype(jnp.bfloat16), "tp", scatter_dimension=0, tiled=True
        ).astype(jnp.float32),
    )
    own_gate = lax.dynamic_slice_in_dim(gate_prob, tp_rank * own_rows, own_rows)
    logit_grad = gate_grad * own_gate * (1.0 - own_gate)
    d_normed_two = d_normed_two + logit_grad[:, None] * shared_gate_vec
    g_gate_vec = jnp.sum(normed_two_own.astype(jnp.float32) * logit_grad[:, None], axis=0)
    hat_two = middle * ffn_inverse
    g_ffn_gain = jnp.sum(d_normed_two * hat_two, axis=0)
    middle_grad = out_grad.astype(jnp.float32) + norm_backward(
        d_normed_two, hat_two, ffn_inverse, ffn_gain
    )
    d_rows = spread(middle_grad.astype(jnp.bfloat16))
    g_out = jnp.dot(heads_out.T, d_rows, preferred_element_type=jnp.float32)
    d_heads = (
        jnp.dot(d_rows, out_full.T, preferred_element_type=jnp.float32)
        .astype(jnp.bfloat16)
        .reshape(length, local_heads, head_dim)
    )
    heads_three = heads_out.reshape(length, local_heads, head_dim)
    scores_again = masked_scores(query, keys, allowed, score_scale)
    probs_full = jnp.exp(scores_again - log_total)
    probs_again = probs_full.astype(jnp.bfloat16)
    d_values = jnp.einsum("hqk,qhd->khd", probs_again, d_heads, preferred_element_type=jnp.float32)
    d_probs = jnp.einsum("qhd,khd->hqk", d_heads, values, preferred_element_type=jnp.float32)
    delta = jnp.sum(d_heads.astype(jnp.float32) * heads_three.astype(jnp.float32), axis=-1)
    d_scores = (probs_full * (d_probs - delta.T[:, :, None])).astype(jnp.bfloat16)
    d_query = (
        jnp.einsum("hqk,khd->qhd", d_scores, keys, preferred_element_type=jnp.float32) * score_scale
    )
    d_keys = (
        jnp.einsum("hqk,qhd->khd", d_scores, query, preferred_element_type=jnp.float32)
        * score_scale
    )
    d_qkv = jnp.stack(
        [unrotate(d_query, cos_table, sin_table), unrotate(d_keys, cos_table, sin_table), d_values],
        axis=1,
    )
    g_bias = jnp.sum(d_qkv, axis=0)
    d_qkv_b = d_qkv.astype(jnp.bfloat16).reshape(length, -1)
    g_qkv = jnp.dot(normed_one.T, d_qkv_b, preferred_element_type=jnp.float32).reshape(
        qkv_full.shape
    )
    d_normed_one = head_total(jnp.dot(d_qkv_b, qkv_flat.T, preferred_element_type=jnp.float32))
    hat_one = hidden_float * attn_inverse
    g_attn_gain = jnp.sum(d_normed_one * hat_one, axis=0)
    hidden_grad = middle_grad + norm_backward(d_normed_one, hat_one, attn_inverse, attn_gain)
    g_qkv, g_bias, g_out, g_shared_gate_up, g_shared_down = (
        lax.psum_scatter(
            g_qkv.astype(jnp.bfloat16), "fsdp", scatter_dimension=0, tiled=True
        ).astype(jnp.float32),
        lax.psum_scatter(
            g_bias.astype(jnp.bfloat16), "fsdp", scatter_dimension=2, tiled=True
        ).astype(jnp.float32),
        lax.psum_scatter(
            g_out.astype(jnp.bfloat16), "fsdp", scatter_dimension=1, tiled=True
        ).astype(jnp.float32),
        lax.psum_scatter(
            g_shared_gate_up.astype(jnp.bfloat16), "fsdp", scatter_dimension=0, tiled=True
        ).astype(jnp.float32),
        lax.psum_scatter(
            g_shared_down.astype(jnp.bfloat16), "fsdp", scatter_dimension=1, tiled=True
        ).astype(jnp.float32),
    )
    g_attn_gain, g_ffn_gain, g_gate_vec = (
        lax.psum_scatter(g_attn_gain, ("fsdp", "tp"), scatter_dimension=0, tiled=True),
        lax.psum_scatter(g_ffn_gain, ("fsdp", "tp"), scatter_dimension=0, tiled=True),
        lax.psum_scatter(g_gate_vec, ("fsdp", "tp"), scatter_dimension=0, tiled=True),
    )
    return (
        hidden_out,
        hidden_grad,
        route_grad,
        g_attn_gain,
        g_ffn_gain,
        g_qkv,
        g_bias,
        g_out,
        g_shared_gate_up,
        g_shared_down,
        g_gate_vec,
        g_expert_gate_up,
        g_expert_down,
    )


MESH = pl.DeviceIdType.MESH


def flipped(index, bit):
    return index + bit - 2 * bit * ((index // bit) % 2)


def place():
    me = lax.axis_index("fsdp")
    rank = lax.axis_index("tp")
    return me, rank


def greet(me, rank, tp):
    barrier = pltpu.get_barrier_semaphore()
    for bit in (1, 2, 4):
        pl.semaphore_signal(
            barrier, inc=1, device_id=(flipped(me, bit), rank), device_id_type=MESH
        )

    @pl.when(rank > 0)
    def _():
        pl.semaphore_signal(barrier, inc=1, device_id=(me, rank - 1), device_id_type=MESH)

    @pl.when(rank < tp - 1)
    def _():
        pl.semaphore_signal(barrier, inc=1, device_id=(me, rank + 1), device_id_type=MESH)

    left = (rank + tp - 1) // tp
    right = (2 * (tp - 1) - rank) // tp
    pl.semaphore_wait(barrier, 3 + left + right)


UNIT = 640
SHARED = 384
NT = (((1,), (1,)), ((), ()))


def ffn_kernel(tp, expert_width, shared_width, *refs):
    part_ref, hidden_ref, gain_ref, vec_ref, scale_ref, grad_ref = refs[:6]
    expert_up, shared_up, expert_down, shared_down = refs[6:10]
    middle_ref, all_ref, grads_ref, d_ref, hid_ref, y_ref, dsum_ref, esum_ref = refs[10:18]
    (
        x_all, g_buf, dh_buf, d_buf, stage, acc, diag_in, last_in, z_in, both_buf, down_buf,
        eu_buf, su_buf, stage_e, acc_e, other_e, diag_e, last_e, z_in_e,
        local_sem, w_sem, dn_sem, g_sem, x_sem, d_sem, h_sem, y_sem, f_sem, f_send, f_recv,
        az_send, az_recv, ap_send, ap_recv, gp_send, gp_recv,
        c_send, c_recv, ce_send, ce_recv, p_send, p_recv, pe_send, pe_recv,
        z_send, z_recv, ze_send, ze_recv,
    ) = refs[18:]
    me, rank = place()
    greet(me, rank, tp)
    f32 = jnp.float32
    bf16 = jnp.bfloat16
    subs, rows, width = hidden_ref.shape
    tile = tp * rows
    pack_rows = subs * tile
    packs = x_all.shape[0]
    near = rank // 2
    order = [rank]
    for bit in (1, 2):
        order = order + [flipped(one, bit) for one in order]
    blocks = [3 * (1 - near), 2 - near, flipped(rank, 1), rank]
    core_of, x_of, y_of = me % 2, (me // 2) % 2, me // 4

    def pack_of(bits):
        return (
            4 * ((y_of + bits // 4) % 2)
            + 2 * ((x_of + (bits // 2) % 2) % 2)
            + (core_of + bits % 2) % 2
        )

    def add(ref, spot, one):
        ref[spot] = (ref[spot].astype(f32) + one.astype(f32)).astype(ref.dtype)

    def remote(src, dst, send, recv, bit):
        return pltpu.make_async_remote_copy(
            src_ref=src,
            dst_ref=dst,
            send_sem=send,
            recv_sem=recv,
            device_id=(flipped(me, bit), rank),
            device_id_type=MESH,
        )

    def remote_z(src, dst, send, recv, right):
        return pltpu.make_async_remote_copy(
            src_ref=src,
            dst_ref=dst,
            send_sem=send,
            recv_sem=recv,
            device_id=(me, rank + 1 if right else rank - 1),
            device_id_type=MESH,
        )

    def gather_z(block, sub, right):
        way = 0 if right else 1
        ref = x_all.at[me, block, sub]
        return remote_z(
            ref, ref, az_send.at[way, block, sub], az_recv.at[way, block, sub], right
        )

    def gather(bit, pack_bits, block, sub, slot, start=0, count=None):
        count = rows if count is None else count
        ref = x_all.at[pack_of(pack_bits), block, sub, pl.ds(start, count)]
        return remote(ref, ref, ap_send.at[slot, block, sub], ap_recv.at[slot, block, sub], bit)

    def to_core(q, block, sub):
        return gather(1, 2 * q, block, sub, q)

    def own_x(block, sub):
        return gather(2, 0, block, sub, 4)

    def own_y(block, sub):
        return gather(4, 0, block, sub, 5)

    def x_to_y(block, sub):
        return gather(4, 2, block, sub, 6, 0, rows // 2)

    def y_to_x(block, sub):
        return gather(2, 4, block, sub, 7, rows // 2, rows // 2)

    def start_plane(block, sub):
        own_x(block, sub).start()
        own_y(block, sub).start()
        to_core(0, block, sub).start()

    def start_rows(sub):
        @pl.when(rank < tp - 1)
        def _():
            gather_z(rank, sub, True).start()

        @pl.when(rank > 0)
        def _():
            gather_z(rank, sub, False).start()

        start_plane(rank, sub)

    def forward(place_in, sub):
        block = order[place_in]
        own_x(block, sub).wait_recv()
        x_to_y(block, sub).start()
        to_core(1, block, sub).start()
        own_y(block, sub).wait_recv()
        y_to_x(block, sub).start()
        to_core(2, block, sub).start()

    def finish(place_in, sub):
        block = order[place_in]
        x_to_y(block, sub).wait_recv()
        y_to_x(block, sub).wait_recv()
        to_core(3, block, sub).start()

    def z_step(step, sub):
        @pl.when(rank >= step)
        def _():
            block = rank - step
            gather_z(block, sub, True).wait_recv()

            @pl.when(rank < tp - 1)
            def _():
                gather_z(block, sub, True).start()

            start_plane(block, sub)

        @pl.when(rank + step < tp)
        def _():
            block = rank + step
            gather_z(block, sub, False).wait_recv()

            @pl.when(rank > 0)
            def _():
                gather_z(block, sub, False).start()

            start_plane(block, sub)

    def control(i):
        steps = {
            0: [(z_step, 1, 1), (finish, 1, 0)],
            1: [(forward, 3, 0)],
            2: [(forward, 0, 1), (finish, 2, 0)],
            3: [(z_step, 2, 1)],
            4: [(finish, 3, 0), (forward, 1, 1)],
            5: [(z_step, 3, 1)],
            6: [(finish, 0, 1)],
            7: [(forward, 2, 1)],
            8: [(finish, 1, 1)],
            9: [(forward, 3, 1)],
            10: [(finish, 2, 1)],
            11: [(finish, 3, 1)],
        }
        for at, todo in steps.items():

            @pl.when(i == at)
            def _():
                for act, what, sub in todo:
                    act(what, sub)

    def grad_region(pack, c, start=0, count=None):
        count = tile if count is None else count
        return grads_ref.at[pl.ds(pack * pack_rows + c * tile + start, count)]

    def grads(bit, pack_bits, c, slot, start=0, count=None):
        dst = grad_region(pack_of(pack_bits), c, start, count)
        src = grad_ref.at[pl.ds(c * tile, tile)] if pack_bits == 0 else dst
        return remote(src, dst, gp_send.at[slot, c], gp_recv.at[slot, c], bit)

    def grad_core(q, c):
        return grads(1, 2 * q, c, q)

    def grad_x(c):
        return grads(2, 0, c, 4)

    def grad_y(c):
        return grads(4, 0, c, 5)

    def grad_x_to_y(c):
        return grads(4, 2, c, 6, 0, tile // 2)

    def grad_y_to_x(c):
        return grads(2, 4, c, 7, tile // 2, tile // 2)

    def grad_forward(c):
        grad_x(c).wait_recv()
        grad_x_to_y(c).start()
        grad_core(1, c).start()
        grad_y(c).wait_recv()
        grad_y_to_x(c).start()
        grad_core(2, c).start()

    def grad_finish(c):
        grad_x_to_y(c).wait_recv()
        grad_y_to_x(c).wait_recv()
        grad_core(3, c).start()

    def core(q, s):
        return remote(stage.at[s], acc.at[q, s], c_send.at[q, s], c_recv.at[q, s], 1)

    def core_e(q):
        return remote(stage_e.at[q], other_e.at[q], ce_send.at[q], ce_recv.at[q], 1)

    low, high = pl.ds(0, tp // 2), pl.ds(tp // 2, tp // 2)

    def across(bit, src, dst, slot, s):
        return remote(src, dst, p_send.at[slot, s], p_recv.at[slot, s], bit)

    def diag_x(s):
        return across(2, acc.at[3, s, low], diag_in.at[s, 0], 0, s)

    def diag_y(s):
        return across(4, acc.at[3, s, high], diag_in.at[s, 1], 1, s)

    def direct_x(s):
        return across(2, acc.at[1, s, low], last_in.at[s, 0, low], 2, s)

    def direct_y(s):
        return across(4, acc.at[2, s, high], last_in.at[s, 1, high], 3, s)

    def summed_x(s):
        return across(2, acc.at[1, s, high], last_in.at[s, 0, high], 4, s)

    def summed_y(s):
        return across(4, acc.at[2, s, low], last_in.at[s, 1, low], 5, s)

    def diag_lines():
        return remote(acc_e.at[3], diag_e, pe_send.at[0], pe_recv.at[0], 2)

    def direct_lines():
        return remote(acc_e.at[1], last_e.at[0], pe_send.at[1], pe_recv.at[1], 2)

    def summed_lines():
        return remote(acc_e.at[2], last_e.at[1], pe_send.at[2], pe_recv.at[2], 4)

    def along_z(j, s, right):
        way = 0 if right else 1
        block = blocks[j]
        return remote_z(
            acc.at[0, s, block],
            z_in.at[way, block, s],
            z_send.at[way, block, s],
            z_recv.at[way, block, s],
            right,
        )

    def lines_z(right):
        way = 0 if right else 1
        return remote_z(
            acc_e.at[1 + way], z_in_e.at[way], ze_send.at[way], ze_recv.at[way], right
        )

    def second(s):
        diag_x(s).wait_recv()
        add(acc, (2, s, low), diag_in[s, 0])
        summed_y(s).start()
        diag_y(s).wait_recv()
        add(acc, (1, s, high), diag_in[s, 1])
        summed_x(s).start()

    def third(j, s):
        block = blocks[j]
        if j == 0:
            direct_x(s).wait_recv()
            direct_y(s).wait_recv()
            summed_x(s).wait_recv()
            summed_y(s).wait_recv()
        total = (
            acc[0, s, block].astype(f32)
            + last_in[s, 0, block].astype(f32)
            + last_in[s, 1, block].astype(f32)
        )
        if j < tp - 1:
            acc[0, s, block] = total.astype(bf16)

            @pl.when((block > rank) & (rank > 0))
            def _():
                along_z(j, s, True).wait_recv()
                add(acc, (0, s, block), z_in[0, block, s])

            @pl.when((block < rank) & (rank < tp - 1))
            def _():
                along_z(j, s, False).wait_recv()
                add(acc, (0, s, block), z_in[1, block, s])

            @pl.when(block > rank)
            def _():
                along_z(j, s, True).start()

            @pl.when(block < rank)
            def _():
                along_z(j, s, False).start()
        else:
            dsum_ref[s] = total

            @pl.when(rank > 0)
            def _():
                along_z(j, s, True).wait_recv()
                dsum_ref[s] += z_in[0, block, s].astype(f32)

            @pl.when(rank < tp - 1)
            def _():
                along_z(j, s, False).wait_recv()
                dsum_ref[s] += z_in[1, block, s].astype(f32)

    def sum_lines():
        direct_lines().wait_recv()
        summed_lines().wait_recv()
        direct_lines().wait_send()
        summed_lines().wait_send()
        own = acc_e[0] + last_e[0] + last_e[1]
        esum_ref[...] = own
        acc_e[1] = own
        acc_e[2] = own

        @pl.when(rank > 0)
        def _():
            lines_z(True).wait_recv()
            esum_ref[...] += z_in_e[0]
            acc_e[1] = own + z_in_e[0]

        @pl.when(rank < tp - 1)
        def _():
            lines_z(True).start()
            lines_z(False).wait_recv()
            esum_ref[...] += z_in_e[1]
            acc_e[2] = own + z_in_e[1]

        @pl.when(rank > 0)
        def _():
            lines_z(False).start()

    def front_load(block, s):
        return pltpu.make_async_copy(
            part_ref.at[block, s], stage.at[s, block], f_sem.at[block, s]
        )

    def front_z(j, s, right):
        way = 0 if right else 1
        block = blocks[j]
        return remote_z(
            stage.at[s, block],
            z_in.at[way, block, s],
            f_send.at[way, block, s],
            f_recv.at[way, block, s],
            right,
        )

    def front(j, s):
        block = blocks[j]
        front_load(block, s).wait()
        if j < tp - 1:

            @pl.when((block > rank) & (rank > 0))
            def _():
                front_z(j, s, True).wait_recv()
                add(stage, (s, block), z_in[0, block, s])

            @pl.when((block < rank) & (rank < tp - 1))
            def _():
                front_z(j, s, False).wait_recv()
                add(stage, (s, block), z_in[1, block, s])

            @pl.when(block > rank)
            def _():
                front_z(j, s, True).start()

            @pl.when(block < rank)
            def _():
                front_z(j, s, False).start()
        else:
            middle_ref[s] = hidden_ref[s].astype(f32) + stage[s, block].astype(f32)

            @pl.when(rank > 0)
            def _():
                front_z(j, s, True).wait_recv()
                middle_ref[s] += z_in[0, block, s].astype(f32)

            @pl.when(rank < tp - 1)
            def _():
                front_z(j, s, False).wait_recv()
                middle_ref[s] += z_in[1, block, s].astype(f32)

            middle = middle_ref[s]
            mean = jnp.mean(middle * middle, axis=-1, keepdims=True)
            normed = middle * lax.rsqrt(mean + epsilon) * gain_ref[...]
            x_all[me, rank, s] = normed.astype(bf16)
            start_rows(s)

    cut = eu_buf.shape[1]
    cuts = width // cut
    units = SHARED + shared_width

    def weight_loads(part, n, slot):
        at = pl.ds(pl.multiple_of(n * cut, cut), cut)
        return (
            pltpu.make_async_copy(expert_up.at[part, at], eu_buf.at[slot], w_sem.at[0, slot]),
            pltpu.make_async_copy(shared_up.at[part, at], su_buf.at[slot], w_sem.at[1, slot]),
        )

    def lay_out(part):
        base = part * UNIT

        def body(n, carry):
            slot = n % 2

            @pl.when(n + 1 < cuts)
            def _():
                for copy in weight_loads(part, n + 1, 1 - slot):
                    copy.start()

            for copy in weight_loads(part, n, slot):
                copy.wait()
            at = pl.ds(pl.multiple_of(n * cut, cut), cut)
            both_buf[at, base : base + UNIT] = jnp.zeros((cut, UNIT), bf16)
            both_buf[at, base : base + expert_width] = eu_buf[slot]
            both_buf[at, base + SHARED : base + units] = su_buf[slot]
            return carry

        for copy in weight_loads(part, 0, 0):
            copy.start()
        lax.fori_loop(0, cuts, body, 0)

    down_loads = (
        pltpu.make_async_copy(expert_down, down_buf.at[pl.ds(0, expert_width)], dn_sem.at[0]),
        pltpu.make_async_copy(shared_down, down_buf.at[pl.ds(SHARED, shared_width)], dn_sem.at[1]),
    )

    def hidden_grads(count, task, own=False):
        def load(n, slot):
            pack_bits, c = task(n)
            src = grad_ref.at[pl.ds(c * tile, tile)] if own else grad_region(pack_of(pack_bits), c)
            return pltpu.make_async_copy(src, g_buf.at[slot], g_sem.at[slot])

        def body(n, carry):
            slot = n % 2

            @pl.when(n + 1 < count)
            def _():
                load(n + 1, 1 - slot).start()

            load(n, slot).wait()
            pack_bits, c = task(n)
            d_hidden = lax.dot_general(
                g_buf[slot], down_buf[...], NT, preferred_element_type=f32
            ).astype(bf16)
            dh_buf[pack_of(pack_bits), pl.ds(2 * c, 2)] = d_hidden.reshape(2, subs, rows, UNIT)
            return carry

        load(0, 0).start()
        lax.fori_loop(0, count, body, 0)
        if own:
            for c in range(2):
                own_store(c).start()
            for c in range(2):
                own_store(c).wait()

    def own_store(c):
        return pltpu.make_async_copy(g_buf.at[c], grad_region(me, c), local_sem.at[c])

    def tile_of(i):
        s = i // 8
        q = order_of(s, i // 2 % 4)
        o = i % 2
        return q, o, s, pack_of(2 * q + 1 - o)

    def order_of(s, r):
        return r + s * (r // 2) * (1 - 2 * (r % 2))

    def d_store(i):
        q, o, s, pack = tile_of(i)
        return pltpu.make_async_copy(d_buf.at[i % 2], d_ref.at[pack, :, s], d_sem.at[i % 2])

    def x_store(i):
        q, o, s, pack = tile_of(i)
        return pltpu.make_async_copy(x_all.at[pack, :, s], all_ref.at[pack, :, s], x_sem.at[i % 2])

    def one_tile(i, carry):
        q, o, s, pack = tile_of(i)
        slot = i % 2

        @pl.when(o == 0)
        def _():
            for block in range(tp):
                ref = x_all.at[pack, block, s]
                remote(
                    ref, ref, ap_send.at[q, block, s], ap_recv.at[q, block, s], 1
                ).wait_recv()

        @pl.when(i >= 2)
        def _():
            d_store(i - 2).wait()
            x_store(i - 2).wait()

        x_store(i).start()
        x = x_all[pack, :, s].reshape(tile, width)
        pre = jnp.dot(x, both_buf[...], preferred_element_type=f32)
        gate, upper = pre[:, :UNIT], pre[:, UNIT:]
        lane = lax.broadcasted_iota(jnp.int32, (1, UNIT), 1)
        logit = jnp.sum(x.astype(f32) * vec_ref[...], axis=-1, keepdims=True)
        gate_prob = 1.0 / (1.0 + jnp.exp(-logit))
        own_scale = jnp.broadcast_to(scale_ref[pack, s], (128, tile)).T[:, :1]
        scale = jnp.where(lane < SHARED, own_scale, gate_prob)
        sigmoid = 1.0 / (1.0 + jnp.exp(-gate))
        act = gate * sigmoid
        slope = sigmoid * (1.0 + gate * (1.0 - sigmoid))
        hidden = act * upper
        d_hidden = dh_buf[pack, :, s].reshape(tile, UNIT).astype(f32)
        line = lax.broadcasted_iota(jnp.int32, (16, UNIT), 0)
        unit = lax.broadcasted_iota(jnp.int32, (16, UNIT), 1)
        of_expert = (line == me) & (unit < SHARED)
        of_shared = (line == 8) & (unit >= SHARED)
        pick = jnp.where(of_expert | of_shared, 1.0, 0.0).astype(bf16)
        lines = lax.dot_general(
            pick, (d_hidden * hidden).astype(bf16), NT, preferred_element_type=f32
        )
        dh_buf[pack, :, s] = (hidden * scale).astype(bf16).reshape(tp, rows, UNIT)
        d_scaled = d_hidden * scale
        d_gate = (d_scaled * upper * slope).astype(bf16)
        d_upper = (d_scaled * act).astype(bf16)
        d_buf[slot, :, :, :UNIT] = d_gate.reshape(tp, rows, UNIT)
        d_buf[slot, :, :, UNIT:] = d_upper.reshape(tp, rows, UNIT)
        control(i)
        d_both = d_buf[slot].reshape(tile, 2 * UNIT)
        d_rows = lax.dot_general(d_both, both_buf[...], NT, preferred_element_type=f32)
        d_rows = d_rows.reshape(tp, rows, width)
        d_store(i).start()

        @pl.when(o == 0)
        def _():
            @pl.when(i % 8 >= 2)
            def _():
                core(order_of(s, i // 2 % 4 - 1), s).wait_send()

            stage[s] = d_rows.astype(bf16)
            stage_e[q, s] = lines
            core(q, s).start()

            @pl.when(s == 1)
            def _():
                core_e(q).start()

        @pl.when(o == 1)
        def _():
            core(q, s).wait_recv()
            add(acc, (q, s), d_rows)
            acc_e[q, s] = lines

            @pl.when(s == 1)
            def _():
                core_e(q).wait_recv()
                acc_e[q] = acc_e[q] + other_e[q]

                @pl.when(q == 1)
                def _():
                    direct_lines().start()

                @pl.when(q == 3)
                def _():
                    diag_lines().start()

            @pl.when(q == 1)
            def _():
                direct_x(s).start()

            @pl.when(q == 2)
            def _():
                direct_y(s).start()

            @pl.when(q == 3)
            def _():
                diag_x(s).start()
                diag_y(s).start()

            @pl.when(i == 11)
            def _():
                second(0)

        return carry

    def y_store(n, slot):
        return pltpu.make_async_copy(
            g_buf.at[slot], y_ref.at[pl.ds(n * tile, tile)], y_sem.at[slot]
        )

    def outputs(first, last):
        def body(n, carry):
            slot = n % 2

            @pl.when(n >= 2)
            def _():
                y_store(n - 2, slot).wait()

            hidden = dh_buf[n // 2, pl.ds(n % 2 * 2, 2)].reshape(tile, UNIT)
            g_buf[slot] = jnp.dot(hidden, down_buf[...], preferred_element_type=f32).astype(bf16)
            y_store(n, slot).start()
            return carry

        lax.fori_loop(first, last, body, 0)

    for c in range(2):
        grad_x(c).start()
        grad_y(c).start()
        grad_core(0, c).start()
    for s in range(subs):
        for block in blocks:
            front_load(block, s).start()
    down_buf[...] = jnp.zeros_like(down_buf)
    for copy in down_loads:
        copy.start()
    front(0, 0)
    lay_out(0)
    front(1, 0)
    lay_out(1)
    front(0, 1)
    front(2, 0)
    for copy in down_loads:
        copy.wait()
    front(3, 0)
    hidden_grads(2, lambda n: (0 * n, n), own=True)
    for c in range(2):
        grad_core(0, c).wait_recv()
    hidden_grads(2, lambda n: (0 * n + 1, n))
    grad_forward(0)
    front(1, 1)
    z_step(1, 0)
    for q in (1, 2):
        grad_core(q, 0).wait_recv()
    hidden_grads(4, lambda n: (2 + n, 0 * n))
    front(2, 1)
    z_step(2, 0)
    front(3, 1)
    z_step(3, 0)
    grad_forward(1)
    for q in (1, 2):
        grad_core(q, 1).wait_recv()
    hidden_grads(4, lambda n: (2 + n, 0 * n + 1))
    for s in range(subs):
        for j in range(tp - 1):
            block = blocks[j]

            @pl.when(block > rank)
            def _():
                front_z(j, s, True).wait_send()

            @pl.when(block < rank)
            def _():
                front_z(j, s, False).wait_send()

    forward(0, 0)
    grad_finish(0)
    forward(1, 0)
    grad_finish(1)
    for c in range(2):
        grad_core(3, c).wait_recv()
    hidden_grads(4, lambda n: (6 + n // 2, n % 2))
    finish(0, 0)
    forward(2, 0)
    lax.fori_loop(0, 16, one_tile, 0)
    hidden_store = pltpu.make_async_copy(dh_buf, hid_ref, h_sem)
    hidden_store.start()
    diag_lines().wait_recv()
    acc_e[2] = acc_e[2] + diag_e[...]
    summed_lines().start()
    outputs(0, 2)
    third(0, 0)
    outputs(2, 4)
    second(1)
    third(1, 0)
    outputs(4, 6)
    third(2, 0)
    outputs(6, 8)
    third(3, 0)
    sum_lines()
    outputs(8, 16)
    for j in range(tp):
        third(j, 1)

    hidden_store.wait()
    for n in (14, 15):
        y_store(n, n % 2).wait()
        d_store(n).wait()
        x_store(n).wait()
    core(3, 0).wait_send()
    core(2, 1).wait_send()
    diag_lines().wait_send()
    for q in range(4):
        core_e(q).wait_send()
    for c in range(2):
        for q in range(4):
            grad_core(q, c).wait_send()
        for copy in (grad_x, grad_y, grad_x_to_y, grad_y_to_x):
            copy(c).wait_send()
    for s in range(subs):
        for copy in (diag_x, diag_y, direct_x, direct_y, summed_x, summed_y):
            copy(s).wait_send()
        for block in range(tp):
            for q in range(4):
                to_core(q, block, s).wait_send()
            for copy in (own_x, own_y, x_to_y, y_to_x):
                copy(block, s).wait_send()

            @pl.when((block <= rank) & (rank < tp - 1))
            def _():
                gather_z(block, s, True).wait_send()

            @pl.when((block >= rank) & (rank > 0))
            def _():
                gather_z(block, s, False).wait_send()

        for j in range(tp - 1):
            block = blocks[j]

            @pl.when(block > rank)
            def _():
                along_z(j, s, True).wait_send()

            @pl.when(block < rank)
            def _():
                along_z(j, s, False).wait_send()

    @pl.when(rank < tp - 1)
    def _():
        lines_z(True).wait_send()

    @pl.when(rank > 0)
    def _():
        lines_z(False).wait_send()


def ffn(
    part, hidden, gain, vec, scale, grad, expert_up, shared_up, expert_down, shared_down,
    fsdp, tp, collective_id,
):
    own, width = hidden.shape
    subs = 2
    rows = own // subs
    tile = tp * rows
    tokens = fsdp * tp * own
    expert_width, shared_width = expert_down.shape[0], shared_down.shape[0]
    bf16 = jnp.bfloat16
    f32 = jnp.float32
    dma = pltpu.SemaphoreType.DMA
    anywhere = pl.BlockSpec(memory_space=pl.ANY)
    vmem = pl.BlockSpec(memory_space=pltpu.VMEM)
    all_rows = (fsdp, tp, subs, rows)
    lines = (subs, 16, tile)
    return pl.pallas_call(
        functools.partial(ffn_kernel, tp, expert_width, shared_width),
        out_shape=[
            jax.ShapeDtypeStruct((subs, rows, width), f32),
            jax.ShapeDtypeStruct(all_rows + (width,), bf16),
            jax.ShapeDtypeStruct((tokens, width), bf16),
            jax.ShapeDtypeStruct(all_rows + (2 * UNIT,), bf16),
            jax.ShapeDtypeStruct(all_rows + (UNIT,), bf16),
            jax.ShapeDtypeStruct((tokens, width), bf16),
            jax.ShapeDtypeStruct((subs, rows, width), f32),
            jax.ShapeDtypeStruct(lines, f32),
        ],
        in_specs=[anywhere] + [vmem] * 4 + [anywhere] * 5,
        out_specs=[vmem] + [anywhere] * 5 + [vmem] * 2,
        scratch_shapes=[
            pltpu.VMEM(all_rows + (width,), bf16),
            pltpu.VMEM((2, tile, width), bf16),
            pltpu.VMEM(all_rows + (UNIT,), bf16),
            pltpu.VMEM((2, tp, rows, 2 * UNIT), bf16),
            pltpu.VMEM((subs, tp, rows, width), bf16),
            pltpu.VMEM((4, subs, tp, rows, width), bf16),
            pltpu.VMEM((subs, 2, tp // 2, rows, width), bf16),
            pltpu.VMEM((subs, 2, tp, rows, width), bf16),
            pltpu.VMEM((2, tp, subs, rows, width), bf16),
            pltpu.VMEM((width, 2 * UNIT), bf16),
            pltpu.VMEM((UNIT, width), bf16),
            pltpu.VMEM((2, width // 8, expert_width), bf16),
            pltpu.VMEM((2, width // 8, shared_width), bf16),
            pltpu.VMEM((4,) + lines, f32),
            pltpu.VMEM((4,) + lines, f32),
            pltpu.VMEM((4,) + lines, f32),
            pltpu.VMEM(lines, f32),
            pltpu.VMEM((2,) + lines, f32),
            pltpu.VMEM((2,) + lines, f32),
            dma((2,)), dma((2, 2)), dma((2,)), dma((2,)), dma((2,)), dma((2,)), dma, dma((2,)),
            dma((tp, subs)), dma((2, tp, subs)), dma((2, tp, subs)),
            dma((2, tp, subs)), dma((2, tp, subs)), dma((8, tp, subs)), dma((8, tp, subs)),
            dma((8, 2)), dma((8, 2)),
            dma((4, subs)), dma((4, subs)), dma((4,)), dma((4,)),
            dma((6, subs)), dma((6, subs)), dma((3,)), dma((3,)),
            dma((2, tp, subs)), dma((2, tp, subs)), dma((2,)), dma((2,)),
        ],
        compiler_params=pltpu.CompilerParams(
            collective_id=collective_id, has_side_effects=True, vmem_limit_bytes=63 << 20
        ),
        name="ffn",
    )(
        part.reshape(tp, subs, rows, width), hidden.reshape(subs, rows, width), gain, vec,
        scale, grad, expert_up, shared_up, expert_down, shared_down,
    )


TN = (((0,), (0,)), ((), ()))
SUB = 2


def outputs_kernel(tp, expert_width, shared_width, *refs):
    y_ref, own_ref, x_ref, d_ref, h_ref, g_ref = refs[:6]
    total_ref, rows_ref, ge_ref, gs_ref, de_ref, ds_ref = refs[6:12]
    (
        mine, other, diag_in, last_in, z_in, d_buf, h_buf, col_buf, ge_buf, gs_buf, de_buf, ds_buf,
        l_sem, c_send, c_recv, p_send, p_recv, z_send, z_recv, a_sem, a_send, a_recv,
        w_sem, col_sem, out_sem,
    ) = refs[12:]
    me, rank = place()
    greet(me, rank, tp)
    f32 = jnp.float32
    bf16 = jnp.bfloat16
    rows = total_ref.shape[0]
    cut = rows // SUB
    half = cut // 2
    near = rank // 2
    blocks = [3 * (1 - near), 2 - near, flipped(rank, 1), rank]
    pieces = range(tp * SUB)
    packs = [me, flipped(me, 2), flipped(me, 4), flipped(flipped(me, 2), 4)]
    low, high = pl.ds(0, half), pl.ds(half, half)

    def gather_z(block, right):
        way = 0 if right else 1
        spot = rows_ref.at[pl.ds(block * rows, rows)]
        return pltpu.make_async_remote_copy(
            src_ref=spot,
            dst_ref=spot,
            send_sem=a_send.at[way, block],
            recv_sem=a_recv.at[way, block],
            device_id=(me, rank + 1 if right else rank - 1),
            device_id_type=MESH,
        )

    def gather_step(step):
        @pl.when(rank >= step)
        def _():
            gather_z(rank - step, True).wait_recv()

            @pl.when(rank < tp - 1)
            def _():
                gather_z(rank - step, True).start()

        @pl.when(rank + step < tp)
        def _():
            gather_z(rank + step, False).wait_recv()

            @pl.when(rank > 0)
            def _():
                gather_z(rank + step, False).start()

    def spot_of(j):
        return blocks[j // SUB] * SUB + j % SUB

    def region(pack, j):
        return y_ref.at[pl.ds((pack * tp * SUB + spot_of(j)) * cut, cut)]

    def local(k, j):
        return pltpu.make_async_copy(region(packs[k], j), mine.at[k, j], l_sem.at[k, j])

    def core(k, j):
        return pltpu.make_async_remote_copy(
            src_ref=region(flipped(packs[k], 1), j),
            dst_ref=other.at[k, j],
            send_sem=c_send.at[k, j],
            recv_sem=c_recv.at[k, j],
            device_id=(flipped(me, 1), rank),
            device_id_type=MESH,
        )

    def across(bit, src, dst, slot, j):
        return pltpu.make_async_remote_copy(
            src_ref=src,
            dst_ref=dst,
            send_sem=p_send.at[slot, j],
            recv_sem=p_recv.at[slot, j],
            device_id=(flipped(me, bit), rank),
            device_id_type=MESH,
        )

    def diag_x(j):
        return across(2, mine.at[3, j, low], diag_in.at[j, 0], 0, j)

    def diag_y(j):
        return across(4, mine.at[3, j, high], diag_in.at[j, 1], 1, j)

    def direct_x(j):
        return across(2, mine.at[1, j, low], last_in.at[j, 0, low], 2, j)

    def direct_y(j):
        return across(4, mine.at[2, j, high], last_in.at[j, 1, high], 3, j)

    def summed_x(j):
        return across(2, mine.at[1, j, high], last_in.at[j, 0, high], 4, j)

    def summed_y(j):
        return across(4, mine.at[2, j, low], last_in.at[j, 1, low], 5, j)

    def along_z(j, right):
        way = 0 if right else 1
        spot = spot_of(j)
        return pltpu.make_async_remote_copy(
            src_ref=mine.at[0, j],
            dst_ref=z_in.at[way, spot],
            send_sem=z_send.at[way, spot],
            recv_sem=z_recv.at[way, spot],
            device_id=(me, rank + 1 if right else rank - 1),
            device_id_type=MESH,
        )

    def add(ref, spot, one):
        ref[spot] = (ref[spot].astype(f32) + one.astype(f32)).astype(ref.dtype)

    def first(j):
        for k in (3, 2, 1, 0):
            core(k, j).wait_recv()
            local(k, j).wait()
            add(mine, (k, j), other[k, j])
            if k == 3:
                diag_x(j).start()
                diag_y(j).start()
            if k == 2:
                direct_y(j).start()
            if k == 1:
                direct_x(j).start()

    def second(j):
        diag_x(j).wait_recv()
        add(mine, (2, j, low), diag_in[j, 0])
        summed_y(j).start()
        diag_y(j).wait_recv()
        add(mine, (1, j, high), diag_in[j, 1])
        summed_x(j).start()

    def third(j):
        block = blocks[j // SUB]
        spot = spot_of(j)
        direct_x(j).wait_recv()
        direct_y(j).wait_recv()
        summed_x(j).wait_recv()
        summed_y(j).wait_recv()
        total = mine[0, j].astype(f32) + last_in[j, 0].astype(f32) + last_in[j, 1].astype(f32)
        if j < (tp - 1) * SUB:
            mine[0, j] = total.astype(bf16)

            @pl.when((block > rank) & (rank > 0))
            def _():
                along_z(j, True).wait_recv()
                add(mine, (0, j), z_in[0, spot])

            @pl.when((block < rank) & (rank < tp - 1))
            def _():
                along_z(j, False).wait_recv()
                add(mine, (0, j), z_in[1, spot])

            @pl.when(block > rank)
            def _():
                along_z(j, True).start()

            @pl.when(block < rank)
            def _():
                along_z(j, False).start()
        else:
            own_rows = pl.ds(j % SUB * cut, cut)
            total_ref[own_rows] = total

            @pl.when(rank > 0)
            def _():
                along_z(j, True).wait_recv()
                total_ref[own_rows] += z_in[0, spot].astype(f32)

            @pl.when(rank < tp - 1)
            def _():
                along_z(j, False).wait_recv()
                total_ref[own_rows] += z_in[1, spot].astype(f32)

    span = col_buf.shape[2]
    steps = x_ref.shape[1] // span
    units = SHARED + shared_width

    def columns(n, slot, of_x):
        ref = x_ref if of_x else g_ref
        return pltpu.make_async_copy(
            ref.at[:, pl.ds(pl.multiple_of(n * span, span), span)],
            col_buf.at[slot],
            col_sem.at[slot],
        )

    def up_stores(n, slot):
        at = pl.ds(pl.multiple_of(n * span, span), span)
        return (
            pltpu.make_async_copy(ge_buf.at[slot], ge_ref.at[:, at], out_sem.at[0, slot]),
            pltpu.make_async_copy(gs_buf.at[slot], gs_ref.at[:, at], out_sem.at[1, slot]),
        )

    def down_stores(n, slot):
        at = pl.ds(pl.multiple_of(n * span, span), span)
        return (
            pltpu.make_async_copy(de_buf.at[slot], de_ref.at[:, at], out_sem.at[2, slot]),
            pltpu.make_async_copy(ds_buf.at[slot], ds_ref.at[n], out_sem.at[3, slot]),
        )

    def up_step(n, carry):
        slot = n % 2

        @pl.when(n + 1 < steps)
        def _():
            columns(n + 1, 1 - slot, True).start()

        @pl.when(n + 1 == steps)
        def _():
            columns(0, 1 - slot, False).start()

        columns(n, slot, True).wait()

        @pl.when(n >= 2)
        def _():
            for copy in up_stores(n - 2, slot):
                copy.wait()

        grads = lax.dot_general(col_buf[slot], d_buf[...], TN, preferred_element_type=f32)
        for part in range(2):
            base = part * UNIT
            ge_buf[slot, part] = grads[:, base : base + expert_width]
            gs_buf[slot, part] = grads[:, base + SHARED : base + units].astype(bf16)
        for copy in up_stores(n, slot):
            copy.start()
        return carry

    def down_step(n, carry):
        slot = n % 2

        @pl.when(n + 1 < steps)
        def _():
            columns(n + 1, 1 - slot, False).start()

        columns(n, slot, False).wait()

        @pl.when(n >= 2)
        def _():
            for copy in down_stores(n - 2, slot):
                copy.wait()

        grads = lax.dot_general(h_buf[...], col_buf[slot], TN, preferred_element_type=f32)
        de_buf[slot] = grads[:expert_width]
        ds_buf[slot] = grads[SHARED:units].astype(bf16)
        for copy in down_stores(n, slot):
            copy.start()
        return carry

    load_d = pltpu.make_async_copy(d_ref, d_buf, w_sem.at[0])
    load_h = pltpu.make_async_copy(h_ref, h_buf, w_sem.at[1])
    own = pltpu.make_async_copy(own_ref, rows_ref.at[pl.ds(rank * rows, rows)], a_sem)
    own.start()
    for j in pieces:
        for k in (3, 2, 1, 0):
            core(k, j).start()
            local(k, j).start()
    load_d.start()
    columns(0, 0, True).start()
    load_h.start()
    own.wait()

    @pl.when(rank < tp - 1)
    def _():
        gather_z(rank, True).start()

    @pl.when(rank > 0)
    def _():
        gather_z(rank, False).start()

    first(0)
    first(1)
    load_d.wait()
    load_h.wait()
    for j in pieces:
        if j < len(pieces) // 2:
            lax.fori_loop(2 * j, 2 * j + 2, up_step, 0)
        else:
            later = j - len(pieces) // 2
            lax.fori_loop(2 * later, 2 * later + 2, down_step, 0)
        second(j)
        if j + 2 < len(pieces):
            first(j + 2)
        if j in (1, 3, 5):
            gather_step((j + 1) // 2)
        if j >= 2:
            third(j - 2)
    third(len(pieces) - 2)
    third(len(pieces) - 1)

    for n in (steps - 2, steps - 1):
        for copy in up_stores(n, n % 2) + down_stores(n, n % 2):
            copy.wait()
    for j in pieces:
        for k in range(4):
            core(k, j).wait_send()
        for copy in (diag_x, diag_y, direct_x, direct_y, summed_x, summed_y):
            copy(j).wait_send()
        block = blocks[j // SUB]
        if j < (tp - 1) * SUB:

            @pl.when(block > rank)
            def _():
                along_z(j, True).wait_send()

            @pl.when(block < rank)
            def _():
                along_z(j, False).wait_send()

    for block in range(tp):

        @pl.when((block <= rank) & (rank < tp - 1))
        def _():
            gather_z(block, True).wait_send()

        @pl.when((block >= rank) & (rank > 0))
        def _():
            gather_z(block, False).wait_send()


def outputs(y, own, x, d, h, g, fsdp, tp, expert_width, shared_width, collective_id):
    rows, width = own.shape
    tokens = y.shape[0]
    span = width // fsdp
    cut = rows // SUB
    bf16 = jnp.bfloat16
    f32 = jnp.float32
    dma = pltpu.SemaphoreType.DMA
    anywhere = pl.BlockSpec(memory_space=pl.ANY)
    return pl.pallas_call(
        functools.partial(outputs_kernel, tp, expert_width, shared_width),
        out_shape=[
            jax.ShapeDtypeStruct((rows, width), f32),
            jax.ShapeDtypeStruct((rows * tp, width), bf16),
            jax.ShapeDtypeStruct((2, width, expert_width), f32),
            jax.ShapeDtypeStruct((2, width, shared_width), bf16),
            jax.ShapeDtypeStruct((expert_width, width), f32),
            jax.ShapeDtypeStruct((fsdp, shared_width, span), bf16),
        ],
        in_specs=[anywhere, pl.BlockSpec(memory_space=pltpu.VMEM)] + [anywhere] * 4,
        out_specs=[pl.BlockSpec(memory_space=pltpu.VMEM)] + [anywhere] * 5,
        scratch_shapes=[
            pltpu.VMEM((4, tp * SUB, cut, width), bf16),
            pltpu.VMEM((4, tp * SUB, cut, width), bf16),
            pltpu.VMEM((tp * SUB, 2, cut // 2, width), bf16),
            pltpu.VMEM((tp * SUB, 2, cut, width), bf16),
            pltpu.VMEM((2, tp * SUB, cut, width), bf16),
            pltpu.VMEM((tokens, 2 * UNIT), bf16),
            pltpu.VMEM((tokens, UNIT), bf16),
            pltpu.VMEM((2, tokens, span), bf16),
            pltpu.VMEM((2, 2, span, expert_width), f32),
            pltpu.VMEM((2, 2, span, shared_width), bf16),
            pltpu.VMEM((2, expert_width, span), f32),
            pltpu.VMEM((2, shared_width, span), bf16),
            dma((4, tp * SUB)), dma((4, tp * SUB)), dma((4, tp * SUB)),
            dma((6, tp * SUB)), dma((6, tp * SUB)),
            dma((2, tp * SUB)), dma((2, tp * SUB)), dma, dma((2, tp)), dma((2, tp)),
            dma((2,)), dma((2,)), dma((4, 2)),
        ],
        compiler_params=pltpu.CompilerParams(
            collective_id=collective_id, has_side_effects=True, vmem_limit_bytes=60 << 20
        ),
        name="outputs",
    )(y, own, x, d, h, g)


def backward_kernel(fsdp, tp, heads, *refs):
    parts = 3
    d_ref, ho_ref, q_ref, k_ref, v_ref, lt_ref, cos_ref, sin_ref = refs[:8]
    seg_row_ref, seg_col_ref, normed_ref, qkv_ref, out_ref = refs[8:13]
    gs_ref, ds_ref, hidden_ref, grad_ref, gain_ref, sums_ref = refs[13:19]
    refs = refs[19:]
    outs, refs = refs[:parts], refs[parts:]
    gs_out, ds_out, hidden_grad_ref, gains_ref = refs[:4]
    refs = refs[4:]
    mine, other, diag_in, last_in = (refs[i * parts : (i + 1) * parts] for i in range(4))
    (
        dh_buf, dqkv_buf, gs_in, ds_in, dn_buf, z_in, v_send, v_in, w_send, w_in,
        c_send, c_recv, p_send, p_recv, s_sem, s_send, s_recv,
        f_send, f_recv, v_ssem, v_rsem, w_ssem, w_rsem,
    ) = refs[4 * parts :]
    me, rank = place()
    f32 = jnp.float32
    bf16 = jnp.bfloat16
    rows, width = hidden_ref.shape
    near = rank // 2
    blocks = [3 * (1 - near), 2 - near, flipped(rank, 1), rank]
    packs = [me, flipped(me, 2), flipped(me, 4), flipped(flipped(me, 2), 4)]
    every = range(parts)
    chunks = outs[0].shape[0]
    sizes = [ref.shape[1] for ref in outs]
    low = [pl.ds(0, size // 2) for size in sizes]
    high = [pl.ds(size // 2, size // 2) for size in sizes]

    def plane(bits):
        peer = me
        for one in (1, 2, 4):
            if bits & one:
                peer = flipped(peer, one)
        return peer

    def line(bits):
        peer = rank
        for one in (1, 2):
            if bits & one:
                peer = flipped(peer, one)
        return peer

    barrier = pltpu.get_barrier_semaphore()
    for bits in range(1, fsdp):
        pl.semaphore_signal(
            barrier, inc=1, device_id=(plane(bits), rank), device_id_type=MESH
        )
    for bits in range(1, tp):
        pl.semaphore_signal(barrier, inc=1, device_id=(me, line(bits)), device_id_type=MESH)
    pl.semaphore_wait(barrier, fsdp - 1 + tp - 1)

    def add(ref, spot, one):
        ref[spot] = (ref[spot].astype(f32) + one.astype(f32)).astype(ref.dtype)

    core_of, x_of, y_of = me % 2, (me // 2) % 2, me // 4

    def pack_of(bits):
        return (
            4 * ((y_of + bits // 4) % 2)
            + 2 * ((x_of + (bits // 2) % 2) % 2)
            + (core_of + bits % 2) % 2
        )

    def core(k, j, i):
        return pltpu.make_async_remote_copy(
            src_ref=mine[i].at[pack_of(2 * k + 1), j],
            dst_ref=other[i].at[k, j],
            send_sem=c_send.at[k, j, i],
            recv_sem=c_recv.at[k, j, i],
            device_id=(flipped(me, 1), rank),
            device_id_type=MESH,
        )

    def across(bit, src, dst, slot, j, i):
        return pltpu.make_async_remote_copy(
            src_ref=src,
            dst_ref=dst,
            send_sem=p_send.at[slot, j, i],
            recv_sem=p_recv.at[slot, j, i],
            device_id=(flipped(me, bit), rank),
            device_id_type=MESH,
        )

    def diag_x(j, i):
        return across(2, mine[i].at[packs[3], j, low[i]], diag_in[i].at[j, 0], 0, j, i)

    def diag_y(j, i):
        return across(4, mine[i].at[packs[3], j, high[i]], diag_in[i].at[j, 1], 1, j, i)

    def direct_x(j, i):
        return across(2, mine[i].at[packs[1], j, low[i]], last_in[i].at[j, 0, low[i]], 2, j, i)

    def direct_y(j, i):
        return across(4, mine[i].at[packs[2], j, high[i]], last_in[i].at[j, 1, high[i]], 3, j, i)

    def summed_x(j, i):
        return across(2, mine[i].at[packs[1], j, high[i]], last_in[i].at[j, 0, high[i]], 4, j, i)

    def summed_y(j, i):
        return across(4, mine[i].at[packs[2], j, low[i]], last_in[i].at[j, 1, low[i]], 5, j, i)

    def send_piece(bits, i):
        k = bits // 2

        @pl.when(bits % 2 == 1)
        def _():
            for j in range(chunks):
                core(k, j, i).start()

        @pl.when(bits % 2 == 0)
        def _():
            for j in range(chunks):
                core(k, j, i).wait_recv()
                add(mine[i], (pack_of(bits), j), other[i][k, j])

            @pl.when(k == 3)
            def _():
                for j in range(chunks):
                    diag_x(j, i).start()
                    diag_y(j, i).start()

            @pl.when(k == 2)
            def _():
                for j in range(chunks):
                    direct_y(j, i).start()

            @pl.when(k == 1)
            def _():
                for j in range(chunks):
                    direct_x(j, i).start()

    def second(j):
        for i in every:
            diag_x(j, i).wait_recv()
            add(mine[i], (packs[2], j, low[i]), diag_in[i][j, 0])
            summed_y(j, i).start()
            diag_y(j, i).wait_recv()
            add(mine[i], (packs[1], j, high[i]), diag_in[i][j, 1])
            summed_x(j, i).start()

    def third(j):
        for i in every:
            direct_x(j, i).wait_recv()
            direct_y(j, i).wait_recv()
            summed_x(j, i).wait_recv()
            summed_y(j, i).wait_recv()
            outs[i][j] = (
                mine[i][me, j].astype(f32)
                + last_in[i][j, 0].astype(f32)
                + last_in[i][j, 1].astype(f32)
            )

    span = ds_ref.shape[2]

    def shared_up(bits):
        at = pl.ds(pl.multiple_of(plane(bits) * span, span), span)
        return pltpu.make_async_remote_copy(
            src_ref=gs_ref.at[:, at],
            dst_ref=gs_in.at[me],
            send_sem=s_send.at[0, bits],
            recv_sem=s_recv.at[0, bits],
            device_id=(plane(bits), rank),
            device_id_type=MESH,
        )

    def shared_down(bits):
        return pltpu.make_async_remote_copy(
            src_ref=ds_ref.at[plane(bits)],
            dst_ref=ds_in.at[me],
            send_sem=s_send.at[1, bits],
            recv_sem=s_recv.at[1, bits],
            device_id=(plane(bits), rank),
            device_id_type=MESH,
        )

    own_up = pltpu.make_async_copy(
        gs_ref.at[:, pl.ds(pl.multiple_of(me * span, span), span)], gs_in.at[me], s_sem.at[0]
    )
    own_down = pltpu.make_async_copy(ds_ref.at[me], ds_in.at[me], s_sem.at[1])

    def front_z(j, right):
        way = 0 if right else 1
        block = blocks[j]
        return pltpu.make_async_remote_copy(
            src_ref=dn_buf.at[block],
            dst_ref=z_in.at[way, block],
            send_sem=f_send.at[way, block],
            recv_sem=f_recv.at[way, block],
            device_id=(me, rank + 1 if right else rank - 1),
            device_id_type=MESH,
        )

    def front(j):
        block = blocks[j]
        if j < tp - 1:

            @pl.when((block > rank) & (rank > 0))
            def _():
                front_z(j, True).wait_recv()
                add(dn_buf, (block,), z_in[0, block])

            @pl.when((block < rank) & (rank < tp - 1))
            def _():
                front_z(j, False).wait_recv()
                add(dn_buf, (block,), z_in[1, block])

            @pl.when(block > rank)
            def _():
                front_z(j, True).start()

            @pl.when(block < rank)
            def _():
                front_z(j, False).start()
        else:
            hidden_grad_ref[...] = dn_buf[block].astype(f32)

            @pl.when(rank > 0)
            def _():
                front_z(j, True).wait_recv()
                hidden_grad_ref[...] += z_in[0, block].astype(f32)

            @pl.when(rank < tp - 1)
            def _():
                front_z(j, False).wait_recv()
                hidden_grad_ref[...] += z_in[1, block].astype(f32)

    share = width // fsdp
    part = share // tp

    def gains_plane(bits):
        return pltpu.make_async_remote_copy(
            src_ref=v_send.at[plane(bits)],
            dst_ref=v_in.at[me],
            send_sem=v_ssem.at[bits],
            recv_sem=v_rsem.at[bits],
            device_id=(plane(bits), rank),
            device_id_type=MESH,
        )

    def gains_line(bits):
        return pltpu.make_async_remote_copy(
            src_ref=w_send.at[line(bits)],
            dst_ref=w_in.at[rank],
            send_sem=w_ssem.at[bits],
            recv_sem=w_rsem.at[bits],
            device_id=(me, line(bits)),
            device_id_type=MESH,
        )

    length = d_ref.shape[0]
    cut = width // fsdp
    size = heads * 128
    scale = 128 ** (-0.5)

    def out_piece(n, carry):
        bits = fsdp - 1 - n
        pack = pack_of(bits)
        at = pl.ds(pl.multiple_of(pack * cut, cut), cut)
        piece = lax.dot_general(d_ref[:, at], ho_ref[...], TN, preferred_element_type=f32)
        mine[1][pack] = piece.astype(bf16).reshape(chunks, cut // chunks, size)
        send_piece(bits, 1)
        return carry

    def qkv_piece(n, carry):
        bits = fsdp - 1 - n
        pack = pack_of(bits)
        at = pl.ds(pl.multiple_of(pack * cut, cut), cut)
        piece = lax.dot_general(normed_ref[:, at], dqkv_buf[...], TN, preferred_element_type=f32)
        mine[0][pack] = piece.astype(bf16).reshape(chunks, cut // chunks, 3 * size)
        send_piece(bits, 0)
        return carry

    def head_grads():
        total = jnp.zeros((length, size), f32)
        for owner in range(fsdp):
            total = total + lax.dot_general(
                d_ref[:, owner * cut : (owner + 1) * cut],
                out_ref[owner * size : (owner + 1) * size, :],
                NT,
                preferred_element_type=f32,
            )
        dh_buf[...] = total.astype(bf16)

    def unrotated(columns):
        return columns * cos_ref[...] - pltpu.roll(columns, 64, 1) * sin_ref[...]

    def attend_back(head):
        at = slice(head * 128, (head + 1) * 128)
        query, keys, values = q_ref[:, at], k_ref[:, at], v_ref[:, at]
        d_head = dh_buf[:, at]
        scores = lax.dot_general(query, keys, NT, preferred_element_type=f32) * scale
        line = lax.broadcasted_iota(jnp.int32, (length, length), 0)
        column = lax.broadcasted_iota(jnp.int32, (length, length), 1)
        allowed = (line >= column) & (seg_col_ref[...] == seg_row_ref[...])
        probs = jnp.exp(jnp.where(allowed, scores, -1e30) - lt_ref[:, head : head + 1])
        d_values = lax.dot_general(probs.astype(bf16), d_head, TN, preferred_element_type=f32)
        d_probs = lax.dot_general(d_head, values, NT, preferred_element_type=f32)
        delta = jnp.sum(
            d_head.astype(f32) * ho_ref[:, at].astype(f32), axis=-1, keepdims=True
        )
        d_scores = (probs * (d_probs - delta)).astype(bf16)
        d_query = jnp.dot(d_scores, keys, preferred_element_type=f32) * scale
        d_keys = lax.dot_general(d_scores, query, TN, preferred_element_type=f32) * scale
        for which, grad in enumerate((unrotated(d_query), unrotated(d_keys), d_values)):
            base = which * size + head * 128
            dqkv_buf[:, base : base + 128] = grad.astype(bf16)
            here = which * heads + head
            mine[2][0, 0, here : here + 1] = jnp.sum(grad, axis=0, keepdims=True)

    def row_grads(half):
        at = pl.ds(pl.multiple_of(half * 2 * rows, 2 * rows), 2 * rows)
        grads = lax.dot_general(dqkv_buf[at, :], qkv_ref[...], NT, preferred_element_type=f32)
        dn_buf[pl.ds(2 * half, 2)] = grads.astype(bf16).reshape(2, rows, width)

    ends = (rank == 0) | (rank == tp - 1)
    for bits in (6, 7, 2, 4, 3, 5, 1):
        shared_up(bits).start()
        shared_down(bits).start()
    own_up.start()
    own_down.start()
    lax.fori_loop(0, fsdp, out_piece, 0)
    head_grads()
    mine[2][...] = jnp.zeros_like(mine[2])
    for head in range(heads):
        attend_back(head)
    row_grads(1 - near)

    @pl.when(ends)
    def _():
        front(0)
        front(1)

    row_grads(near)
    for owner in range(1, fsdp):
        mine[2][owner] = mine[2][0]
    lax.fori_loop(0, fsdp, qkv_piece, 0)
    for n in range(fsdp):
        send_piece(jnp.int32(fsdp - 1 - n), 2)

    @pl.when(jnp.logical_not(ends))
    def _():
        front(0)

    second(0)

    @pl.when(jnp.logical_not(ends))
    def _():
        front(1)

    second(1)
    front(2)
    front(3)
    d_normed = hidden_grad_ref[...]
    hidden = hidden_ref[...].astype(f32)
    inverse = lax.rsqrt(jnp.mean(hidden * hidden, axis=-1, keepdims=True) + epsilon)
    hat = hidden * inverse
    v_send[...] = jnp.zeros_like(v_send)
    attn_gain = jnp.sum(d_normed * hat, axis=0, keepdims=True)
    for owner in range(fsdp):
        at = slice(owner * share, (owner + 1) * share)
        v_send[owner, 0:1] = attn_gain[:, at]
        v_send[owner, 1:3] = sums_ref[:, at]
    for bits in range(1, fsdp):
        gains_plane(bits).start()
    d_hat = d_normed * gain_ref[...]
    mean = jnp.mean(d_hat * hat, axis=-1, keepdims=True)
    hidden_grad_ref[...] = grad_ref[...] + inverse * (d_hat - hat * mean)
    third(0)
    total = v_send[me]
    for bits in range(1, fsdp):
        gains_plane(bits).wait_recv()
        total = total + v_in[plane(bits)]
    w_send[...] = jnp.zeros_like(w_send)
    for owner in range(tp):
        w_send[owner, :, :part] = total[:, owner * part : (owner + 1) * part]
    for bits in range(1, tp):
        gains_line(bits).start()
    third(1)
    own_up.wait()
    own_down.wait()
    for bits in range(1, fsdp):
        shared_up(bits).wait_recv()
        shared_down(bits).wait_recv()
    units = gs_in.shape[3]
    for owner in range(fsdp):
        at = slice(owner * units, (owner + 1) * units)
        gs_out[:, :, at] = gs_in[owner].astype(f32)
        ds_out[at] = ds_in[owner].astype(f32)
    total = w_send[rank]
    for bits in range(1, tp):
        gains_line(bits).wait_recv()
        total = total + w_in[line(bits)]
    gains_ref[...] = total

    for j in range(chunks):
        for i in every:
            for k in range(4):
                core(k, j, i).wait_send()
            for copy in (diag_x, diag_y, direct_x, direct_y, summed_x, summed_y):
                copy(j, i).wait_send()
    for bits in range(1, fsdp):
        shared_up(bits).wait_send()
        shared_down(bits).wait_send()
        gains_plane(bits).wait_send()
    for bits in range(1, tp):
        gains_line(bits).wait_send()
    for j in range(tp - 1):
        block = blocks[j]

        @pl.when(block > rank)
        def _():
            front_z(j, True).wait_send()

        @pl.when(block < rank)
        def _():
            front_z(j, False).wait_send()


def backward(
    d_rows, heads_out, query, keys, values, log_total, cos, sin, segments, normed, qkv, out,
    shared_up, shared_down, hidden, grad, gain, sums, fsdp, tp, heads, number,
):
    chunks = 2
    rows, width = hidden.shape
    length = rows * tp
    units = shared_up.shape[2]
    span = shared_down.shape[2]
    size = heads * 128
    bf16 = jnp.bfloat16
    f32 = jnp.float32
    shapes = [(width // (fsdp * chunks), 3 * size, bf16), (span // chunks, size, bf16), (16, 128, f32)]
    scratch = [pltpu.VMEM((fsdp, chunks, count, w), kind) for count, w, kind in shapes]
    scratch += [pltpu.VMEM((4, chunks, count, w), kind) for count, w, kind in shapes]
    scratch += [pltpu.VMEM((chunks, 2, count // 2, w), kind) for count, w, kind in shapes]
    scratch += [pltpu.VMEM((chunks, 2, count, w), kind) for count, w, kind in shapes]
    dma = pltpu.SemaphoreType.DMA
    anywhere = pl.BlockSpec(memory_space=pl.ANY)
    vmem = pl.BlockSpec(memory_space=pltpu.VMEM)
    out_shape = [jax.ShapeDtypeStruct((chunks, count, w), f32) for count, w, _ in shapes]
    out_shape += [
        jax.ShapeDtypeStruct((2, span, fsdp * units), f32),
        jax.ShapeDtypeStruct((fsdp * units, span), f32),
        jax.ShapeDtypeStruct((rows, width), f32),
        jax.ShapeDtypeStruct((8, 128), f32),
    ]
    return pl.pallas_call(
        functools.partial(backward_kernel, fsdp, tp, heads),
        out_shape=out_shape,
        in_specs=[vmem] * 13 + [anywhere] * 2 + [vmem] * 4,
        out_specs=[vmem] * len(out_shape),
        scratch_shapes=scratch
        + [
            pltpu.VMEM((length, size), bf16),
            pltpu.VMEM((length, 3 * size), bf16),
            pltpu.VMEM((fsdp, 2, span, units), shared_up.dtype),
            pltpu.VMEM((fsdp, units, span), shared_down.dtype),
            pltpu.VMEM((tp, rows, width), bf16),
            pltpu.VMEM((2, tp, rows, width), bf16),
            pltpu.VMEM((fsdp, 8, width // fsdp), f32),
            pltpu.VMEM((fsdp, 8, width // fsdp), f32),
            pltpu.VMEM((tp, 8, 128), f32),
            pltpu.VMEM((tp, 8, 128), f32),
            dma((4, chunks, 3)), dma((4, chunks, 3)),
            dma((6, chunks, 3)), dma((6, chunks, 3)),
            dma((2,)), dma((2, fsdp)), dma((2, fsdp)),
            dma((2, tp)), dma((2, tp)),
            dma((fsdp,)), dma((fsdp,)), dma((tp,)), dma((tp,)),
        ],
        compiler_params=pltpu.CompilerParams(
            collective_id=number, has_side_effects=True, vmem_limit_bytes=61 << 20
        ),
        name="backward",
    )(
        d_rows, heads_out, query, keys, values, log_total, cos, sin, segments.reshape(1, -1),
        segments.reshape(-1, 1), normed, qkv, out, shared_up, shared_down, hidden, grad, gain, sums,
    )


def plane_peer(me, bits):
    for one in (1, 2, 4):
        if bits & one:
            me = flipped(me, one)
    return me


def attend_kernel(tp, heads, halved, *refs):
    parts = len(halved)
    hidden_ref, gain_ref, grad_ref, seg_row_ref, seg_col_ref, cos_ref, sin_ref = refs[:7]
    up_ref, down_ref = refs[7:9]
    pieces, refs = refs[9 : 9 + parts], refs[9 + parts :]
    rows_out, grads_ref, q_ref, k_ref, v_ref, lt_ref, heads_ref, part_ref = refs[:8]
    up_out, down_out = refs[8:10]
    fulls_out, refs = refs[10 : 10 + parts], refs[10 + parts :]
    rows_ref, fulls, refs = refs[0], refs[1 : 1 + parts], refs[1 + parts :]
    (
        up_buf, down_buf, l_sem, e_sem, z_send, z_recv, g_send, g_recv, p_send, p_recv, s_sem, s_send, s_recv,
    ) = refs
    me, rank = place()
    f32 = jnp.float32
    bf16 = jnp.bfloat16
    rows, width = hidden_ref.shape
    length = rows * tp

    barrier = pltpu.get_barrier_semaphore()
    for bits in range(1, 8):
        pl.semaphore_signal(
            barrier, inc=1, device_id=(plane_peer(me, bits), rank), device_id_type=MESH
        )

    @pl.when(rank > 0)
    def _():
        pl.semaphore_signal(barrier, inc=1, device_id=(me, rank - 1), device_id_type=MESH)

    @pl.when(rank < tp - 1)
    def _():
        pl.semaphore_signal(barrier, inc=1, device_id=(me, rank + 1), device_id_type=MESH)

    left = (rank + tp - 1) // tp
    right = (2 * (tp - 1) - rank) // tp
    pl.semaphore_wait(barrier, 7 + left + right)

    def along_z(ref, sends, recvs, block, to_right):
        way = 0 if to_right else 1
        spot = ref.at[pl.ds(block * rows, rows)]
        return pltpu.make_async_remote_copy(
            src_ref=spot,
            dst_ref=spot,
            send_sem=sends.at[way, block],
            recv_sem=recvs.at[way, block],
            device_id=(me, rank + 1 if to_right else rank - 1),
            device_id_type=MESH,
        )

    def row_z(block, to_right):
        return along_z(rows_ref, z_send, z_recv, block, to_right)

    def grad_z(block, to_right):
        return along_z(grads_ref, g_send, g_recv, block, to_right)

    def z_start(copy):
        @pl.when(rank < tp - 1)
        def _():
            copy(rank, True).start()

        @pl.when(rank > 0)
        def _():
            copy(rank, False).start()

    def z_step(copy, step):
        @pl.when(rank >= step)
        def _():
            copy(rank - step, True).wait_recv()

            @pl.when(rank < tp - 1)
            def _():
                copy(rank - step, True).start()

        @pl.when(rank + step < tp)
        def _():
            copy(rank + step, False).wait_recv()

            @pl.when(rank > 0)
            def _():
                copy(rank + step, False).start()

    def z_end(copy):
        for block in range(tp):

            @pl.when((block <= rank) & (rank < tp - 1))
            def _():
                copy(block, True).wait_send()

            @pl.when((block >= rank) & (rank > 0))
            def _():
                copy(block, False).wait_send()

    def region(i, owner_bits, start=0, count=None):
        size = pieces[i].shape[0]
        count = size if count is None else count
        return fulls[i].at[pl.ds(plane_peer(me, owner_bits) * size + start, count)]

    def across(i, bit, owner_bits, slot, start=0, count=None):
        spot = region(i, owner_bits, start, count)
        return pltpu.make_async_remote_copy(
            src_ref=pieces[i] if owner_bits == 0 else spot,
            dst_ref=spot,
            send_sem=p_send.at[slot, i],
            recv_sem=p_recv.at[slot, i],
            device_id=(flipped(me, bit), rank),
            device_id_type=MESH,
        )

    def to_core(q, i):
        return across(i, 1, 2 * q, q)

    def own_x(i):
        return across(i, 2, 0, 4)

    def own_y(i):
        return across(i, 4, 0, 5)

    def x_to_y(i):
        size = pieces[i].shape[0]
        return across(i, 4, 2, 6, 0, size // 2 if halved[i] else size)

    def y_to_x(i):
        size = pieces[i].shape[0]
        return across(i, 2, 4, 7, size // 2, size // 2)

    def local(i):
        return pltpu.make_async_copy(pieces[i], region(i, 0), l_sem.at[i])

    def export(i):
        return pltpu.make_async_copy(fulls[i], fulls_out[i], e_sem.at[i])

    def forward(i):
        own_x(i).wait_recv()
        x_to_y(i).start()
        to_core(1, i).start()
        own_y(i).wait_recv()
        if halved[i]:
            y_to_x(i).start()
        to_core(2, i).start()

    def finish(i):
        x_to_y(i).wait_recv()
        if halved[i]:
            y_to_x(i).wait_recv()
        to_core(3, i).start()

    def arrived(i):
        local(i).wait()
        for q in range(4):
            to_core(q, i).wait_recv()
        export(i).start()

    up_rows = up_ref.shape[2]
    span = down_ref.shape[2]

    def shared_up(bits):
        return pltpu.make_async_remote_copy(
            src_ref=up_ref.at[plane_peer(me, bits)],
            dst_ref=up_out.at[:, pl.ds(pl.multiple_of(me * up_rows, up_rows), up_rows)],
            send_sem=s_send.at[0, bits],
            recv_sem=s_recv.at[0, bits],
            device_id=(plane_peer(me, bits), rank),
            device_id_type=MESH,
        )

    def shared_down(bits):
        return pltpu.make_async_remote_copy(
            src_ref=down_ref.at[plane_peer(me, bits)],
            dst_ref=down_out.at[:, pl.ds(pl.multiple_of(me * span, span), span)],
            send_sem=s_send.at[1, bits],
            recv_sem=s_recv.at[1, bits],
            device_id=(plane_peer(me, bits), rank),
            device_id_type=MESH,
        )

    own_loads = (
        pltpu.make_async_copy(up_ref.at[me], up_buf, s_sem.at[0]),
        pltpu.make_async_copy(down_ref.at[me], down_buf, s_sem.at[1]),
    )
    own_stores = (
        pltpu.make_async_copy(
            up_buf,
            up_out.at[:, pl.ds(pl.multiple_of(me * up_rows, up_rows), up_rows)],
            s_sem.at[0],
        ),
        pltpu.make_async_copy(
            down_buf, down_out.at[:, pl.ds(pl.multiple_of(me * span, span), span)], s_sem.at[1]
        ),
    )

    def project(which):
        at = slice(which * heads * 128, (which + 1) * heads * 128)
        return jnp.dot(rows_ref[...], fulls[0][:, at], preferred_element_type=f32)

    def bias(which, head):
        line = which * heads + head
        size = pieces[3].shape[0]
        share = 128 // 8
        return jnp.concatenate(
            [fulls[3][owner * size + line : owner * size + line + 1, :share] for owner in range(8)],
            axis=1,
        )

    def rotated(columns):
        return columns * cos_ref[...] + pltpu.roll(columns, 64, 1) * sin_ref[...]

    def make_heads():
        for which, ref in ((0, q_ref), (1, k_ref), (2, v_ref)):
            all_heads = project(which)
            for head in range(heads):
                at = slice(head * 128, (head + 1) * 128)
                one = all_heads[:, at] + bias(which, head)
                if which < 2:
                    one = rotated(one)
                ref[:, at] = one.astype(bf16)

    def attend(head):
        at = slice(head * 128, (head + 1) * 128)
        scores = lax.dot_general(q_ref[:, at], k_ref[:, at], NT, preferred_element_type=f32)
        line = lax.broadcasted_iota(jnp.int32, (length, length), 0)
        column = lax.broadcasted_iota(jnp.int32, (length, length), 1)
        allowed = (line >= column) & (seg_col_ref[...] == seg_row_ref[...])
        scores = jnp.where(allowed, scores * 128 ** (-0.5), -1e30)
        peak = jnp.max(scores, axis=-1, keepdims=True)
        log_total = peak + jnp.log(jnp.sum(jnp.exp(scores - peak), axis=-1, keepdims=True))
        probs = jnp.exp(scores - log_total).astype(bf16)
        lane = lax.broadcasted_iota(jnp.int32, (length, 128), 1)
        before = jnp.zeros((length, 128), f32) if head == 0 else lt_ref[...]
        lt_ref[...] = jnp.where(lane == head, log_total, before)
        heads_ref[:, at] = jnp.dot(probs, v_ref[:, at], preferred_element_type=f32).astype(bf16)

    def project_out():
        size = pieces[1].shape[0]
        share = width // 8
        for owner in range(8):
            part_ref[:, owner * share : (owner + 1) * share] = jnp.dot(
                heads_ref[...],
                fulls[1][owner * size : (owner + 1) * size, :],
                preferred_element_type=f32,
            ).astype(bf16)

    for i in range(parts):
        own_x(i).start()
        own_y(i).start()
        to_core(0, i).start()
    hidden = hidden_ref[...].astype(f32)
    inverse = lax.rsqrt(jnp.mean(hidden * hidden, axis=-1, keepdims=True) + epsilon)
    own_rows = pl.ds(pl.multiple_of(rank * rows, rows), rows)
    rows_ref[own_rows, :] = (hidden * inverse * gain_ref[...]).astype(bf16)
    z_start(row_z)
    own_grad = pltpu.make_async_copy(grad_ref, grads_ref.at[own_rows], l_sem.at[parts])
    own_grad.start()
    for i in range(parts):
        local(i).start()
    for copy in own_loads:
        copy.start()
    z_step(row_z, 1)
    forward(0)
    for load, store in zip(own_loads, own_stores):
        load.wait()
        store.start()
    z_step(row_z, 2)
    own_grad.wait()
    z_start(grad_z)
    for i in range(1, parts):
        forward(i)
    for bits in (6, 7, 2, 4, 3, 5, 1):
        shared_up(bits).start()
        shared_down(bits).start()
    finish(0)
    z_step(row_z, 3)
    rows_export = pltpu.make_async_copy(rows_ref, rows_out, e_sem.at[parts])
    rows_export.start()
    for i in range(1, parts):
        finish(i)
    z_step(grad_z, 1)
    for i in range(parts):
        arrived(i)
    make_heads()
    z_step(grad_z, 2)
    for head in range(heads):
        attend(head)
    project_out()
    z_step(grad_z, 3)

    rows_export.wait()
    for store in own_stores:
        store.wait()
    for i in range(parts):
        export(i).wait()
        for q in range(4):
            to_core(q, i).wait_send()
        own_x(i).wait_send()
        own_y(i).wait_send()
        x_to_y(i).wait_send()
        if halved[i]:
            y_to_x(i).wait_send()
    for bits in range(1, 8):
        for copy in (shared_up, shared_down):
            copy(bits).wait_recv()
            copy(bits).wait_send()
    z_end(row_z)
    z_end(grad_z)


def attend_pack(
    hidden, gain, grad, segments, cos, sin, shared_up, shared_down, pieces, fsdp, tp, heads, number
):
    rows, width = hidden.shape
    length = rows * tp
    parts = len(pieces)
    halved = [one.shape[0] >= 32 for one in pieces]
    bf16 = jnp.bfloat16
    f32 = jnp.float32
    dma = pltpu.SemaphoreType.DMA
    anywhere = pl.BlockSpec(memory_space=pl.ANY)
    vmem = pl.BlockSpec(memory_space=pltpu.VMEM)
    fulls = [(one.shape[0] * fsdp, one.shape[1]) for one in pieces]
    of_heads = jax.ShapeDtypeStruct((length, heads * 128), bf16)
    return pl.pallas_call(
        functools.partial(attend_kernel, tp, heads, halved),
        out_shape=[
            jax.ShapeDtypeStruct((length, width), bf16),
            jax.ShapeDtypeStruct((length, width), bf16),
            of_heads,
            of_heads,
            of_heads,
            jax.ShapeDtypeStruct((length, 128), f32),
            of_heads,
            jax.ShapeDtypeStruct((length, width), bf16),
            jax.ShapeDtypeStruct(
                (2, shared_up.shape[2] * fsdp, shared_up.shape[3]), shared_up.dtype
            ),
            jax.ShapeDtypeStruct((shared_down.shape[1], width), shared_down.dtype),
        ]
        + [jax.ShapeDtypeStruct(shape, one.dtype) for shape, one in zip(fulls, pieces)],
        in_specs=[vmem] * 7 + [anywhere] * (2 + parts),
        out_specs=[anywhere, anywhere] + [vmem] * 6 + [anywhere] * (2 + parts),
        scratch_shapes=[pltpu.VMEM((length, width), bf16)]
        + [pltpu.VMEM(shape, one.dtype) for shape, one in zip(fulls, pieces)]
        + [
            pltpu.VMEM(shared_up.shape[1:], shared_up.dtype),
            pltpu.VMEM(shared_down.shape[1:], shared_down.dtype),
            dma((parts + 1,)), dma((parts + 1,)),
            dma((2, tp)), dma((2, tp)), dma((2, tp)), dma((2, tp)),
            dma((8, parts)), dma((8, parts)), dma((2,)), dma((2, 8)), dma((2, 8)),
        ],
        compiler_params=pltpu.CompilerParams(
            collective_id=number, has_side_effects=True, vmem_limit_bytes=48 << 20
        ),
        name="attend",
    )(
        hidden, gain, grad, segments.reshape(1, -1), segments.reshape(-1, 1), cos, sin,
        shared_up, shared_down, *pieces,
    )


def dense_plan(
    hidden_in,
    out_grad,
    segment_ids,
    expert_ids,
    route_weights,
    attn_gain,
    ffn_gain,
    qkv_weight,
    qkv_bias,
    out_weight,
    shared_gate_up,
    shared_down,
    shared_gate_vec,
    expert_gate_up,
    expert_down,
):
    every = ("fsdp", "tp")
    tp_rank = lax.axis_index("tp")
    experts = lax.axis_size("fsdp")
    packs = experts
    length = segment_ids.shape[1]
    own_rows = hidden_in.shape[0]
    own_units = shared_gate_up.shape[0]
    model_width = hidden_in.shape[1]
    bf16 = jnp.bfloat16
    f32 = jnp.float32

    expert_up = expert_gate_up[0]
    expert_dn = expert_down[0]
    expert_width = expert_up.shape[2]
    shared_width = shared_gate_up.shape[2] // experts

    chosen = expert_ids[:, :, None] == jnp.arange(experts, dtype=jnp.int32)
    table = jnp.sum(jnp.where(chosen, route_weights[:, :, None], 0.0), axis=1)
    local_heads = qkv_weight.shape[2]
    head_dim = qkv_weight.shape[3]
    cos_table, sin_table = rope_tables(length, head_dim)
    segments = segment_ids[0]
    hidden_float = hidden_in.astype(f32)
    attn_inverse = inverse_rms(hidden_float)
    bias_rows = 3 * local_heads
    bias_columns = qkv_bias.shape[2]
    bias_piece = jnp.pad(
        qkv_bias.reshape(bias_rows, bias_columns), ((0, 16 - bias_rows), (0, 128 - bias_columns))
    )
    heads_width = local_heads * head_dim
    up_pieces = shared_gate_up.reshape(own_units, 2, experts, shared_width).transpose(2, 1, 0, 3)
    cos_two = jnp.concatenate([cos_table[:, 0], cos_table[:, 0]], axis=1)
    sin_two = jnp.concatenate([-sin_table[:, 0], sin_table[:, 0]], axis=1)
    (
        normed_one,
        grad_pack,
        query,
        keys,
        values,
        log_total,
        heads_out,
        projected,
        shared_up,
        shared_dn,
        qkv_flat,
        out_pieces,
        tables,
        bias_pieces,
    ) = attend_pack(
        hidden_in,
        attn_gain[None],
        out_grad,
        segments,
        cos_two,
        sin_two,
        up_pieces,
        shared_down.reshape(experts, shared_width, -1),
        [qkv_weight.reshape(-1, 3 * heads_width), out_weight, table.T, bias_piece],
        experts,
        lax.axis_size("tp"),
        local_heads,
        4,
    )
    expert_scale = lax.dynamic_index_in_dim(
        tables.reshape(packs, experts, length), lax.axis_index("fsdp"), axis=1, keepdims=False
    ).reshape(-1)
    scales = expert_scale.reshape(packs, lax.axis_size("tp"), 2, own_rows // 2)
    scales = scales.transpose(0, 2, 1, 3).reshape(packs, 2, 1, length // 2)
    middle, normed_all, grad_all, d_all, hidden_all, token_part, d_normed_two, lines = ffn(
        projected,
        hidden_in,
        ffn_gain[None],
        shared_gate_vec[None],
        scales,
        grad_pack,
        expert_up.transpose(1, 0, 2),
        shared_up,
        expert_dn,
        shared_dn,
        experts,
        lax.axis_size("tp"),
        1,
    )
    tokens = token_part.shape[0]
    middle = middle.reshape(own_rows, model_width)
    normed_all = normed_all.reshape(tokens, model_width)
    d_all = d_all.reshape(tokens, -1)
    hidden_all = hidden_all.reshape(tokens, -1)
    d_normed_two = d_normed_two.reshape(own_rows, model_width)
    lines = lax.dynamic_slice_in_dim(lines, tp_rank * (own_rows // 2), own_rows // 2, axis=2)
    extra_sum = lines.transpose(1, 0, 2).reshape(16, own_rows)
    ffn_inverse = inverse_rms(middle)
    normed_two_own = (middle * ffn_inverse * ffn_gain).astype(bf16)
    own_start = tp_rank * own_rows
    ids_own = lax.dynamic_slice_in_dim(expert_ids, own_start, own_rows)
    picked = ids_own[:, :, None] == jnp.arange(experts, dtype=jnp.int32)
    route_grad = jnp.sum(jnp.where(picked, extra_sum[:experts].T[:, None, :], 0.0), axis=-1)
    gate_grad = extra_sum[experts]
    own_gate = jax.nn.sigmoid(jnp.sum(normed_two_own.astype(f32) * shared_gate_vec, axis=-1))
    logit_grad = gate_grad * own_gate * (1.0 - own_gate)
    d_normed_two = d_normed_two + logit_grad[:, None] * shared_gate_vec
    g_gate_vec = jnp.sum(normed_two_own.astype(f32) * logit_grad[:, None], axis=0)
    hat_two = middle * ffn_inverse
    g_ffn_gain = jnp.sum(d_normed_two * hat_two, axis=0)
    middle_grad = out_grad.astype(f32) + norm_backward(d_normed_two, hat_two, ffn_inverse, ffn_gain)
    total, d_rows, g_expert_up, g_shared_up, g_expert_down, g_shared_down = outputs(
        token_part,
        middle_grad.astype(bf16),
        normed_all,
        d_all,
        hidden_all,
        grad_all,
        experts,
        lax.axis_size("tp"),
        expert_width,
        shared_width,
        2,
    )
    hidden_out = (middle + total).astype(bf16)
    g_qkv, g_out, g_bias, g_shared_up, g_shared_down, hidden_grad, gains = backward(
        d_rows,
        heads_out,
        query,
        keys,
        values,
        log_total,
        cos_two,
        sin_two,
        segments,
        normed_one,
        qkv_flat,
        out_pieces,
        g_shared_up,
        g_shared_down,
        hidden_in,
        middle_grad,
        attn_gain[None],
        jnp.stack([g_ffn_gain, g_gate_vec]),
        experts,
        lax.axis_size("tp"),
        local_heads,
        3,
    )
    share = model_width // (experts * lax.axis_size("tp"))
    g_bias = lax.dynamic_slice_in_dim(
        g_bias.reshape(32, 128)[:bias_rows], lax.axis_index("fsdp") * bias_columns, bias_columns, 1
    )
    return (
        hidden_out,
        hidden_grad,
        route_grad,
        gains[0, :share],
        gains[1, :share],
        g_qkv.reshape(-1, 3, local_heads, head_dim),
        g_bias.reshape(qkv_bias.shape),
        g_out.reshape(out_weight.shape[::-1]).T,
        g_shared_up.transpose(1, 0, 2),
        g_shared_down,
        gains[2, :share],
        g_expert_up.transpose(1, 0, 2)[None],
        g_expert_down[None],
    )


def on_device(*arrays):
    if lax.axis_size("fsdp") == 8 and lax.axis_size("tp") == 4 and arrays[3].shape[1] >= 3:
        return dense_plan(*arrays)
    return routed_plan(*arrays)


def solution(mesh):
    placed = (
        P(("fsdp", "tp"), None),
        P(("fsdp", "tp"), None),
        P("fsdp", None),
        P("fsdp", None),
        P("fsdp", None),
        P(),
        P(),
        P("fsdp", None, "tp", None),
        P(None, "tp", "fsdp"),
        P("tp", "fsdp"),
        P("fsdp", None, "tp"),
        P("tp", "fsdp"),
        P(),
        P("fsdp", None, None, "tp"),
        P("fsdp", "tp", None),
    )
    return jax.shard_map(
        on_device,
        mesh=mesh,
        in_specs=placed,
        out_specs=(
            P(("fsdp", "tp"), None),
            P(("fsdp", "tp"), None),
            P(("fsdp", "tp"), None),
            P(("fsdp", "tp")),
            P(("fsdp", "tp")),
            P("fsdp", None, "tp", None),
            P(None, "tp", "fsdp"),
            P("tp", "fsdp"),
            P("fsdp", None, "tp"),
            P("tp", "fsdp"),
            P(("fsdp", "tp")),
            P("fsdp", None, None, "tp"),
            P("fsdp", "tp", None),
        ),
        check_vma=False,
    )
```

```python
import functools

import jax
import jax.experimental.pallas as pl
import jax.experimental.pallas.tpu as pltpu
import jax.numpy as jnp
from jax import lax
from jax.sharding import PartitionSpec as P

epsilon = 1e-06


def rope_tables(length, head_dim):
    half_dim = head_dim // 2
    ratios = jnp.arange(half_dim, dtype=jnp.float32) * (2.0 / head_dim)
    frequency = jnp.exp(-jnp.log(10000.0) * ratios)
    angles = jnp.arange(length, dtype=jnp.float32)[:, None] * frequency[None, :]
    return (jnp.cos(angles)[:, None, :], jnp.sin(angles)[:, None, :])


def rotate(tensor, cos_table, sin_table):
    half_dim = tensor.shape[-1] // 2
    front_half = tensor[..., :half_dim]
    back_half = tensor[..., half_dim:]
    return jnp.concatenate(
        [
            front_half * cos_table - back_half * sin_table,
            back_half * cos_table + front_half * sin_table,
        ],
        axis=-1,
    )


def unrotate(tensor, cos_table, sin_table):
    half_dim = tensor.shape[-1] // 2
    front_half = tensor[..., :half_dim]
    back_half = tensor[..., half_dim:]
    return jnp.concatenate(
        [
            front_half * cos_table + back_half * sin_table,
            back_half * cos_table - front_half * sin_table,
        ],
        axis=-1,
    )


def silu_parts(gate_in):
    sigmoid_value = jax.nn.sigmoid(gate_in)
    return (gate_in * sigmoid_value, sigmoid_value * (1.0 + gate_in * (1.0 - sigmoid_value)))


def slot_table(route_ids, experts, capacity):
    flat_ids = route_ids.reshape(-1)
    onehot = (flat_ids[:, None] == jnp.arange(experts, dtype=jnp.int32)[None, :]).astype(jnp.int32)
    before = jnp.cumsum(onehot, axis=0, dtype=jnp.int32) - onehot
    ranks = jnp.sum(before * onehot, axis=1, dtype=jnp.int32)
    places = flat_ids * capacity + ranks
    filler = jnp.arange(flat_ids.shape[0], dtype=jnp.int32) + 1
    slot_rows = jnp.zeros((experts * capacity,), jnp.int32).at[places].set(filler)
    return (places.reshape(route_ids.shape), slot_rows.reshape(experts, capacity))


def inverse_rms(tensor):
    return lax.rsqrt(jnp.mean(tensor * tensor, axis=-1, keepdims=True) + epsilon)


def norm_backward(d_normed, hat_rows, inverse, gain_vec):
    d_hat = d_normed * gain_vec
    return inverse * (d_hat - hat_rows * jnp.mean(d_hat * hat_rows, axis=-1, keepdims=True))


def masked_scores(query, keys, allowed, score_scale):
    raw = jnp.einsum("qhd,khd->hqk", query, keys, preferred_element_type=jnp.float32) * score_scale
    return jnp.where(allowed[None], raw, -1e30)


def spread(rows):
    return lax.all_gather(rows, "tp", axis=0, tiled=True)


def head_total(partial_rows):
    return lax.psum_scatter(
        partial_rows.astype(jnp.bfloat16), "tp", scatter_dimension=0, tiled=True
    ).astype(jnp.float32)


def to_experts(buffer):
    return lax.all_to_all(buffer, "fsdp", split_axis=0, concat_axis=0, tiled=True)


def from_experts(buffer):
    return lax.all_to_all(buffer, "fsdp", split_axis=0, concat_axis=0, tiled=True)


def routed_plan(
    hidden_in,
    out_grad,
    segment_ids,
    expert_ids,
    route_weights,
    attn_gain,
    ffn_gain,
    qkv_weight,
    qkv_bias,
    out_weight,
    shared_gate_up,
    shared_down,
    shared_gate_vec,
    expert_gate_up,
    expert_down,
):
    tp_rank = lax.axis_index("tp")
    experts = lax.axis_size("fsdp")
    length = segment_ids.shape[1]
    top_count = expert_ids.shape[1]
    capacity = 3 * length * top_count // (2 * experts)
    own_rows = hidden_in.shape[0]
    model_width = hidden_in.shape[1]
    qkv_full, bias_full, out_full, shared_full, shared_down_full = (
        lax.all_gather(qkv_weight, "fsdp", axis=0, tiled=True),
        lax.all_gather(qkv_bias.astype(jnp.bfloat16), "fsdp", axis=2, tiled=True).astype(
            qkv_bias.dtype
        ),
        lax.all_gather(out_weight, "fsdp", axis=1, tiled=True),
        lax.all_gather(shared_gate_up, "fsdp", axis=0, tiled=True),
        lax.all_gather(shared_down, "fsdp", axis=1, tiled=True),
    )
    local_heads = qkv_full.shape[2]
    head_dim = qkv_full.shape[3]
    score_scale = head_dim ** (-0.5)
    cos_table, sin_table = rope_tables(length, head_dim)
    positions = jnp.arange(length, dtype=jnp.int32)
    segments = segment_ids[0]
    allowed = (positions[:, None] >= positions[None, :]) & (segments[:, None] == segments[None, :])
    hidden_float = hidden_in.astype(jnp.float32)
    attn_inverse = inverse_rms(hidden_float)
    normed_one = spread((hidden_float * attn_inverse * attn_gain).astype(jnp.bfloat16))
    qkv_flat = qkv_full.reshape(model_width, -1)
    qkv = (
        jnp.dot(normed_one, qkv_flat, preferred_element_type=jnp.float32).reshape(
            length, 3, local_heads, head_dim
        )
        + bias_full
    )
    query = rotate(qkv[:, 0], cos_table, sin_table).astype(jnp.bfloat16)
    keys = rotate(qkv[:, 1], cos_table, sin_table).astype(jnp.bfloat16)
    values = qkv[:, 2].astype(jnp.bfloat16)
    scores = masked_scores(query, keys, allowed, score_scale)
    row_peak = jnp.max(scores, axis=-1, keepdims=True)
    log_total = row_peak + jnp.log(jnp.sum(jnp.exp(scores - row_peak), axis=-1, keepdims=True))
    probs_b = jnp.exp(scores - log_total).astype(jnp.bfloat16)
    heads_out = (
        jnp.einsum("hqk,khd->qhd", probs_b, values, preferred_element_type=jnp.float32)
        .astype(jnp.bfloat16)
        .reshape(length, -1)
    )
    middle = hidden_float + head_total(
        jnp.dot(heads_out, out_full, preferred_element_type=jnp.float32)
    )
    ffn_inverse = inverse_rms(middle)
    normed_two_own = (middle * ffn_inverse * ffn_gain).astype(jnp.bfloat16)
    normed_two = spread(normed_two_own)
    gate_prob = jax.nn.sigmoid(jnp.sum(normed_two.astype(jnp.float32) * shared_gate_vec, axis=-1))
    shared_flat = shared_full.reshape(model_width, -1)
    shared_width = shared_full.shape[2]
    shared_pre = jnp.dot(normed_two, shared_flat, preferred_element_type=jnp.float32)
    shared_act, shared_slope = silu_parts(shared_pre[:, :shared_width])
    shared_upper = shared_pre[:, shared_width:]
    shared_hidden = (shared_act * shared_upper).astype(jnp.bfloat16)
    shared_part = jnp.dot(shared_hidden, shared_down_full, preferred_element_type=jnp.float32)
    places, slot_rows = slot_table(expert_ids, experts, capacity)
    filled = slot_rows > 0
    route_index = jnp.maximum(slot_rows - 1, 0)
    source_rows = route_index // top_count
    flat_weights = route_weights.reshape(-1)
    slot_weights = jnp.where(filled, flat_weights[route_index], 0.0)
    send_rows = jnp.where(filled[:, :, None], normed_two[source_rows], jnp.zeros((), jnp.bfloat16))
    arrived = to_experts(send_rows).reshape(-1, model_width)
    expert_flat = expert_gate_up[0].reshape(model_width, -1)
    expert_width = expert_gate_up.shape[3]
    down_local = expert_down[0]
    expert_pre = jnp.dot(arrived, expert_flat, preferred_element_type=jnp.float32)
    expert_act, expert_slope = silu_parts(expert_pre[:, :expert_width])
    expert_upper = expert_pre[:, expert_width:]
    expert_hidden = (expert_act * expert_upper).astype(jnp.bfloat16)
    expert_part = jnp.dot(expert_hidden, down_local, preferred_element_type=jnp.float32).astype(
        jnp.bfloat16
    )
    returned = from_experts(expert_part.reshape(experts, capacity, model_width)).reshape(
        experts * capacity, model_width
    )
    picked = returned[places].astype(jnp.float32)
    token_term = gate_prob[:, None] * shared_part + jnp.sum(
        route_weights[:, :, None] * picked, axis=1
    )
    own_extra = 0.0
    total = (
        lax.psum_scatter(
            token_term.astype(jnp.bfloat16), "tp", scatter_dimension=0, tiled=True
        ).astype(jnp.float32)
        + own_extra
    )
    hidden_out = (middle + total).astype(jnp.bfloat16)
    grad_rows = spread(out_grad)
    grad_float = grad_rows.astype(jnp.float32)
    gate_part = jnp.sum(grad_float * shared_part, axis=-1)
    scaled_grad = (gate_prob[:, None] * grad_float).astype(jnp.bfloat16)
    shared_d_hidden = jnp.dot(scaled_grad, shared_down_full.T, preferred_element_type=jnp.float32)
    shared_d_cat = jnp.concatenate(
        [
            (shared_d_hidden * shared_upper * shared_slope).astype(jnp.bfloat16),
            (shared_d_hidden * shared_act).astype(jnp.bfloat16),
        ],
        axis=1,
    )
    g_shared_down = jnp.dot(shared_hidden.T, scaled_grad, preferred_element_type=jnp.float32)
    g_shared_gate_up = jnp.dot(
        normed_two.T, shared_d_cat, preferred_element_type=jnp.float32
    ).reshape(shared_full.shape)
    d_normed_part = jnp.dot(shared_d_cat, shared_flat.T, preferred_element_type=jnp.float32)
    expert_grad_in = (slot_weights[:, :, None] * grad_float[source_rows]).astype(jnp.bfloat16)
    arrived_grad = to_experts(expert_grad_in).reshape(-1, model_width)
    back_act, back_slope, back_upper, back_hidden = (
        expert_act,
        expert_slope,
        expert_upper,
        expert_hidden,
    )
    expert_d_hidden = jnp.dot(arrived_grad, down_local.T, preferred_element_type=jnp.float32)
    expert_d_cat = jnp.concatenate(
        [
            (expert_d_hidden * back_upper * back_slope).astype(jnp.bfloat16),
            (expert_d_hidden * back_act).astype(jnp.bfloat16),
        ],
        axis=1,
    )
    g_expert_down = jnp.dot(back_hidden.T, arrived_grad, preferred_element_type=jnp.float32)[None]
    g_expert_gate_up = jnp.dot(arrived.T, expert_d_cat, preferred_element_type=jnp.float32).reshape(
        expert_gate_up.shape
    )
    expert_d_part = jnp.dot(expert_d_cat, expert_flat.T, preferred_element_type=jnp.float32).astype(
        jnp.bfloat16
    )
    route_part = jnp.sum(grad_float[:, None, :] * picked, axis=-1)
    returned_grad = from_experts(expert_d_part.reshape(experts, capacity, model_width)).reshape(
        experts * capacity, model_width
    )
    d_normed_part = d_normed_part + jnp.sum(returned_grad[places].astype(jnp.float32), axis=1)
    d_normed_two, route_grad, gate_grad = (
        lax.psum_scatter(
            d_normed_part.astype(jnp.bfloat16), "tp", scatter_dimension=0, tiled=True
        ).astype(jnp.float32),
        lax.psum_scatter(
            route_part.astype(jnp.bfloat16), "tp", scatter_dimension=0, tiled=True
        ).astype(jnp.float32),
        lax.psum_scatter(
            gate_part.astype(jnp.bfloat16), "tp", scatter_dimension=0, tiled=True
        ).astype(jnp.float32),
    )
    own_gate = lax.dynamic_slice_in_dim(gate_prob, tp_rank * own_rows, own_rows)
    logit_grad = gate_grad * own_gate * (1.0 - own_gate)
    d_normed_two = d_normed_two + logit_grad[:, None] * shared_gate_vec
    g_gate_vec = jnp.sum(normed_two_own.astype(jnp.float32) * logit_grad[:, None], axis=0)
    hat_two = middle * ffn_inverse
    g_ffn_gain = jnp.sum(d_normed_two * hat_two, axis=0)
    middle_grad = out_grad.astype(jnp.float32) + norm_backward(
        d_normed_two, hat_two, ffn_inverse, ffn_gain
    )
    d_rows = spread(middle_grad.astype(jnp.bfloat16))
    g_out = jnp.dot(heads_out.T, d_rows, preferred_element_type=jnp.float32)
    d_heads = (
        jnp.dot(d_rows, out_full.T, preferred_element_type=jnp.float32)
        .astype(jnp.bfloat16)
        .reshape(length, local_heads, head_dim)
    )
    heads_three = heads_out.reshape(length, local_heads, head_dim)
    scores_again = masked_scores(query, keys, allowed, score_scale)
    probs_full = jnp.exp(scores_again - log_total)
    probs_again = probs_full.astype(jnp.bfloat16)
    d_values = jnp.einsum("hqk,qhd->khd", probs_again, d_heads, preferred_element_type=jnp.float32)
    d_probs = jnp.einsum("qhd,khd->hqk", d_heads, values, preferred_element_type=jnp.float32)
    delta = jnp.sum(d_heads.astype(jnp.float32) * heads_three.astype(jnp.float32), axis=-1)
    d_scores = (probs_full * (d_probs - delta.T[:, :, None])).astype(jnp.bfloat16)
    d_query = (
        jnp.einsum("hqk,khd->qhd", d_scores, keys, preferred_element_type=jnp.float32) * score_scale
    )
    d_keys = (
        jnp.einsum("hqk,qhd->khd", d_scores, query, preferred_element_type=jnp.float32)
        * score_scale
    )
    d_qkv = jnp.stack(
        [unrotate(d_query, cos_table, sin_table), unrotate(d_keys, cos_table, sin_table), d_values],
        axis=1,
    )
    g_bias = jnp.sum(d_qkv, axis=0)
    d_qkv_b = d_qkv.astype(jnp.bfloat16).reshape(length, -1)
    g_qkv = jnp.dot(normed_one.T, d_qkv_b, preferred_element_type=jnp.float32).reshape(
        qkv_full.shape
    )
    d_normed_one = head_total(jnp.dot(d_qkv_b, qkv_flat.T, preferred_element_type=jnp.float32))
    hat_one = hidden_float * attn_inverse
    g_attn_gain = jnp.sum(d_normed_one * hat_one, axis=0)
    hidden_grad = middle_grad + norm_backward(d_normed_one, hat_one, attn_inverse, attn_gain)
    g_qkv, g_bias, g_out, g_shared_gate_up, g_shared_down = (
        lax.psum_scatter(
            g_qkv.astype(jnp.bfloat16), "fsdp", scatter_dimension=0, tiled=True
        ).astype(jnp.float32),
        lax.psum_scatter(
            g_bias.astype(jnp.bfloat16), "fsdp", scatter_dimension=2, tiled=True
        ).astype(jnp.float32),
        lax.psum_scatter(
            g_out.astype(jnp.bfloat16), "fsdp", scatter_dimension=1, tiled=True
        ).astype(jnp.float32),
        lax.psum_scatter(
            g_shared_gate_up.astype(jnp.bfloat16), "fsdp", scatter_dimension=0, tiled=True
        ).astype(jnp.float32),
        lax.psum_scatter(
            g_shared_down.astype(jnp.bfloat16), "fsdp", scatter_dimension=1, tiled=True
        ).astype(jnp.float32),
    )
    g_attn_gain, g_ffn_gain, g_gate_vec = (
        lax.psum_scatter(g_attn_gain, ("fsdp", "tp"), scatter_dimension=0, tiled=True),
        lax.psum_scatter(g_ffn_gain, ("fsdp", "tp"), scatter_dimension=0, tiled=True),
        lax.psum_scatter(g_gate_vec, ("fsdp", "tp"), scatter_dimension=0, tiled=True),
    )
    return (
        hidden_out,
        hidden_grad,
        route_grad,
        g_attn_gain,
        g_ffn_gain,
        g_qkv,
        g_bias,
        g_out,
        g_shared_gate_up,
        g_shared_down,
        g_gate_vec,
        g_expert_gate_up,
        g_expert_down,
    )


MESH = pl.DeviceIdType.MESH


def flipped(index, bit):
    return index + bit - 2 * bit * ((index // bit) % 2)


def place():
    me = lax.axis_index("fsdp")
    rank = lax.axis_index("tp")
    return me, rank


def greet(me, rank, tp):
    barrier = pltpu.get_barrier_semaphore()
    for bit in (1, 2, 4):
        pl.semaphore_signal(
            barrier, inc=1, device_id=(flipped(me, bit), rank), device_id_type=MESH
        )

    @pl.when(rank > 0)
    def _():
        pl.semaphore_signal(barrier, inc=1, device_id=(me, rank - 1), device_id_type=MESH)

    @pl.when(rank < tp - 1)
    def _():
        pl.semaphore_signal(barrier, inc=1, device_id=(me, rank + 1), device_id_type=MESH)

    left = (rank + tp - 1) // tp
    right = (2 * (tp - 1) - rank) // tp
    pl.semaphore_wait(barrier, 3 + left + right)


def plane_peer(me, bits):
    for one in (1, 2, 4):
        if bits & one:
            me = flipped(me, one)
    return me


def greet_plane(me, rank, tp):
    barrier = pltpu.get_barrier_semaphore()
    for bits in range(1, 8):
        pl.semaphore_signal(
            barrier, inc=1, device_id=(plane_peer(me, bits), rank), device_id_type=MESH
        )

    @pl.when(rank > 0)
    def _():
        pl.semaphore_signal(barrier, inc=1, device_id=(me, rank - 1), device_id_type=MESH)

    @pl.when(rank < tp - 1)
    def _():
        pl.semaphore_signal(barrier, inc=1, device_id=(me, rank + 1), device_id_type=MESH)

    left = (rank + tp - 1) // tp
    right = (2 * (tp - 1) - rank) // tp
    pl.semaphore_wait(barrier, 7 + left + right)


UNIT = 640
SHARED = 384
NT = (((1,), (1,)), ((), ()))


def ffn_kernel(tp, expert_width, shared_width, *refs):
    part_ref, hidden_ref, gain_ref, vec_ref, scale_ref, grads_ref = refs[:6]
    expert_up, up_ref, expert_down, down_ref = refs[6:10]
    middle_ref, all_ref, up_in, d_ref, hid_ref, y_ref, dsum_ref, esum_ref = refs[10:18]
    (
        x_all, g_buf, dh_buf, d_buf, stage, acc, diag_in, last_in, z_in, both_buf, down_buf,
        eu_buf, su_buf, stage_e, acc_e, other_e, diag_e, last_e, z_in_e,
        w_sem, dn_sem, g_sem, x_sem, d_sem, h_sem, y_sem, f_sem, f_send, f_recv,
        az_send, az_recv, ap_send, ap_recv, s_send, s_recv,
        c_send, c_recv, ce_send, ce_recv, p_send, p_recv, pe_send, pe_recv,
        z_send, z_recv, ze_send, ze_recv,
    ) = refs[18:]
    me, rank = place()
    greet_plane(me, rank, tp)
    f32 = jnp.float32
    bf16 = jnp.bfloat16
    subs, rows, width = hidden_ref.shape
    tile = tp * rows
    pack_rows = subs * tile
    packs = x_all.shape[0]
    near = rank // 2
    order = [rank]
    for bit in (1, 2):
        order = order + [flipped(one, bit) for one in order]
    blocks = [3 * (1 - near), 2 - near, flipped(rank, 1), rank]
    core_of, x_of, y_of = me % 2, (me // 2) % 2, me // 4

    def pack_of(bits):
        return (
            4 * ((y_of + bits // 4) % 2)
            + 2 * ((x_of + (bits // 2) % 2) % 2)
            + (core_of + bits % 2) % 2
        )

    def add(ref, spot, one):
        ref[spot] = (ref[spot].astype(f32) + one.astype(f32)).astype(ref.dtype)

    def remote(src, dst, send, recv, bit):
        return pltpu.make_async_remote_copy(
            src_ref=src,
            dst_ref=dst,
            send_sem=send,
            recv_sem=recv,
            device_id=(flipped(me, bit), rank),
            device_id_type=MESH,
        )

    def remote_z(src, dst, send, recv, right):
        return pltpu.make_async_remote_copy(
            src_ref=src,
            dst_ref=dst,
            send_sem=send,
            recv_sem=recv,
            device_id=(me, rank + 1 if right else rank - 1),
            device_id_type=MESH,
        )

    def gather_z(block, sub, right):
        way = 0 if right else 1
        ref = x_all.at[me, block, sub]
        return remote_z(
            ref, ref, az_send.at[way, block, sub], az_recv.at[way, block, sub], right
        )

    def gather(bit, pack_bits, block, sub, slot, start=0, count=None):
        count = rows if count is None else count
        ref = x_all.at[pack_of(pack_bits), block, sub, pl.ds(start, count)]
        return remote(ref, ref, ap_send.at[slot, block, sub], ap_recv.at[slot, block, sub], bit)

    def to_core(q, block, sub):
        return gather(1, 2 * q, block, sub, q)

    def own_x(block, sub):
        return gather(2, 0, block, sub, 4)

    def own_y(block, sub):
        return gather(4, 0, block, sub, 5)

    def x_to_y(block, sub):
        return gather(4, 2, block, sub, 6, 0, rows // 2)

    def y_to_x(block, sub):
        return gather(2, 4, block, sub, 7, rows // 2, rows // 2)

    def start_plane(block, sub):
        own_x(block, sub).start()
        own_y(block, sub).start()
        to_core(0, block, sub).start()

    def start_rows(sub):
        @pl.when(rank < tp - 1)
        def _():
            gather_z(rank, sub, True).start()

        @pl.when(rank > 0)
        def _():
            gather_z(rank, sub, False).start()

        start_plane(rank, sub)

    def forward(place_in, sub):
        block = order[place_in]
        own_x(block, sub).wait_recv()
        x_to_y(block, sub).start()
        to_core(1, block, sub).start()
        own_y(block, sub).wait_recv()
        y_to_x(block, sub).start()
        to_core(2, block, sub).start()

    def finish(place_in, sub):
        block = order[place_in]
        x_to_y(block, sub).wait_recv()
        y_to_x(block, sub).wait_recv()
        to_core(3, block, sub).start()

    def z_step(step, sub):
        @pl.when(rank >= step)
        def _():
            block = rank - step
            gather_z(block, sub, True).wait_recv()

            @pl.when(rank < tp - 1)
            def _():
                gather_z(block, sub, True).start()

            start_plane(block, sub)

        @pl.when(rank + step < tp)
        def _():
            block = rank + step
            gather_z(block, sub, False).wait_recv()

            @pl.when(rank > 0)
            def _():
                gather_z(block, sub, False).start()

            start_plane(block, sub)

    def control(i):
        steps = {
            1: [(forward, 3, 0)],
            2: [(forward, 0, 1), (finish, 2, 0)],
            3: [(z_step, 2, 1)],
            4: [(finish, 3, 0), (forward, 1, 1)],
            5: [(z_step, 3, 1)],
            6: [(finish, 0, 1)],
            7: [(forward, 2, 1)],
            8: [(finish, 1, 1)],
            9: [(forward, 3, 1)],
            10: [(finish, 2, 1)],
            11: [(finish, 3, 1)],
        }
        for at, todo in steps.items():

            @pl.when(i == at)
            def _():
                for act, what, sub in todo:
                    act(what, sub)

    up_rows = up_ref.shape[2]
    span = down_ref.shape[2]

    def up_to(bits):
        return pltpu.make_async_remote_copy(
            src_ref=up_ref.at[plane_peer(me, bits)],
            dst_ref=up_in.at[:, pl.ds(pl.multiple_of(me * up_rows, up_rows), up_rows)],
            send_sem=s_send.at[0, bits],
            recv_sem=s_recv.at[0, bits],
            device_id=(plane_peer(me, bits), rank),
            device_id_type=MESH,
        )

    def down_spot():
        return down_buf.at[
            pl.ds(SHARED, shared_width), pl.ds(pl.multiple_of(me * span, span), span)
        ]

    def down_to(bits):
        return pltpu.make_async_remote_copy(
            src_ref=down_ref.at[plane_peer(me, bits)],
            dst_ref=down_spot(),
            send_sem=s_send.at[1, bits],
            recv_sem=s_recv.at[1, bits],
            device_id=(plane_peer(me, bits), rank),
            device_id_type=MESH,
        )

    def core(q, s):
        return remote(stage.at[s], acc.at[q, s], c_send.at[q, s], c_recv.at[q, s], 1)

    def core_e(q):
        return remote(stage_e.at[q], other_e.at[q], ce_send.at[q], ce_recv.at[q], 1)

    low, high = pl.ds(0, tp // 2), pl.ds(tp // 2, tp // 2)

    def across(bit, src, dst, slot, s):
        return remote(src, dst, p_send.at[slot, s], p_recv.at[slot, s], bit)

    def diag_x(s):
        return across(2, acc.at[3, s, low], diag_in.at[s, 0], 0, s)

    def diag_y(s):
        return across(4, acc.at[3, s, high], diag_in.at[s, 1], 1, s)

    def direct_x(s):
        return across(2, acc.at[1, s, low], last_in.at[s, 0, low], 2, s)

    def direct_y(s):
        return across(4, acc.at[2, s, high], last_in.at[s, 1, high], 3, s)

    def summed_x(s):
        return across(2, acc.at[1, s, high], last_in.at[s, 0, high], 4, s)

    def summed_y(s):
        return across(4, acc.at[2, s, low], last_in.at[s, 1, low], 5, s)

    def diag_lines():
        return remote(acc_e.at[3], diag_e, pe_send.at[0], pe_recv.at[0], 2)

    def direct_lines():
        return remote(acc_e.at[1], last_e.at[0], pe_send.at[1], pe_recv.at[1], 2)

    def summed_lines():
        return remote(acc_e.at[2], last_e.at[1], pe_send.at[2], pe_recv.at[2], 4)

    def along_z(j, s, right):
        way = 0 if right else 1
        block = blocks[j]
        return remote_z(
            acc.at[0, s, block],
            z_in.at[way, block, s],
            z_send.at[way, block, s],
            z_recv.at[way, block, s],
            right,
        )

    def lines_z(right):
        way = 0 if right else 1
        return remote_z(
            acc_e.at[1 + way], z_in_e.at[way], ze_send.at[way], ze_recv.at[way], right
        )

    def second(s):
        diag_x(s).wait_recv()
        add(acc, (2, s, low), diag_in[s, 0])
        summed_y(s).start()
        diag_y(s).wait_recv()
        add(acc, (1, s, high), diag_in[s, 1])
        summed_x(s).start()

    def third(j, s):
        block = blocks[j]
        if j == 0:
            direct_x(s).wait_recv()
            direct_y(s).wait_recv()
            summed_x(s).wait_recv()
            summed_y(s).wait_recv()
        total = (
            acc[0, s, block].astype(f32)
            + last_in[s, 0, block].astype(f32)
            + last_in[s, 1, block].astype(f32)
        )
        if j < tp - 1:
            acc[0, s, block] = total.astype(bf16)

            @pl.when((block > rank) & (rank > 0))
            def _():
                along_z(j, s, True).wait_recv()
                add(acc, (0, s, block), z_in[0, block, s])

            @pl.when((block < rank) & (rank < tp - 1))
            def _():
                along_z(j, s, False).wait_recv()
                add(acc, (0, s, block), z_in[1, block, s])

            @pl.when(block > rank)
            def _():
                along_z(j, s, True).start()

            @pl.when(block < rank)
            def _():
                along_z(j, s, False).start()
        else:
            dsum_ref[s] = total

            @pl.when(rank > 0)
            def _():
                along_z(j, s, True).wait_recv()
                dsum_ref[s] += z_in[0, block, s].astype(f32)

            @pl.when(rank < tp - 1)
            def _():
                along_z(j, s, False).wait_recv()
                dsum_ref[s] += z_in[1, block, s].astype(f32)

    def sum_lines():
        direct_lines().wait_recv()
        summed_lines().wait_recv()
        direct_lines().wait_send()
        summed_lines().wait_send()
        own = acc_e[0] + last_e[0] + last_e[1]
        esum_ref[...] = own
        acc_e[1] = own
        acc_e[2] = own

        @pl.when(rank > 0)
        def _():
            lines_z(True).wait_recv()
            esum_ref[...] += z_in_e[0]
            acc_e[1] = own + z_in_e[0]

        @pl.when(rank < tp - 1)
        def _():
            lines_z(True).start()
            lines_z(False).wait_recv()
            esum_ref[...] += z_in_e[1]
            acc_e[2] = own + z_in_e[1]

        @pl.when(rank > 0)
        def _():
            lines_z(False).start()

    def front_load(block, s):
        return pltpu.make_async_copy(
            part_ref.at[block, s], stage.at[s, block], f_sem.at[block, s]
        )

    def front_z(j, s, right):
        way = 0 if right else 1
        block = blocks[j]
        return remote_z(
            stage.at[s, block],
            z_in.at[way, block, s],
            f_send.at[way, block, s],
            f_recv.at[way, block, s],
            right,
        )

    def front(j, s):
        block = blocks[j]
        front_load(block, s).wait()
        if j < tp - 1:

            @pl.when((block > rank) & (rank > 0))
            def _():
                front_z(j, s, True).wait_recv()
                add(stage, (s, block), z_in[0, block, s])

            @pl.when((block < rank) & (rank < tp - 1))
            def _():
                front_z(j, s, False).wait_recv()
                add(stage, (s, block), z_in[1, block, s])

            @pl.when(block > rank)
            def _():
                front_z(j, s, True).start()

            @pl.when(block < rank)
            def _():
                front_z(j, s, False).start()
        else:
            middle_ref[s] = hidden_ref[s].astype(f32) + stage[s, block].astype(f32)

            @pl.when(rank > 0)
            def _():
                front_z(j, s, True).wait_recv()
                middle_ref[s] += z_in[0, block, s].astype(f32)

            @pl.when(rank < tp - 1)
            def _():
                front_z(j, s, False).wait_recv()
                middle_ref[s] += z_in[1, block, s].astype(f32)

            middle = middle_ref[s]
            mean = jnp.mean(middle * middle, axis=-1, keepdims=True)
            normed = middle * lax.rsqrt(mean + epsilon) * gain_ref[...]
            x_all[me, rank, s] = normed.astype(bf16)
            start_rows(s)

    cut = eu_buf.shape[1]
    cuts = width // cut
    units = SHARED + shared_width

    def weight_loads(part, n, slot):
        at = pl.ds(pl.multiple_of(n * cut, cut), cut)
        return (
            pltpu.make_async_copy(expert_up.at[part, at], eu_buf.at[slot], w_sem.at[0, slot]),
            pltpu.make_async_copy(up_in.at[part, at], su_buf.at[slot], w_sem.at[1, slot]),
        )

    def start_loads(part, n, slot):
        of_expert, of_shared = weight_loads(part, n, slot)
        of_expert.start()

        @pl.when(n == me)
        def _():
            own = up_ref.at[me, part]
            pltpu.make_async_copy(own, su_buf.at[slot], w_sem.at[1, slot]).start()

        @pl.when(n != me)
        def _():
            of_shared.start()

    def lay_out(part):
        base = part * UNIT

        def body(n, carry):
            slot = n % 2

            @pl.when(n + 1 < cuts)
            def _():
                start_loads(part, n + 1, 1 - slot)

            for copy in weight_loads(part, n, slot):
                copy.wait()
            at = pl.ds(pl.multiple_of(n * cut, cut), cut)
            both_buf[at, base : base + UNIT] = jnp.zeros((cut, UNIT), bf16)
            both_buf[at, base : base + expert_width] = eu_buf[slot]
            both_buf[at, base + SHARED : base + units] = su_buf[slot]
            return carry

        start_loads(part, 0, 0)
        lax.fori_loop(0, cuts, body, 0)

    down_loads = (
        pltpu.make_async_copy(expert_down, down_buf.at[pl.ds(0, expert_width)], dn_sem.at[0]),
        pltpu.make_async_copy(down_ref.at[me], down_spot(), dn_sem.at[1]),
    )

    def grad_load(n, slot):
        at = pl.ds(n * tile, tile)
        return pltpu.make_async_copy(grads_ref.at[at], g_buf.at[slot], g_sem.at[slot])

    def hidden_grads(first, last):
        def body(n, carry):
            slot = n % 2

            @pl.when(n + 1 < 2 * packs)
            def _():
                grad_load(n + 1, 1 - slot).start()

            grad_load(n, slot).wait()
            d_hidden = lax.dot_general(
                g_buf[slot], down_buf[...], NT, preferred_element_type=f32
            ).astype(bf16)
            dh_buf[n // 2, pl.ds(n % 2 * 2, 2)] = d_hidden.reshape(2, subs, rows, UNIT)
            return carry

        lax.fori_loop(first, last, body, 0)

    def tile_of(i):
        s = i // 8
        q = order_of(s, i // 2 % 4)
        o = i % 2
        return q, o, s, pack_of(2 * q + 1 - o)

    def order_of(s, r):
        return r + s * (r // 2) * (1 - 2 * (r % 2))

    def d_store(i):
        q, o, s, pack = tile_of(i)
        return pltpu.make_async_copy(d_buf.at[i % 2], d_ref.at[pack, :, s], d_sem.at[i % 2])

    def x_store(i):
        q, o, s, pack = tile_of(i)
        return pltpu.make_async_copy(x_all.at[pack, :, s], all_ref.at[pack, :, s], x_sem.at[i % 2])

    def one_tile(i, carry):
        q, o, s, pack = tile_of(i)
        slot = i % 2

        @pl.when(o == 0)
        def _():
            for block in range(tp):
                ref = x_all.at[pack, block, s]
                remote(
                    ref, ref, ap_send.at[q, block, s], ap_recv.at[q, block, s], 1
                ).wait_recv()

        @pl.when(i >= 2)
        def _():
            d_store(i - 2).wait()
            x_store(i - 2).wait()

        x_store(i).start()
        x = x_all[pack, :, s].reshape(tile, width)
        pre = jnp.dot(x, both_buf[...], preferred_element_type=f32)
        gate, upper = pre[:, :UNIT], pre[:, UNIT:]
        lane = lax.broadcasted_iota(jnp.int32, (1, UNIT), 1)
        logit = jnp.sum(x.astype(f32) * vec_ref[...], axis=-1, keepdims=True)
        gate_prob = 1.0 / (1.0 + jnp.exp(-logit))
        own_scale = jnp.broadcast_to(scale_ref[pack, s], (128, tile)).T[:, :1]
        scale = jnp.where(lane < SHARED, own_scale, gate_prob)
        sigmoid = 1.0 / (1.0 + jnp.exp(-gate))
        act = gate * sigmoid
        slope = sigmoid * (1.0 + gate * (1.0 - sigmoid))
        hidden = act * upper
        d_hidden = dh_buf[pack, :, s].reshape(tile, UNIT).astype(f32)
        line = lax.broadcasted_iota(jnp.int32, (16, UNIT), 0)
        unit = lax.broadcasted_iota(jnp.int32, (16, UNIT), 1)
        of_expert = (line == me) & (unit < SHARED)
        of_shared = (line == 8) & (unit >= SHARED)
        pick = jnp.where(of_expert | of_shared, 1.0, 0.0).astype(bf16)
        lines = lax.dot_general(
            pick, (d_hidden * hidden).astype(bf16), NT, preferred_element_type=f32
        )
        dh_buf[pack, :, s] = (hidden * scale).astype(bf16).reshape(tp, rows, UNIT)
        d_scaled = d_hidden * scale
        d_gate = (d_scaled * upper * slope).astype(bf16)
        d_upper = (d_scaled * act).astype(bf16)
        d_buf[slot, :, :, :UNIT] = d_gate.reshape(tp, rows, UNIT)
        d_buf[slot, :, :, UNIT:] = d_upper.reshape(tp, rows, UNIT)
        control(i)
        d_both = d_buf[slot].reshape(tile, 2 * UNIT)
        d_rows = lax.dot_general(d_both, both_buf[...], NT, preferred_element_type=f32)
        d_rows = d_rows.reshape(tp, rows, width)
        d_store(i).start()

        @pl.when(o == 0)
        def _():
            @pl.when(i % 8 >= 2)
            def _():
                core(order_of(s, i // 2 % 4 - 1), s).wait_send()

            stage[s] = d_rows.astype(bf16)
            stage_e[q, s] = lines
            core(q, s).start()

            @pl.when(s == 1)
            def _():
                core_e(q).start()

        @pl.when(o == 1)
        def _():
            core(q, s).wait_recv()
            add(acc, (q, s), d_rows)
            acc_e[q, s] = lines

            @pl.when(s == 1)
            def _():
                core_e(q).wait_recv()
                acc_e[q] = acc_e[q] + other_e[q]

                @pl.when(q == 1)
                def _():
                    direct_lines().start()

                @pl.when(q == 3)
                def _():
                    diag_lines().start()

            @pl.when(q == 1)
            def _():
                direct_x(s).start()

            @pl.when(q == 2)
            def _():
                direct_y(s).start()

            @pl.when(q == 3)
            def _():
                diag_x(s).start()
                diag_y(s).start()

            @pl.when(i == 9)
            def _():
                second(0)

            @pl.when(i == 15)
            def _():
                third(0, 0)

        return carry

    def y_store(n, slot):
        return pltpu.make_async_copy(
            g_buf.at[slot], y_ref.at[pl.ds(n * tile, tile)], y_sem.at[slot]
        )

    def outputs(first, last):
        def body(n, carry):
            slot = n % 2

            @pl.when(n >= 2)
            def _():
                y_store(n - 2, slot).wait()

            hidden = dh_buf[n // 2, pl.ds(n % 2 * 2, 2)].reshape(tile, UNIT)
            g_buf[slot] = jnp.dot(hidden, down_buf[...], preferred_element_type=f32).astype(bf16)
            y_store(n, slot).start()
            return carry

        lax.fori_loop(first, last, body, 0)

    for bits in (6, 7, 2, 4, 3, 5, 1):
        down_to(bits).start()
    for bits in (6, 7, 2, 4, 3, 5, 1):
        up_to(bits).start()
    grad_load(0, 0).start()
    for s in range(subs):
        for block in blocks:
            front_load(block, s).start()
    down_buf[expert_width:SHARED, :] = jnp.zeros((SHARED - expert_width, width), bf16)
    down_buf[units:, :] = jnp.zeros((UNIT - units, width), bf16)
    for copy in down_loads:
        copy.start()
    ends = (rank == 0) | (rank == tp - 1)
    inner = (rank > 0) & (rank < tp - 1)
    front(0, 0)
    front(1, 0)
    front(2, 0)

    @pl.when(ends)
    def _():
        front(0, 1)

    for copy in down_loads:
        copy.wait()
    for bits in range(1, 8):
        down_to(bits).wait_recv()

    @pl.when(ends)
    def _():
        hidden_grads(0, 6)

    front(3, 0)

    @pl.when(ends)
    def _():
        front(1, 1)
        front(2, 1)

    @pl.when(inner)
    def _():
        front(0, 1)

    z_step(1, 0)
    forward(0, 0)

    @pl.when(inner)
    def _():
        hidden_grads(0, 4)

    z_step(2, 0)

    @pl.when(inner)
    def _():
        front(1, 1)
        hidden_grads(4, 6)
        front(2, 1)

    for bits in range(1, 8):
        up_to(bits).wait_recv()
    lay_out(0)
    z_step(3, 0)
    forward(1, 0)
    finish(0, 0)
    front(3, 1)
    lay_out(1)
    forward(2, 0)
    z_step(1, 1)
    hidden_grads(6, 11)
    finish(1, 0)
    hidden_grads(11, 2 * packs)
    for s in range(subs):
        for j in range(tp - 1):
            block = blocks[j]

            @pl.when(block > rank)
            def _():
                front_z(j, s, True).wait_send()

            @pl.when(block < rank)
            def _():
                front_z(j, s, False).wait_send()

    lax.fori_loop(0, 16, one_tile, 0)
    hidden_store = pltpu.make_async_copy(dh_buf, hid_ref, h_sem)
    hidden_store.start()
    diag_lines().wait_recv()
    acc_e[2] = acc_e[2] + diag_e[...]
    summed_lines().start()
    outputs(0, 2)
    second(1)
    third(1, 0)
    outputs(2, 4)
    third(2, 0)
    outputs(4, 6)
    third(3, 0)
    sum_lines()
    outputs(6, 8)
    third(0, 1)
    outputs(8, 10)
    third(1, 1)
    outputs(10, 12)
    third(2, 1)
    outputs(12, 14)
    third(3, 1)
    outputs(14, 16)
    hidden_store.wait()
    for n in (14, 15):
        y_store(n, n % 2).wait()
        d_store(n).wait()
        x_store(n).wait()
    core(3, 0).wait_send()
    core(2, 1).wait_send()
    diag_lines().wait_send()
    for q in range(4):
        core_e(q).wait_send()
    for bits in range(1, 8):
        up_to(bits).wait_send()
        down_to(bits).wait_send()
    for s in range(subs):
        for copy in (diag_x, diag_y, direct_x, direct_y, summed_x, summed_y):
            copy(s).wait_send()
        for block in range(tp):
            for q in range(4):
                to_core(q, block, s).wait_send()
            for copy in (own_x, own_y, x_to_y, y_to_x):
                copy(block, s).wait_send()

            @pl.when((block <= rank) & (rank < tp - 1))
            def _():
                gather_z(block, s, True).wait_send()

            @pl.when((block >= rank) & (rank > 0))
            def _():
                gather_z(block, s, False).wait_send()

        for j in range(tp - 1):
            block = blocks[j]

            @pl.when(block > rank)
            def _():
                along_z(j, s, True).wait_send()

            @pl.when(block < rank)
            def _():
                along_z(j, s, False).wait_send()

    @pl.when(rank < tp - 1)
    def _():
        lines_z(True).wait_send()

    @pl.when(rank > 0)
    def _():
        lines_z(False).wait_send()


def ffn(
    part, hidden, gain, vec, scale, grads, expert_up, shared_up, expert_down, shared_down,
    fsdp, tp, collective_id,
):
    own, width = hidden.shape
    subs = 2
    rows = own // subs
    tile = tp * rows
    tokens = fsdp * tp * own
    expert_width, shared_width = expert_down.shape[0], shared_down.shape[1]
    bf16 = jnp.bfloat16
    f32 = jnp.float32
    dma = pltpu.SemaphoreType.DMA
    anywhere = pl.BlockSpec(memory_space=pl.ANY)
    vmem = pl.BlockSpec(memory_space=pltpu.VMEM)
    all_rows = (fsdp, tp, subs, rows)
    lines = (subs, 16, tile)
    return pl.pallas_call(
        functools.partial(ffn_kernel, tp, expert_width, shared_width),
        out_shape=[
            jax.ShapeDtypeStruct((subs, rows, width), f32),
            jax.ShapeDtypeStruct(all_rows + (width,), bf16),
            jax.ShapeDtypeStruct((2, width, shared_width), bf16),
            jax.ShapeDtypeStruct(all_rows + (2 * UNIT,), bf16),
            jax.ShapeDtypeStruct(all_rows + (UNIT,), bf16),
            jax.ShapeDtypeStruct((tokens, width), bf16),
            jax.ShapeDtypeStruct((subs, rows, width), f32),
            jax.ShapeDtypeStruct(lines, f32),
        ],
        in_specs=[anywhere] + [vmem] * 4 + [anywhere] * 5,
        out_specs=[vmem] + [anywhere] * 5 + [vmem] * 2,
        scratch_shapes=[
            pltpu.VMEM(all_rows + (width,), bf16),
            pltpu.VMEM((2, tile, width), bf16),
            pltpu.VMEM(all_rows + (UNIT,), bf16),
            pltpu.VMEM((2, tp, rows, 2 * UNIT), bf16),
            pltpu.VMEM((subs, tp, rows, width), bf16),
            pltpu.VMEM((4, subs, tp, rows, width), bf16),
            pltpu.VMEM((subs, 2, tp // 2, rows, width), bf16),
            pltpu.VMEM((subs, 2, tp, rows, width), bf16),
            pltpu.VMEM((2, tp, subs, rows, width), bf16),
            pltpu.VMEM((width, 2 * UNIT), bf16),
            pltpu.VMEM((UNIT, width), bf16),
            pltpu.VMEM((2, width // 8, expert_width), bf16),
            pltpu.VMEM((2, width // 8, shared_width), bf16),
            pltpu.VMEM((4,) + lines, f32),
            pltpu.VMEM((4,) + lines, f32),
            pltpu.VMEM((4,) + lines, f32),
            pltpu.VMEM(lines, f32),
            pltpu.VMEM((2,) + lines, f32),
            pltpu.VMEM((2,) + lines, f32),
            dma((2, 2)), dma((2,)), dma((2,)), dma((2,)), dma((2,)), dma, dma((2,)),
            dma((tp, subs)), dma((2, tp, subs)), dma((2, tp, subs)),
            dma((2, tp, subs)), dma((2, tp, subs)), dma((8, tp, subs)), dma((8, tp, subs)),
            dma((2, fsdp)), dma((2, fsdp)),
            dma((4, subs)), dma((4, subs)), dma((4,)), dma((4,)),
            dma((6, subs)), dma((6, subs)), dma((3,)), dma((3,)),
            dma((2, tp, subs)), dma((2, tp, subs)), dma((2,)), dma((2,)),
        ],
        compiler_params=pltpu.CompilerParams(
            collective_id=collective_id, has_side_effects=True, vmem_limit_bytes=63 << 20
        ),
        name="ffn",
    )(
        part.reshape(tp, subs, rows, width), hidden.reshape(subs, rows, width), gain, vec,
        scale, grads, expert_up, shared_up, expert_down, shared_down,
    )


TN = (((0,), (0,)), ((), ()))
SUB = 2


def outputs_kernel(tp, expert_width, shared_width, *refs):
    y_ref, own_ref, x_ref, d_ref, h_ref, g_ref = refs[:6]
    total_ref, rows_ref, ge_ref, gs_ref, de_ref, ds_ref = refs[6:12]
    (
        mine, other, diag_in, last_in, z_in, d_buf, h_buf, col_buf, ge_buf, gs_buf, de_buf, ds_buf,
        l_sem, c_send, c_recv, p_send, p_recv, z_send, z_recv, a_sem, a_send, a_recv,
        w_sem, col_sem, out_sem,
    ) = refs[12:]
    me, rank = place()
    greet(me, rank, tp)
    f32 = jnp.float32
    bf16 = jnp.bfloat16
    rows = total_ref.shape[0]
    cut = rows // SUB
    half = cut // 2
    near = rank // 2
    blocks = [3 * (1 - near), 2 - near, flipped(rank, 1), rank]
    pieces = range(tp * SUB)
    packs = [me, flipped(me, 2), flipped(me, 4), flipped(flipped(me, 2), 4)]
    low, high = pl.ds(0, half), pl.ds(half, half)

    def gather_z(block, right):
        way = 0 if right else 1
        spot = rows_ref.at[pl.ds(block * rows, rows)]
        return pltpu.make_async_remote_copy(
            src_ref=spot,
            dst_ref=spot,
            send_sem=a_send.at[way, block],
            recv_sem=a_recv.at[way, block],
            device_id=(me, rank + 1 if right else rank - 1),
            device_id_type=MESH,
        )

    def gather_step(step):
        @pl.when(rank >= step)
        def _():
            gather_z(rank - step, True).wait_recv()

            @pl.when(rank < tp - 1)
            def _():
                gather_z(rank - step, True).start()

        @pl.when(rank + step < tp)
        def _():
            gather_z(rank + step, False).wait_recv()

            @pl.when(rank > 0)
            def _():
                gather_z(rank + step, False).start()

    def spot_of(j):
        return blocks[j // SUB] * SUB + j % SUB

    def region(pack, j):
        return y_ref.at[pl.ds((pack * tp * SUB + spot_of(j)) * cut, cut)]

    def local(k, j):
        return pltpu.make_async_copy(region(packs[k], j), mine.at[k, j], l_sem.at[k, j])

    def core(k, j):
        return pltpu.make_async_remote_copy(
            src_ref=region(flipped(packs[k], 1), j),
            dst_ref=other.at[k, j],
            send_sem=c_send.at[k, j],
            recv_sem=c_recv.at[k, j],
            device_id=(flipped(me, 1), rank),
            device_id_type=MESH,
        )

    def across(bit, src, dst, slot, j):
        return pltpu.make_async_remote_copy(
            src_ref=src,
            dst_ref=dst,
            send_sem=p_send.at[slot, j],
            recv_sem=p_recv.at[slot, j],
            device_id=(flipped(me, bit), rank),
            device_id_type=MESH,
        )

    def diag_x(j):
        return across(2, mine.at[3, j, low], diag_in.at[j, 0], 0, j)

    def diag_y(j):
        return across(4, mine.at[3, j, high], diag_in.at[j, 1], 1, j)

    def direct_x(j):
        return across(2, mine.at[1, j, low], last_in.at[j, 0, low], 2, j)

    def direct_y(j):
        return across(4, mine.at[2, j, high], last_in.at[j, 1, high], 3, j)

    def summed_x(j):
        return across(2, mine.at[1, j, high], last_in.at[j, 0, high], 4, j)

    def summed_y(j):
        return across(4, mine.at[2, j, low], last_in.at[j, 1, low], 5, j)

    def along_z(j, right):
        way = 0 if right else 1
        spot = spot_of(j)
        return pltpu.make_async_remote_copy(
            src_ref=mine.at[0, j],
            dst_ref=z_in.at[way, spot],
            send_sem=z_send.at[way, spot],
            recv_sem=z_recv.at[way, spot],
            device_id=(me, rank + 1 if right else rank - 1),
            device_id_type=MESH,
        )

    def add(ref, spot, one):
        ref[spot] = (ref[spot].astype(f32) + one.astype(f32)).astype(ref.dtype)

    def first(j):
        for k in (3, 2, 1, 0):
            core(k, j).wait_recv()
            local(k, j).wait()
            add(mine, (k, j), other[k, j])
            if k == 3:
                diag_x(j).start()
                diag_y(j).start()
            if k == 2:
                direct_y(j).start()
            if k == 1:
                direct_x(j).start()

    def second(j):
        diag_x(j).wait_recv()
        add(mine, (2, j, low), diag_in[j, 0])
        summed_y(j).start()
        diag_y(j).wait_recv()
        add(mine, (1, j, high), diag_in[j, 1])
        summed_x(j).start()

    def third(j):
        block = blocks[j // SUB]
        spot = spot_of(j)
        direct_x(j).wait_recv()
        direct_y(j).wait_recv()
        summed_x(j).wait_recv()
        summed_y(j).wait_recv()
        total = mine[0, j].astype(f32) + last_in[j, 0].astype(f32) + last_in[j, 1].astype(f32)
        if j < (tp - 1) * SUB:
            mine[0, j] = total.astype(bf16)

            @pl.when((block > rank) & (rank > 0))
            def _():
                along_z(j, True).wait_recv()
                add(mine, (0, j), z_in[0, spot])

            @pl.when((block < rank) & (rank < tp - 1))
            def _():
                along_z(j, False).wait_recv()
                add(mine, (0, j), z_in[1, spot])

            @pl.when(block > rank)
            def _():
                along_z(j, True).start()

            @pl.when(block < rank)
            def _():
                along_z(j, False).start()
        else:
            own_rows = pl.ds(j % SUB * cut, cut)
            total_ref[own_rows] = total

            @pl.when(rank > 0)
            def _():
                along_z(j, True).wait_recv()
                total_ref[own_rows] += z_in[0, spot].astype(f32)

            @pl.when(rank < tp - 1)
            def _():
                along_z(j, False).wait_recv()
                total_ref[own_rows] += z_in[1, spot].astype(f32)

    span = col_buf.shape[2]
    steps = x_ref.shape[1] // span
    units = SHARED + shared_width

    def columns(n, slot, of_x):
        ref = x_ref if of_x else g_ref
        return pltpu.make_async_copy(
            ref.at[:, pl.ds(pl.multiple_of(n * span, span), span)],
            col_buf.at[slot],
            col_sem.at[slot],
        )

    def up_stores(n, slot):
        at = pl.ds(pl.multiple_of(n * span, span), span)
        return (
            pltpu.make_async_copy(ge_buf.at[slot], ge_ref.at[:, at], out_sem.at[0, slot]),
            pltpu.make_async_copy(gs_buf.at[slot], gs_ref.at[:, at], out_sem.at[1, slot]),
        )

    def down_stores(n, slot):
        at = pl.ds(pl.multiple_of(n * span, span), span)
        return (
            pltpu.make_async_copy(de_buf.at[slot], de_ref.at[:, at], out_sem.at[2, slot]),
            pltpu.make_async_copy(ds_buf.at[slot], ds_ref.at[n], out_sem.at[3, slot]),
        )

    def up_step(n, carry):
        slot = n % 2

        @pl.when(n + 1 < steps)
        def _():
            columns(n + 1, 1 - slot, True).start()

        @pl.when(n + 1 == steps)
        def _():
            columns(0, 1 - slot, False).start()

        columns(n, slot, True).wait()

        @pl.when(n >= 2)
        def _():
            for copy in up_stores(n - 2, slot):
                copy.wait()

        grads = lax.dot_general(col_buf[slot], d_buf[...], TN, preferred_element_type=f32)
        for part in range(2):
            base = part * UNIT
            ge_buf[slot, part] = grads[:, base : base + expert_width]
            gs_buf[slot, part] = grads[:, base + SHARED : base + units].astype(bf16)
        for copy in up_stores(n, slot):
            copy.start()
        return carry

    def down_step(n, carry):
        slot = n % 2

        @pl.when(n + 1 < steps)
        def _():
            columns(n + 1, 1 - slot, False).start()

        columns(n, slot, False).wait()

        @pl.when(n >= 2)
        def _():
            for copy in down_stores(n - 2, slot):
                copy.wait()

        grads = lax.dot_general(h_buf[...], col_buf[slot], TN, preferred_element_type=f32)
        de_buf[slot] = grads[:expert_width]
        ds_buf[slot] = grads[SHARED:units].astype(bf16)
        for copy in down_stores(n, slot):
            copy.start()
        return carry

    load_d = pltpu.make_async_copy(d_ref, d_buf, w_sem.at[0])
    load_h = pltpu.make_async_copy(h_ref, h_buf, w_sem.at[1])
    own = pltpu.make_async_copy(own_ref, rows_ref.at[pl.ds(rank * rows, rows)], a_sem)
    own.start()
    for j in pieces:
        for k in (3, 2, 1, 0):
            core(k, j).start()
            local(k, j).start()
    load_d.start()
    columns(0, 0, True).start()
    load_h.start()
    own.wait()

    @pl.when(rank < tp - 1)
    def _():
        gather_z(rank, True).start()

    @pl.when(rank > 0)
    def _():
        gather_z(rank, False).start()

    first(0)
    first(1)
    load_d.wait()
    load_h.wait()
    for j in pieces:
        if j < len(pieces) // 2:
            lax.fori_loop(2 * j, 2 * j + 2, up_step, 0)
        else:
            later = j - len(pieces) // 2
            lax.fori_loop(2 * later, 2 * later + 2, down_step, 0)
        second(j)
        if j + 2 < len(pieces):
            first(j + 2)
        if j in (1, 3, 5):
            gather_step((j + 1) // 2)
        if j >= 2:
            third(j - 2)
    third(len(pieces) - 2)
    third(len(pieces) - 1)

    for n in (steps - 2, steps - 1):
        for copy in up_stores(n, n % 2) + down_stores(n, n % 2):
            copy.wait()
    for j in pieces:
        for k in range(4):
            core(k, j).wait_send()
        for copy in (diag_x, diag_y, direct_x, direct_y, summed_x, summed_y):
            copy(j).wait_send()
        block = blocks[j // SUB]
        if j < (tp - 1) * SUB:

            @pl.when(block > rank)
            def _():
                along_z(j, True).wait_send()

            @pl.when(block < rank)
            def _():
                along_z(j, False).wait_send()

    for block in range(tp):

        @pl.when((block <= rank) & (rank < tp - 1))
        def _():
            gather_z(block, True).wait_send()

        @pl.when((block >= rank) & (rank > 0))
        def _():
            gather_z(block, False).wait_send()


def outputs(y, own, x, d, h, g, fsdp, tp, expert_width, shared_width, collective_id):
    rows, width = own.shape
    tokens = y.shape[0]
    span = width // fsdp
    cut = rows // SUB
    bf16 = jnp.bfloat16
    f32 = jnp.float32
    dma = pltpu.SemaphoreType.DMA
    anywhere = pl.BlockSpec(memory_space=pl.ANY)
    return pl.pallas_call(
        functools.partial(outputs_kernel, tp, expert_width, shared_width),
        out_shape=[
            jax.ShapeDtypeStruct((rows, width), f32),
            jax.ShapeDtypeStruct((rows * tp, width), bf16),
            jax.ShapeDtypeStruct((2, width, expert_width), f32),
            jax.ShapeDtypeStruct((2, width, shared_width), bf16),
            jax.ShapeDtypeStruct((expert_width, width), f32),
            jax.ShapeDtypeStruct((fsdp, shared_width, span), bf16),
        ],
        in_specs=[anywhere, pl.BlockSpec(memory_space=pltpu.VMEM)] + [anywhere] * 4,
        out_specs=[pl.BlockSpec(memory_space=pltpu.VMEM)] + [anywhere] * 5,
        scratch_shapes=[
            pltpu.VMEM((4, tp * SUB, cut, width), bf16),
            pltpu.VMEM((4, tp * SUB, cut, width), bf16),
            pltpu.VMEM((tp * SUB, 2, cut // 2, width), bf16),
            pltpu.VMEM((tp * SUB, 2, cut, width), bf16),
            pltpu.VMEM((2, tp * SUB, cut, width), bf16),
            pltpu.VMEM((tokens, 2 * UNIT), bf16),
            pltpu.VMEM((tokens, UNIT), bf16),
            pltpu.VMEM((2, tokens, span), bf16),
            pltpu.VMEM((2, 2, span, expert_width), f32),
            pltpu.VMEM((2, 2, span, shared_width), bf16),
            pltpu.VMEM((2, expert_width, span), f32),
            pltpu.VMEM((2, shared_width, span), bf16),
            dma((4, tp * SUB)), dma((4, tp * SUB)), dma((4, tp * SUB)),
            dma((6, tp * SUB)), dma((6, tp * SUB)),
            dma((2, tp * SUB)), dma((2, tp * SUB)), dma, dma((2, tp)), dma((2, tp)),
            dma((2,)), dma((2,)), dma((4, 2)),
        ],
        compiler_params=pltpu.CompilerParams(
            collective_id=collective_id, has_side_effects=True, vmem_limit_bytes=60 << 20
        ),
        name="outputs",
    )(y, own, x, d, h, g)


def backward_kernel(fsdp, tp, heads, *refs):
    parts = 3
    d_ref, ho_ref, q_ref, k_ref, v_ref, lt_ref, cos_ref, sin_ref = refs[:8]
    seg_row_ref, seg_col_ref, normed_ref, qkv_ref, out_ref = refs[8:13]
    gs_ref, ds_ref, hidden_ref, grad_ref, gain_ref, sums_ref = refs[13:19]
    refs = refs[19:]
    outs, refs = refs[:parts], refs[parts:]
    gs_out, ds_out, hidden_grad_ref, gains_ref = refs[:4]
    refs = refs[4:]
    mine, other, diag_in, last_in = (refs[i * parts : (i + 1) * parts] for i in range(4))
    (
        dh_buf, dqkv_buf, gs_in, ds_in, dn_buf, z_in, v_send, v_in, w_send, w_in,
        c_send, c_recv, p_send, p_recv, s_sem, s_send, s_recv,
        f_send, f_recv, v_ssem, v_rsem, w_ssem, w_rsem,
    ) = refs[4 * parts :]
    me, rank = place()
    f32 = jnp.float32
    bf16 = jnp.bfloat16
    rows, width = hidden_ref.shape
    near = rank // 2
    blocks = [3 * (1 - near), 2 - near, flipped(rank, 1), rank]
    packs = [me, flipped(me, 2), flipped(me, 4), flipped(flipped(me, 2), 4)]
    every = range(parts)
    chunks = outs[0].shape[0]
    sizes = [ref.shape[1] for ref in outs]
    low = [pl.ds(0, size // 2) for size in sizes]
    high = [pl.ds(size // 2, size // 2) for size in sizes]

    def plane(bits):
        peer = me
        for one in (1, 2, 4):
            if bits & one:
                peer = flipped(peer, one)
        return peer

    def line(bits):
        peer = rank
        for one in (1, 2):
            if bits & one:
                peer = flipped(peer, one)
        return peer

    barrier = pltpu.get_barrier_semaphore()
    for bits in range(1, fsdp):
        pl.semaphore_signal(
            barrier, inc=1, device_id=(plane(bits), rank), device_id_type=MESH
        )
    for bits in range(1, tp):
        pl.semaphore_signal(barrier, inc=1, device_id=(me, line(bits)), device_id_type=MESH)
    pl.semaphore_wait(barrier, fsdp - 1 + tp - 1)

    def add(ref, spot, one):
        ref[spot] = (ref[spot].astype(f32) + one.astype(f32)).astype(ref.dtype)

    core_of, x_of, y_of = me % 2, (me // 2) % 2, me // 4

    def pack_of(bits):
        return (
            4 * ((y_of + bits // 4) % 2)
            + 2 * ((x_of + (bits // 2) % 2) % 2)
            + (core_of + bits % 2) % 2
        )

    def core(k, j, i):
        return pltpu.make_async_remote_copy(
            src_ref=mine[i].at[pack_of(2 * k + 1), j],
            dst_ref=other[i].at[k, j],
            send_sem=c_send.at[k, j, i],
            recv_sem=c_recv.at[k, j, i],
            device_id=(flipped(me, 1), rank),
            device_id_type=MESH,
        )

    def across(bit, src, dst, slot, j, i):
        return pltpu.make_async_remote_copy(
            src_ref=src,
            dst_ref=dst,
            send_sem=p_send.at[slot, j, i],
            recv_sem=p_recv.at[slot, j, i],
            device_id=(flipped(me, bit), rank),
            device_id_type=MESH,
        )

    def diag_x(j, i):
        return across(2, mine[i].at[packs[3], j, low[i]], diag_in[i].at[j, 0], 0, j, i)

    def diag_y(j, i):
        return across(4, mine[i].at[packs[3], j, high[i]], diag_in[i].at[j, 1], 1, j, i)

    def direct_x(j, i):
        return across(2, mine[i].at[packs[1], j, low[i]], last_in[i].at[j, 0, low[i]], 2, j, i)

    def direct_y(j, i):
        return across(4, mine[i].at[packs[2], j, high[i]], last_in[i].at[j, 1, high[i]], 3, j, i)

    def summed_x(j, i):
        return across(2, mine[i].at[packs[1], j, high[i]], last_in[i].at[j, 0, high[i]], 4, j, i)

    def summed_y(j, i):
        return across(4, mine[i].at[packs[2], j, low[i]], last_in[i].at[j, 1, low[i]], 5, j, i)

    def send_piece(bits, i):
        k = bits // 2

        @pl.when(bits % 2 == 1)
        def _():
            for j in range(chunks):
                core(k, j, i).start()

        @pl.when(bits % 2 == 0)
        def _():
            for j in range(chunks):
                core(k, j, i).wait_recv()
                add(mine[i], (pack_of(bits), j), other[i][k, j])

            @pl.when(k == 3)
            def _():
                for j in range(chunks):
                    diag_x(j, i).start()
                    diag_y(j, i).start()

            @pl.when(k == 2)
            def _():
                for j in range(chunks):
                    direct_y(j, i).start()

            @pl.when(k == 1)
            def _():
                for j in range(chunks):
                    direct_x(j, i).start()

    def second(j):
        for i in every:
            diag_x(j, i).wait_recv()
            add(mine[i], (packs[2], j, low[i]), diag_in[i][j, 0])
            summed_y(j, i).start()
            diag_y(j, i).wait_recv()
            add(mine[i], (packs[1], j, high[i]), diag_in[i][j, 1])
            summed_x(j, i).start()

    def third(j):
        for i in every:
            direct_x(j, i).wait_recv()
            direct_y(j, i).wait_recv()
            summed_x(j, i).wait_recv()
            summed_y(j, i).wait_recv()
            outs[i][j] = (
                mine[i][me, j].astype(f32)
                + last_in[i][j, 0].astype(f32)
                + last_in[i][j, 1].astype(f32)
            )

    span = ds_ref.shape[2]

    def shared_up(bits):
        at = pl.ds(pl.multiple_of(plane(bits) * span, span), span)
        return pltpu.make_async_remote_copy(
            src_ref=gs_ref.at[:, at],
            dst_ref=gs_in.at[me],
            send_sem=s_send.at[0, bits],
            recv_sem=s_recv.at[0, bits],
            device_id=(plane(bits), rank),
            device_id_type=MESH,
        )

    def shared_down(bits):
        return pltpu.make_async_remote_copy(
            src_ref=ds_ref.at[plane(bits)],
            dst_ref=ds_in.at[me],
            send_sem=s_send.at[1, bits],
            recv_sem=s_recv.at[1, bits],
            device_id=(plane(bits), rank),
            device_id_type=MESH,
        )

    own_up = pltpu.make_async_copy(
        gs_ref.at[:, pl.ds(pl.multiple_of(me * span, span), span)], gs_in.at[me], s_sem.at[0]
    )
    own_down = pltpu.make_async_copy(ds_ref.at[me], ds_in.at[me], s_sem.at[1])

    def front_z(j, right):
        way = 0 if right else 1
        block = blocks[j]
        return pltpu.make_async_remote_copy(
            src_ref=dn_buf.at[block],
            dst_ref=z_in.at[way, block],
            send_sem=f_send.at[way, block],
            recv_sem=f_recv.at[way, block],
            device_id=(me, rank + 1 if right else rank - 1),
            device_id_type=MESH,
        )

    def front(j):
        block = blocks[j]
        if j < tp - 1:

            @pl.when((block > rank) & (rank > 0))
            def _():
                front_z(j, True).wait_recv()
                add(dn_buf, (block,), z_in[0, block])

            @pl.when((block < rank) & (rank < tp - 1))
            def _():
                front_z(j, False).wait_recv()
                add(dn_buf, (block,), z_in[1, block])

            @pl.when(block > rank)
            def _():
                front_z(j, True).start()

            @pl.when(block < rank)
            def _():
                front_z(j, False).start()
        else:
            hidden_grad_ref[...] = dn_buf[block].astype(f32)

            @pl.when(rank > 0)
            def _():
                front_z(j, True).wait_recv()
                hidden_grad_ref[...] += z_in[0, block].astype(f32)

            @pl.when(rank < tp - 1)
            def _():
                front_z(j, False).wait_recv()
                hidden_grad_ref[...] += z_in[1, block].astype(f32)

    share = width // fsdp
    part = share // tp

    def gains_plane(bits):
        return pltpu.make_async_remote_copy(
            src_ref=v_send.at[plane(bits)],
            dst_ref=v_in.at[me],
            send_sem=v_ssem.at[bits],
            recv_sem=v_rsem.at[bits],
            device_id=(plane(bits), rank),
            device_id_type=MESH,
        )

    def gains_line(bits):
        return pltpu.make_async_remote_copy(
            src_ref=w_send.at[line(bits)],
            dst_ref=w_in.at[rank],
            send_sem=w_ssem.at[bits],
            recv_sem=w_rsem.at[bits],
            device_id=(me, line(bits)),
            device_id_type=MESH,
        )

    length = d_ref.shape[0]
    cut = width // fsdp
    size = heads * 128
    scale = 128 ** (-0.5)

    def out_piece(n, carry):
        bits = fsdp - 1 - n
        pack = pack_of(bits)
        at = pl.ds(pl.multiple_of(pack * cut, cut), cut)
        piece = lax.dot_general(d_ref[:, at], ho_ref[...], TN, preferred_element_type=f32)
        mine[1][pack] = piece.astype(bf16).reshape(chunks, cut // chunks, size)
        send_piece(bits, 1)
        return carry

    def qkv_piece(n, carry):
        bits = fsdp - 1 - n
        pack = pack_of(bits)
        at = pl.ds(pl.multiple_of(pack * cut, cut), cut)
        piece = lax.dot_general(normed_ref[:, at], dqkv_buf[...], TN, preferred_element_type=f32)
        mine[0][pack] = piece.astype(bf16).reshape(chunks, cut // chunks, 3 * size)
        send_piece(bits, 0)
        return carry

    def head_grads():
        total = jnp.zeros((length, size), f32)
        for owner in range(fsdp):
            total = total + lax.dot_general(
                d_ref[:, owner * cut : (owner + 1) * cut],
                out_ref[owner * size : (owner + 1) * size, :],
                NT,
                preferred_element_type=f32,
            )
        dh_buf[...] = total.astype(bf16)

    def unrotated(columns):
        return columns * cos_ref[...] - pltpu.roll(columns, 64, 1) * sin_ref[...]

    def attend_back(head):
        at = slice(head * 128, (head + 1) * 128)
        query, keys, values = q_ref[:, at], k_ref[:, at], v_ref[:, at]
        d_head = dh_buf[:, at]
        scores = lax.dot_general(query, keys, NT, preferred_element_type=f32) * scale
        line = lax.broadcasted_iota(jnp.int32, (length, length), 0)
        column = lax.broadcasted_iota(jnp.int32, (length, length), 1)
        allowed = (line >= column) & (seg_col_ref[...] == seg_row_ref[...])
        probs = jnp.exp(jnp.where(allowed, scores, -1e30) - lt_ref[:, head : head + 1])
        d_values = lax.dot_general(probs.astype(bf16), d_head, TN, preferred_element_type=f32)
        d_probs = lax.dot_general(d_head, values, NT, preferred_element_type=f32)
        delta = jnp.sum(
            d_head.astype(f32) * ho_ref[:, at].astype(f32), axis=-1, keepdims=True
        )
        d_scores = (probs * (d_probs - delta)).astype(bf16)
        d_query = jnp.dot(d_scores, keys, preferred_element_type=f32) * scale
        d_keys = lax.dot_general(d_scores, query, TN, preferred_element_type=f32) * scale
        for which, grad in enumerate((unrotated(d_query), unrotated(d_keys), d_values)):
            base = which * size + head * 128
            dqkv_buf[:, base : base + 128] = grad.astype(bf16)
            here = which * heads + head
            mine[2][0, 0, here : here + 1] = jnp.sum(grad, axis=0, keepdims=True)

    def row_grads(half):
        at = pl.ds(pl.multiple_of(half * 2 * rows, 2 * rows), 2 * rows)
        grads = lax.dot_general(dqkv_buf[at, :], qkv_ref[...], NT, preferred_element_type=f32)
        dn_buf[pl.ds(2 * half, 2)] = grads.astype(bf16).reshape(2, rows, width)

    ends = (rank == 0) | (rank == tp - 1)
    for bits in (6, 7, 2, 4):
        shared_up(bits).start()
        shared_down(bits).start()
    own_up.start()
    own_down.start()
    lax.fori_loop(0, fsdp, out_piece, 0)
    head_grads()
    mine[2][...] = jnp.zeros_like(mine[2])
    for head in range(heads):
        attend_back(head)
    row_grads(1 - near)

    @pl.when(ends)
    def _():
        front(0)
        front(1)

    row_grads(near)
    for owner in range(1, fsdp):
        mine[2][owner] = mine[2][0]
    lax.fori_loop(0, fsdp, qkv_piece, 0)
    for n in range(fsdp):
        send_piece(jnp.int32(fsdp - 1 - n), 2)

    @pl.when(jnp.logical_not(ends))
    def _():
        front(0)

    second(0)

    @pl.when(jnp.logical_not(ends))
    def _():
        front(1)

    second(1)
    for bits in (3, 5, 1):
        shared_up(bits).start()
        shared_down(bits).start()
    front(2)
    front(3)
    d_normed = hidden_grad_ref[...]
    hidden = hidden_ref[...].astype(f32)
    inverse = lax.rsqrt(jnp.mean(hidden * hidden, axis=-1, keepdims=True) + epsilon)
    hat = hidden * inverse
    v_send[...] = jnp.zeros_like(v_send)
    attn_gain = jnp.sum(d_normed * hat, axis=0, keepdims=True)
    for owner in range(fsdp):
        at = slice(owner * share, (owner + 1) * share)
        v_send[owner, 0:1] = attn_gain[:, at]
        v_send[owner, 1:3] = sums_ref[:, at]
    for bits in range(1, fsdp):
        gains_plane(bits).start()
    d_hat = d_normed * gain_ref[...]
    mean = jnp.mean(d_hat * hat, axis=-1, keepdims=True)
    hidden_grad_ref[...] = grad_ref[...] + inverse * (d_hat - hat * mean)
    third(0)
    total = v_send[me]
    for bits in range(1, fsdp):
        gains_plane(bits).wait_recv()
        total = total + v_in[plane(bits)]
    w_send[...] = jnp.zeros_like(w_send)
    for owner in range(tp):
        w_send[owner, :, :part] = total[:, owner * part : (owner + 1) * part]
    for bits in range(1, tp):
        gains_line(bits).start()
    third(1)
    own_up.wait()
    own_down.wait()
    for bits in range(1, fsdp):
        shared_up(bits).wait_recv()
        shared_down(bits).wait_recv()
    units = gs_in.shape[3]
    for owner in range(fsdp):
        at = slice(owner * units, (owner + 1) * units)
        gs_out[:, :, at] = gs_in[owner].astype(f32)
        ds_out[at] = ds_in[owner].astype(f32)
    total = w_send[rank]
    for bits in range(1, tp):
        gains_line(bits).wait_recv()
        total = total + w_in[line(bits)]
    gains_ref[...] = total

    for j in range(chunks):
        for i in every:
            for k in range(4):
                core(k, j, i).wait_send()
            for copy in (diag_x, diag_y, direct_x, direct_y, summed_x, summed_y):
                copy(j, i).wait_send()
    for bits in range(1, fsdp):
        shared_up(bits).wait_send()
        shared_down(bits).wait_send()
        gains_plane(bits).wait_send()
    for bits in range(1, tp):
        gains_line(bits).wait_send()
    for j in range(tp - 1):
        block = blocks[j]

        @pl.when(block > rank)
        def _():
            front_z(j, True).wait_send()

        @pl.when(block < rank)
        def _():
            front_z(j, False).wait_send()


def backward(
    d_rows, heads_out, query, keys, values, log_total, cos, sin, segments, normed, qkv, out,
    shared_up, shared_down, hidden, grad, gain, sums, fsdp, tp, heads, number,
):
    chunks = 2
    rows, width = hidden.shape
    length = rows * tp
    units = shared_up.shape[2]
    span = shared_down.shape[2]
    size = heads * 128
    bf16 = jnp.bfloat16
    f32 = jnp.float32
    shapes = [(width // (fsdp * chunks), 3 * size, bf16), (span // chunks, size, bf16), (16, 128, f32)]
    scratch = [pltpu.VMEM((fsdp, chunks, count, w), kind) for count, w, kind in shapes]
    scratch += [pltpu.VMEM((4, chunks, count, w), kind) for count, w, kind in shapes]
    scratch += [pltpu.VMEM((chunks, 2, count // 2, w), kind) for count, w, kind in shapes]
    scratch += [pltpu.VMEM((chunks, 2, count, w), kind) for count, w, kind in shapes]
    dma = pltpu.SemaphoreType.DMA
    anywhere = pl.BlockSpec(memory_space=pl.ANY)
    vmem = pl.BlockSpec(memory_space=pltpu.VMEM)
    out_shape = [jax.ShapeDtypeStruct((chunks, count, w), f32) for count, w, _ in shapes]
    out_shape += [
        jax.ShapeDtypeStruct((2, span, fsdp * units), f32),
        jax.ShapeDtypeStruct((fsdp * units, span), f32),
        jax.ShapeDtypeStruct((rows, width), f32),
        jax.ShapeDtypeStruct((8, 128), f32),
    ]
    return pl.pallas_call(
        functools.partial(backward_kernel, fsdp, tp, heads),
        out_shape=out_shape,
        in_specs=[vmem] * 13 + [anywhere] * 2 + [vmem] * 4,
        out_specs=[vmem] * len(out_shape),
        scratch_shapes=scratch
        + [
            pltpu.VMEM((length, size), bf16),
            pltpu.VMEM((length, 3 * size), bf16),
            pltpu.VMEM((fsdp, 2, span, units), shared_up.dtype),
            pltpu.VMEM((fsdp, units, span), shared_down.dtype),
            pltpu.VMEM((tp, rows, width), bf16),
            pltpu.VMEM((2, tp, rows, width), bf16),
            pltpu.VMEM((fsdp, 8, width // fsdp), f32),
            pltpu.VMEM((fsdp, 8, width // fsdp), f32),
            pltpu.VMEM((tp, 8, 128), f32),
            pltpu.VMEM((tp, 8, 128), f32),
            dma((4, chunks, 3)), dma((4, chunks, 3)),
            dma((6, chunks, 3)), dma((6, chunks, 3)),
            dma((2,)), dma((2, fsdp)), dma((2, fsdp)),
            dma((2, tp)), dma((2, tp)),
            dma((fsdp,)), dma((fsdp,)), dma((tp,)), dma((tp,)),
        ],
        compiler_params=pltpu.CompilerParams(
            collective_id=number, has_side_effects=True, vmem_limit_bytes=61 << 20
        ),
        name="backward",
    )(
        d_rows, heads_out, query, keys, values, log_total, cos, sin, segments.reshape(1, -1),
        segments.reshape(-1, 1), normed, qkv, out, shared_up, shared_down, hidden, grad, gain, sums,
    )


def attend_kernel(tp, heads, halved, *refs):
    parts = len(halved)
    hidden_ref, gain_ref, grad_ref, seg_row_ref, seg_col_ref, cos_ref, sin_ref = refs[:7]
    pieces, refs = refs[7 : 7 + parts], refs[7 + parts :]
    rows_out, grads_ref, q_ref, k_ref, v_ref, lt_ref, heads_ref, part_ref = refs[:8]
    fulls_out, refs = refs[8 : 8 + parts], refs[8 + parts :]
    rows_ref, fulls, refs = refs[0], refs[1 : 1 + parts], refs[1 + parts :]
    (
        l_sem, e_sem, z_send, z_recv, g_send, g_recv, p_send, p_recv, gp_send, gp_recv,
    ) = refs
    me, rank = place()
    f32 = jnp.float32
    bf16 = jnp.bfloat16
    rows, width = hidden_ref.shape
    length = rows * tp

    greet(me, rank, tp)

    def along_z(spot, sends, recvs, block, to_right):
        way = 0 if to_right else 1
        return pltpu.make_async_remote_copy(
            src_ref=spot,
            dst_ref=spot,
            send_sem=sends.at[way, block],
            recv_sem=recvs.at[way, block],
            device_id=(me, rank + 1 if to_right else rank - 1),
            device_id_type=MESH,
        )

    def row_z(block, to_right):
        spot = rows_ref.at[pl.ds(block * rows, rows)]
        return along_z(spot, z_send, z_recv, block, to_right)

    def grad_z(block, to_right):
        return along_z(grad_region(me, block), g_send, g_recv, block, to_right)

    def z_start(copy):
        @pl.when(rank < tp - 1)
        def _():
            copy(rank, True).start()

        @pl.when(rank > 0)
        def _():
            copy(rank, False).start()

    def z_step(copy, step, then=None):
        @pl.when(rank >= step)
        def _():
            copy(rank - step, True).wait_recv()

            @pl.when(rank < tp - 1)
            def _():
                copy(rank - step, True).start()

            if then is not None:
                then(rank - step)

        @pl.when(rank + step < tp)
        def _():
            copy(rank + step, False).wait_recv()

            @pl.when(rank > 0)
            def _():
                copy(rank + step, False).start()

            if then is not None:
                then(rank + step)

    def z_end(copy):
        for block in range(tp):

            @pl.when((block <= rank) & (rank < tp - 1))
            def _():
                copy(block, True).wait_send()

            @pl.when((block >= rank) & (rank > 0))
            def _():
                copy(block, False).wait_send()

    def region(i, owner_bits, start=0, count=None):
        size = pieces[i].shape[0]
        count = size if count is None else count
        return fulls[i].at[pl.ds(plane_peer(me, owner_bits) * size + start, count)]

    def across(i, bit, owner_bits, slot, start=0, count=None):
        spot = region(i, owner_bits, start, count)
        return pltpu.make_async_remote_copy(
            src_ref=pieces[i] if owner_bits == 0 else spot,
            dst_ref=spot,
            send_sem=p_send.at[slot, i],
            recv_sem=p_recv.at[slot, i],
            device_id=(flipped(me, bit), rank),
            device_id_type=MESH,
        )

    def to_core(q, i):
        return across(i, 1, 2 * q, q)

    def own_x(i):
        return across(i, 2, 0, 4)

    def own_y(i):
        return across(i, 4, 0, 5)

    def x_to_y(i):
        size = pieces[i].shape[0]
        return across(i, 4, 2, 6, 0, size // 2 if halved[i] else size)

    def y_to_x(i):
        size = pieces[i].shape[0]
        return across(i, 2, 4, 7, size // 2, size // 2)

    def local(i):
        return pltpu.make_async_copy(pieces[i], region(i, 0), l_sem.at[i])

    def export(i):
        return pltpu.make_async_copy(fulls[i], fulls_out[i], e_sem.at[i])

    def forward(i):
        own_x(i).wait_recv()
        x_to_y(i).start()
        to_core(1, i).start()
        own_y(i).wait_recv()
        if halved[i]:
            y_to_x(i).start()
        to_core(2, i).start()

    def finish(i):
        x_to_y(i).wait_recv()
        if halved[i]:
            y_to_x(i).wait_recv()
        to_core(3, i).start()

    def arrived(i):
        local(i).wait()
        for q in range(4):
            to_core(q, i).wait_recv()
        export(i).start()

    order = [rank]
    for bit in (1, 2):
        order = order + [flipped(one, bit) for one in order]

    def grad_region(pack, block, start=0, count=None):
        count = rows if count is None else count
        return grads_ref.at[pl.ds(pack * length + block * rows + start, count)]

    def grad_across(bit, pack_bits, block, slot, start=0, count=None):
        spot = grad_region(plane_peer(me, pack_bits), block, start, count)
        return pltpu.make_async_remote_copy(
            src_ref=spot,
            dst_ref=spot,
            send_sem=gp_send.at[slot, block],
            recv_sem=gp_recv.at[slot, block],
            device_id=(flipped(me, bit), rank),
            device_id_type=MESH,
        )

    def grad_core(q, block):
        return grad_across(1, 2 * q, block, q)

    def grad_x(block):
        return grad_across(2, 0, block, 4)

    def grad_y(block):
        return grad_across(4, 0, block, 5)

    def grad_x_to_y(block):
        return grad_across(4, 2, block, 6, 0, rows // 2)

    def grad_y_to_x(block):
        return grad_across(2, 4, block, 7, rows // 2, rows // 2)

    def grad_plane(block):
        grad_x(block).start()
        grad_y(block).start()
        grad_core(0, block).start()

    def grad_forward(block):
        grad_x(block).wait_recv()
        grad_x_to_y(block).start()
        grad_core(1, block).start()
        grad_y(block).wait_recv()
        grad_y_to_x(block).start()
        grad_core(2, block).start()

    def grad_finish(block):
        grad_x_to_y(block).wait_recv()
        grad_y_to_x(block).wait_recv()
        grad_core(3, block).start()

    def project(which):
        at = slice(which * heads * 128, (which + 1) * heads * 128)
        return jnp.dot(rows_ref[...], fulls[0][:, at], preferred_element_type=f32)

    def bias(which, head):
        line = which * heads + head
        size = pieces[3].shape[0]
        share = 128 // 8
        return jnp.concatenate(
            [fulls[3][owner * size + line : owner * size + line + 1, :share] for owner in range(8)],
            axis=1,
        )

    def rotated(columns):
        return columns * cos_ref[...] + pltpu.roll(columns, 64, 1) * sin_ref[...]

    def make_heads():
        for which, ref in ((0, q_ref), (1, k_ref), (2, v_ref)):
            all_heads = project(which)
            for head in range(heads):
                at = slice(head * 128, (head + 1) * 128)
                one = all_heads[:, at] + bias(which, head)
                if which < 2:
                    one = rotated(one)
                ref[:, at] = one.astype(bf16)

    def attend(head):
        at = slice(head * 128, (head + 1) * 128)
        scores = lax.dot_general(q_ref[:, at], k_ref[:, at], NT, preferred_element_type=f32)
        line = lax.broadcasted_iota(jnp.int32, (length, length), 0)
        column = lax.broadcasted_iota(jnp.int32, (length, length), 1)
        allowed = (line >= column) & (seg_col_ref[...] == seg_row_ref[...])
        scores = jnp.where(allowed, scores * 128 ** (-0.5), -1e30)
        peak = jnp.max(scores, axis=-1, keepdims=True)
        log_total = peak + jnp.log(jnp.sum(jnp.exp(scores - peak), axis=-1, keepdims=True))
        probs = jnp.exp(scores - log_total).astype(bf16)
        lane = lax.broadcasted_iota(jnp.int32, (length, 128), 1)
        before = jnp.zeros((length, 128), f32) if head == 0 else lt_ref[...]
        lt_ref[...] = jnp.where(lane == head, log_total, before)
        heads_ref[:, at] = jnp.dot(probs, v_ref[:, at], preferred_element_type=f32).astype(bf16)

    def project_out():
        size = pieces[1].shape[0]
        share = width // 8
        for owner in range(8):
            part_ref[:, owner * share : (owner + 1) * share] = jnp.dot(
                heads_ref[...],
                fulls[1][owner * size : (owner + 1) * size, :],
                preferred_element_type=f32,
            ).astype(bf16)

    for i in range(parts):
        own_x(i).start()
        own_y(i).start()
        to_core(0, i).start()
    hidden = hidden_ref[...].astype(f32)
    inverse = lax.rsqrt(jnp.mean(hidden * hidden, axis=-1, keepdims=True) + epsilon)
    own_rows = pl.ds(pl.multiple_of(rank * rows, rows), rows)
    rows_ref[own_rows, :] = (hidden * inverse * gain_ref[...]).astype(bf16)
    z_start(row_z)
    own_grad = pltpu.make_async_copy(grad_ref, grad_region(me, rank), l_sem.at[parts])
    own_grad.start()
    for i in range(parts):
        local(i).start()
    own_grad.wait()
    grad_plane(rank)
    z_step(row_z, 1)
    forward(0)
    z_step(row_z, 2)
    z_start(grad_z)
    for i in range(1, parts):
        forward(i)
    finish(0)
    z_step(row_z, 3)
    rows_export = pltpu.make_async_copy(rows_ref, rows_out, e_sem.at[parts])
    rows_export.start()
    for i in range(1, parts):
        finish(i)
    grad_forward(order[0])
    z_step(grad_z, 1, grad_plane)
    for i in range(parts):
        arrived(i)
    make_heads()
    grad_finish(order[0])
    z_step(grad_z, 2, grad_plane)
    attend(0)
    attend(1)
    grad_forward(order[1])
    z_step(grad_z, 3, grad_plane)
    for head in range(2, heads):
        attend(head)
    grad_finish(order[1])
    grad_forward(order[2])
    project_out()
    grad_finish(order[2])
    grad_forward(order[3])
    grad_finish(order[3])
    for block in order:
        for q in range(4):
            grad_core(q, block).wait_recv()

    rows_export.wait()
    for i in range(parts):
        export(i).wait()
        for q in range(4):
            to_core(q, i).wait_send()
        own_x(i).wait_send()
        own_y(i).wait_send()
        x_to_y(i).wait_send()
        if halved[i]:
            y_to_x(i).wait_send()
    for block in order:
        for q in range(4):
            grad_core(q, block).wait_send()
        for copy in (grad_x, grad_y, grad_x_to_y, grad_y_to_x):
            copy(block).wait_send()
    z_end(row_z)
    z_end(grad_z)


def attend_pack(hidden, gain, grad, segments, cos, sin, pieces, fsdp, tp, heads, number):
    rows, width = hidden.shape
    length = rows * tp
    parts = len(pieces)
    halved = [one.shape[0] >= 32 for one in pieces]
    bf16 = jnp.bfloat16
    f32 = jnp.float32
    dma = pltpu.SemaphoreType.DMA
    anywhere = pl.BlockSpec(memory_space=pl.ANY)
    vmem = pl.BlockSpec(memory_space=pltpu.VMEM)
    fulls = [(one.shape[0] * fsdp, one.shape[1]) for one in pieces]
    of_heads = jax.ShapeDtypeStruct((length, heads * 128), bf16)
    return pl.pallas_call(
        functools.partial(attend_kernel, tp, heads, halved),
        out_shape=[
            jax.ShapeDtypeStruct((length, width), bf16),
            jax.ShapeDtypeStruct((length * fsdp, width), bf16),
            of_heads,
            of_heads,
            of_heads,
            jax.ShapeDtypeStruct((length, 128), f32),
            of_heads,
            jax.ShapeDtypeStruct((length, width), bf16),
        ]
        + [jax.ShapeDtypeStruct(shape, one.dtype) for shape, one in zip(fulls, pieces)],
        in_specs=[vmem] * 7 + [anywhere] * parts,
        out_specs=[anywhere, anywhere] + [vmem] * 6 + [anywhere] * parts,
        scratch_shapes=[pltpu.VMEM((length, width), bf16)]
        + [pltpu.VMEM(shape, one.dtype) for shape, one in zip(fulls, pieces)]
        + [
            dma((parts + 1,)), dma((parts + 1,)),
            dma((2, tp)), dma((2, tp)), dma((2, tp)), dma((2, tp)),
            dma((8, parts)), dma((8, parts)), dma((8, tp)), dma((8, tp)),
        ],
        compiler_params=pltpu.CompilerParams(
            collective_id=number, has_side_effects=True, vmem_limit_bytes=48 << 20
        ),
        name="attend",
    )(
        hidden, gain, grad, segments.reshape(1, -1), segments.reshape(-1, 1), cos, sin,
        *pieces,
    )


def dense_plan(
    hidden_in,
    out_grad,
    segment_ids,
    expert_ids,
    route_weights,
    attn_gain,
    ffn_gain,
    qkv_weight,
    qkv_bias,
    out_weight,
    shared_gate_up,
    shared_down,
    shared_gate_vec,
    expert_gate_up,
    expert_down,
):
    every = ("fsdp", "tp")
    tp_rank = lax.axis_index("tp")
    experts = lax.axis_size("fsdp")
    packs = experts
    length = segment_ids.shape[1]
    own_rows = hidden_in.shape[0]
    own_units = shared_gate_up.shape[0]
    model_width = hidden_in.shape[1]
    bf16 = jnp.bfloat16
    f32 = jnp.float32

    expert_up = expert_gate_up[0]
    expert_dn = expert_down[0]
    expert_width = expert_up.shape[2]
    shared_width = shared_gate_up.shape[2] // experts

    chosen = expert_ids[:, :, None] == jnp.arange(experts, dtype=jnp.int32)
    table = jnp.sum(jnp.where(chosen, route_weights[:, :, None], 0.0), axis=1)
    local_heads = qkv_weight.shape[2]
    head_dim = qkv_weight.shape[3]
    cos_table, sin_table = rope_tables(length, head_dim)
    segments = segment_ids[0]
    hidden_float = hidden_in.astype(f32)
    attn_inverse = inverse_rms(hidden_float)
    bias_rows = 3 * local_heads
    bias_columns = qkv_bias.shape[2]
    bias_piece = jnp.pad(
        qkv_bias.reshape(bias_rows, bias_columns), ((0, 16 - bias_rows), (0, 128 - bias_columns))
    )
    heads_width = local_heads * head_dim
    up_pieces = shared_gate_up.reshape(own_units, 2, experts, shared_width).transpose(2, 1, 0, 3)
    cos_two = jnp.concatenate([cos_table[:, 0], cos_table[:, 0]], axis=1)
    sin_two = jnp.concatenate([-sin_table[:, 0], sin_table[:, 0]], axis=1)
    (
        normed_one,
        grad_all,
        query,
        keys,
        values,
        log_total,
        heads_out,
        projected,
        qkv_flat,
        out_pieces,
        tables,
        bias_pieces,
    ) = attend_pack(
        hidden_in,
        attn_gain[None],
        out_grad,
        segments,
        cos_two,
        sin_two,
        [qkv_weight.reshape(-1, 3 * heads_width), out_weight, table.T, bias_piece],
        experts,
        lax.axis_size("tp"),
        local_heads,
        4,
    )
    expert_scale = lax.dynamic_index_in_dim(
        tables.reshape(packs, experts, length), lax.axis_index("fsdp"), axis=1, keepdims=False
    ).reshape(-1)
    scales = expert_scale.reshape(packs, lax.axis_size("tp"), 2, own_rows // 2)
    scales = scales.transpose(0, 2, 1, 3).reshape(packs, 2, 1, length // 2)
    middle, normed_all, _, d_all, hidden_all, token_part, d_normed_two, lines = ffn(
        projected,
        hidden_in,
        ffn_gain[None],
        shared_gate_vec[None],
        scales,
        grad_all,
        expert_up.transpose(1, 0, 2),
        up_pieces,
        expert_dn,
        shared_down.reshape(experts, shared_width, -1),
        experts,
        lax.axis_size("tp"),
        1,
    )
    tokens = token_part.shape[0]
    middle = middle.reshape(own_rows, model_width)
    normed_all = normed_all.reshape(tokens, model_width)
    d_all = d_all.reshape(tokens, -1)
    hidden_all = hidden_all.reshape(tokens, -1)
    d_normed_two = d_normed_two.reshape(own_rows, model_width)
    lines = lax.dynamic_slice_in_dim(lines, tp_rank * (own_rows // 2), own_rows // 2, axis=2)
    extra_sum = lines.transpose(1, 0, 2).reshape(16, own_rows)
    ffn_inverse = inverse_rms(middle)
    normed_two_own = (middle * ffn_inverse * ffn_gain).astype(bf16)
    own_start = tp_rank * own_rows
    ids_own = lax.dynamic_slice_in_dim(expert_ids, own_start, own_rows)
    picked = ids_own[:, :, None] == jnp.arange(experts, dtype=jnp.int32)
    route_grad = jnp.sum(jnp.where(picked, extra_sum[:experts].T[:, None, :], 0.0), axis=-1)
    gate_grad = extra_sum[experts]
    own_gate = jax.nn.sigmoid(jnp.sum(normed_two_own.astype(f32) * shared_gate_vec, axis=-1))
    logit_grad = gate_grad * own_gate * (1.0 - own_gate)
    d_normed_two = d_normed_two + logit_grad[:, None] * shared_gate_vec
    g_gate_vec = jnp.sum(normed_two_own.astype(f32) * logit_grad[:, None], axis=0)
    hat_two = middle * ffn_inverse
    g_ffn_gain = jnp.sum(d_normed_two * hat_two, axis=0)
    middle_grad = out_grad.astype(f32) + norm_backward(d_normed_two, hat_two, ffn_inverse, ffn_gain)
    total, d_rows, g_expert_up, g_shared_up, g_expert_down, g_shared_down = outputs(
        token_part,
        middle_grad.astype(bf16),
        normed_all,
        d_all,
        hidden_all,
        grad_all,
        experts,
        lax.axis_size("tp"),
        expert_width,
        shared_width,
        2,
    )
    hidden_out = (middle + total).astype(bf16)
    g_qkv, g_out, g_bias, g_shared_up, g_shared_down, hidden_grad, gains = backward(
        d_rows,
        heads_out,
        query,
        keys,
        values,
        log_total,
        cos_two,
        sin_two,
        segments,
        normed_one,
        qkv_flat,
        out_pieces,
        g_shared_up,
        g_shared_down,
        hidden_in,
        middle_grad,
        attn_gain[None],
        jnp.stack([g_ffn_gain, g_gate_vec]),
        experts,
        lax.axis_size("tp"),
        local_heads,
        3,
    )
    share = model_width // (experts * lax.axis_size("tp"))
    g_bias = lax.dynamic_slice_in_dim(
        g_bias.reshape(32, 128)[:bias_rows], lax.axis_index("fsdp") * bias_columns, bias_columns, 1
    )
    return (
        hidden_out,
        hidden_grad,
        route_grad,
        gains[0, :share],
        gains[1, :share],
        g_qkv.reshape(-1, 3, local_heads, head_dim),
        g_bias.reshape(qkv_bias.shape),
        g_out.reshape(out_weight.shape[::-1]).T,
        g_shared_up.transpose(1, 0, 2),
        g_shared_down,
        gains[2, :share],
        g_expert_up.transpose(1, 0, 2)[None],
        g_expert_down[None],
    )


def on_device(*arrays):
    if lax.axis_size("fsdp") == 8 and lax.axis_size("tp") == 4 and arrays[3].shape[1] >= 3:
        return dense_plan(*arrays)
    return routed_plan(*arrays)


def solution(mesh):
    placed = (
        P(("fsdp", "tp"), None),
        P(("fsdp", "tp"), None),
        P("fsdp", None),
        P("fsdp", None),
        P("fsdp", None),
        P(),
        P(),
        P("fsdp", None, "tp", None),
        P(None, "tp", "fsdp"),
        P("tp", "fsdp"),
        P("fsdp", None, "tp"),
        P("tp", "fsdp"),
        P(),
        P("fsdp", None, None, "tp"),
        P("fsdp", "tp", None),
    )
    return jax.shard_map(
        on_device,
        mesh=mesh,
        in_specs=placed,
        out_specs=(
            P(("fsdp", "tp"), None),
            P(("fsdp", "tp"), None),
            P(("fsdp", "tp"), None),
            P(("fsdp", "tp")),
            P(("fsdp", "tp")),
            P("fsdp", None, "tp", None),
            P(None, "tp", "fsdp"),
            P("tp", "fsdp"),
            P("fsdp", None, "tp"),
            P("tp", "fsdp"),
            P(("fsdp", "tp")),
            P("fsdp", None, None, "tp"),
            P("fsdp", "tp", None),
        ),
        check_vma=False,
    )
```

```python
import functools

import jax
import jax.experimental.pallas as pl
import jax.experimental.pallas.tpu as pltpu
import jax.numpy as jnp
from jax import lax
from jax.sharding import PartitionSpec as P

epsilon = 1e-06


def rope_tables(length, head_dim):
    half_dim = head_dim // 2
    ratios = jnp.arange(half_dim, dtype=jnp.float32) * (2.0 / head_dim)
    frequency = jnp.exp(-jnp.log(10000.0) * ratios)
    angles = jnp.arange(length, dtype=jnp.float32)[:, None] * frequency[None, :]
    return (jnp.cos(angles)[:, None, :], jnp.sin(angles)[:, None, :])


def rotate(tensor, cos_table, sin_table):
    half_dim = tensor.shape[-1] // 2
    front_half = tensor[..., :half_dim]
    back_half = tensor[..., half_dim:]
    return jnp.concatenate(
        [
            front_half * cos_table - back_half * sin_table,
            back_half * cos_table + front_half * sin_table,
        ],
        axis=-1,
    )


def unrotate(tensor, cos_table, sin_table):
    half_dim = tensor.shape[-1] // 2
    front_half = tensor[..., :half_dim]
    back_half = tensor[..., half_dim:]
    return jnp.concatenate(
        [
            front_half * cos_table + back_half * sin_table,
            back_half * cos_table - front_half * sin_table,
        ],
        axis=-1,
    )


def silu_parts(gate_in):
    sigmoid_value = jax.nn.sigmoid(gate_in)
    return (gate_in * sigmoid_value, sigmoid_value * (1.0 + gate_in * (1.0 - sigmoid_value)))


def slot_table(route_ids, experts, capacity):
    flat_ids = route_ids.reshape(-1)
    onehot = (flat_ids[:, None] == jnp.arange(experts, dtype=jnp.int32)[None, :]).astype(jnp.int32)
    before = jnp.cumsum(onehot, axis=0, dtype=jnp.int32) - onehot
    ranks = jnp.sum(before * onehot, axis=1, dtype=jnp.int32)
    places = flat_ids * capacity + ranks
    filler = jnp.arange(flat_ids.shape[0], dtype=jnp.int32) + 1
    slot_rows = jnp.zeros((experts * capacity,), jnp.int32).at[places].set(filler)
    return (places.reshape(route_ids.shape), slot_rows.reshape(experts, capacity))


def inverse_rms(tensor):
    return lax.rsqrt(jnp.mean(tensor * tensor, axis=-1, keepdims=True) + epsilon)


def norm_backward(d_normed, hat_rows, inverse, gain_vec):
    d_hat = d_normed * gain_vec
    return inverse * (d_hat - hat_rows * jnp.mean(d_hat * hat_rows, axis=-1, keepdims=True))


def masked_scores(query, keys, allowed, score_scale):
    raw = jnp.einsum("qhd,khd->hqk", query, keys, preferred_element_type=jnp.float32) * score_scale
    return jnp.where(allowed[None], raw, -1e30)


def spread(rows):
    return lax.all_gather(rows, "tp", axis=0, tiled=True)


def head_total(partial_rows):
    return lax.psum_scatter(
        partial_rows.astype(jnp.bfloat16), "tp", scatter_dimension=0, tiled=True
    ).astype(jnp.float32)


def to_experts(buffer):
    return lax.all_to_all(buffer, "fsdp", split_axis=0, concat_axis=0, tiled=True)


def from_experts(buffer):
    return lax.all_to_all(buffer, "fsdp", split_axis=0, concat_axis=0, tiled=True)


def routed_plan(
    hidden_in,
    out_grad,
    segment_ids,
    expert_ids,
    route_weights,
    attn_gain,
    ffn_gain,
    qkv_weight,
    qkv_bias,
    out_weight,
    shared_gate_up,
    shared_down,
    shared_gate_vec,
    expert_gate_up,
    expert_down,
):
    tp_rank = lax.axis_index("tp")
    experts = lax.axis_size("fsdp")
    length = segment_ids.shape[1]
    top_count = expert_ids.shape[1]
    capacity = 3 * length * top_count // (2 * experts)
    own_rows = hidden_in.shape[0]
    model_width = hidden_in.shape[1]
    qkv_full, bias_full, out_full, shared_full, shared_down_full = (
        lax.all_gather(qkv_weight, "fsdp", axis=0, tiled=True),
        lax.all_gather(qkv_bias.astype(jnp.bfloat16), "fsdp", axis=2, tiled=True).astype(
            qkv_bias.dtype
        ),
        lax.all_gather(out_weight, "fsdp", axis=1, tiled=True),
        lax.all_gather(shared_gate_up, "fsdp", axis=0, tiled=True),
        lax.all_gather(shared_down, "fsdp", axis=1, tiled=True),
    )
    local_heads = qkv_full.shape[2]
    head_dim = qkv_full.shape[3]
    score_scale = head_dim ** (-0.5)
    cos_table, sin_table = rope_tables(length, head_dim)
    positions = jnp.arange(length, dtype=jnp.int32)
    segments = segment_ids[0]
    allowed = (positions[:, None] >= positions[None, :]) & (segments[:, None] == segments[None, :])
    hidden_float = hidden_in.astype(jnp.float32)
    attn_inverse = inverse_rms(hidden_float)
    normed_one = spread((hidden_float * attn_inverse * attn_gain).astype(jnp.bfloat16))
    qkv_flat = qkv_full.reshape(model_width, -1)
    qkv = (
        jnp.dot(normed_one, qkv_flat, preferred_element_type=jnp.float32).reshape(
            length, 3, local_heads, head_dim
        )
        + bias_full
    )
    query = rotate(qkv[:, 0], cos_table, sin_table).astype(jnp.bfloat16)
    keys = rotate(qkv[:, 1], cos_table, sin_table).astype(jnp.bfloat16)
    values = qkv[:, 2].astype(jnp.bfloat16)
    scores = masked_scores(query, keys, allowed, score_scale)
    row_peak = jnp.max(scores, axis=-1, keepdims=True)
    log_total = row_peak + jnp.log(jnp.sum(jnp.exp(scores - row_peak), axis=-1, keepdims=True))
    probs_b = jnp.exp(scores - log_total).astype(jnp.bfloat16)
    heads_out = (
        jnp.einsum("hqk,khd->qhd", probs_b, values, preferred_element_type=jnp.float32)
        .astype(jnp.bfloat16)
        .reshape(length, -1)
    )
    middle = hidden_float + head_total(
        jnp.dot(heads_out, out_full, preferred_element_type=jnp.float32)
    )
    ffn_inverse = inverse_rms(middle)
    normed_two_own = (middle * ffn_inverse * ffn_gain).astype(jnp.bfloat16)
    normed_two = spread(normed_two_own)
    gate_prob = jax.nn.sigmoid(jnp.sum(normed_two.astype(jnp.float32) * shared_gate_vec, axis=-1))
    shared_flat = shared_full.reshape(model_width, -1)
    shared_width = shared_full.shape[2]
    shared_pre = jnp.dot(normed_two, shared_flat, preferred_element_type=jnp.float32)
    shared_act, shared_slope = silu_parts(shared_pre[:, :shared_width])
    shared_upper = shared_pre[:, shared_width:]
    shared_hidden = (shared_act * shared_upper).astype(jnp.bfloat16)
    shared_part = jnp.dot(shared_hidden, shared_down_full, preferred_element_type=jnp.float32)
    places, slot_rows = slot_table(expert_ids, experts, capacity)
    filled = slot_rows > 0
    route_index = jnp.maximum(slot_rows - 1, 0)
    source_rows = route_index // top_count
    flat_weights = route_weights.reshape(-1)
    slot_weights = jnp.where(filled, flat_weights[route_index], 0.0)
    send_rows = jnp.where(filled[:, :, None], normed_two[source_rows], jnp.zeros((), jnp.bfloat16))
    arrived = to_experts(send_rows).reshape(-1, model_width)
    expert_flat = expert_gate_up[0].reshape(model_width, -1)
    expert_width = expert_gate_up.shape[3]
    down_local = expert_down[0]
    expert_pre = jnp.dot(arrived, expert_flat, preferred_element_type=jnp.float32)
    expert_act, expert_slope = silu_parts(expert_pre[:, :expert_width])
    expert_upper = expert_pre[:, expert_width:]
    expert_hidden = (expert_act * expert_upper).astype(jnp.bfloat16)
    expert_part = jnp.dot(expert_hidden, down_local, preferred_element_type=jnp.float32).astype(
        jnp.bfloat16
    )
    returned = from_experts(expert_part.reshape(experts, capacity, model_width)).reshape(
        experts * capacity, model_width
    )
    picked = returned[places].astype(jnp.float32)
    token_term = gate_prob[:, None] * shared_part + jnp.sum(
        route_weights[:, :, None] * picked, axis=1
    )
    own_extra = 0.0
    total = (
        lax.psum_scatter(
            token_term.astype(jnp.bfloat16), "tp", scatter_dimension=0, tiled=True
        ).astype(jnp.float32)
        + own_extra
    )
    hidden_out = (middle + total).astype(jnp.bfloat16)
    grad_rows = spread(out_grad)
    grad_float = grad_rows.astype(jnp.float32)
    gate_part = jnp.sum(grad_float * shared_part, axis=-1)
    scaled_grad = (gate_prob[:, None] * grad_float).astype(jnp.bfloat16)
    shared_d_hidden = jnp.dot(scaled_grad, shared_down_full.T, preferred_element_type=jnp.float32)
    shared_d_cat = jnp.concatenate(
        [
            (shared_d_hidden * shared_upper * shared_slope).astype(jnp.bfloat16),
            (shared_d_hidden * shared_act).astype(jnp.bfloat16),
        ],
        axis=1,
    )
    g_shared_down = jnp.dot(shared_hidden.T, scaled_grad, preferred_element_type=jnp.float32)
    g_shared_gate_up = jnp.dot(
        normed_two.T, shared_d_cat, preferred_element_type=jnp.float32
    ).reshape(shared_full.shape)
    d_normed_part = jnp.dot(shared_d_cat, shared_flat.T, preferred_element_type=jnp.float32)
    expert_grad_in = (slot_weights[:, :, None] * grad_float[source_rows]).astype(jnp.bfloat16)
    arrived_grad = to_experts(expert_grad_in).reshape(-1, model_width)
    back_act, back_slope, back_upper, back_hidden = (
        expert_act,
        expert_slope,
        expert_upper,
        expert_hidden,
    )
    expert_d_hidden = jnp.dot(arrived_grad, down_local.T, preferred_element_type=jnp.float32)
    expert_d_cat = jnp.concatenate(
        [
            (expert_d_hidden * back_upper * back_slope).astype(jnp.bfloat16),
            (expert_d_hidden * back_act).astype(jnp.bfloat16),
        ],
        axis=1,
    )
    g_expert_down = jnp.dot(back_hidden.T, arrived_grad, preferred_element_type=jnp.float32)[None]
    g_expert_gate_up = jnp.dot(arrived.T, expert_d_cat, preferred_element_type=jnp.float32).reshape(
        expert_gate_up.shape
    )
    expert_d_part = jnp.dot(expert_d_cat, expert_flat.T, preferred_element_type=jnp.float32).astype(
        jnp.bfloat16
    )
    route_part = jnp.sum(grad_float[:, None, :] * picked, axis=-1)
    returned_grad = from_experts(expert_d_part.reshape(experts, capacity, model_width)).reshape(
        experts * capacity, model_width
    )
    d_normed_part = d_normed_part + jnp.sum(returned_grad[places].astype(jnp.float32), axis=1)
    d_normed_two, route_grad, gate_grad = (
        lax.psum_scatter(
            d_normed_part.astype(jnp.bfloat16), "tp", scatter_dimension=0, tiled=True
        ).astype(jnp.float32),
        lax.psum_scatter(
            route_part.astype(jnp.bfloat16), "tp", scatter_dimension=0, tiled=True
        ).astype(jnp.float32),
        lax.psum_scatter(
            gate_part.astype(jnp.bfloat16), "tp", scatter_dimension=0, tiled=True
        ).astype(jnp.float32),
    )
    own_gate = lax.dynamic_slice_in_dim(gate_prob, tp_rank * own_rows, own_rows)
    logit_grad = gate_grad * own_gate * (1.0 - own_gate)
    d_normed_two = d_normed_two + logit_grad[:, None] * shared_gate_vec
    g_gate_vec = jnp.sum(normed_two_own.astype(jnp.float32) * logit_grad[:, None], axis=0)
    hat_two = middle * ffn_inverse
    g_ffn_gain = jnp.sum(d_normed_two * hat_two, axis=0)
    middle_grad = out_grad.astype(jnp.float32) + norm_backward(
        d_normed_two, hat_two, ffn_inverse, ffn_gain
    )
    d_rows = spread(middle_grad.astype(jnp.bfloat16))
    g_out = jnp.dot(heads_out.T, d_rows, preferred_element_type=jnp.float32)
    d_heads = (
        jnp.dot(d_rows, out_full.T, preferred_element_type=jnp.float32)
        .astype(jnp.bfloat16)
        .reshape(length, local_heads, head_dim)
    )
    heads_three = heads_out.reshape(length, local_heads, head_dim)
    scores_again = masked_scores(query, keys, allowed, score_scale)
    probs_full = jnp.exp(scores_again - log_total)
    probs_again = probs_full.astype(jnp.bfloat16)
    d_values = jnp.einsum("hqk,qhd->khd", probs_again, d_heads, preferred_element_type=jnp.float32)
    d_probs = jnp.einsum("qhd,khd->hqk", d_heads, values, preferred_element_type=jnp.float32)
    delta = jnp.sum(d_heads.astype(jnp.float32) * heads_three.astype(jnp.float32), axis=-1)
    d_scores = (probs_full * (d_probs - delta.T[:, :, None])).astype(jnp.bfloat16)
    d_query = (
        jnp.einsum("hqk,khd->qhd", d_scores, keys, preferred_element_type=jnp.float32) * score_scale
    )
    d_keys = (
        jnp.einsum("hqk,qhd->khd", d_scores, query, preferred_element_type=jnp.float32)
        * score_scale
    )
    d_qkv = jnp.stack(
        [unrotate(d_query, cos_table, sin_table), unrotate(d_keys, cos_table, sin_table), d_values],
        axis=1,
    )
    g_bias = jnp.sum(d_qkv, axis=0)
    d_qkv_b = d_qkv.astype(jnp.bfloat16).reshape(length, -1)
    g_qkv = jnp.dot(normed_one.T, d_qkv_b, preferred_element_type=jnp.float32).reshape(
        qkv_full.shape
    )
    d_normed_one = head_total(jnp.dot(d_qkv_b, qkv_flat.T, preferred_element_type=jnp.float32))
    hat_one = hidden_float * attn_inverse
    g_attn_gain = jnp.sum(d_normed_one * hat_one, axis=0)
    hidden_grad = middle_grad + norm_backward(d_normed_one, hat_one, attn_inverse, attn_gain)
    g_qkv, g_bias, g_out, g_shared_gate_up, g_shared_down = (
        lax.psum_scatter(
            g_qkv.astype(jnp.bfloat16), "fsdp", scatter_dimension=0, tiled=True
        ).astype(jnp.float32),
        lax.psum_scatter(
            g_bias.astype(jnp.bfloat16), "fsdp", scatter_dimension=2, tiled=True
        ).astype(jnp.float32),
        lax.psum_scatter(
            g_out.astype(jnp.bfloat16), "fsdp", scatter_dimension=1, tiled=True
        ).astype(jnp.float32),
        lax.psum_scatter(
            g_shared_gate_up.astype(jnp.bfloat16), "fsdp", scatter_dimension=0, tiled=True
        ).astype(jnp.float32),
        lax.psum_scatter(
            g_shared_down.astype(jnp.bfloat16), "fsdp", scatter_dimension=1, tiled=True
        ).astype(jnp.float32),
    )
    g_attn_gain, g_ffn_gain, g_gate_vec = (
        lax.psum_scatter(g_attn_gain, ("fsdp", "tp"), scatter_dimension=0, tiled=True),
        lax.psum_scatter(g_ffn_gain, ("fsdp", "tp"), scatter_dimension=0, tiled=True),
        lax.psum_scatter(g_gate_vec, ("fsdp", "tp"), scatter_dimension=0, tiled=True),
    )
    return (
        hidden_out,
        hidden_grad,
        route_grad,
        g_attn_gain,
        g_ffn_gain,
        g_qkv,
        g_bias,
        g_out,
        g_shared_gate_up,
        g_shared_down,
        g_gate_vec,
        g_expert_gate_up,
        g_expert_down,
    )


MESH = pl.DeviceIdType.MESH


def flipped(index, bit):
    return index + bit - 2 * bit * ((index // bit) % 2)


def place():
    me = lax.axis_index("fsdp")
    rank = lax.axis_index("tp")
    return me, rank


def greet(me, rank, tp):
    barrier = pltpu.get_barrier_semaphore()
    for bit in (1, 2, 4):
        pl.semaphore_signal(
            barrier, inc=1, device_id=(flipped(me, bit), rank), device_id_type=MESH
        )

    @pl.when(rank > 0)
    def _():
        pl.semaphore_signal(barrier, inc=1, device_id=(me, rank - 1), device_id_type=MESH)

    @pl.when(rank < tp - 1)
    def _():
        pl.semaphore_signal(barrier, inc=1, device_id=(me, rank + 1), device_id_type=MESH)

    left = (rank + tp - 1) // tp
    right = (2 * (tp - 1) - rank) // tp
    pl.semaphore_wait(barrier, 3 + left + right)


def plane_peer(me, bits):
    for one in (1, 2, 4):
        if bits & one:
            me = flipped(me, one)
    return me


def greet_plane(me, rank, tp):
    barrier = pltpu.get_barrier_semaphore()
    for bits in range(1, 8):
        pl.semaphore_signal(
            barrier, inc=1, device_id=(plane_peer(me, bits), rank), device_id_type=MESH
        )

    @pl.when(rank > 0)
    def _():
        pl.semaphore_signal(barrier, inc=1, device_id=(me, rank - 1), device_id_type=MESH)

    @pl.when(rank < tp - 1)
    def _():
        pl.semaphore_signal(barrier, inc=1, device_id=(me, rank + 1), device_id_type=MESH)

    left = (rank + tp - 1) // tp
    right = (2 * (tp - 1) - rank) // tp
    pl.semaphore_wait(barrier, 7 + left + right)


UNIT = 640
SHARED = 384
NT = (((1,), (1,)), ((), ()))


def ffn_kernel(tp, expert_width, shared_width, *refs):
    part_ref, hidden_ref, gain_ref, vec_ref, scale_ref, grads_ref = refs[:6]
    expert_up, up_ref, expert_down, down_ref = refs[6:10]
    middle_ref, all_ref, up_in, d_ref, hid_ref, y_ref, dsum_ref, esum_ref = refs[10:18]
    (
        x_all, g_buf, dh_buf, d_buf, stage, acc, diag_in, last_in, z_in, both_buf, down_buf,
        eu_buf, su_buf, stage_e, acc_e, other_e, diag_e, last_e, z_in_e,
        w_sem, dn_sem, g_sem, x_sem, d_sem, h_sem, y_sem, f_sem, f_send, f_recv,
        az_send, az_recv, ap_send, ap_recv, s_send, s_recv,
        c_send, c_recv, ce_send, ce_recv, p_send, p_recv, pe_send, pe_recv,
        z_send, z_recv, ze_send, ze_recv,
    ) = refs[18:]
    me, rank = place()
    greet_plane(me, rank, tp)
    f32 = jnp.float32
    bf16 = jnp.bfloat16
    subs, rows, width = hidden_ref.shape
    tile = tp * rows
    pack_rows = subs * tile
    packs = x_all.shape[0]
    near = rank // 2
    order = [rank]
    for bit in (1, 2):
        order = order + [flipped(one, bit) for one in order]
    blocks = [3 * (1 - near), 2 - near, flipped(rank, 1), rank]
    core_of, x_of, y_of = me % 2, (me // 2) % 2, me // 4

    def pack_of(bits):
        return (
            4 * ((y_of + bits // 4) % 2)
            + 2 * ((x_of + (bits // 2) % 2) % 2)
            + (core_of + bits % 2) % 2
        )

    def add(ref, spot, one):
        ref[spot] = (ref[spot].astype(f32) + one.astype(f32)).astype(ref.dtype)

    def remote(src, dst, send, recv, bit):
        return pltpu.make_async_remote_copy(
            src_ref=src,
            dst_ref=dst,
            send_sem=send,
            recv_sem=recv,
            device_id=(flipped(me, bit), rank),
            device_id_type=MESH,
        )

    def remote_z(src, dst, send, recv, right):
        return pltpu.make_async_remote_copy(
            src_ref=src,
            dst_ref=dst,
            send_sem=send,
            recv_sem=recv,
            device_id=(me, rank + 1 if right else rank - 1),
            device_id_type=MESH,
        )

    def gather_z(block, sub, right):
        way = 0 if right else 1
        ref = x_all.at[me, block, sub]
        return remote_z(
            ref, ref, az_send.at[way, block, sub], az_recv.at[way, block, sub], right
        )

    def gather(bit, pack_bits, block, sub, slot, start=0, count=None):
        count = rows if count is None else count
        ref = x_all.at[pack_of(pack_bits), block, sub, pl.ds(start, count)]
        return remote(ref, ref, ap_send.at[slot, block, sub], ap_recv.at[slot, block, sub], bit)

    def to_core(q, block, sub):
        return gather(1, 2 * q, block, sub, q)

    def own_x(block, sub):
        return gather(2, 0, block, sub, 4)

    def own_y(block, sub):
        return gather(4, 0, block, sub, 5)

    def x_to_y(block, sub):
        return gather(4, 2, block, sub, 6, 0, rows // 2)

    def y_to_x(block, sub):
        return gather(2, 4, block, sub, 7, rows // 2, rows // 2)

    def start_plane(block, sub):
        own_x(block, sub).start()
        own_y(block, sub).start()
        to_core(0, block, sub).start()

    def start_rows(sub):
        @pl.when(rank < tp - 1)
        def _():
            gather_z(rank, sub, True).start()

        @pl.when(rank > 0)
        def _():
            gather_z(rank, sub, False).start()

        start_plane(rank, sub)

    def forward(place_in, sub):
        block = order[place_in]
        own_x(block, sub).wait_recv()
        x_to_y(block, sub).start()
        to_core(1, block, sub).start()
        own_y(block, sub).wait_recv()
        y_to_x(block, sub).start()
        to_core(2, block, sub).start()

    def finish(place_in, sub):
        block = order[place_in]
        x_to_y(block, sub).wait_recv()
        y_to_x(block, sub).wait_recv()
        to_core(3, block, sub).start()

    def z_step(step, sub):
        @pl.when(rank >= step)
        def _():
            block = rank - step
            gather_z(block, sub, True).wait_recv()

            @pl.when(rank < tp - 1)
            def _():
                gather_z(block, sub, True).start()

            start_plane(block, sub)

        @pl.when(rank + step < tp)
        def _():
            block = rank + step
            gather_z(block, sub, False).wait_recv()

            @pl.when(rank > 0)
            def _():
                gather_z(block, sub, False).start()

            start_plane(block, sub)

    def control(i):
        steps = {
            1: [(forward, 3, 0)],
            2: [(forward, 0, 1), (finish, 2, 0)],
            3: [(z_step, 2, 1)],
            4: [(finish, 3, 0), (forward, 1, 1)],
            5: [(z_step, 3, 1)],
            6: [(finish, 0, 1)],
            7: [(forward, 2, 1)],
            8: [(finish, 1, 1)],
            9: [(forward, 3, 1)],
            10: [(finish, 2, 1)],
            11: [(finish, 3, 1)],
        }
        for at, todo in steps.items():

            @pl.when(i == at)
            def _():
                for act, what, sub in todo:
                    act(what, sub)

    up_rows = up_ref.shape[2]
    span = down_ref.shape[2]

    def up_to(bits):
        return pltpu.make_async_remote_copy(
            src_ref=up_ref.at[plane_peer(me, bits)],
            dst_ref=up_in.at[:, pl.ds(pl.multiple_of(me * up_rows, up_rows), up_rows)],
            send_sem=s_send.at[0, bits],
            recv_sem=s_recv.at[0, bits],
            device_id=(plane_peer(me, bits), rank),
            device_id_type=MESH,
        )

    def down_spot():
        return down_buf.at[
            pl.ds(SHARED, shared_width), pl.ds(pl.multiple_of(me * span, span), span)
        ]

    def down_to(bits):
        return pltpu.make_async_remote_copy(
            src_ref=down_ref.at[plane_peer(me, bits)],
            dst_ref=down_spot(),
            send_sem=s_send.at[1, bits],
            recv_sem=s_recv.at[1, bits],
            device_id=(plane_peer(me, bits), rank),
            device_id_type=MESH,
        )

    def core(q, s):
        return remote(stage.at[s], acc.at[q, s], c_send.at[q, s], c_recv.at[q, s], 1)

    def core_e(q):
        return remote(stage_e.at[q], other_e.at[q], ce_send.at[q], ce_recv.at[q], 1)

    low, high = pl.ds(0, tp // 2), pl.ds(tp // 2, tp // 2)

    def across(bit, src, dst, slot, s):
        return remote(src, dst, p_send.at[slot, s], p_recv.at[slot, s], bit)

    def diag_x(s):
        return across(2, acc.at[3, s, low], diag_in.at[s, 0], 0, s)

    def diag_y(s):
        return across(4, acc.at[3, s, high], diag_in.at[s, 1], 1, s)

    def direct_x(s):
        return across(2, acc.at[1, s, low], last_in.at[s, 0, low], 2, s)

    def direct_y(s):
        return across(4, acc.at[2, s, high], last_in.at[s, 1, high], 3, s)

    def summed_x(s):
        return across(2, acc.at[1, s, high], last_in.at[s, 0, high], 4, s)

    def summed_y(s):
        return across(4, acc.at[2, s, low], last_in.at[s, 1, low], 5, s)

    def diag_lines():
        return remote(acc_e.at[3], diag_e, pe_send.at[0], pe_recv.at[0], 2)

    def direct_lines():
        return remote(acc_e.at[1], last_e.at[0], pe_send.at[1], pe_recv.at[1], 2)

    def summed_lines():
        return remote(acc_e.at[2], last_e.at[1], pe_send.at[2], pe_recv.at[2], 4)

    def along_z(j, s, right):
        way = 0 if right else 1
        block = blocks[j]
        return remote_z(
            acc.at[0, s, block],
            z_in.at[way, block, s],
            z_send.at[way, block, s],
            z_recv.at[way, block, s],
            right,
        )

    def lines_z(right):
        way = 0 if right else 1
        return remote_z(
            acc_e.at[1 + way], z_in_e.at[way], ze_send.at[way], ze_recv.at[way], right
        )

    def second(s):
        diag_x(s).wait_recv()
        add(acc, (2, s, low), diag_in[s, 0])
        summed_y(s).start()
        diag_y(s).wait_recv()
        add(acc, (1, s, high), diag_in[s, 1])
        summed_x(s).start()

    def third(j, s):
        block = blocks[j]
        if j == 0:
            direct_x(s).wait_recv()
            direct_y(s).wait_recv()
            summed_x(s).wait_recv()
            summed_y(s).wait_recv()
        total = (
            acc[0, s, block].astype(f32)
            + last_in[s, 0, block].astype(f32)
            + last_in[s, 1, block].astype(f32)
        )
        if j < tp - 1:
            acc[0, s, block] = total.astype(bf16)

            @pl.when((block > rank) & (rank > 0))
            def _():
                along_z(j, s, True).wait_recv()
                add(acc, (0, s, block), z_in[0, block, s])

            @pl.when((block < rank) & (rank < tp - 1))
            def _():
                along_z(j, s, False).wait_recv()
                add(acc, (0, s, block), z_in[1, block, s])

            @pl.when(block > rank)
            def _():
                along_z(j, s, True).start()

            @pl.when(block < rank)
            def _():
                along_z(j, s, False).start()
        else:
            dsum_ref[s] = total

            @pl.when(rank > 0)
            def _():
                along_z(j, s, True).wait_recv()
                dsum_ref[s] += z_in[0, block, s].astype(f32)

            @pl.when(rank < tp - 1)
            def _():
                along_z(j, s, False).wait_recv()
                dsum_ref[s] += z_in[1, block, s].astype(f32)

    def sum_lines():
        direct_lines().wait_recv()
        summed_lines().wait_recv()
        direct_lines().wait_send()
        summed_lines().wait_send()
        own = acc_e[0] + last_e[0] + last_e[1]
        esum_ref[...] = own
        acc_e[1] = own
        acc_e[2] = own

        @pl.when(rank > 0)
        def _():
            lines_z(True).wait_recv()
            esum_ref[...] += z_in_e[0]
            acc_e[1] = own + z_in_e[0]

        @pl.when(rank < tp - 1)
        def _():
            lines_z(True).start()
            lines_z(False).wait_recv()
            esum_ref[...] += z_in_e[1]
            acc_e[2] = own + z_in_e[1]

        @pl.when(rank > 0)
        def _():
            lines_z(False).start()

    def front_load(block, s):
        return pltpu.make_async_copy(
            part_ref.at[block, s], stage.at[s, block], f_sem.at[block, s]
        )

    def front_z(j, s, right):
        way = 0 if right else 1
        block = blocks[j]
        return remote_z(
            stage.at[s, block],
            z_in.at[way, block, s],
            f_send.at[way, block, s],
            f_recv.at[way, block, s],
            right,
        )

    def front(j, s):
        block = blocks[j]
        front_load(block, s).wait()
        if j < tp - 1:

            @pl.when((block > rank) & (rank > 0))
            def _():
                front_z(j, s, True).wait_recv()
                add(stage, (s, block), z_in[0, block, s])

            @pl.when((block < rank) & (rank < tp - 1))
            def _():
                front_z(j, s, False).wait_recv()
                add(stage, (s, block), z_in[1, block, s])

            @pl.when(block > rank)
            def _():
                front_z(j, s, True).start()

            @pl.when(block < rank)
            def _():
                front_z(j, s, False).start()
        else:
            middle_ref[s] = hidden_ref[s].astype(f32) + stage[s, block].astype(f32)

            @pl.when(rank > 0)
            def _():
                front_z(j, s, True).wait_recv()
                middle_ref[s] += z_in[0, block, s].astype(f32)

            @pl.when(rank < tp - 1)
            def _():
                front_z(j, s, False).wait_recv()
                middle_ref[s] += z_in[1, block, s].astype(f32)

            middle = middle_ref[s]
            mean = jnp.mean(middle * middle, axis=-1, keepdims=True)
            normed = middle * lax.rsqrt(mean + epsilon) * gain_ref[...]
            x_all[me, rank, s] = normed.astype(bf16)
            start_rows(s)

    cut = eu_buf.shape[1]
    cuts = width // cut
    units = SHARED + shared_width

    def weight_loads(part, n, slot):
        at = pl.ds(pl.multiple_of(n * cut, cut), cut)
        return (
            pltpu.make_async_copy(expert_up.at[part, at], eu_buf.at[slot], w_sem.at[0, slot]),
            pltpu.make_async_copy(up_in.at[part, at], su_buf.at[slot], w_sem.at[1, slot]),
        )

    def start_loads(part, n, slot):
        of_expert, of_shared = weight_loads(part, n, slot)
        of_expert.start()

        @pl.when(n == me)
        def _():
            own = up_ref.at[me, part]
            pltpu.make_async_copy(own, su_buf.at[slot], w_sem.at[1, slot]).start()

        @pl.when(n != me)
        def _():
            of_shared.start()

    def lay_out(part):
        base = part * UNIT

        def body(n, carry):
            slot = n % 2

            @pl.when(n + 1 < cuts)
            def _():
                start_loads(part, n + 1, 1 - slot)

            for copy in weight_loads(part, n, slot):
                copy.wait()
            at = pl.ds(pl.multiple_of(n * cut, cut), cut)
            both_buf[at, base : base + UNIT] = jnp.zeros((cut, UNIT), bf16)
            both_buf[at, base : base + expert_width] = eu_buf[slot]
            both_buf[at, base + SHARED : base + units] = su_buf[slot]
            return carry

        start_loads(part, 0, 0)
        lax.fori_loop(0, cuts, body, 0)

    down_loads = (
        pltpu.make_async_copy(expert_down, down_buf.at[pl.ds(0, expert_width)], dn_sem.at[0]),
        pltpu.make_async_copy(down_ref.at[me], down_spot(), dn_sem.at[1]),
    )

    def grad_load(n, slot):
        at = pl.ds(n * tile, tile)
        return pltpu.make_async_copy(grads_ref.at[at], g_buf.at[slot], g_sem.at[slot])

    def hidden_grads(first, last):
        def body(n, carry):
            slot = n % 2

            @pl.when(n + 1 < 2 * packs)
            def _():
                grad_load(n + 1, 1 - slot).start()

            grad_load(n, slot).wait()
            d_hidden = lax.dot_general(
                g_buf[slot], down_buf[...], NT, preferred_element_type=f32
            ).astype(bf16)
            dh_buf[n // 2, pl.ds(n % 2 * 2, 2)] = d_hidden.reshape(2, subs, rows, UNIT)
            return carry

        lax.fori_loop(first, last, body, 0)

    def tile_of(i):
        s = i // 8
        q = order_of(s, i // 2 % 4)
        o = i % 2
        return q, o, s, pack_of(2 * q + 1 - o)

    def order_of(s, r):
        return r + s * (r // 2) * (1 - 2 * (r % 2))

    def d_store(i):
        q, o, s, pack = tile_of(i)
        return pltpu.make_async_copy(d_buf.at[i % 2], d_ref.at[pack, :, s], d_sem.at[i % 2])

    def x_store(i):
        q, o, s, pack = tile_of(i)
        return pltpu.make_async_copy(x_all.at[pack, :, s], all_ref.at[pack, :, s], x_sem.at[i % 2])

    def one_tile(i, carry):
        q, o, s, pack = tile_of(i)
        slot = i % 2

        @pl.when(o == 0)
        def _():
            for block in range(tp):
                ref = x_all.at[pack, block, s]
                remote(
                    ref, ref, ap_send.at[q, block, s], ap_recv.at[q, block, s], 1
                ).wait_recv()

        @pl.when(i >= 2)
        def _():
            d_store(i - 2).wait()
            x_store(i - 2).wait()

        x_store(i).start()
        x = x_all[pack, :, s].reshape(tile, width)
        pre = jnp.dot(x, both_buf[...], preferred_element_type=f32)
        gate, upper = pre[:, :UNIT], pre[:, UNIT:]
        lane = lax.broadcasted_iota(jnp.int32, (1, UNIT), 1)
        logit = jnp.sum(x.astype(f32) * vec_ref[...], axis=-1, keepdims=True)
        gate_prob = 1.0 / (1.0 + jnp.exp(-logit))
        own_scale = jnp.broadcast_to(scale_ref[pack, s], (128, tile)).T[:, :1]
        scale = jnp.where(lane < SHARED, own_scale, gate_prob)
        sigmoid = 1.0 / (1.0 + jnp.exp(-gate))
        act = gate * sigmoid
        slope = sigmoid * (1.0 + gate * (1.0 - sigmoid))
        hidden = act * upper
        d_hidden = dh_buf[pack, :, s].reshape(tile, UNIT).astype(f32)
        line = lax.broadcasted_iota(jnp.int32, (16, UNIT), 0)
        unit = lax.broadcasted_iota(jnp.int32, (16, UNIT), 1)
        of_expert = (line == me) & (unit < SHARED)
        of_shared = (line == 8) & (unit >= SHARED)
        pick = jnp.where(of_expert | of_shared, 1.0, 0.0).astype(bf16)
        lines = lax.dot_general(
            pick, (d_hidden * hidden).astype(bf16), NT, preferred_element_type=f32
        )
        dh_buf[pack, :, s] = (hidden * scale).astype(bf16).reshape(tp, rows, UNIT)
        d_scaled = d_hidden * scale
        d_gate = (d_scaled * upper * slope).astype(bf16)
        d_upper = (d_scaled * act).astype(bf16)
        d_buf[slot, :, :, :UNIT] = d_gate.reshape(tp, rows, UNIT)
        d_buf[slot, :, :, UNIT:] = d_upper.reshape(tp, rows, UNIT)
        control(i)
        d_both = d_buf[slot].reshape(tile, 2 * UNIT)
        d_rows = lax.dot_general(d_both, both_buf[...], NT, preferred_element_type=f32)
        d_rows = d_rows.reshape(tp, rows, width)
        d_store(i).start()

        @pl.when(o == 0)
        def _():
            @pl.when(i % 8 >= 2)
            def _():
                core(order_of(s, i // 2 % 4 - 1), s).wait_send()

            stage[s] = d_rows.astype(bf16)
            stage_e[q, s] = lines
            core(q, s).start()

            @pl.when(s == 1)
            def _():
                core_e(q).start()

        @pl.when(o == 1)
        def _():
            core(q, s).wait_recv()
            add(acc, (q, s), d_rows)
            acc_e[q, s] = lines

            @pl.when(s == 1)
            def _():
                core_e(q).wait_recv()
                acc_e[q] = acc_e[q] + other_e[q]

                @pl.when(q == 1)
                def _():
                    direct_lines().start()

                @pl.when(q == 3)
                def _():
                    diag_lines().start()

            @pl.when(q == 1)
            def _():
                direct_x(s).start()

            @pl.when(q == 2)
            def _():
                direct_y(s).start()

            @pl.when(q == 3)
            def _():
                diag_x(s).start()
                diag_y(s).start()

            @pl.when(i == 9)
            def _():
                second(0)

            @pl.when(i == 15)
            def _():
                third(0, 0)

        return carry

    def y_store(n, slot):
        return pltpu.make_async_copy(
            g_buf.at[slot], y_ref.at[pl.ds(n * tile, tile)], y_sem.at[slot]
        )

    def outputs(first, last):
        def body(n, carry):
            slot = n % 2

            @pl.when(n >= 2)
            def _():
                y_store(n - 2, slot).wait()

            hidden = dh_buf[n // 2, pl.ds(n % 2 * 2, 2)].reshape(tile, UNIT)
            g_buf[slot] = jnp.dot(hidden, down_buf[...], preferred_element_type=f32).astype(bf16)
            y_store(n, slot).start()
            return carry

        lax.fori_loop(first, last, body, 0)

    for bits in (6, 7, 2, 4, 3, 5, 1):
        down_to(bits).start()
    for bits in (6, 7, 2, 4, 3, 5, 1):
        up_to(bits).start()
    grad_load(0, 0).start()
    for s in range(subs):
        for block in blocks:
            front_load(block, s).start()
    down_buf[expert_width:SHARED, :] = jnp.zeros((SHARED - expert_width, width), bf16)
    down_buf[units:, :] = jnp.zeros((UNIT - units, width), bf16)
    for copy in down_loads:
        copy.start()
    ends = (rank == 0) | (rank == tp - 1)
    inner = (rank > 0) & (rank < tp - 1)
    front(0, 0)
    front(1, 0)
    front(2, 0)

    @pl.when(ends)
    def _():
        front(0, 1)

    for copy in down_loads:
        copy.wait()
    for bits in range(1, 8):
        down_to(bits).wait_recv()

    @pl.when(ends)
    def _():
        hidden_grads(0, 6)

    front(3, 0)

    @pl.when(ends)
    def _():
        front(1, 1)
        front(2, 1)

    @pl.when(inner)
    def _():
        front(0, 1)

    z_step(1, 0)
    forward(0, 0)

    @pl.when(inner)
    def _():
        hidden_grads(0, 4)

    z_step(2, 0)

    @pl.when(inner)
    def _():
        front(1, 1)
        hidden_grads(4, 6)
        front(2, 1)

    for bits in range(1, 8):
        up_to(bits).wait_recv()
    lay_out(0)
    z_step(3, 0)
    forward(1, 0)
    finish(0, 0)
    front(3, 1)
    lay_out(1)
    forward(2, 0)
    z_step(1, 1)
    hidden_grads(6, 11)
    finish(1, 0)
    hidden_grads(11, 2 * packs)
    for s in range(subs):
        for j in range(tp - 1):
            block = blocks[j]

            @pl.when(block > rank)
            def _():
                front_z(j, s, True).wait_send()

            @pl.when(block < rank)
            def _():
                front_z(j, s, False).wait_send()

    lax.fori_loop(0, 16, one_tile, 0)
    hidden_store = pltpu.make_async_copy(dh_buf, hid_ref, h_sem)
    hidden_store.start()
    diag_lines().wait_recv()
    acc_e[2] = acc_e[2] + diag_e[...]
    summed_lines().start()
    outputs(0, 2)
    second(1)
    third(1, 0)
    outputs(2, 4)
    third(2, 0)
    outputs(4, 6)
    third(3, 0)
    sum_lines()
    outputs(6, 8)
    third(0, 1)
    outputs(8, 10)
    third(1, 1)
    outputs(10, 12)
    third(2, 1)
    outputs(12, 14)
    third(3, 1)
    outputs(14, 16)
    hidden_store.wait()
    for n in (14, 15):
        y_store(n, n % 2).wait()
        d_store(n).wait()
        x_store(n).wait()
    core(3, 0).wait_send()
    core(2, 1).wait_send()
    diag_lines().wait_send()
    for q in range(4):
        core_e(q).wait_send()
    for bits in range(1, 8):
        up_to(bits).wait_send()
        down_to(bits).wait_send()
    for s in range(subs):
        for copy in (diag_x, diag_y, direct_x, direct_y, summed_x, summed_y):
            copy(s).wait_send()
        for block in range(tp):
            for q in range(4):
                to_core(q, block, s).wait_send()
            for copy in (own_x, own_y, x_to_y, y_to_x):
                copy(block, s).wait_send()

            @pl.when((block <= rank) & (rank < tp - 1))
            def _():
                gather_z(block, s, True).wait_send()

            @pl.when((block >= rank) & (rank > 0))
            def _():
                gather_z(block, s, False).wait_send()

        for j in range(tp - 1):
            block = blocks[j]

            @pl.when(block > rank)
            def _():
                along_z(j, s, True).wait_send()

            @pl.when(block < rank)
            def _():
                along_z(j, s, False).wait_send()

    @pl.when(rank < tp - 1)
    def _():
        lines_z(True).wait_send()

    @pl.when(rank > 0)
    def _():
        lines_z(False).wait_send()


def ffn(
    part, hidden, gain, vec, scale, grads, expert_up, shared_up, expert_down, shared_down,
    fsdp, tp, collective_id,
):
    own, width = hidden.shape
    subs = 2
    rows = own // subs
    tile = tp * rows
    tokens = fsdp * tp * own
    expert_width, shared_width = expert_down.shape[0], shared_down.shape[1]
    bf16 = jnp.bfloat16
    f32 = jnp.float32
    dma = pltpu.SemaphoreType.DMA
    anywhere = pl.BlockSpec(memory_space=pl.ANY)
    vmem = pl.BlockSpec(memory_space=pltpu.VMEM)
    all_rows = (fsdp, tp, subs, rows)
    lines = (subs, 16, tile)
    return pl.pallas_call(
        functools.partial(ffn_kernel, tp, expert_width, shared_width),
        out_shape=[
            jax.ShapeDtypeStruct((subs, rows, width), f32),
            jax.ShapeDtypeStruct(all_rows + (width,), bf16),
            jax.ShapeDtypeStruct((2, width, shared_width), bf16),
            jax.ShapeDtypeStruct(all_rows + (2 * UNIT,), bf16),
            jax.ShapeDtypeStruct(all_rows + (UNIT,), bf16),
            jax.ShapeDtypeStruct((tokens, width), bf16),
            jax.ShapeDtypeStruct((subs, rows, width), f32),
            jax.ShapeDtypeStruct(lines, f32),
        ],
        in_specs=[anywhere] + [vmem] * 4 + [anywhere] * 5,
        out_specs=[vmem] + [anywhere] * 5 + [vmem] * 2,
        scratch_shapes=[
            pltpu.VMEM(all_rows + (width,), bf16),
            pltpu.VMEM((2, tile, width), bf16),
            pltpu.VMEM(all_rows + (UNIT,), bf16),
            pltpu.VMEM((2, tp, rows, 2 * UNIT), bf16),
            pltpu.VMEM((subs, tp, rows, width), bf16),
            pltpu.VMEM((4, subs, tp, rows, width), bf16),
            pltpu.VMEM((subs, 2, tp // 2, rows, width), bf16),
            pltpu.VMEM((subs, 2, tp, rows, width), bf16),
            pltpu.VMEM((2, tp, subs, rows, width), bf16),
            pltpu.VMEM((width, 2 * UNIT), bf16),
            pltpu.VMEM((UNIT, width), bf16),
            pltpu.VMEM((2, width // 8, expert_width), bf16),
            pltpu.VMEM((2, width // 8, shared_width), bf16),
            pltpu.VMEM((4,) + lines, f32),
            pltpu.VMEM((4,) + lines, f32),
            pltpu.VMEM((4,) + lines, f32),
            pltpu.VMEM(lines, f32),
            pltpu.VMEM((2,) + lines, f32),
            pltpu.VMEM((2,) + lines, f32),
            dma((2, 2)), dma((2,)), dma((2,)), dma((2,)), dma((2,)), dma, dma((2,)),
            dma((tp, subs)), dma((2, tp, subs)), dma((2, tp, subs)),
            dma((2, tp, subs)), dma((2, tp, subs)), dma((8, tp, subs)), dma((8, tp, subs)),
            dma((2, fsdp)), dma((2, fsdp)),
            dma((4, subs)), dma((4, subs)), dma((4,)), dma((4,)),
            dma((6, subs)), dma((6, subs)), dma((3,)), dma((3,)),
            dma((2, tp, subs)), dma((2, tp, subs)), dma((2,)), dma((2,)),
        ],
        compiler_params=pltpu.CompilerParams(
            collective_id=collective_id, has_side_effects=True, vmem_limit_bytes=63 << 20
        ),
        name="ffn",
    )(
        part.reshape(tp, subs, rows, width), hidden.reshape(subs, rows, width), gain, vec,
        scale, grads, expert_up, shared_up, expert_down, shared_down,
    )


TN = (((0,), (0,)), ((), ()))
SUB = 2


def outputs_kernel(tp, expert_width, shared_width, *refs):
    y_ref, x_ref, d_ref, h_ref, g_ref = refs[:5]
    middle_ref, dsum_ref, gate_ref, og_ref, gain_ref, vec_ref = refs[5:11]
    hidden_ref, grad_ref, sums_ref, rows_ref, ge_ref, gs_ref, de_ref, ds_ref = refs[11:19]
    (
        total_ref, own_ref, mine, other, diag_in, last_in, z_in, d_buf, h_buf, col_buf, ge_buf, gs_buf, de_buf, ds_buf,
        l_sem, c_send, c_recv, p_send, p_recv, z_send, z_recv, a_sem, a_send, a_recv,
        w_sem, col_sem, out_sem,
    ) = refs[19:]
    me, rank = place()
    greet(me, rank, tp)
    f32 = jnp.float32
    bf16 = jnp.bfloat16
    rows = total_ref.shape[0]
    cut = rows // SUB
    half = cut // 2
    near = rank // 2
    blocks = [3 * (1 - near), 2 - near, flipped(rank, 1), rank]
    pieces = range(tp * SUB)
    packs = [me, flipped(me, 2), flipped(me, 4), flipped(flipped(me, 2), 4)]
    low, high = pl.ds(0, half), pl.ds(half, half)

    def gather_z(block, right):
        way = 0 if right else 1
        spot = rows_ref.at[pl.ds(block * rows, rows)]
        return pltpu.make_async_remote_copy(
            src_ref=spot,
            dst_ref=spot,
            send_sem=a_send.at[way, block],
            recv_sem=a_recv.at[way, block],
            device_id=(me, rank + 1 if right else rank - 1),
            device_id_type=MESH,
        )

    def gather_step(step):
        @pl.when(rank >= step)
        def _():
            gather_z(rank - step, True).wait_recv()

            @pl.when(rank < tp - 1)
            def _():
                gather_z(rank - step, True).start()

        @pl.when(rank + step < tp)
        def _():
            gather_z(rank + step, False).wait_recv()

            @pl.when(rank > 0)
            def _():
                gather_z(rank + step, False).start()

    def spot_of(j):
        return blocks[j // SUB] * SUB + j % SUB

    def region(pack, j):
        return y_ref.at[pl.ds((pack * tp * SUB + spot_of(j)) * cut, cut)]

    def local(k, j):
        return pltpu.make_async_copy(region(packs[k], j), mine.at[k, j], l_sem.at[k, j])

    def core(k, j):
        return pltpu.make_async_remote_copy(
            src_ref=region(flipped(packs[k], 1), j),
            dst_ref=other.at[k, j],
            send_sem=c_send.at[k, j],
            recv_sem=c_recv.at[k, j],
            device_id=(flipped(me, 1), rank),
            device_id_type=MESH,
        )

    def across(bit, src, dst, slot, j):
        return pltpu.make_async_remote_copy(
            src_ref=src,
            dst_ref=dst,
            send_sem=p_send.at[slot, j],
            recv_sem=p_recv.at[slot, j],
            device_id=(flipped(me, bit), rank),
            device_id_type=MESH,
        )

    def diag_x(j):
        return across(2, mine.at[3, j, low], diag_in.at[j, 0], 0, j)

    def diag_y(j):
        return across(4, mine.at[3, j, high], diag_in.at[j, 1], 1, j)

    def direct_x(j):
        return across(2, mine.at[1, j, low], last_in.at[j, 0, low], 2, j)

    def direct_y(j):
        return across(4, mine.at[2, j, high], last_in.at[j, 1, high], 3, j)

    def summed_x(j):
        return across(2, mine.at[1, j, high], last_in.at[j, 0, high], 4, j)

    def summed_y(j):
        return across(4, mine.at[2, j, low], last_in.at[j, 1, low], 5, j)

    def along_z(j, right):
        way = 0 if right else 1
        spot = spot_of(j)
        return pltpu.make_async_remote_copy(
            src_ref=mine.at[0, j],
            dst_ref=z_in.at[way, spot],
            send_sem=z_send.at[way, spot],
            recv_sem=z_recv.at[way, spot],
            device_id=(me, rank + 1 if right else rank - 1),
            device_id_type=MESH,
        )

    def add(ref, spot, one):
        ref[spot] = (ref[spot].astype(f32) + one.astype(f32)).astype(ref.dtype)

    def first(j):
        for k in (3, 2, 1, 0):
            core(k, j).wait_recv()
            local(k, j).wait()
            add(mine, (k, j), other[k, j])
            if k == 3:
                diag_x(j).start()
                diag_y(j).start()
            if k == 2:
                direct_y(j).start()
            if k == 1:
                direct_x(j).start()

    def second(j):
        diag_x(j).wait_recv()
        add(mine, (2, j, low), diag_in[j, 0])
        summed_y(j).start()
        diag_y(j).wait_recv()
        add(mine, (1, j, high), diag_in[j, 1])
        summed_x(j).start()

    def third(j):
        block = blocks[j // SUB]
        spot = spot_of(j)
        direct_x(j).wait_recv()
        direct_y(j).wait_recv()
        summed_x(j).wait_recv()
        summed_y(j).wait_recv()
        total = mine[0, j].astype(f32) + last_in[j, 0].astype(f32) + last_in[j, 1].astype(f32)
        if j < (tp - 1) * SUB:
            mine[0, j] = total.astype(bf16)

            @pl.when((block > rank) & (rank > 0))
            def _():
                along_z(j, True).wait_recv()
                add(mine, (0, j), z_in[0, spot])

            @pl.when((block < rank) & (rank < tp - 1))
            def _():
                along_z(j, False).wait_recv()
                add(mine, (0, j), z_in[1, spot])

            @pl.when(block > rank)
            def _():
                along_z(j, True).start()

            @pl.when(block < rank)
            def _():
                along_z(j, False).start()
        else:
            own_rows = pl.ds(j % SUB * cut, cut)
            total_ref[own_rows] = total

            @pl.when(rank > 0)
            def _():
                along_z(j, True).wait_recv()
                total_ref[own_rows] += z_in[0, spot].astype(f32)

            @pl.when(rank < tp - 1)
            def _():
                along_z(j, False).wait_recv()
                total_ref[own_rows] += z_in[1, spot].astype(f32)

    span = col_buf.shape[2]
    steps = x_ref.shape[1] // span
    units = SHARED + shared_width

    def columns(n, slot, of_x):
        ref = x_ref if of_x else g_ref
        return pltpu.make_async_copy(
            ref.at[:, pl.ds(pl.multiple_of(n * span, span), span)],
            col_buf.at[slot],
            col_sem.at[slot],
        )

    def up_stores(n, slot):
        at = pl.ds(pl.multiple_of(n * span, span), span)
        return (
            pltpu.make_async_copy(ge_buf.at[slot], ge_ref.at[:, at], out_sem.at[0, slot]),
            pltpu.make_async_copy(gs_buf.at[slot], gs_ref.at[:, at], out_sem.at[1, slot]),
        )

    def down_stores(n, slot):
        at = pl.ds(pl.multiple_of(n * span, span), span)
        return (
            pltpu.make_async_copy(de_buf.at[slot], de_ref.at[:, at], out_sem.at[2, slot]),
            pltpu.make_async_copy(ds_buf.at[slot], ds_ref.at[n], out_sem.at[3, slot]),
        )

    def up_step(n, carry):
        slot = n % 2

        @pl.when(n + 1 < steps)
        def _():
            columns(n + 1, 1 - slot, True).start()

        @pl.when(n + 1 == steps)
        def _():
            columns(0, 1 - slot, False).start()

        columns(n, slot, True).wait()

        @pl.when(n >= 2)
        def _():
            for copy in up_stores(n - 2, slot):
                copy.wait()

        grads = lax.dot_general(col_buf[slot], d_buf[...], TN, preferred_element_type=f32)
        for part in range(2):
            base = part * UNIT
            ge_buf[slot, part] = grads[:, base : base + expert_width]
            gs_buf[slot, part] = grads[:, base + SHARED : base + units].astype(bf16)
        for copy in up_stores(n, slot):
            copy.start()
        return carry

    def down_step(n, carry):
        slot = n % 2

        @pl.when(n + 1 < steps)
        def _():
            columns(n + 1, 1 - slot, False).start()

        columns(n, slot, False).wait()

        @pl.when(n >= 2)
        def _():
            for copy in down_stores(n - 2, slot):
                copy.wait()

        grads = lax.dot_general(h_buf[...], col_buf[slot], TN, preferred_element_type=f32)
        de_buf[slot] = grads[:expert_width]
        ds_buf[slot] = grads[SHARED:units].astype(bf16)
        for copy in down_stores(n, slot):
            copy.start()
        return carry

    def norm_back():
        middle = middle_ref[...]
        gain, vec = gain_ref[...], vec_ref[...]
        inverse = lax.rsqrt(jnp.mean(middle * middle, axis=-1, keepdims=True) + epsilon)
        hat = middle * inverse
        normed = (hat * gain).astype(bf16).astype(f32)
        logit = jnp.sum(normed * vec, axis=-1, keepdims=True)
        gate_prob = 1.0 / (1.0 + jnp.exp(-logit))
        logit_grad = gate_ref[...] * gate_prob * (1.0 - gate_prob)
        d_normed = dsum_ref[...] + logit_grad * vec
        sums_ref[0:1] = jnp.sum(d_normed * hat, axis=0, keepdims=True)
        sums_ref[1:2] = jnp.sum(normed * logit_grad, axis=0, keepdims=True)
        d_hat = d_normed * gain
        mean = jnp.mean(d_hat * hat, axis=-1, keepdims=True)
        grad = og_ref[...].astype(f32) + inverse * (d_hat - hat * mean)
        grad_ref[...] = grad
        own_ref[...] = grad.astype(bf16)

    load_d = pltpu.make_async_copy(d_ref, d_buf, w_sem.at[0])
    load_h = pltpu.make_async_copy(h_ref, h_buf, w_sem.at[1])
    own = pltpu.make_async_copy(own_ref, rows_ref.at[pl.ds(rank * rows, rows)], a_sem)
    for j in pieces:
        for k in (3, 2, 1, 0):
            core(k, j).start()
            local(k, j).start()
    load_d.start()
    columns(0, 0, True).start()
    load_h.start()
    norm_back()
    own.start()
    own.wait()

    @pl.when(rank < tp - 1)
    def _():
        gather_z(rank, True).start()

    @pl.when(rank > 0)
    def _():
        gather_z(rank, False).start()

    first(0)
    first(1)
    load_d.wait()
    load_h.wait()
    for j in pieces:
        if j < len(pieces) // 2:
            lax.fori_loop(2 * j, 2 * j + 2, up_step, 0)
        else:
            later = j - len(pieces) // 2
            lax.fori_loop(2 * later, 2 * later + 2, down_step, 0)
        second(j)
        if j + 2 < len(pieces):
            first(j + 2)
        if j in (1, 3, 5):
            gather_step((j + 1) // 2)
        if j >= 2:
            third(j - 2)
    third(len(pieces) - 2)
    third(len(pieces) - 1)
    hidden_ref[...] = (middle_ref[...] + total_ref[...]).astype(bf16)

    for n in (steps - 2, steps - 1):
        for copy in up_stores(n, n % 2) + down_stores(n, n % 2):
            copy.wait()
    for j in pieces:
        for k in range(4):
            core(k, j).wait_send()
        for copy in (diag_x, diag_y, direct_x, direct_y, summed_x, summed_y):
            copy(j).wait_send()
        block = blocks[j // SUB]
        if j < (tp - 1) * SUB:

            @pl.when(block > rank)
            def _():
                along_z(j, True).wait_send()

            @pl.when(block < rank)
            def _():
                along_z(j, False).wait_send()

    for block in range(tp):

        @pl.when((block <= rank) & (rank < tp - 1))
        def _():
            gather_z(block, True).wait_send()

        @pl.when((block >= rank) & (rank > 0))
        def _():
            gather_z(block, False).wait_send()


def outputs(
    y, x, d, h, g, middle, d_normed, gate_grad, out_grad, gain, vec,
    fsdp, tp, expert_width, shared_width, collective_id,
):
    rows, width = middle.shape
    tokens = y.shape[0]
    span = width // fsdp
    cut = rows // SUB
    bf16 = jnp.bfloat16
    f32 = jnp.float32
    dma = pltpu.SemaphoreType.DMA
    anywhere = pl.BlockSpec(memory_space=pl.ANY)
    return pl.pallas_call(
        functools.partial(outputs_kernel, tp, expert_width, shared_width),
        out_shape=[
            jax.ShapeDtypeStruct((rows, width), bf16),
            jax.ShapeDtypeStruct((rows, width), f32),
            jax.ShapeDtypeStruct((2, width), f32),
            jax.ShapeDtypeStruct((rows * tp, width), bf16),
            jax.ShapeDtypeStruct((2, width, expert_width), f32),
            jax.ShapeDtypeStruct((2, width, shared_width), bf16),
            jax.ShapeDtypeStruct((expert_width, width), f32),
            jax.ShapeDtypeStruct((fsdp, shared_width, span), bf16),
        ],
        in_specs=[anywhere] * 5 + [pl.BlockSpec(memory_space=pltpu.VMEM)] * 6,
        out_specs=[pl.BlockSpec(memory_space=pltpu.VMEM)] * 3 + [anywhere] * 5,
        scratch_shapes=[
            pltpu.VMEM((rows, width), f32),
            pltpu.VMEM((rows, width), bf16),
            pltpu.VMEM((4, tp * SUB, cut, width), bf16),
            pltpu.VMEM((4, tp * SUB, cut, width), bf16),
            pltpu.VMEM((tp * SUB, 2, cut // 2, width), bf16),
            pltpu.VMEM((tp * SUB, 2, cut, width), bf16),
            pltpu.VMEM((2, tp * SUB, cut, width), bf16),
            pltpu.VMEM((tokens, 2 * UNIT), bf16),
            pltpu.VMEM((tokens, UNIT), bf16),
            pltpu.VMEM((2, tokens, span), bf16),
            pltpu.VMEM((2, 2, span, expert_width), f32),
            pltpu.VMEM((2, 2, span, shared_width), bf16),
            pltpu.VMEM((2, expert_width, span), f32),
            pltpu.VMEM((2, shared_width, span), bf16),
            dma((4, tp * SUB)), dma((4, tp * SUB)), dma((4, tp * SUB)),
            dma((6, tp * SUB)), dma((6, tp * SUB)),
            dma((2, tp * SUB)), dma((2, tp * SUB)), dma, dma((2, tp)), dma((2, tp)),
            dma((2,)), dma((2,)), dma((4, 2)),
        ],
        compiler_params=pltpu.CompilerParams(
            collective_id=collective_id, has_side_effects=True, vmem_limit_bytes=60 << 20
        ),
        name="outputs",
    )(y, x, d, h, g, middle, d_normed, gate_grad, out_grad, gain, vec)


def backward_kernel(fsdp, tp, heads, *refs):
    parts = 3
    d_ref, ho_ref, q_ref, k_ref, v_ref, lt_ref, cos_ref, sin_ref = refs[:8]
    seg_row_ref, seg_col_ref, normed_in, qkv_in, out_in = refs[8:13]
    gs_ref, ds_ref, hidden_ref, grad_ref, gain_ref, sums_ref = refs[13:19]
    refs = refs[19:]
    outs, refs = refs[:parts], refs[parts:]
    gs_out, ds_out, hidden_grad_ref, gains_ref = refs[:4]
    refs = refs[4:]
    mine, other, diag_in, last_in = (refs[i * parts : (i + 1) * parts] for i in range(4))
    (
        normed_ref, qkv_ref, out_ref, in_sem, dh_buf, dqkv_buf, gs_in, ds_in, dn_buf, z_in, v_send, v_in, w_send, w_in,
        c_send, c_recv, p_send, p_recv, s_sem, s_send, s_recv,
        f_send, f_recv, v_ssem, v_rsem, w_ssem, w_rsem,
    ) = refs[4 * parts :]
    me, rank = place()
    f32 = jnp.float32
    bf16 = jnp.bfloat16
    rows, width = hidden_ref.shape
    near = rank // 2
    blocks = [3 * (1 - near), 2 - near, flipped(rank, 1), rank]
    packs = [me, flipped(me, 2), flipped(me, 4), flipped(flipped(me, 2), 4)]
    every = range(parts)
    chunks = outs[0].shape[0]
    sizes = [ref.shape[1] for ref in outs]
    low = [pl.ds(0, size // 2) for size in sizes]
    high = [pl.ds(size // 2, size // 2) for size in sizes]

    def plane(bits):
        peer = me
        for one in (1, 2, 4):
            if bits & one:
                peer = flipped(peer, one)
        return peer

    def line(bits):
        peer = rank
        for one in (1, 2):
            if bits & one:
                peer = flipped(peer, one)
        return peer

    barrier = pltpu.get_barrier_semaphore()
    for bits in range(1, fsdp):
        pl.semaphore_signal(
            barrier, inc=1, device_id=(plane(bits), rank), device_id_type=MESH
        )
    for bits in range(1, tp):
        pl.semaphore_signal(barrier, inc=1, device_id=(me, line(bits)), device_id_type=MESH)
    pl.semaphore_wait(barrier, fsdp - 1 + tp - 1)

    def add(ref, spot, one):
        ref[spot] = (ref[spot].astype(f32) + one.astype(f32)).astype(ref.dtype)

    core_of, x_of, y_of = me % 2, (me // 2) % 2, me // 4

    def pack_of(bits):
        return (
            4 * ((y_of + bits // 4) % 2)
            + 2 * ((x_of + (bits // 2) % 2) % 2)
            + (core_of + bits % 2) % 2
        )

    def core(k, j, i):
        return pltpu.make_async_remote_copy(
            src_ref=mine[i].at[pack_of(2 * k + 1), j],
            dst_ref=other[i].at[k, j],
            send_sem=c_send.at[k, j, i],
            recv_sem=c_recv.at[k, j, i],
            device_id=(flipped(me, 1), rank),
            device_id_type=MESH,
        )

    def across(bit, src, dst, slot, j, i):
        return pltpu.make_async_remote_copy(
            src_ref=src,
            dst_ref=dst,
            send_sem=p_send.at[slot, j, i],
            recv_sem=p_recv.at[slot, j, i],
            device_id=(flipped(me, bit), rank),
            device_id_type=MESH,
        )

    def diag_x(j, i):
        return across(2, mine[i].at[packs[3], j, low[i]], diag_in[i].at[j, 0], 0, j, i)

    def diag_y(j, i):
        return across(4, mine[i].at[packs[3], j, high[i]], diag_in[i].at[j, 1], 1, j, i)

    def direct_x(j, i):
        return across(2, mine[i].at[packs[1], j, low[i]], last_in[i].at[j, 0, low[i]], 2, j, i)

    def direct_y(j, i):
        return across(4, mine[i].at[packs[2], j, high[i]], last_in[i].at[j, 1, high[i]], 3, j, i)

    def summed_x(j, i):
        return across(2, mine[i].at[packs[1], j, high[i]], last_in[i].at[j, 0, high[i]], 4, j, i)

    def summed_y(j, i):
        return across(4, mine[i].at[packs[2], j, low[i]], last_in[i].at[j, 1, low[i]], 5, j, i)

    def send_piece(bits, i):
        k = bits // 2

        @pl.when(bits % 2 == 1)
        def _():
            for j in range(chunks):
                core(k, j, i).start()

        @pl.when(bits % 2 == 0)
        def _():
            for j in range(chunks):
                core(k, j, i).wait_recv()
                add(mine[i], (pack_of(bits), j), other[i][k, j])

            @pl.when(k == 3)
            def _():
                for j in range(chunks):
                    diag_x(j, i).start()
                    diag_y(j, i).start()

            @pl.when(k == 2)
            def _():
                for j in range(chunks):
                    direct_y(j, i).start()

            @pl.when(k == 1)
            def _():
                for j in range(chunks):
                    direct_x(j, i).start()

    def second(j):
        for i in every:
            diag_x(j, i).wait_recv()
            add(mine[i], (packs[2], j, low[i]), diag_in[i][j, 0])
            summed_y(j, i).start()
            diag_y(j, i).wait_recv()
            add(mine[i], (packs[1], j, high[i]), diag_in[i][j, 1])
            summed_x(j, i).start()

    def third(j):
        for i in every:
            direct_x(j, i).wait_recv()
            direct_y(j, i).wait_recv()
            summed_x(j, i).wait_recv()
            summed_y(j, i).wait_recv()
            outs[i][j] = (
                mine[i][me, j].astype(f32)
                + last_in[i][j, 0].astype(f32)
                + last_in[i][j, 1].astype(f32)
            )

    span = ds_ref.shape[2]

    def shared_up(bits):
        at = pl.ds(pl.multiple_of(plane(bits) * span, span), span)
        return pltpu.make_async_remote_copy(
            src_ref=gs_ref.at[:, at],
            dst_ref=gs_in.at[me],
            send_sem=s_send.at[0, bits],
            recv_sem=s_recv.at[0, bits],
            device_id=(plane(bits), rank),
            device_id_type=MESH,
        )

    def shared_down(bits):
        return pltpu.make_async_remote_copy(
            src_ref=ds_ref.at[plane(bits)],
            dst_ref=ds_in.at[me],
            send_sem=s_send.at[1, bits],
            recv_sem=s_recv.at[1, bits],
            device_id=(plane(bits), rank),
            device_id_type=MESH,
        )

    own_up = pltpu.make_async_copy(
        gs_ref.at[:, pl.ds(pl.multiple_of(me * span, span), span)], gs_in.at[me], s_sem.at[0]
    )
    own_down = pltpu.make_async_copy(ds_ref.at[me], ds_in.at[me], s_sem.at[1])

    def front_z(j, right):
        way = 0 if right else 1
        block = blocks[j]
        return pltpu.make_async_remote_copy(
            src_ref=dn_buf.at[block],
            dst_ref=z_in.at[way, block],
            send_sem=f_send.at[way, block],
            recv_sem=f_recv.at[way, block],
            device_id=(me, rank + 1 if right else rank - 1),
            device_id_type=MESH,
        )

    def front(j):
        block = blocks[j]
        if j < tp - 1:

            @pl.when((block > rank) & (rank > 0))
            def _():
                front_z(j, True).wait_recv()
                add(dn_buf, (block,), z_in[0, block])

            @pl.when((block < rank) & (rank < tp - 1))
            def _():
                front_z(j, False).wait_recv()
                add(dn_buf, (block,), z_in[1, block])

            @pl.when(block > rank)
            def _():
                front_z(j, True).start()

            @pl.when(block < rank)
            def _():
                front_z(j, False).start()
        else:
            hidden_grad_ref[...] = dn_buf[block].astype(f32)

            @pl.when(rank > 0)
            def _():
                front_z(j, True).wait_recv()
                hidden_grad_ref[...] += z_in[0, block].astype(f32)

            @pl.when(rank < tp - 1)
            def _():
                front_z(j, False).wait_recv()
                hidden_grad_ref[...] += z_in[1, block].astype(f32)

    share = width // fsdp
    part = share // tp

    def gains_plane(bits):
        return pltpu.make_async_remote_copy(
            src_ref=v_send.at[plane(bits)],
            dst_ref=v_in.at[me],
            send_sem=v_ssem.at[bits],
            recv_sem=v_rsem.at[bits],
            device_id=(plane(bits), rank),
            device_id_type=MESH,
        )

    def gains_line(bits):
        return pltpu.make_async_remote_copy(
            src_ref=w_send.at[line(bits)],
            dst_ref=w_in.at[rank],
            send_sem=w_ssem.at[bits],
            recv_sem=w_rsem.at[bits],
            device_id=(me, line(bits)),
            device_id_type=MESH,
        )

    length = d_ref.shape[0]
    cut = width // fsdp
    size = heads * 128
    scale = 128 ** (-0.5)

    def out_piece(n, carry):
        bits = fsdp - 1 - n
        pack = pack_of(bits)
        at = pl.ds(pl.multiple_of(pack * cut, cut), cut)
        piece = lax.dot_general(d_ref[:, at], ho_ref[...], TN, preferred_element_type=f32)
        mine[1][pack] = piece.astype(bf16).reshape(chunks, cut // chunks, size)
        send_piece(bits, 1)
        return carry

    def qkv_piece(n, carry):
        bits = fsdp - 1 - n
        pack = pack_of(bits)
        at = pl.ds(pl.multiple_of(pack * cut, cut), cut)
        piece = lax.dot_general(normed_ref[:, at], dqkv_buf[...], TN, preferred_element_type=f32)
        mine[0][pack] = piece.astype(bf16).reshape(chunks, cut // chunks, 3 * size)
        send_piece(bits, 0)
        return carry

    def head_grads():
        total = jnp.zeros((length, size), f32)
        for owner in range(fsdp):
            total = total + lax.dot_general(
                d_ref[:, owner * cut : (owner + 1) * cut],
                out_ref[owner * size : (owner + 1) * size, :],
                NT,
                preferred_element_type=f32,
            )
        dh_buf[...] = total.astype(bf16)

    def unrotated(columns):
        return columns * cos_ref[...] - pltpu.roll(columns, 64, 1) * sin_ref[...]

    def attend_back(head):
        at = slice(head * 128, (head + 1) * 128)
        query, keys, values = q_ref[:, at], k_ref[:, at], v_ref[:, at]
        d_head = dh_buf[:, at]
        scores = lax.dot_general(query, keys, NT, preferred_element_type=f32) * scale
        line = lax.broadcasted_iota(jnp.int32, (length, length), 0)
        column = lax.broadcasted_iota(jnp.int32, (length, length), 1)
        allowed = (line >= column) & (seg_col_ref[...] == seg_row_ref[...])
        probs = jnp.exp(jnp.where(allowed, scores, -1e30) - lt_ref[:, head : head + 1])
        d_values = lax.dot_general(probs.astype(bf16), d_head, TN, preferred_element_type=f32)
        d_probs = lax.dot_general(d_head, values, NT, preferred_element_type=f32)
        delta = jnp.sum(
            d_head.astype(f32) * ho_ref[:, at].astype(f32), axis=-1, keepdims=True
        )
        d_scores = (probs * (d_probs - delta)).astype(bf16)
        d_query = jnp.dot(d_scores, keys, preferred_element_type=f32) * scale
        d_keys = lax.dot_general(d_scores, query, TN, preferred_element_type=f32) * scale
        for which, grad in enumerate((unrotated(d_query), unrotated(d_keys), d_values)):
            base = which * size + head * 128
            dqkv_buf[:, base : base + 128] = grad.astype(bf16)
            here = which * heads + head
            mine[2][0, 0, here : here + 1] = jnp.sum(grad, axis=0, keepdims=True)

    def row_grads(half):
        at = pl.ds(pl.multiple_of(half * 2 * rows, 2 * rows), 2 * rows)
        grads = lax.dot_general(dqkv_buf[at, :], qkv_ref[...], NT, preferred_element_type=f32)
        dn_buf[pl.ds(2 * half, 2)] = grads.astype(bf16).reshape(2, rows, width)

    ends = (rank == 0) | (rank == tp - 1)
    for bits in (6, 7, 2, 4):
        shared_up(bits).start()
        shared_down(bits).start()
    own_up.start()
    own_down.start()
    loads = [
        pltpu.make_async_copy(src, dst, in_sem.at[i])
        for i, (src, dst) in enumerate(
            ((out_in, out_ref), (qkv_in, qkv_ref), (normed_in, normed_ref))
        )
    ]
    for load in loads:
        load.start()
    lax.fori_loop(0, fsdp, out_piece, 0)
    loads[0].wait()
    head_grads()
    mine[2][...] = jnp.zeros_like(mine[2])
    for head in range(heads):
        attend_back(head)
    loads[1].wait()
    row_grads(1 - near)

    @pl.when(ends)
    def _():
        front(0)
        front(1)

    row_grads(near)
    for owner in range(1, fsdp):
        mine[2][owner] = mine[2][0]
    loads[2].wait()
    lax.fori_loop(0, fsdp, qkv_piece, 0)
    for n in range(fsdp):
        send_piece(jnp.int32(fsdp - 1 - n), 2)

    @pl.when(jnp.logical_not(ends))
    def _():
        front(0)

    second(0)

    @pl.when(jnp.logical_not(ends))
    def _():
        front(1)

    second(1)
    for bits in (3, 5, 1):
        shared_up(bits).start()
        shared_down(bits).start()
    front(2)
    front(3)
    d_normed = hidden_grad_ref[...]
    hidden = hidden_ref[...].astype(f32)
    inverse = lax.rsqrt(jnp.mean(hidden * hidden, axis=-1, keepdims=True) + epsilon)
    hat = hidden * inverse
    v_send[...] = jnp.zeros_like(v_send)
    attn_gain = jnp.sum(d_normed * hat, axis=0, keepdims=True)
    for owner in range(fsdp):
        at = slice(owner * share, (owner + 1) * share)
        v_send[owner, 0:1] = attn_gain[:, at]
        v_send[owner, 1:3] = sums_ref[:, at]
    for bits in range(1, fsdp):
        gains_plane(bits).start()
    d_hat = d_normed * gain_ref[...]
    mean = jnp.mean(d_hat * hat, axis=-1, keepdims=True)
    hidden_grad_ref[...] = grad_ref[...] + inverse * (d_hat - hat * mean)
    third(0)
    total = v_send[me]
    for bits in range(1, fsdp):
        gains_plane(bits).wait_recv()
        total = total + v_in[plane(bits)]
    w_send[...] = jnp.zeros_like(w_send)
    for owner in range(tp):
        w_send[owner, :, :part] = total[:, owner * part : (owner + 1) * part]
    for bits in range(1, tp):
        gains_line(bits).start()
    third(1)
    own_up.wait()
    own_down.wait()
    for bits in range(1, fsdp):
        shared_up(bits).wait_recv()
        shared_down(bits).wait_recv()
    units = gs_in.shape[3]
    for owner in range(fsdp):
        at = slice(owner * units, (owner + 1) * units)
        gs_out[:, :, at] = gs_in[owner].astype(f32)
        ds_out[at] = ds_in[owner].astype(f32)
    total = w_send[rank]
    for bits in range(1, tp):
        gains_line(bits).wait_recv()
        total = total + w_in[line(bits)]
    gains_ref[...] = total

    for j in range(chunks):
        for i in every:
            for k in range(4):
                core(k, j, i).wait_send()
            for copy in (diag_x, diag_y, direct_x, direct_y, summed_x, summed_y):
                copy(j, i).wait_send()
    for bits in range(1, fsdp):
        shared_up(bits).wait_send()
        shared_down(bits).wait_send()
        gains_plane(bits).wait_send()
    for bits in range(1, tp):
        gains_line(bits).wait_send()
    for j in range(tp - 1):
        block = blocks[j]

        @pl.when(block > rank)
        def _():
            front_z(j, True).wait_send()

        @pl.when(block < rank)
        def _():
            front_z(j, False).wait_send()


def backward(
    d_rows, heads_out, query, keys, values, log_total, cos, sin, segments, normed, qkv, out,
    shared_up, shared_down, hidden, grad, gain, sums, fsdp, tp, heads, number,
):
    chunks = 2
    rows, width = hidden.shape
    length = rows * tp
    units = shared_up.shape[2]
    span = shared_down.shape[2]
    size = heads * 128
    bf16 = jnp.bfloat16
    f32 = jnp.float32
    shapes = [(width // (fsdp * chunks), 3 * size, bf16), (span // chunks, size, bf16), (16, 128, f32)]
    scratch = [pltpu.VMEM((fsdp, chunks, count, w), kind) for count, w, kind in shapes]
    scratch += [pltpu.VMEM((4, chunks, count, w), kind) for count, w, kind in shapes]
    scratch += [pltpu.VMEM((chunks, 2, count // 2, w), kind) for count, w, kind in shapes]
    scratch += [pltpu.VMEM((chunks, 2, count, w), kind) for count, w, kind in shapes]
    dma = pltpu.SemaphoreType.DMA
    anywhere = pl.BlockSpec(memory_space=pl.ANY)
    vmem = pl.BlockSpec(memory_space=pltpu.VMEM)
    out_shape = [jax.ShapeDtypeStruct((chunks, count, w), f32) for count, w, _ in shapes]
    out_shape += [
        jax.ShapeDtypeStruct((2, span, fsdp * units), f32),
        jax.ShapeDtypeStruct((fsdp * units, span), f32),
        jax.ShapeDtypeStruct((rows, width), f32),
        jax.ShapeDtypeStruct((8, 128), f32),
    ]
    return pl.pallas_call(
        functools.partial(backward_kernel, fsdp, tp, heads),
        out_shape=out_shape,
        in_specs=[vmem] * 10 + [anywhere] * 5 + [vmem] * 4,
        out_specs=[vmem] * len(out_shape),
        scratch_shapes=scratch
        + [
            pltpu.VMEM(normed.shape, bf16),
            pltpu.VMEM(qkv.shape, bf16),
            pltpu.VMEM(out.shape, bf16),
            dma((3,)),
            pltpu.VMEM((length, size), bf16),
            pltpu.VMEM((length, 3 * size), bf16),
            pltpu.VMEM((fsdp, 2, span, units), shared_up.dtype),
            pltpu.VMEM((fsdp, units, span), shared_down.dtype),
            pltpu.VMEM((tp, rows, width), bf16),
            pltpu.VMEM((2, tp, rows, width), bf16),
            pltpu.VMEM((fsdp, 8, width // fsdp), f32),
            pltpu.VMEM((fsdp, 8, width // fsdp), f32),
            pltpu.VMEM((tp, 8, 128), f32),
            pltpu.VMEM((tp, 8, 128), f32),
            dma((4, chunks, 3)), dma((4, chunks, 3)),
            dma((6, chunks, 3)), dma((6, chunks, 3)),
            dma((2,)), dma((2, fsdp)), dma((2, fsdp)),
            dma((2, tp)), dma((2, tp)),
            dma((fsdp,)), dma((fsdp,)), dma((tp,)), dma((tp,)),
        ],
        compiler_params=pltpu.CompilerParams(
            collective_id=number, has_side_effects=True, vmem_limit_bytes=61 << 20
        ),
        name="backward",
    )(
        d_rows, heads_out, query, keys, values, log_total, cos, sin, segments.reshape(1, -1),
        segments.reshape(-1, 1), normed, qkv, out, shared_up, shared_down, hidden, grad, gain, sums,
    )


def attend_kernel(tp, heads, halved, *refs):
    parts = len(halved)
    hidden_ref, gain_ref, grad_ref, seg_row_ref, seg_col_ref, cos_ref, sin_ref = refs[:7]
    pieces, refs = refs[7 : 7 + parts], refs[7 + parts :]
    rows_out, grads_ref, q_ref, k_ref, v_ref, lt_ref, heads_ref, part_ref = refs[:8]
    fulls_out, refs = refs[8 : 8 + parts], refs[8 + parts :]
    rows_ref, fulls, refs = refs[0], refs[1 : 1 + parts], refs[1 + parts :]
    (
        l_sem, e_sem, z_send, z_recv, g_send, g_recv, p_send, p_recv, gp_send, gp_recv,
    ) = refs
    me, rank = place()
    f32 = jnp.float32
    bf16 = jnp.bfloat16
    rows, width = hidden_ref.shape
    length = rows * tp

    greet(me, rank, tp)

    def along_z(spot, sends, recvs, block, to_right):
        way = 0 if to_right else 1
        return pltpu.make_async_remote_copy(
            src_ref=spot,
            dst_ref=spot,
            send_sem=sends.at[way, block],
            recv_sem=recvs.at[way, block],
            device_id=(me, rank + 1 if to_right else rank - 1),
            device_id_type=MESH,
        )

    def row_z(block, to_right):
        spot = rows_ref.at[pl.ds(block * rows, rows)]
        return along_z(spot, z_send, z_recv, block, to_right)

    def grad_z(block, to_right):
        return along_z(grad_region(me, block), g_send, g_recv, block, to_right)

    def z_start(copy):
        @pl.when(rank < tp - 1)
        def _():
            copy(rank, True).start()

        @pl.when(rank > 0)
        def _():
            copy(rank, False).start()

    def z_step(copy, step, then=None):
        @pl.when(rank >= step)
        def _():
            copy(rank - step, True).wait_recv()

            @pl.when(rank < tp - 1)
            def _():
                copy(rank - step, True).start()

            if then is not None:
                then(rank - step)

        @pl.when(rank + step < tp)
        def _():
            copy(rank + step, False).wait_recv()

            @pl.when(rank > 0)
            def _():
                copy(rank + step, False).start()

            if then is not None:
                then(rank + step)

    def z_end(copy):
        for block in range(tp):

            @pl.when((block <= rank) & (rank < tp - 1))
            def _():
                copy(block, True).wait_send()

            @pl.when((block >= rank) & (rank > 0))
            def _():
                copy(block, False).wait_send()

    def region(i, owner_bits, start=0, count=None):
        size = pieces[i].shape[0]
        count = size if count is None else count
        return fulls[i].at[pl.ds(plane_peer(me, owner_bits) * size + start, count)]

    def across(i, bit, owner_bits, slot, start=0, count=None):
        spot = region(i, owner_bits, start, count)
        return pltpu.make_async_remote_copy(
            src_ref=pieces[i] if owner_bits == 0 else spot,
            dst_ref=spot,
            send_sem=p_send.at[slot, i],
            recv_sem=p_recv.at[slot, i],
            device_id=(flipped(me, bit), rank),
            device_id_type=MESH,
        )

    def to_core(q, i):
        return across(i, 1, 2 * q, q)

    def own_x(i):
        return across(i, 2, 0, 4)

    def own_y(i):
        return across(i, 4, 0, 5)

    def x_to_y(i):
        size = pieces[i].shape[0]
        return across(i, 4, 2, 6, 0, size // 2 if halved[i] else size)

    def y_to_x(i):
        size = pieces[i].shape[0]
        return across(i, 2, 4, 7, size // 2, size // 2)

    def local(i):
        return pltpu.make_async_copy(pieces[i], region(i, 0), l_sem.at[i])

    def export(i):
        return pltpu.make_async_copy(fulls[i], fulls_out[i], e_sem.at[i])

    def forward(i):
        own_x(i).wait_recv()
        x_to_y(i).start()
        to_core(1, i).start()
        own_y(i).wait_recv()
        if halved[i]:
            y_to_x(i).start()
        to_core(2, i).start()

    def finish(i):
        x_to_y(i).wait_recv()
        if halved[i]:
            y_to_x(i).wait_recv()
        to_core(3, i).start()

    def arrived(i):
        local(i).wait()
        for q in range(4):
            to_core(q, i).wait_recv()
        export(i).start()

    order = [rank]
    for bit in (1, 2):
        order = order + [flipped(one, bit) for one in order]

    def grad_region(pack, block, start=0, count=None):
        count = rows if count is None else count
        return grads_ref.at[pl.ds(pack * length + block * rows + start, count)]

    def grad_across(bit, pack_bits, block, slot, start=0, count=None):
        spot = grad_region(plane_peer(me, pack_bits), block, start, count)
        return pltpu.make_async_remote_copy(
            src_ref=spot,
            dst_ref=spot,
            send_sem=gp_send.at[slot, block],
            recv_sem=gp_recv.at[slot, block],
            device_id=(flipped(me, bit), rank),
            device_id_type=MESH,
        )

    def grad_core(q, block):
        return grad_across(1, 2 * q, block, q)

    def grad_x(block):
        return grad_across(2, 0, block, 4)

    def grad_y(block):
        return grad_across(4, 0, block, 5)

    def grad_x_to_y(block):
        return grad_across(4, 2, block, 6, 0, rows // 2)

    def grad_y_to_x(block):
        return grad_across(2, 4, block, 7, rows // 2, rows // 2)

    def grad_plane(block):
        grad_x(block).start()
        grad_y(block).start()
        grad_core(0, block).start()

    def grad_forward(block):
        grad_x(block).wait_recv()
        grad_x_to_y(block).start()
        grad_core(1, block).start()
        grad_y(block).wait_recv()
        grad_y_to_x(block).start()
        grad_core(2, block).start()

    def grad_finish(block):
        grad_x_to_y(block).wait_recv()
        grad_y_to_x(block).wait_recv()
        grad_core(3, block).start()

    def project(which):
        at = slice(which * heads * 128, (which + 1) * heads * 128)
        return jnp.dot(rows_ref[...], fulls[0][:, at], preferred_element_type=f32)

    def bias(which, head):
        line = which * heads + head
        size = pieces[3].shape[0]
        share = 128 // 8
        return jnp.concatenate(
            [fulls[3][owner * size + line : owner * size + line + 1, :share] for owner in range(8)],
            axis=1,
        )

    def rotated(columns):
        return columns * cos_ref[...] + pltpu.roll(columns, 64, 1) * sin_ref[...]

    def make_heads():
        for which, ref in ((0, q_ref), (1, k_ref), (2, v_ref)):
            all_heads = project(which)
            for head in range(heads):
                at = slice(head * 128, (head + 1) * 128)
                one = all_heads[:, at] + bias(which, head)
                if which < 2:
                    one = rotated(one)
                ref[:, at] = one.astype(bf16)

    def attend(head):
        at = slice(head * 128, (head + 1) * 128)
        scores = lax.dot_general(q_ref[:, at], k_ref[:, at], NT, preferred_element_type=f32)
        line = lax.broadcasted_iota(jnp.int32, (length, length), 0)
        column = lax.broadcasted_iota(jnp.int32, (length, length), 1)
        allowed = (line >= column) & (seg_col_ref[...] == seg_row_ref[...])
        scores = jnp.where(allowed, scores * 128 ** (-0.5), -1e30)
        peak = jnp.max(scores, axis=-1, keepdims=True)
        log_total = peak + jnp.log(jnp.sum(jnp.exp(scores - peak), axis=-1, keepdims=True))
        probs = jnp.exp(scores - log_total).astype(bf16)
        lane = lax.broadcasted_iota(jnp.int32, (length, 128), 1)
        before = jnp.zeros((length, 128), f32) if head == 0 else lt_ref[...]
        lt_ref[...] = jnp.where(lane == head, log_total, before)
        heads_ref[:, at] = jnp.dot(probs, v_ref[:, at], preferred_element_type=f32).astype(bf16)

    def project_out():
        size = pieces[1].shape[0]
        share = width // 8
        for owner in range(8):
            part_ref[:, owner * share : (owner + 1) * share] = jnp.dot(
                heads_ref[...],
                fulls[1][owner * size : (owner + 1) * size, :],
                preferred_element_type=f32,
            ).astype(bf16)

    for i in range(parts):
        own_x(i).start()
        own_y(i).start()
        to_core(0, i).start()
    hidden = hidden_ref[...].astype(f32)
    inverse = lax.rsqrt(jnp.mean(hidden * hidden, axis=-1, keepdims=True) + epsilon)
    own_rows = pl.ds(pl.multiple_of(rank * rows, rows), rows)
    rows_ref[own_rows, :] = (hidden * inverse * gain_ref[...]).astype(bf16)
    z_start(row_z)
    own_grad = pltpu.make_async_copy(grad_ref, grad_region(me, rank), l_sem.at[parts])
    own_grad.start()
    for i in range(parts):
        local(i).start()
    own_grad.wait()
    grad_plane(rank)
    z_step(row_z, 1)
    forward(0)
    z_step(row_z, 2)
    z_start(grad_z)
    for i in range(1, parts):
        forward(i)
    finish(0)
    z_step(row_z, 3)
    rows_export = pltpu.make_async_copy(rows_ref, rows_out, e_sem.at[parts])
    rows_export.start()
    for i in range(1, parts):
        finish(i)
    grad_forward(order[0])
    z_step(grad_z, 1, grad_plane)
    for i in range(parts):
        arrived(i)
    make_heads()
    grad_finish(order[0])
    z_step(grad_z, 2, grad_plane)
    attend(0)
    attend(1)
    grad_forward(order[1])
    z_step(grad_z, 3, grad_plane)
    for head in range(2, heads):
        attend(head)
    grad_finish(order[1])
    grad_forward(order[2])
    project_out()
    grad_finish(order[2])
    grad_forward(order[3])
    grad_finish(order[3])
    for block in order:
        for q in range(4):
            grad_core(q, block).wait_recv()

    rows_export.wait()
    for i in range(parts):
        export(i).wait()
        for q in range(4):
            to_core(q, i).wait_send()
        own_x(i).wait_send()
        own_y(i).wait_send()
        x_to_y(i).wait_send()
        if halved[i]:
            y_to_x(i).wait_send()
    for block in order:
        for q in range(4):
            grad_core(q, block).wait_send()
        for copy in (grad_x, grad_y, grad_x_to_y, grad_y_to_x):
            copy(block).wait_send()
    z_end(row_z)
    z_end(grad_z)


def attend_pack(hidden, gain, grad, segments, cos, sin, pieces, fsdp, tp, heads, number):
    rows, width = hidden.shape
    length = rows * tp
    parts = len(pieces)
    halved = [one.shape[0] >= 32 for one in pieces]
    bf16 = jnp.bfloat16
    f32 = jnp.float32
    dma = pltpu.SemaphoreType.DMA
    anywhere = pl.BlockSpec(memory_space=pl.ANY)
    vmem = pl.BlockSpec(memory_space=pltpu.VMEM)
    fulls = [(one.shape[0] * fsdp, one.shape[1]) for one in pieces]
    of_heads = jax.ShapeDtypeStruct((length, heads * 128), bf16)
    return pl.pallas_call(
        functools.partial(attend_kernel, tp, heads, halved),
        out_shape=[
            jax.ShapeDtypeStruct((length, width), bf16),
            jax.ShapeDtypeStruct((length * fsdp, width), bf16),
            of_heads,
            of_heads,
            of_heads,
            jax.ShapeDtypeStruct((length, 128), f32),
            of_heads,
            jax.ShapeDtypeStruct((length, width), bf16),
        ]
        + [jax.ShapeDtypeStruct(shape, one.dtype) for shape, one in zip(fulls, pieces)],
        in_specs=[vmem] * 7 + [anywhere] * parts,
        out_specs=[anywhere, anywhere] + [vmem] * 6 + [anywhere] * parts,
        scratch_shapes=[pltpu.VMEM((length, width), bf16)]
        + [pltpu.VMEM(shape, one.dtype) for shape, one in zip(fulls, pieces)]
        + [
            dma((parts + 1,)), dma((parts + 1,)),
            dma((2, tp)), dma((2, tp)), dma((2, tp)), dma((2, tp)),
            dma((8, parts)), dma((8, parts)), dma((8, tp)), dma((8, tp)),
        ],
        compiler_params=pltpu.CompilerParams(
            collective_id=number, has_side_effects=True, vmem_limit_bytes=48 << 20
        ),
        name="attend",
    )(
        hidden, gain, grad, segments.reshape(1, -1), segments.reshape(-1, 1), cos, sin,
        *pieces,
    )


def dense_plan(
    hidden_in,
    out_grad,
    segment_ids,
    expert_ids,
    route_weights,
    attn_gain,
    ffn_gain,
    qkv_weight,
    qkv_bias,
    out_weight,
    shared_gate_up,
    shared_down,
    shared_gate_vec,
    expert_gate_up,
    expert_down,
):
    every = ("fsdp", "tp")
    tp_rank = lax.axis_index("tp")
    experts = lax.axis_size("fsdp")
    packs = experts
    length = segment_ids.shape[1]
    own_rows = hidden_in.shape[0]
    own_units = shared_gate_up.shape[0]
    model_width = hidden_in.shape[1]
    bf16 = jnp.bfloat16
    f32 = jnp.float32

    expert_up = expert_gate_up[0]
    expert_dn = expert_down[0]
    expert_width = expert_up.shape[2]
    shared_width = shared_gate_up.shape[2] // experts

    chosen = expert_ids[:, :, None] == jnp.arange(experts, dtype=jnp.int32)
    table = jnp.sum(jnp.where(chosen, route_weights[:, :, None], 0.0), axis=1)
    local_heads = qkv_weight.shape[2]
    head_dim = qkv_weight.shape[3]
    cos_table, sin_table = rope_tables(length, head_dim)
    segments = segment_ids[0]
    hidden_float = hidden_in.astype(f32)
    attn_inverse = inverse_rms(hidden_float)
    bias_rows = 3 * local_heads
    bias_columns = qkv_bias.shape[2]
    bias_piece = jnp.pad(
        qkv_bias.reshape(bias_rows, bias_columns), ((0, 16 - bias_rows), (0, 128 - bias_columns))
    )
    heads_width = local_heads * head_dim
    up_pieces = shared_gate_up.reshape(own_units, 2, experts, shared_width).transpose(2, 1, 0, 3)
    cos_two = jnp.concatenate([cos_table[:, 0], cos_table[:, 0]], axis=1)
    sin_two = jnp.concatenate([-sin_table[:, 0], sin_table[:, 0]], axis=1)
    (
        normed_one,
        grad_all,
        query,
        keys,
        values,
        log_total,
        heads_out,
        projected,
        qkv_flat,
        out_pieces,
        tables,
        bias_pieces,
    ) = attend_pack(
        hidden_in,
        attn_gain[None],
        out_grad,
        segments,
        cos_two,
        sin_two,
        [qkv_weight.reshape(-1, 3 * heads_width), out_weight, table.T, bias_piece],
        experts,
        lax.axis_size("tp"),
        local_heads,
        4,
    )
    expert_scale = lax.dynamic_index_in_dim(
        tables.reshape(packs, experts, length), lax.axis_index("fsdp"), axis=1, keepdims=False
    ).reshape(-1)
    scales = expert_scale.reshape(packs, lax.axis_size("tp"), 2, own_rows // 2)
    scales = scales.transpose(0, 2, 1, 3).reshape(packs, 2, 1, length // 2)
    middle, normed_all, _, d_all, hidden_all, token_part, d_normed_two, lines = ffn(
        projected,
        hidden_in,
        ffn_gain[None],
        shared_gate_vec[None],
        scales,
        grad_all,
        expert_up.transpose(1, 0, 2),
        up_pieces,
        expert_dn,
        shared_down.reshape(experts, shared_width, -1),
        experts,
        lax.axis_size("tp"),
        1,
    )
    tokens = token_part.shape[0]
    middle = middle.reshape(own_rows, model_width)
    normed_all = normed_all.reshape(tokens, model_width)
    d_all = d_all.reshape(tokens, -1)
    hidden_all = hidden_all.reshape(tokens, -1)
    d_normed_two = d_normed_two.reshape(own_rows, model_width)
    lines = lax.dynamic_slice_in_dim(lines, tp_rank * (own_rows // 2), own_rows // 2, axis=2)
    extra_sum = lines.transpose(1, 0, 2).reshape(16, own_rows)
    own_start = tp_rank * own_rows
    ids_own = lax.dynamic_slice_in_dim(expert_ids, own_start, own_rows)
    picked = ids_own[:, :, None] == jnp.arange(experts, dtype=jnp.int32)
    route_grad = jnp.sum(jnp.where(picked, extra_sum[:experts].T[:, None, :], 0.0), axis=-1)
    gate_grad = extra_sum[experts]
    (
        hidden_out,
        middle_grad,
        norm_sums,
        d_rows,
        g_expert_up,
        g_shared_up,
        g_expert_down,
        g_shared_down,
    ) = outputs(
        token_part,
        normed_all,
        d_all,
        hidden_all,
        grad_all,
        middle,
        d_normed_two,
        gate_grad[:, None],
        out_grad,
        ffn_gain[None],
        shared_gate_vec[None],
        experts,
        lax.axis_size("tp"),
        expert_width,
        shared_width,
        2,
    )
    g_qkv, g_out, g_bias, g_shared_up, g_shared_down, hidden_grad, gains = backward(
        d_rows,
        heads_out,
        query,
        keys,
        values,
        log_total,
        cos_two,
        sin_two,
        segments,
        normed_one,
        qkv_flat,
        out_pieces,
        g_shared_up,
        g_shared_down,
        hidden_in,
        middle_grad,
        attn_gain[None],
        norm_sums,
        experts,
        lax.axis_size("tp"),
        local_heads,
        3,
    )
    share = model_width // (experts * lax.axis_size("tp"))
    g_bias = lax.dynamic_slice_in_dim(
        g_bias.reshape(32, 128)[:bias_rows], lax.axis_index("fsdp") * bias_columns, bias_columns, 1
    )
    return (
        hidden_out,
        hidden_grad,
        route_grad,
        gains[0, :share],
        gains[1, :share],
        g_qkv.reshape(-1, 3, local_heads, head_dim),
        g_bias.reshape(qkv_bias.shape),
        g_out.reshape(out_weight.shape[::-1]).T,
        g_shared_up.transpose(1, 0, 2),
        g_shared_down,
        gains[2, :share],
        g_expert_up.transpose(1, 0, 2)[None],
        g_expert_down[None],
    )


def on_device(*arrays):
    if lax.axis_size("fsdp") == 8 and lax.axis_size("tp") == 4 and arrays[3].shape[1] >= 3:
        return dense_plan(*arrays)
    return routed_plan(*arrays)


def solution(mesh):
    placed = (
        P(("fsdp", "tp"), None),
        P(("fsdp", "tp"), None),
        P("fsdp", None),
        P("fsdp", None),
        P("fsdp", None),
        P(),
        P(),
        P("fsdp", None, "tp", None),
        P(None, "tp", "fsdp"),
        P("tp", "fsdp"),
        P("fsdp", None, "tp"),
        P("tp", "fsdp"),
        P(),
        P("fsdp", None, None, "tp"),
        P("fsdp", "tp", None),
    )
    return jax.shard_map(
        on_device,
        mesh=mesh,
        in_specs=placed,
        out_specs=(
            P(("fsdp", "tp"), None),
            P(("fsdp", "tp"), None),
            P(("fsdp", "tp"), None),
            P(("fsdp", "tp")),
            P(("fsdp", "tp")),
            P("fsdp", None, "tp", None),
            P(None, "tp", "fsdp"),
            P("tp", "fsdp"),
            P("fsdp", None, "tp"),
            P("tp", "fsdp"),
            P(("fsdp", "tp")),
            P("fsdp", None, None, "tp"),
            P("fsdp", "tp", None),
        ),
        check_vma=False,
    )
```

```python
import functools

import jax
import jax.experimental.pallas as pl
import jax.experimental.pallas.tpu as pltpu
import jax.numpy as jnp
from jax import lax
from jax.sharding import PartitionSpec as P

epsilon = 1e-06


def rope_tables(length, head_dim):
    half_dim = head_dim // 2
    ratios = jnp.arange(half_dim, dtype=jnp.float32) * (2.0 / head_dim)
    frequency = jnp.exp(-jnp.log(10000.0) * ratios)
    angles = jnp.arange(length, dtype=jnp.float32)[:, None] * frequency[None, :]
    return (jnp.cos(angles)[:, None, :], jnp.sin(angles)[:, None, :])


def rotate(tensor, cos_table, sin_table):
    half_dim = tensor.shape[-1] // 2
    front_half = tensor[..., :half_dim]
    back_half = tensor[..., half_dim:]
    return jnp.concatenate(
        [
            front_half * cos_table - back_half * sin_table,
            back_half * cos_table + front_half * sin_table,
        ],
        axis=-1,
    )


def unrotate(tensor, cos_table, sin_table):
    half_dim = tensor.shape[-1] // 2
    front_half = tensor[..., :half_dim]
    back_half = tensor[..., half_dim:]
    return jnp.concatenate(
        [
            front_half * cos_table + back_half * sin_table,
            back_half * cos_table - front_half * sin_table,
        ],
        axis=-1,
    )


def silu_parts(gate_in):
    sigmoid_value = jax.nn.sigmoid(gate_in)
    return (gate_in * sigmoid_value, sigmoid_value * (1.0 + gate_in * (1.0 - sigmoid_value)))


def slot_table(route_ids, experts, capacity):
    flat_ids = route_ids.reshape(-1)
    onehot = (flat_ids[:, None] == jnp.arange(experts, dtype=jnp.int32)[None, :]).astype(jnp.int32)
    before = jnp.cumsum(onehot, axis=0, dtype=jnp.int32) - onehot
    ranks = jnp.sum(before * onehot, axis=1, dtype=jnp.int32)
    places = flat_ids * capacity + ranks
    filler = jnp.arange(flat_ids.shape[0], dtype=jnp.int32) + 1
    slot_rows = jnp.zeros((experts * capacity,), jnp.int32).at[places].set(filler)
    return (places.reshape(route_ids.shape), slot_rows.reshape(experts, capacity))


def inverse_rms(tensor):
    return lax.rsqrt(jnp.mean(tensor * tensor, axis=-1, keepdims=True) + epsilon)


def norm_backward(d_normed, hat_rows, inverse, gain_vec):
    d_hat = d_normed * gain_vec
    return inverse * (d_hat - hat_rows * jnp.mean(d_hat * hat_rows, axis=-1, keepdims=True))


def masked_scores(query, keys, allowed, score_scale):
    raw = jnp.einsum("qhd,khd->hqk", query, keys, preferred_element_type=jnp.float32) * score_scale
    return jnp.where(allowed[None], raw, -1e30)


def spread(rows):
    return lax.all_gather(rows, "tp", axis=0, tiled=True)


def head_total(partial_rows):
    return lax.psum_scatter(
        partial_rows.astype(jnp.bfloat16), "tp", scatter_dimension=0, tiled=True
    ).astype(jnp.float32)


def to_experts(buffer):
    return lax.all_to_all(buffer, "fsdp", split_axis=0, concat_axis=0, tiled=True)


def from_experts(buffer):
    return lax.all_to_all(buffer, "fsdp", split_axis=0, concat_axis=0, tiled=True)


def routed_plan(
    hidden_in,
    out_grad,
    segment_ids,
    expert_ids,
    route_weights,
    attn_gain,
    ffn_gain,
    qkv_weight,
    qkv_bias,
    out_weight,
    shared_gate_up,
    shared_down,
    shared_gate_vec,
    expert_gate_up,
    expert_down,
):
    tp_rank = lax.axis_index("tp")
    experts = lax.axis_size("fsdp")
    length = segment_ids.shape[1]
    top_count = expert_ids.shape[1]
    capacity = 3 * length * top_count // (2 * experts)
    own_rows = hidden_in.shape[0]
    model_width = hidden_in.shape[1]
    qkv_full, bias_full, out_full, shared_full, shared_down_full = (
        lax.all_gather(qkv_weight, "fsdp", axis=0, tiled=True),
        lax.all_gather(qkv_bias.astype(jnp.bfloat16), "fsdp", axis=2, tiled=True).astype(
            qkv_bias.dtype
        ),
        lax.all_gather(out_weight, "fsdp", axis=1, tiled=True),
        lax.all_gather(shared_gate_up, "fsdp", axis=0, tiled=True),
        lax.all_gather(shared_down, "fsdp", axis=1, tiled=True),
    )
    local_heads = qkv_full.shape[2]
    head_dim = qkv_full.shape[3]
    score_scale = head_dim ** (-0.5)
    cos_table, sin_table = rope_tables(length, head_dim)
    positions = jnp.arange(length, dtype=jnp.int32)
    segments = segment_ids[0]
    allowed = (positions[:, None] >= positions[None, :]) & (segments[:, None] == segments[None, :])
    hidden_float = hidden_in.astype(jnp.float32)
    attn_inverse = inverse_rms(hidden_float)
    normed_one = spread((hidden_float * attn_inverse * attn_gain).astype(jnp.bfloat16))
    qkv_flat = qkv_full.reshape(model_width, -1)
    qkv = (
        jnp.dot(normed_one, qkv_flat, preferred_element_type=jnp.float32).reshape(
            length, 3, local_heads, head_dim
        )
        + bias_full
    )
    query = rotate(qkv[:, 0], cos_table, sin_table).astype(jnp.bfloat16)
    keys = rotate(qkv[:, 1], cos_table, sin_table).astype(jnp.bfloat16)
    values = qkv[:, 2].astype(jnp.bfloat16)
    scores = masked_scores(query, keys, allowed, score_scale)
    row_peak = jnp.max(scores, axis=-1, keepdims=True)
    log_total = row_peak + jnp.log(jnp.sum(jnp.exp(scores - row_peak), axis=-1, keepdims=True))
    probs_b = jnp.exp(scores - log_total).astype(jnp.bfloat16)
    heads_out = (
        jnp.einsum("hqk,khd->qhd", probs_b, values, preferred_element_type=jnp.float32)
        .astype(jnp.bfloat16)
        .reshape(length, -1)
    )
    middle = hidden_float + head_total(
        jnp.dot(heads_out, out_full, preferred_element_type=jnp.float32)
    )
    ffn_inverse = inverse_rms(middle)
    normed_two_own = (middle * ffn_inverse * ffn_gain).astype(jnp.bfloat16)
    normed_two = spread(normed_two_own)
    gate_prob = jax.nn.sigmoid(jnp.sum(normed_two.astype(jnp.float32) * shared_gate_vec, axis=-1))
    shared_flat = shared_full.reshape(model_width, -1)
    shared_width = shared_full.shape[2]
    shared_pre = jnp.dot(normed_two, shared_flat, preferred_element_type=jnp.float32)
    shared_act, shared_slope = silu_parts(shared_pre[:, :shared_width])
    shared_upper = shared_pre[:, shared_width:]
    shared_hidden = (shared_act * shared_upper).astype(jnp.bfloat16)
    shared_part = jnp.dot(shared_hidden, shared_down_full, preferred_element_type=jnp.float32)
    places, slot_rows = slot_table(expert_ids, experts, capacity)
    filled = slot_rows > 0
    route_index = jnp.maximum(slot_rows - 1, 0)
    source_rows = route_index // top_count
    flat_weights = route_weights.reshape(-1)
    slot_weights = jnp.where(filled, flat_weights[route_index], 0.0)
    send_rows = jnp.where(filled[:, :, None], normed_two[source_rows], jnp.zeros((), jnp.bfloat16))
    arrived = to_experts(send_rows).reshape(-1, model_width)
    expert_flat = expert_gate_up[0].reshape(model_width, -1)
    expert_width = expert_gate_up.shape[3]
    down_local = expert_down[0]
    expert_pre = jnp.dot(arrived, expert_flat, preferred_element_type=jnp.float32)
    expert_act, expert_slope = silu_parts(expert_pre[:, :expert_width])
    expert_upper = expert_pre[:, expert_width:]
    expert_hidden = (expert_act * expert_upper).astype(jnp.bfloat16)
    expert_part = jnp.dot(expert_hidden, down_local, preferred_element_type=jnp.float32).astype(
        jnp.bfloat16
    )
    returned = from_experts(expert_part.reshape(experts, capacity, model_width)).reshape(
        experts * capacity, model_width
    )
    picked = returned[places].astype(jnp.float32)
    token_term = gate_prob[:, None] * shared_part + jnp.sum(
        route_weights[:, :, None] * picked, axis=1
    )
    own_extra = 0.0
    total = (
        lax.psum_scatter(
            token_term.astype(jnp.bfloat16), "tp", scatter_dimension=0, tiled=True
        ).astype(jnp.float32)
        + own_extra
    )
    hidden_out = (middle + total).astype(jnp.bfloat16)
    grad_rows = spread(out_grad)
    grad_float = grad_rows.astype(jnp.float32)
    gate_part = jnp.sum(grad_float * shared_part, axis=-1)
    scaled_grad = (gate_prob[:, None] * grad_float).astype(jnp.bfloat16)
    shared_d_hidden = jnp.dot(scaled_grad, shared_down_full.T, preferred_element_type=jnp.float32)
    shared_d_cat = jnp.concatenate(
        [
            (shared_d_hidden * shared_upper * shared_slope).astype(jnp.bfloat16),
            (shared_d_hidden * shared_act).astype(jnp.bfloat16),
        ],
        axis=1,
    )
    g_shared_down = jnp.dot(shared_hidden.T, scaled_grad, preferred_element_type=jnp.float32)
    g_shared_gate_up = jnp.dot(
        normed_two.T, shared_d_cat, preferred_element_type=jnp.float32
    ).reshape(shared_full.shape)
    d_normed_part = jnp.dot(shared_d_cat, shared_flat.T, preferred_element_type=jnp.float32)
    expert_grad_in = (slot_weights[:, :, None] * grad_float[source_rows]).astype(jnp.bfloat16)
    arrived_grad = to_experts(expert_grad_in).reshape(-1, model_width)
    back_act, back_slope, back_upper, back_hidden = (
        expert_act,
        expert_slope,
        expert_upper,
        expert_hidden,
    )
    expert_d_hidden = jnp.dot(arrived_grad, down_local.T, preferred_element_type=jnp.float32)
    expert_d_cat = jnp.concatenate(
        [
            (expert_d_hidden * back_upper * back_slope).astype(jnp.bfloat16),
            (expert_d_hidden * back_act).astype(jnp.bfloat16),
        ],
        axis=1,
    )
    g_expert_down = jnp.dot(back_hidden.T, arrived_grad, preferred_element_type=jnp.float32)[None]
    g_expert_gate_up = jnp.dot(arrived.T, expert_d_cat, preferred_element_type=jnp.float32).reshape(
        expert_gate_up.shape
    )
    expert_d_part = jnp.dot(expert_d_cat, expert_flat.T, preferred_element_type=jnp.float32).astype(
        jnp.bfloat16
    )
    route_part = jnp.sum(grad_float[:, None, :] * picked, axis=-1)
    returned_grad = from_experts(expert_d_part.reshape(experts, capacity, model_width)).reshape(
        experts * capacity, model_width
    )
    d_normed_part = d_normed_part + jnp.sum(returned_grad[places].astype(jnp.float32), axis=1)
    d_normed_two, route_grad, gate_grad = (
        lax.psum_scatter(
            d_normed_part.astype(jnp.bfloat16), "tp", scatter_dimension=0, tiled=True
        ).astype(jnp.float32),
        lax.psum_scatter(
            route_part.astype(jnp.bfloat16), "tp", scatter_dimension=0, tiled=True
        ).astype(jnp.float32),
        lax.psum_scatter(
            gate_part.astype(jnp.bfloat16), "tp", scatter_dimension=0, tiled=True
        ).astype(jnp.float32),
    )
    own_gate = lax.dynamic_slice_in_dim(gate_prob, tp_rank * own_rows, own_rows)
    logit_grad = gate_grad * own_gate * (1.0 - own_gate)
    d_normed_two = d_normed_two + logit_grad[:, None] * shared_gate_vec
    g_gate_vec = jnp.sum(normed_two_own.astype(jnp.float32) * logit_grad[:, None], axis=0)
    hat_two = middle * ffn_inverse
    g_ffn_gain = jnp.sum(d_normed_two * hat_two, axis=0)
    middle_grad = out_grad.astype(jnp.float32) + norm_backward(
        d_normed_two, hat_two, ffn_inverse, ffn_gain
    )
    d_rows = spread(middle_grad.astype(jnp.bfloat16))
    g_out = jnp.dot(heads_out.T, d_rows, preferred_element_type=jnp.float32)
    d_heads = (
        jnp.dot(d_rows, out_full.T, preferred_element_type=jnp.float32)
        .astype(jnp.bfloat16)
        .reshape(length, local_heads, head_dim)
    )
    heads_three = heads_out.reshape(length, local_heads, head_dim)
    scores_again = masked_scores(query, keys, allowed, score_scale)
    probs_full = jnp.exp(scores_again - log_total)
    probs_again = probs_full.astype(jnp.bfloat16)
    d_values = jnp.einsum("hqk,qhd->khd", probs_again, d_heads, preferred_element_type=jnp.float32)
    d_probs = jnp.einsum("qhd,khd->hqk", d_heads, values, preferred_element_type=jnp.float32)
    delta = jnp.sum(d_heads.astype(jnp.float32) * heads_three.astype(jnp.float32), axis=-1)
    d_scores = (probs_full * (d_probs - delta.T[:, :, None])).astype(jnp.bfloat16)
    d_query = (
        jnp.einsum("hqk,khd->qhd", d_scores, keys, preferred_element_type=jnp.float32) * score_scale
    )
    d_keys = (
        jnp.einsum("hqk,qhd->khd", d_scores, query, preferred_element_type=jnp.float32)
        * score_scale
    )
    d_qkv = jnp.stack(
        [unrotate(d_query, cos_table, sin_table), unrotate(d_keys, cos_table, sin_table), d_values],
        axis=1,
    )
    g_bias = jnp.sum(d_qkv, axis=0)
    d_qkv_b = d_qkv.astype(jnp.bfloat16).reshape(length, -1)
    g_qkv = jnp.dot(normed_one.T, d_qkv_b, preferred_element_type=jnp.float32).reshape(
        qkv_full.shape
    )
    d_normed_one = head_total(jnp.dot(d_qkv_b, qkv_flat.T, preferred_element_type=jnp.float32))
    hat_one = hidden_float * attn_inverse
    g_attn_gain = jnp.sum(d_normed_one * hat_one, axis=0)
    hidden_grad = middle_grad + norm_backward(d_normed_one, hat_one, attn_inverse, attn_gain)
    g_qkv, g_bias, g_out, g_shared_gate_up, g_shared_down = (
        lax.psum_scatter(
            g_qkv.astype(jnp.bfloat16), "fsdp", scatter_dimension=0, tiled=True
        ).astype(jnp.float32),
        lax.psum_scatter(
            g_bias.astype(jnp.bfloat16), "fsdp", scatter_dimension=2, tiled=True
        ).astype(jnp.float32),
        lax.psum_scatter(
            g_out.astype(jnp.bfloat16), "fsdp", scatter_dimension=1, tiled=True
        ).astype(jnp.float32),
        lax.psum_scatter(
            g_shared_gate_up.astype(jnp.bfloat16), "fsdp", scatter_dimension=0, tiled=True
        ).astype(jnp.float32),
        lax.psum_scatter(
            g_shared_down.astype(jnp.bfloat16), "fsdp", scatter_dimension=1, tiled=True
        ).astype(jnp.float32),
    )
    g_attn_gain, g_ffn_gain, g_gate_vec = (
        lax.psum_scatter(g_attn_gain, ("fsdp", "tp"), scatter_dimension=0, tiled=True),
        lax.psum_scatter(g_ffn_gain, ("fsdp", "tp"), scatter_dimension=0, tiled=True),
        lax.psum_scatter(g_gate_vec, ("fsdp", "tp"), scatter_dimension=0, tiled=True),
    )
    return (
        hidden_out,
        hidden_grad,
        route_grad,
        g_attn_gain,
        g_ffn_gain,
        g_qkv,
        g_bias,
        g_out,
        g_shared_gate_up,
        g_shared_down,
        g_gate_vec,
        g_expert_gate_up,
        g_expert_down,
    )


MESH = pl.DeviceIdType.MESH


def flipped(index, bit):
    return index + bit - 2 * bit * ((index // bit) % 2)


def place():
    me = lax.axis_index("fsdp")
    rank = lax.axis_index("tp")
    return me, rank


def greet(me, rank, tp):
    barrier = pltpu.get_barrier_semaphore()
    for bit in (1, 2, 4):
        pl.semaphore_signal(
            barrier, inc=1, device_id=(flipped(me, bit), rank), device_id_type=MESH
        )

    @pl.when(rank > 0)
    def _():
        pl.semaphore_signal(barrier, inc=1, device_id=(me, rank - 1), device_id_type=MESH)

    @pl.when(rank < tp - 1)
    def _():
        pl.semaphore_signal(barrier, inc=1, device_id=(me, rank + 1), device_id_type=MESH)

    left = (rank + tp - 1) // tp
    right = (2 * (tp - 1) - rank) // tp
    pl.semaphore_wait(barrier, 3 + left + right)


def plane_peer(me, bits):
    for one in (1, 2, 4):
        if bits & one:
            me = flipped(me, one)
    return me


def greet_plane(me, rank, tp):
    barrier = pltpu.get_barrier_semaphore()
    for bits in range(1, 8):
        pl.semaphore_signal(
            barrier, inc=1, device_id=(plane_peer(me, bits), rank), device_id_type=MESH
        )

    @pl.when(rank > 0)
    def _():
        pl.semaphore_signal(barrier, inc=1, device_id=(me, rank - 1), device_id_type=MESH)

    @pl.when(rank < tp - 1)
    def _():
        pl.semaphore_signal(barrier, inc=1, device_id=(me, rank + 1), device_id_type=MESH)

    left = (rank + tp - 1) // tp
    right = (2 * (tp - 1) - rank) // tp
    pl.semaphore_wait(barrier, 7 + left + right)


UNIT = 640
SHARED = 384
NT = (((1,), (1,)), ((), ()))


def ffn_kernel(tp, expert_width, shared_width, *refs):
    part_ref, hidden_ref, gain_ref, vec_ref, scale_ref, grads_ref = refs[:6]
    expert_up, up_ref, expert_down, down_ref = refs[6:10]
    middle_ref, all_ref, up_in, d_ref, hid_ref, y_ref, dsum_ref, esum_ref = refs[10:18]
    (
        x_all, g_buf, dh_buf, d_buf, stage, acc, diag_in, last_in, z_in, both_buf, down_buf,
        eu_buf, su_buf, stage_e, acc_e, other_e, diag_e, last_e, z_in_e,
        w_sem, dn_sem, g_sem, x_sem, d_sem, h_sem, y_sem, f_sem, f_send, f_recv,
        az_send, az_recv, ap_send, ap_recv, s_send, s_recv,
        c_send, c_recv, ce_send, ce_recv, p_send, p_recv, pe_send, pe_recv,
        z_send, z_recv, ze_send, ze_recv,
    ) = refs[18:]
    me, rank = place()
    greet_plane(me, rank, tp)
    f32 = jnp.float32
    bf16 = jnp.bfloat16
    subs, rows, width = hidden_ref.shape
    tile = tp * rows
    pack_rows = subs * tile
    packs = x_all.shape[0]
    near = rank // 2
    order = [rank]
    for bit in (1, 2):
        order = order + [flipped(one, bit) for one in order]
    blocks = [3 * (1 - near), 2 - near, flipped(rank, 1), rank]
    core_of, x_of, y_of = me % 2, (me // 2) % 2, me // 4

    def pack_of(bits):
        return (
            4 * ((y_of + bits // 4) % 2)
            + 2 * ((x_of + (bits // 2) % 2) % 2)
            + (core_of + bits % 2) % 2
        )

    def add(ref, spot, one):
        ref[spot] = (ref[spot].astype(f32) + one.astype(f32)).astype(ref.dtype)

    def remote(src, dst, send, recv, bit):
        return pltpu.make_async_remote_copy(
            src_ref=src,
            dst_ref=dst,
            send_sem=send,
            recv_sem=recv,
            device_id=(flipped(me, bit), rank),
            device_id_type=MESH,
        )

    def remote_z(src, dst, send, recv, right):
        return pltpu.make_async_remote_copy(
            src_ref=src,
            dst_ref=dst,
            send_sem=send,
            recv_sem=recv,
            device_id=(me, rank + 1 if right else rank - 1),
            device_id_type=MESH,
        )

    def gather_z(block, sub, right):
        way = 0 if right else 1
        ref = x_all.at[me, block, sub]
        return remote_z(
            ref, ref, az_send.at[way, block, sub], az_recv.at[way, block, sub], right
        )

    def gather(bit, pack_bits, block, sub, slot, start=0, count=None):
        count = rows if count is None else count
        ref = x_all.at[pack_of(pack_bits), block, sub, pl.ds(start, count)]
        return remote(ref, ref, ap_send.at[slot, block, sub], ap_recv.at[slot, block, sub], bit)

    def to_core(q, block, sub):
        return gather(1, 2 * q, block, sub, q)

    def own_x(block, sub):
        return gather(2, 0, block, sub, 4)

    def own_y(block, sub):
        return gather(4, 0, block, sub, 5)

    def x_to_y(block, sub):
        return gather(4, 2, block, sub, 6, 0, rows // 2)

    def y_to_x(block, sub):
        return gather(2, 4, block, sub, 7, rows // 2, rows // 2)

    def start_plane(block, sub):
        own_x(block, sub).start()
        own_y(block, sub).start()
        to_core(0, block, sub).start()

    def start_rows(sub):
        @pl.when(rank < tp - 1)
        def _():
            gather_z(rank, sub, True).start()

        @pl.when(rank > 0)
        def _():
            gather_z(rank, sub, False).start()

        start_plane(rank, sub)

    def forward(place_in, sub):
        block = order[place_in]
        own_x(block, sub).wait_recv()
        x_to_y(block, sub).start()
        to_core(1, block, sub).start()
        own_y(block, sub).wait_recv()
        y_to_x(block, sub).start()
        to_core(2, block, sub).start()

    def finish(place_in, sub):
        block = order[place_in]
        x_to_y(block, sub).wait_recv()
        y_to_x(block, sub).wait_recv()
        to_core(3, block, sub).start()

    def z_step(step, sub):
        @pl.when(rank >= step)
        def _():
            block = rank - step
            gather_z(block, sub, True).wait_recv()

            @pl.when(rank < tp - 1)
            def _():
                gather_z(block, sub, True).start()

            start_plane(block, sub)

        @pl.when(rank + step < tp)
        def _():
            block = rank + step
            gather_z(block, sub, False).wait_recv()

            @pl.when(rank > 0)
            def _():
                gather_z(block, sub, False).start()

            start_plane(block, sub)

    def control(i):
        steps = {
            1: [(forward, 3, 0)],
            2: [(forward, 0, 1), (finish, 2, 0)],
            3: [(z_step, 2, 1)],
            4: [(finish, 3, 0), (forward, 1, 1)],
            5: [(z_step, 3, 1)],
            6: [(finish, 0, 1)],
            7: [(forward, 2, 1)],
            8: [(finish, 1, 1)],
            9: [(forward, 3, 1)],
            10: [(finish, 2, 1)],
            11: [(finish, 3, 1)],
        }
        for at, todo in steps.items():

            @pl.when(i == at)
            def _():
                for act, what, sub in todo:
                    act(what, sub)

    up_rows = up_ref.shape[2]
    span = down_ref.shape[2]

    def up_to(bits):
        return pltpu.make_async_remote_copy(
            src_ref=up_ref.at[plane_peer(me, bits)],
            dst_ref=up_in.at[:, pl.ds(pl.multiple_of(me * up_rows, up_rows), up_rows)],
            send_sem=s_send.at[0, bits],
            recv_sem=s_recv.at[0, bits],
            device_id=(plane_peer(me, bits), rank),
            device_id_type=MESH,
        )

    def down_spot():
        return down_buf.at[
            pl.ds(SHARED, shared_width), pl.ds(pl.multiple_of(me * span, span), span)
        ]

    def down_to(bits):
        return pltpu.make_async_remote_copy(
            src_ref=down_ref.at[plane_peer(me, bits)],
            dst_ref=down_spot(),
            send_sem=s_send.at[1, bits],
            recv_sem=s_recv.at[1, bits],
            device_id=(plane_peer(me, bits), rank),
            device_id_type=MESH,
        )

    def core(q, s):
        return remote(stage.at[s], acc.at[q, s], c_send.at[q, s], c_recv.at[q, s], 1)

    def core_e(q):
        return remote(stage_e.at[q], other_e.at[q], ce_send.at[q], ce_recv.at[q], 1)

    low, high = pl.ds(0, tp // 2), pl.ds(tp // 2, tp // 2)

    def across(bit, src, dst, slot, s):
        return remote(src, dst, p_send.at[slot, s], p_recv.at[slot, s], bit)

    def diag_x(s):
        return across(2, acc.at[3, s, low], diag_in.at[s, 0], 0, s)

    def diag_y(s):
        return across(4, acc.at[3, s, high], diag_in.at[s, 1], 1, s)

    def direct_x(s):
        return across(2, acc.at[1, s, low], last_in.at[s, 0, low], 2, s)

    def direct_y(s):
        return across(4, acc.at[2, s, high], last_in.at[s, 1, high], 3, s)

    def summed_x(s):
        return across(2, acc.at[1, s, high], last_in.at[s, 0, high], 4, s)

    def summed_y(s):
        return across(4, acc.at[2, s, low], last_in.at[s, 1, low], 5, s)

    def diag_lines():
        return remote(acc_e.at[3], diag_e, pe_send.at[0], pe_recv.at[0], 2)

    def direct_lines():
        return remote(acc_e.at[1], last_e.at[0], pe_send.at[1], pe_recv.at[1], 2)

    def summed_lines():
        return remote(acc_e.at[2], last_e.at[1], pe_send.at[2], pe_recv.at[2], 4)

    def along_z(j, s, right):
        way = 0 if right else 1
        block = blocks[j]
        return remote_z(
            acc.at[0, s, block],
            z_in.at[way, block, s],
            z_send.at[way, block, s],
            z_recv.at[way, block, s],
            right,
        )

    def lines_z(right):
        way = 0 if right else 1
        return remote_z(
            acc_e.at[1 + way], z_in_e.at[way], ze_send.at[way], ze_recv.at[way], right
        )

    def second(s):
        diag_x(s).wait_recv()
        add(acc, (2, s, low), diag_in[s, 0])
        summed_y(s).start()
        diag_y(s).wait_recv()
        add(acc, (1, s, high), diag_in[s, 1])
        summed_x(s).start()

    def third(j, s):
        block = blocks[j]
        if j == 0:
            direct_x(s).wait_recv()
            direct_y(s).wait_recv()
            summed_x(s).wait_recv()
            summed_y(s).wait_recv()
        total = (
            acc[0, s, block].astype(f32)
            + last_in[s, 0, block].astype(f32)
            + last_in[s, 1, block].astype(f32)
        )
        if j < tp - 1:
            acc[0, s, block] = total.astype(bf16)

            @pl.when((block > rank) & (rank > 0))
            def _():
                along_z(j, s, True).wait_recv()
                add(acc, (0, s, block), z_in[0, block, s])

            @pl.when((block < rank) & (rank < tp - 1))
            def _():
                along_z(j, s, False).wait_recv()
                add(acc, (0, s, block), z_in[1, block, s])

            @pl.when(block > rank)
            def _():
                along_z(j, s, True).start()

            @pl.when(block < rank)
            def _():
                along_z(j, s, False).start()
        else:
            dsum_ref[s] = total

            @pl.when(rank > 0)
            def _():
                along_z(j, s, True).wait_recv()
                dsum_ref[s] += z_in[0, block, s].astype(f32)

            @pl.when(rank < tp - 1)
            def _():
                along_z(j, s, False).wait_recv()
                dsum_ref[s] += z_in[1, block, s].astype(f32)

    def sum_lines():
        direct_lines().wait_recv()
        summed_lines().wait_recv()
        direct_lines().wait_send()
        summed_lines().wait_send()
        own = acc_e[0] + last_e[0] + last_e[1]
        esum_ref[...] = own
        acc_e[1] = own
        acc_e[2] = own

        @pl.when(rank > 0)
        def _():
            lines_z(True).wait_recv()
            esum_ref[...] += z_in_e[0]
            acc_e[1] = own + z_in_e[0]

        @pl.when(rank < tp - 1)
        def _():
            lines_z(True).start()
            lines_z(False).wait_recv()
            esum_ref[...] += z_in_e[1]
            acc_e[2] = own + z_in_e[1]

        @pl.when(rank > 0)
        def _():
            lines_z(False).start()

    def front_load(block, s):
        return pltpu.make_async_copy(
            part_ref.at[block, s], stage.at[s, block], f_sem.at[block, s]
        )

    def front_z(j, s, right):
        way = 0 if right else 1
        block = blocks[j]
        return remote_z(
            stage.at[s, block],
            z_in.at[way, block, s],
            f_send.at[way, block, s],
            f_recv.at[way, block, s],
            right,
        )

    def front(j, s):
        block = blocks[j]
        front_load(block, s).wait()
        if j < tp - 1:

            @pl.when((block > rank) & (rank > 0))
            def _():
                front_z(j, s, True).wait_recv()
                add(stage, (s, block), z_in[0, block, s])

            @pl.when((block < rank) & (rank < tp - 1))
            def _():
                front_z(j, s, False).wait_recv()
                add(stage, (s, block), z_in[1, block, s])

            @pl.when(block > rank)
            def _():
                front_z(j, s, True).start()

            @pl.when(block < rank)
            def _():
                front_z(j, s, False).start()
        else:
            middle_ref[s] = hidden_ref[s].astype(f32) + stage[s, block].astype(f32)

            @pl.when(rank > 0)
            def _():
                front_z(j, s, True).wait_recv()
                middle_ref[s] += z_in[0, block, s].astype(f32)

            @pl.when(rank < tp - 1)
            def _():
                front_z(j, s, False).wait_recv()
                middle_ref[s] += z_in[1, block, s].astype(f32)

            middle = middle_ref[s]
            mean = jnp.mean(middle * middle, axis=-1, keepdims=True)
            normed = middle * lax.rsqrt(mean + epsilon) * gain_ref[...]
            x_all[me, rank, s] = normed.astype(bf16)
            start_rows(s)

    cut = eu_buf.shape[1]
    cuts = width // cut
    units = SHARED + shared_width

    def weight_loads(part, n, slot):
        at = pl.ds(pl.multiple_of(n * cut, cut), cut)
        return (
            pltpu.make_async_copy(expert_up.at[part, at], eu_buf.at[slot], w_sem.at[0, slot]),
            pltpu.make_async_copy(up_in.at[part, at], su_buf.at[slot], w_sem.at[1, slot]),
        )

    def start_loads(part, n, slot):
        of_expert, of_shared = weight_loads(part, n, slot)
        of_expert.start()

        @pl.when(n == me)
        def _():
            own = up_ref.at[me, part]
            pltpu.make_async_copy(own, su_buf.at[slot], w_sem.at[1, slot]).start()

        @pl.when(n != me)
        def _():
            of_shared.start()

    def lay_out(part):
        base = part * UNIT

        def body(n, carry):
            slot = n % 2

            @pl.when(n + 1 < cuts)
            def _():
                start_loads(part, n + 1, 1 - slot)

            for copy in weight_loads(part, n, slot):
                copy.wait()
            at = pl.ds(pl.multiple_of(n * cut, cut), cut)
            both_buf[at, base : base + UNIT] = jnp.zeros((cut, UNIT), bf16)
            both_buf[at, base : base + expert_width] = eu_buf[slot]
            both_buf[at, base + SHARED : base + units] = su_buf[slot]
            return carry

        start_loads(part, 0, 0)
        lax.fori_loop(0, cuts, body, 0)

    down_loads = (
        pltpu.make_async_copy(expert_down, down_buf.at[pl.ds(0, expert_width)], dn_sem.at[0]),
        pltpu.make_async_copy(down_ref.at[me], down_spot(), dn_sem.at[1]),
    )

    def grad_load(n, slot):
        at = pl.ds(n * tile, tile)
        return pltpu.make_async_copy(grads_ref.at[at], g_buf.at[slot], g_sem.at[slot])

    def hidden_grads(first, last):
        def body(n, carry):
            slot = n % 2

            @pl.when(n + 1 < 2 * packs)
            def _():
                grad_load(n + 1, 1 - slot).start()

            grad_load(n, slot).wait()
            d_hidden = lax.dot_general(
                g_buf[slot], down_buf[...], NT, preferred_element_type=f32
            ).astype(bf16)
            dh_buf[n // 2, pl.ds(n % 2 * 2, 2)] = d_hidden.reshape(2, subs, rows, UNIT)
            return carry

        lax.fori_loop(first, last, body, 0)

    def tile_of(i):
        s = i // 8
        q = order_of(s, i // 2 % 4)
        o = i % 2
        return q, o, s, pack_of(2 * q + 1 - o)

    def order_of(s, r):
        return r + s * (r // 2) * (1 - 2 * (r % 2))

    def d_store(i):
        q, o, s, pack = tile_of(i)
        return pltpu.make_async_copy(d_buf.at[i % 2], d_ref.at[pack, :, s], d_sem.at[i % 2])

    def x_store(i):
        q, o, s, pack = tile_of(i)
        return pltpu.make_async_copy(x_all.at[pack, :, s], all_ref.at[pack, :, s], x_sem.at[i % 2])

    def one_tile(i, carry):
        q, o, s, pack = tile_of(i)
        slot = i % 2

        @pl.when(o == 0)
        def _():
            for block in range(tp):
                ref = x_all.at[pack, block, s]
                remote(
                    ref, ref, ap_send.at[q, block, s], ap_recv.at[q, block, s], 1
                ).wait_recv()

        @pl.when(i >= 2)
        def _():
            d_store(i - 2).wait()
            x_store(i - 2).wait()

        x_store(i).start()
        x = x_all[pack, :, s].reshape(tile, width)
        pre = jnp.dot(x, both_buf[...], preferred_element_type=f32)
        gate, upper = pre[:, :UNIT], pre[:, UNIT:]
        lane = lax.broadcasted_iota(jnp.int32, (1, UNIT), 1)
        logit = jnp.sum(x.astype(f32) * vec_ref[...], axis=-1, keepdims=True)
        gate_prob = 1.0 / (1.0 + jnp.exp(-logit))
        own_scale = jnp.broadcast_to(scale_ref[pack, s], (128, tile)).T[:, :1]
        scale = jnp.where(lane < SHARED, own_scale, gate_prob)
        sigmoid = 1.0 / (1.0 + jnp.exp(-gate))
        act = gate * sigmoid
        slope = sigmoid * (1.0 + gate * (1.0 - sigmoid))
        hidden = act * upper
        d_hidden = dh_buf[pack, :, s].reshape(tile, UNIT).astype(f32)
        line = lax.broadcasted_iota(jnp.int32, (16, UNIT), 0)
        unit = lax.broadcasted_iota(jnp.int32, (16, UNIT), 1)
        of_expert = (line == me) & (unit < SHARED)
        of_shared = (line == 8) & (unit >= SHARED)
        pick = jnp.where(of_expert | of_shared, 1.0, 0.0).astype(bf16)
        lines = lax.dot_general(
            pick, (d_hidden * hidden).astype(bf16), NT, preferred_element_type=f32
        )
        dh_buf[pack, :, s] = (hidden * scale).astype(bf16).reshape(tp, rows, UNIT)
        d_scaled = d_hidden * scale
        d_gate = (d_scaled * upper * slope).astype(bf16)
        d_upper = (d_scaled * act).astype(bf16)
        d_buf[slot, :, :, :UNIT] = d_gate.reshape(tp, rows, UNIT)
        d_buf[slot, :, :, UNIT:] = d_upper.reshape(tp, rows, UNIT)
        control(i)
        d_both = d_buf[slot].reshape(tile, 2 * UNIT)
        d_rows = lax.dot_general(d_both, both_buf[...], NT, preferred_element_type=f32)
        d_rows = d_rows.reshape(tp, rows, width)
        d_store(i).start()

        @pl.when(o == 0)
        def _():
            @pl.when(i % 8 >= 2)
            def _():
                core(order_of(s, i // 2 % 4 - 1), s).wait_send()

            stage[s] = d_rows.astype(bf16)
            stage_e[q, s] = lines
            core(q, s).start()

            @pl.when(s == 1)
            def _():
                core_e(q).start()

        @pl.when(o == 1)
        def _():
            core(q, s).wait_recv()
            add(acc, (q, s), d_rows)
            acc_e[q, s] = lines

            @pl.when(s == 1)
            def _():
                core_e(q).wait_recv()
                acc_e[q] = acc_e[q] + other_e[q]

                @pl.when(q == 1)
                def _():
                    direct_lines().start()

                @pl.when(q == 3)
                def _():
                    diag_lines().start()

            @pl.when(q == 1)
            def _():
                direct_x(s).start()

            @pl.when(q == 2)
            def _():
                direct_y(s).start()

            @pl.when(q == 3)
            def _():
                diag_x(s).start()
                diag_y(s).start()

            @pl.when(i == 9)
            def _():
                second(0)

            @pl.when(i == 15)
            def _():
                third(0, 0)

        return carry

    def y_store(n, slot):
        return pltpu.make_async_copy(
            g_buf.at[slot], y_ref.at[pl.ds(n * tile, tile)], y_sem.at[slot]
        )

    def outputs(first, last):
        def body(n, carry):
            slot = n % 2

            @pl.when(n >= 2)
            def _():
                y_store(n - 2, slot).wait()

            hidden = dh_buf[n // 2, pl.ds(n % 2 * 2, 2)].reshape(tile, UNIT)
            g_buf[slot] = jnp.dot(hidden, down_buf[...], preferred_element_type=f32).astype(bf16)
            y_store(n, slot).start()
            return carry

        lax.fori_loop(first, last, body, 0)

    for bits in (6, 7, 2, 4, 3, 5, 1):
        down_to(bits).start()
    for bits in (6, 7, 2, 4, 3, 5, 1):
        up_to(bits).start()
    grad_load(0, 0).start()
    for s in range(subs):
        for block in blocks:
            front_load(block, s).start()
    down_buf[expert_width:SHARED, :] = jnp.zeros((SHARED - expert_width, width), bf16)
    down_buf[units:, :] = jnp.zeros((UNIT - units, width), bf16)
    for copy in down_loads:
        copy.start()
    ends = (rank == 0) | (rank == tp - 1)
    inner = (rank > 0) & (rank < tp - 1)
    front(0, 0)
    front(1, 0)
    front(2, 0)

    @pl.when(ends)
    def _():
        front(0, 1)

    for copy in down_loads:
        copy.wait()
    for bits in range(1, 8):
        down_to(bits).wait_recv()

    @pl.when(ends)
    def _():
        hidden_grads(0, 6)

    front(3, 0)

    @pl.when(ends)
    def _():
        front(1, 1)
        front(2, 1)

    @pl.when(inner)
    def _():
        front(0, 1)

    z_step(1, 0)
    forward(0, 0)

    @pl.when(inner)
    def _():
        hidden_grads(0, 4)

    z_step(2, 0)

    @pl.when(inner)
    def _():
        front(1, 1)
        hidden_grads(4, 6)
        front(2, 1)

    for bits in range(1, 8):
        up_to(bits).wait_recv()
    lay_out(0)
    z_step(3, 0)
    forward(1, 0)
    finish(0, 0)
    front(3, 1)
    lay_out(1)
    forward(2, 0)
    z_step(1, 1)
    hidden_grads(6, 11)
    finish(1, 0)
    hidden_grads(11, 2 * packs)
    for s in range(subs):
        for j in range(tp - 1):
            block = blocks[j]

            @pl.when(block > rank)
            def _():
                front_z(j, s, True).wait_send()

            @pl.when(block < rank)
            def _():
                front_z(j, s, False).wait_send()

    lax.fori_loop(0, 16, one_tile, 0)
    hidden_store = pltpu.make_async_copy(dh_buf, hid_ref, h_sem)
    hidden_store.start()
    diag_lines().wait_recv()
    acc_e[2] = acc_e[2] + diag_e[...]
    summed_lines().start()
    outputs(0, 2)
    second(1)
    third(1, 0)
    outputs(2, 4)
    third(2, 0)
    outputs(4, 6)
    third(3, 0)
    sum_lines()
    outputs(6, 8)
    third(0, 1)
    outputs(8, 10)
    third(1, 1)
    outputs(10, 12)
    third(2, 1)
    outputs(12, 14)
    third(3, 1)
    outputs(14, 16)
    hidden_store.wait()
    for n in (14, 15):
        y_store(n, n % 2).wait()
        d_store(n).wait()
        x_store(n).wait()
    core(3, 0).wait_send()
    core(2, 1).wait_send()
    diag_lines().wait_send()
    for q in range(4):
        core_e(q).wait_send()
    for bits in range(1, 8):
        up_to(bits).wait_send()
        down_to(bits).wait_send()
    for s in range(subs):
        for copy in (diag_x, diag_y, direct_x, direct_y, summed_x, summed_y):
            copy(s).wait_send()
        for block in range(tp):
            for q in range(4):
                to_core(q, block, s).wait_send()
            for copy in (own_x, own_y, x_to_y, y_to_x):
                copy(block, s).wait_send()

            @pl.when((block <= rank) & (rank < tp - 1))
            def _():
                gather_z(block, s, True).wait_send()

            @pl.when((block >= rank) & (rank > 0))
            def _():
                gather_z(block, s, False).wait_send()

        for j in range(tp - 1):
            block = blocks[j]

            @pl.when(block > rank)
            def _():
                along_z(j, s, True).wait_send()

            @pl.when(block < rank)
            def _():
                along_z(j, s, False).wait_send()

    @pl.when(rank < tp - 1)
    def _():
        lines_z(True).wait_send()

    @pl.when(rank > 0)
    def _():
        lines_z(False).wait_send()


def ffn(
    part, hidden, gain, vec, scale, grads, expert_up, shared_up, expert_down, shared_down,
    fsdp, tp, collective_id,
):
    own, width = hidden.shape
    subs = 2
    rows = own // subs
    tile = tp * rows
    tokens = fsdp * tp * own
    expert_width, shared_width = expert_down.shape[0], shared_down.shape[1]
    bf16 = jnp.bfloat16
    f32 = jnp.float32
    dma = pltpu.SemaphoreType.DMA
    anywhere = pl.BlockSpec(memory_space=pl.ANY)
    vmem = pl.BlockSpec(memory_space=pltpu.VMEM)
    all_rows = (fsdp, tp, subs, rows)
    lines = (subs, 16, tile)
    return pl.pallas_call(
        functools.partial(ffn_kernel, tp, expert_width, shared_width),
        out_shape=[
            jax.ShapeDtypeStruct((subs, rows, width), f32),
            jax.ShapeDtypeStruct(all_rows + (width,), bf16),
            jax.ShapeDtypeStruct((2, width, shared_width), bf16),
            jax.ShapeDtypeStruct(all_rows + (2 * UNIT,), bf16),
            jax.ShapeDtypeStruct(all_rows + (UNIT,), bf16),
            jax.ShapeDtypeStruct((tokens, width), bf16),
            jax.ShapeDtypeStruct((subs, rows, width), f32),
            jax.ShapeDtypeStruct(lines, f32),
        ],
        in_specs=[anywhere] + [vmem] * 4 + [anywhere] * 5,
        out_specs=[vmem] + [anywhere] * 5 + [vmem] * 2,
        scratch_shapes=[
            pltpu.VMEM(all_rows + (width,), bf16),
            pltpu.VMEM((2, tile, width), bf16),
            pltpu.VMEM(all_rows + (UNIT,), bf16),
            pltpu.VMEM((2, tp, rows, 2 * UNIT), bf16),
            pltpu.VMEM((subs, tp, rows, width), bf16),
            pltpu.VMEM((4, subs, tp, rows, width), bf16),
            pltpu.VMEM((subs, 2, tp // 2, rows, width), bf16),
            pltpu.VMEM((subs, 2, tp, rows, width), bf16),
            pltpu.VMEM((2, tp, subs, rows, width), bf16),
            pltpu.VMEM((width, 2 * UNIT), bf16),
            pltpu.VMEM((UNIT, width), bf16),
            pltpu.VMEM((2, width // 8, expert_width), bf16),
            pltpu.VMEM((2, width // 8, shared_width), bf16),
            pltpu.VMEM((4,) + lines, f32),
            pltpu.VMEM((4,) + lines, f32),
            pltpu.VMEM((4,) + lines, f32),
            pltpu.VMEM(lines, f32),
            pltpu.VMEM((2,) + lines, f32),
            pltpu.VMEM((2,) + lines, f32),
            dma((2, 2)), dma((2,)), dma((2,)), dma((2,)), dma((2,)), dma, dma((2,)),
            dma((tp, subs)), dma((2, tp, subs)), dma((2, tp, subs)),
            dma((2, tp, subs)), dma((2, tp, subs)), dma((8, tp, subs)), dma((8, tp, subs)),
            dma((2, fsdp)), dma((2, fsdp)),
            dma((4, subs)), dma((4, subs)), dma((4,)), dma((4,)),
            dma((6, subs)), dma((6, subs)), dma((3,)), dma((3,)),
            dma((2, tp, subs)), dma((2, tp, subs)), dma((2,)), dma((2,)),
        ],
        compiler_params=pltpu.CompilerParams(
            collective_id=collective_id, has_side_effects=True, vmem_limit_bytes=63 << 20
        ),
        name="ffn",
    )(
        part.reshape(tp, subs, rows, width), hidden.reshape(subs, rows, width), gain, vec,
        scale, grads, expert_up, shared_up, expert_down, shared_down,
    )


TN = (((0,), (0,)), ((), ()))
SUB = 2


def outputs_kernel(tp, expert_width, shared_width, *refs):
    y_ref, x_ref, d_ref, h_ref, g_ref = refs[:5]
    middle_ref, dsum_ref, gate_ref, og_ref, gain_ref, vec_ref = refs[5:11]
    hidden_ref, grad_ref, sums_ref, rows_ref, ge_ref, gs_ref, de_ref, ds_ref = refs[11:19]
    (
        total_ref, own_ref, mine, other, diag_in, last_in, z_in, d_buf, h_buf, col_buf, ge_buf, gs_buf, de_buf, ds_buf,
        l_sem, c_send, c_recv, p_send, p_recv, z_send, z_recv, a_sem, a_send, a_recv,
        w_sem, col_sem, out_sem,
    ) = refs[19:]
    me, rank = place()
    greet(me, rank, tp)
    f32 = jnp.float32
    bf16 = jnp.bfloat16
    rows = total_ref.shape[0]
    cut = rows // SUB
    half = cut // 2
    near = rank // 2
    blocks = [3 * (1 - near), 2 - near, flipped(rank, 1), rank]
    pieces = range(tp * SUB)
    packs = [me, flipped(me, 2), flipped(me, 4), flipped(flipped(me, 2), 4)]
    low, high = pl.ds(0, half), pl.ds(half, half)

    def gather_z(block, right):
        way = 0 if right else 1
        spot = rows_ref.at[pl.ds(block * rows, rows)]
        return pltpu.make_async_remote_copy(
            src_ref=spot,
            dst_ref=spot,
            send_sem=a_send.at[way, block],
            recv_sem=a_recv.at[way, block],
            device_id=(me, rank + 1 if right else rank - 1),
            device_id_type=MESH,
        )

    def gather_step(step):
        @pl.when(rank >= step)
        def _():
            gather_z(rank - step, True).wait_recv()

            @pl.when(rank < tp - 1)
            def _():
                gather_z(rank - step, True).start()

        @pl.when(rank + step < tp)
        def _():
            gather_z(rank + step, False).wait_recv()

            @pl.when(rank > 0)
            def _():
                gather_z(rank + step, False).start()

    def spot_of(j):
        return blocks[j // SUB] * SUB + j % SUB

    def region(pack, j):
        return y_ref.at[pl.ds((pack * tp * SUB + spot_of(j)) * cut, cut)]

    def local(k, j):
        return pltpu.make_async_copy(region(packs[k], j), mine.at[k, j], l_sem.at[k, j])

    def core(k, j):
        return pltpu.make_async_remote_copy(
            src_ref=region(flipped(packs[k], 1), j),
            dst_ref=other.at[k, j],
            send_sem=c_send.at[k, j],
            recv_sem=c_recv.at[k, j],
            device_id=(flipped(me, 1), rank),
            device_id_type=MESH,
        )

    def across(bit, src, dst, slot, j):
        return pltpu.make_async_remote_copy(
            src_ref=src,
            dst_ref=dst,
            send_sem=p_send.at[slot, j],
            recv_sem=p_recv.at[slot, j],
            device_id=(flipped(me, bit), rank),
            device_id_type=MESH,
        )

    def diag_x(j):
        return across(2, mine.at[3, j, low], diag_in.at[j, 0], 0, j)

    def diag_y(j):
        return across(4, mine.at[3, j, high], diag_in.at[j, 1], 1, j)

    def direct_x(j):
        return across(2, mine.at[1, j, low], last_in.at[j, 0, low], 2, j)

    def direct_y(j):
        return across(4, mine.at[2, j, high], last_in.at[j, 1, high], 3, j)

    def summed_x(j):
        return across(2, mine.at[1, j, high], last_in.at[j, 0, high], 4, j)

    def summed_y(j):
        return across(4, mine.at[2, j, low], last_in.at[j, 1, low], 5, j)

    def along_z(j, right):
        way = 0 if right else 1
        spot = spot_of(j)
        return pltpu.make_async_remote_copy(
            src_ref=mine.at[0, j],
            dst_ref=z_in.at[way, spot],
            send_sem=z_send.at[way, spot],
            recv_sem=z_recv.at[way, spot],
            device_id=(me, rank + 1 if right else rank - 1),
            device_id_type=MESH,
        )

    def add(ref, spot, one):
        ref[spot] = (ref[spot].astype(f32) + one.astype(f32)).astype(ref.dtype)

    def first(j):
        for k in (3, 2, 1, 0):
            core(k, j).wait_recv()
            local(k, j).wait()
            add(mine, (k, j), other[k, j])
            if k == 3:
                diag_x(j).start()
                diag_y(j).start()
            if k == 2:
                direct_y(j).start()
            if k == 1:
                direct_x(j).start()

    def second(j):
        diag_x(j).wait_recv()
        add(mine, (2, j, low), diag_in[j, 0])
        summed_y(j).start()
        diag_y(j).wait_recv()
        add(mine, (1, j, high), diag_in[j, 1])
        summed_x(j).start()

    def third(j):
        block = blocks[j // SUB]
        spot = spot_of(j)
        direct_x(j).wait_recv()
        direct_y(j).wait_recv()
        summed_x(j).wait_recv()
        summed_y(j).wait_recv()
        total = mine[0, j].astype(f32) + last_in[j, 0].astype(f32) + last_in[j, 1].astype(f32)
        if j < (tp - 1) * SUB:
            mine[0, j] = total.astype(bf16)

            @pl.when((block > rank) & (rank > 0))
            def _():
                along_z(j, True).wait_recv()
                add(mine, (0, j), z_in[0, spot])

            @pl.when((block < rank) & (rank < tp - 1))
            def _():
                along_z(j, False).wait_recv()
                add(mine, (0, j), z_in[1, spot])

            @pl.when(block > rank)
            def _():
                along_z(j, True).start()

            @pl.when(block < rank)
            def _():
                along_z(j, False).start()
        else:
            own_rows = pl.ds(j % SUB * cut, cut)
            total_ref[own_rows] = total

            @pl.when(rank > 0)
            def _():
                along_z(j, True).wait_recv()
                total_ref[own_rows] += z_in[0, spot].astype(f32)

            @pl.when(rank < tp - 1)
            def _():
                along_z(j, False).wait_recv()
                total_ref[own_rows] += z_in[1, spot].astype(f32)

    span = col_buf.shape[2]
    steps = x_ref.shape[1] // span
    units = SHARED + shared_width

    def columns(n, slot, of_x):
        ref = x_ref if of_x else g_ref
        return pltpu.make_async_copy(
            ref.at[:, pl.ds(pl.multiple_of(n * span, span), span)],
            col_buf.at[slot],
            col_sem.at[slot],
        )

    def up_stores(n, slot):
        at = pl.ds(pl.multiple_of(n * span, span), span)
        return (
            pltpu.make_async_copy(ge_buf.at[slot], ge_ref.at[:, at], out_sem.at[0, slot]),
            pltpu.make_async_copy(gs_buf.at[slot], gs_ref.at[:, at], out_sem.at[1, slot]),
        )

    def down_stores(n, slot):
        at = pl.ds(pl.multiple_of(n * span, span), span)
        return (
            pltpu.make_async_copy(de_buf.at[slot], de_ref.at[:, at], out_sem.at[2, slot]),
            pltpu.make_async_copy(ds_buf.at[slot], ds_ref.at[n], out_sem.at[3, slot]),
        )

    def up_step(n, carry):
        slot = n % 2

        @pl.when(n + 1 < steps)
        def _():
            columns(n + 1, 1 - slot, True).start()

        @pl.when(n + 1 == steps)
        def _():
            columns(0, 1 - slot, False).start()

        columns(n, slot, True).wait()

        @pl.when(n >= 2)
        def _():
            for copy in up_stores(n - 2, slot):
                copy.wait()

        grads = lax.dot_general(col_buf[slot], d_buf[...], TN, preferred_element_type=f32)
        for part in range(2):
            base = part * UNIT
            ge_buf[slot, part] = grads[:, base : base + expert_width]
            gs_buf[slot, part] = grads[:, base + SHARED : base + units].astype(bf16)
        for copy in up_stores(n, slot):
            copy.start()
        return carry

    def down_step(n, carry):
        slot = n % 2

        @pl.when(n + 1 < steps)
        def _():
            columns(n + 1, 1 - slot, False).start()

        columns(n, slot, False).wait()

        @pl.when(n >= 2)
        def _():
            for copy in down_stores(n - 2, slot):
                copy.wait()

        grads = lax.dot_general(h_buf[...], col_buf[slot], TN, preferred_element_type=f32)
        de_buf[slot] = grads[:expert_width]
        ds_buf[slot] = grads[SHARED:units].astype(bf16)
        for copy in down_stores(n, slot):
            copy.start()
        return carry

    def norm_back():
        middle = middle_ref[...]
        gain, vec = gain_ref[...], vec_ref[...]
        inverse = lax.rsqrt(jnp.mean(middle * middle, axis=-1, keepdims=True) + epsilon)
        hat = middle * inverse
        normed = (hat * gain).astype(bf16).astype(f32)
        logit = jnp.sum(normed * vec, axis=-1, keepdims=True)
        gate_prob = 1.0 / (1.0 + jnp.exp(-logit))
        logit_grad = gate_ref[...] * gate_prob * (1.0 - gate_prob)
        d_normed = dsum_ref[...] + logit_grad * vec
        sums_ref[0:1] = jnp.sum(d_normed * hat, axis=0, keepdims=True)
        sums_ref[1:2] = jnp.sum(normed * logit_grad, axis=0, keepdims=True)
        d_hat = d_normed * gain
        mean = jnp.mean(d_hat * hat, axis=-1, keepdims=True)
        grad = og_ref[...].astype(f32) + inverse * (d_hat - hat * mean)
        grad_ref[...] = grad
        own_ref[...] = grad.astype(bf16)

    load_d = pltpu.make_async_copy(d_ref, d_buf, w_sem.at[0])
    load_h = pltpu.make_async_copy(h_ref, h_buf, w_sem.at[1])
    own = pltpu.make_async_copy(own_ref, rows_ref.at[pl.ds(rank * rows, rows)], a_sem)
    for j in pieces:
        for k in (3, 2, 1, 0):
            core(k, j).start()
            local(k, j).start()
    load_d.start()
    columns(0, 0, True).start()
    load_h.start()
    norm_back()
    own.start()
    own.wait()

    @pl.when(rank < tp - 1)
    def _():
        gather_z(rank, True).start()

    @pl.when(rank > 0)
    def _():
        gather_z(rank, False).start()

    first(0)
    first(1)
    first(2)
    load_d.wait()
    load_h.wait()
    for j in pieces:
        if j < len(pieces) // 2:
            lax.fori_loop(2 * j, 2 * j + 2, up_step, 0)
        else:
            later = j - len(pieces) // 2
            lax.fori_loop(2 * later, 2 * later + 2, down_step, 0)
        second(j)
        if j + 3 < len(pieces):
            first(j + 3)
        if j in (1, 3, 5):
            gather_step((j + 1) // 2)
        if j >= 2:
            third(j - 2)
    third(len(pieces) - 2)
    third(len(pieces) - 1)
    hidden_ref[...] = (middle_ref[...] + total_ref[...]).astype(bf16)

    for n in (steps - 2, steps - 1):
        for copy in up_stores(n, n % 2) + down_stores(n, n % 2):
            copy.wait()
    for j in pieces:
        for k in range(4):
            core(k, j).wait_send()
        for copy in (diag_x, diag_y, direct_x, direct_y, summed_x, summed_y):
            copy(j).wait_send()
        block = blocks[j // SUB]
        if j < (tp - 1) * SUB:

            @pl.when(block > rank)
            def _():
                along_z(j, True).wait_send()

            @pl.when(block < rank)
            def _():
                along_z(j, False).wait_send()

    for block in range(tp):

        @pl.when((block <= rank) & (rank < tp - 1))
        def _():
            gather_z(block, True).wait_send()

        @pl.when((block >= rank) & (rank > 0))
        def _():
            gather_z(block, False).wait_send()


def outputs(
    y, x, d, h, g, middle, d_normed, gate_grad, out_grad, gain, vec,
    fsdp, tp, expert_width, shared_width, collective_id,
):
    rows, width = middle.shape
    tokens = y.shape[0]
    span = width // fsdp
    cut = rows // SUB
    bf16 = jnp.bfloat16
    f32 = jnp.float32
    dma = pltpu.SemaphoreType.DMA
    anywhere = pl.BlockSpec(memory_space=pl.ANY)
    return pl.pallas_call(
        functools.partial(outputs_kernel, tp, expert_width, shared_width),
        out_shape=[
            jax.ShapeDtypeStruct((rows, width), bf16),
            jax.ShapeDtypeStruct((rows, width), f32),
            jax.ShapeDtypeStruct((2, width), f32),
            jax.ShapeDtypeStruct((rows * tp, width), bf16),
            jax.ShapeDtypeStruct((2, width, expert_width), f32),
            jax.ShapeDtypeStruct((2, width, shared_width), bf16),
            jax.ShapeDtypeStruct((expert_width, width), f32),
            jax.ShapeDtypeStruct((fsdp, shared_width, span), bf16),
        ],
        in_specs=[anywhere] * 5 + [pl.BlockSpec(memory_space=pltpu.VMEM)] * 6,
        out_specs=[pl.BlockSpec(memory_space=pltpu.VMEM)] * 3 + [anywhere] * 5,
        scratch_shapes=[
            pltpu.VMEM((rows, width), f32),
            pltpu.VMEM((rows, width), bf16),
            pltpu.VMEM((4, tp * SUB, cut, width), bf16),
            pltpu.VMEM((4, tp * SUB, cut, width), bf16),
            pltpu.VMEM((tp * SUB, 2, cut // 2, width), bf16),
            pltpu.VMEM((tp * SUB, 2, cut, width), bf16),
            pltpu.VMEM((2, tp * SUB, cut, width), bf16),
            pltpu.VMEM((tokens, 2 * UNIT), bf16),
            pltpu.VMEM((tokens, UNIT), bf16),
            pltpu.VMEM((2, tokens, span), bf16),
            pltpu.VMEM((2, 2, span, expert_width), f32),
            pltpu.VMEM((2, 2, span, shared_width), bf16),
            pltpu.VMEM((2, expert_width, span), f32),
            pltpu.VMEM((2, shared_width, span), bf16),
            dma((4, tp * SUB)), dma((4, tp * SUB)), dma((4, tp * SUB)),
            dma((6, tp * SUB)), dma((6, tp * SUB)),
            dma((2, tp * SUB)), dma((2, tp * SUB)), dma, dma((2, tp)), dma((2, tp)),
            dma((2,)), dma((2,)), dma((4, 2)),
        ],
        compiler_params=pltpu.CompilerParams(
            collective_id=collective_id, has_side_effects=True, vmem_limit_bytes=60 << 20
        ),
        name="outputs",
    )(y, x, d, h, g, middle, d_normed, gate_grad, out_grad, gain, vec)


def backward_kernel(fsdp, tp, heads, *refs):
    parts = 3
    d_ref, ho_ref, q_ref, k_ref, v_ref, lt_ref, cos_ref, sin_ref = refs[:8]
    seg_row_ref, seg_col_ref, normed_in, qkv_in, out_in = refs[8:13]
    gs_ref, ds_ref, hidden_ref, grad_ref, gain_ref, sums_ref = refs[13:19]
    refs = refs[19:]
    outs, refs = refs[:parts], refs[parts:]
    gs_out, ds_out, hidden_grad_ref, gains_ref = refs[:4]
    refs = refs[4:]
    mine, other, diag_in, last_in = (refs[i * parts : (i + 1) * parts] for i in range(4))
    (
        normed_ref, qkv_ref, out_ref, in_sem, dh_buf, dqkv_buf, gs_in, ds_in, dn_buf, z_in, v_send, v_in, w_send, w_in,
        c_send, c_recv, p_send, p_recv, s_sem, s_send, s_recv,
        f_send, f_recv, v_ssem, v_rsem, w_ssem, w_rsem,
    ) = refs[4 * parts :]
    me, rank = place()
    f32 = jnp.float32
    bf16 = jnp.bfloat16
    rows, width = hidden_ref.shape
    near = rank // 2
    blocks = [3 * (1 - near), 2 - near, flipped(rank, 1), rank]
    packs = [me, flipped(me, 2), flipped(me, 4), flipped(flipped(me, 2), 4)]
    every = range(parts)
    chunks = outs[0].shape[0]
    sizes = [ref.shape[1] for ref in outs]
    low = [pl.ds(0, size // 2) for size in sizes]
    high = [pl.ds(size // 2, size // 2) for size in sizes]

    def plane(bits):
        peer = me
        for one in (1, 2, 4):
            if bits & one:
                peer = flipped(peer, one)
        return peer

    def line(bits):
        peer = rank
        for one in (1, 2):
            if bits & one:
                peer = flipped(peer, one)
        return peer

    barrier = pltpu.get_barrier_semaphore()
    for bits in range(1, fsdp):
        pl.semaphore_signal(
            barrier, inc=1, device_id=(plane(bits), rank), device_id_type=MESH
        )
    for bits in range(1, tp):
        pl.semaphore_signal(barrier, inc=1, device_id=(me, line(bits)), device_id_type=MESH)
    pl.semaphore_wait(barrier, fsdp - 1 + tp - 1)

    def add(ref, spot, one):
        ref[spot] = (ref[spot].astype(f32) + one.astype(f32)).astype(ref.dtype)

    core_of, x_of, y_of = me % 2, (me // 2) % 2, me // 4

    def pack_of(bits):
        return (
            4 * ((y_of + bits // 4) % 2)
            + 2 * ((x_of + (bits // 2) % 2) % 2)
            + (core_of + bits % 2) % 2
        )

    def core(k, j, i):
        return pltpu.make_async_remote_copy(
            src_ref=mine[i].at[pack_of(2 * k + 1), j],
            dst_ref=other[i].at[k, j],
            send_sem=c_send.at[k, j, i],
            recv_sem=c_recv.at[k, j, i],
            device_id=(flipped(me, 1), rank),
            device_id_type=MESH,
        )

    def across(bit, src, dst, slot, j, i):
        return pltpu.make_async_remote_copy(
            src_ref=src,
            dst_ref=dst,
            send_sem=p_send.at[slot, j, i],
            recv_sem=p_recv.at[slot, j, i],
            device_id=(flipped(me, bit), rank),
            device_id_type=MESH,
        )

    def diag_x(j, i):
        return across(2, mine[i].at[packs[3], j, low[i]], diag_in[i].at[j, 0], 0, j, i)

    def diag_y(j, i):
        return across(4, mine[i].at[packs[3], j, high[i]], diag_in[i].at[j, 1], 1, j, i)

    def direct_x(j, i):
        return across(2, mine[i].at[packs[1], j, low[i]], last_in[i].at[j, 0, low[i]], 2, j, i)

    def direct_y(j, i):
        return across(4, mine[i].at[packs[2], j, high[i]], last_in[i].at[j, 1, high[i]], 3, j, i)

    def summed_x(j, i):
        return across(2, mine[i].at[packs[1], j, high[i]], last_in[i].at[j, 0, high[i]], 4, j, i)

    def summed_y(j, i):
        return across(4, mine[i].at[packs[2], j, low[i]], last_in[i].at[j, 1, low[i]], 5, j, i)

    def send_piece(bits, i):
        k = bits // 2

        @pl.when(bits % 2 == 1)
        def _():
            for j in range(chunks):
                core(k, j, i).start()

        @pl.when(bits % 2 == 0)
        def _():
            for j in range(chunks):
                core(k, j, i).wait_recv()
                add(mine[i], (pack_of(bits), j), other[i][k, j])

            @pl.when(k == 3)
            def _():
                for j in range(chunks):
                    diag_x(j, i).start()
                    diag_y(j, i).start()

            @pl.when(k == 2)
            def _():
                for j in range(chunks):
                    direct_y(j, i).start()

            @pl.when(k == 1)
            def _():
                for j in range(chunks):
                    direct_x(j, i).start()

    def second(j):
        for i in every:
            diag_x(j, i).wait_recv()
            add(mine[i], (packs[2], j, low[i]), diag_in[i][j, 0])
            summed_y(j, i).start()
            diag_y(j, i).wait_recv()
            add(mine[i], (packs[1], j, high[i]), diag_in[i][j, 1])
            summed_x(j, i).start()

    def third(j):
        for i in every:
            direct_x(j, i).wait_recv()
            direct_y(j, i).wait_recv()
            summed_x(j, i).wait_recv()
            summed_y(j, i).wait_recv()
            outs[i][j] = (
                mine[i][me, j].astype(f32)
                + last_in[i][j, 0].astype(f32)
                + last_in[i][j, 1].astype(f32)
            )

    span = ds_ref.shape[2]

    def shared_up(bits):
        at = pl.ds(pl.multiple_of(plane(bits) * span, span), span)
        return pltpu.make_async_remote_copy(
            src_ref=gs_ref.at[:, at],
            dst_ref=gs_in.at[me],
            send_sem=s_send.at[0, bits],
            recv_sem=s_recv.at[0, bits],
            device_id=(plane(bits), rank),
            device_id_type=MESH,
        )

    def shared_down(bits):
        return pltpu.make_async_remote_copy(
            src_ref=ds_ref.at[plane(bits)],
            dst_ref=ds_in.at[me],
            send_sem=s_send.at[1, bits],
            recv_sem=s_recv.at[1, bits],
            device_id=(plane(bits), rank),
            device_id_type=MESH,
        )

    own_up = pltpu.make_async_copy(
        gs_ref.at[:, pl.ds(pl.multiple_of(me * span, span), span)], gs_in.at[me], s_sem.at[0]
    )
    own_down = pltpu.make_async_copy(ds_ref.at[me], ds_in.at[me], s_sem.at[1])

    def front_z(j, right):
        way = 0 if right else 1
        block = blocks[j]
        return pltpu.make_async_remote_copy(
            src_ref=dn_buf.at[block],
            dst_ref=z_in.at[way, block],
            send_sem=f_send.at[way, block],
            recv_sem=f_recv.at[way, block],
            device_id=(me, rank + 1 if right else rank - 1),
            device_id_type=MESH,
        )

    def front(j):
        block = blocks[j]
        if j < tp - 1:

            @pl.when((block > rank) & (rank > 0))
            def _():
                front_z(j, True).wait_recv()
                add(dn_buf, (block,), z_in[0, block])

            @pl.when((block < rank) & (rank < tp - 1))
            def _():
                front_z(j, False).wait_recv()
                add(dn_buf, (block,), z_in[1, block])

            @pl.when(block > rank)
            def _():
                front_z(j, True).start()

            @pl.when(block < rank)
            def _():
                front_z(j, False).start()
        else:
            hidden_grad_ref[...] = dn_buf[block].astype(f32)

            @pl.when(rank > 0)
            def _():
                front_z(j, True).wait_recv()
                hidden_grad_ref[...] += z_in[0, block].astype(f32)

            @pl.when(rank < tp - 1)
            def _():
                front_z(j, False).wait_recv()
                hidden_grad_ref[...] += z_in[1, block].astype(f32)

    share = width // fsdp
    part = share // tp

    def gains_plane(bits):
        return pltpu.make_async_remote_copy(
            src_ref=v_send.at[plane(bits)],
            dst_ref=v_in.at[me],
            send_sem=v_ssem.at[bits],
            recv_sem=v_rsem.at[bits],
            device_id=(plane(bits), rank),
            device_id_type=MESH,
        )

    def gains_line(bits):
        return pltpu.make_async_remote_copy(
            src_ref=w_send.at[line(bits)],
            dst_ref=w_in.at[rank],
            send_sem=w_ssem.at[bits],
            recv_sem=w_rsem.at[bits],
            device_id=(me, line(bits)),
            device_id_type=MESH,
        )

    length = d_ref.shape[0]
    cut = width // fsdp
    size = heads * 128
    scale = 128 ** (-0.5)

    def out_piece(n, carry):
        bits = fsdp - 1 - n
        pack = pack_of(bits)
        at = pl.ds(pl.multiple_of(pack * cut, cut), cut)
        piece = lax.dot_general(d_ref[:, at], ho_ref[...], TN, preferred_element_type=f32)
        mine[1][pack] = piece.astype(bf16).reshape(chunks, cut // chunks, size)
        send_piece(bits, 1)
        return carry

    def qkv_piece(n, carry):
        bits = fsdp - 1 - n
        pack = pack_of(bits)
        at = pl.ds(pl.multiple_of(pack * cut, cut), cut)
        piece = lax.dot_general(normed_ref[:, at], dqkv_buf[...], TN, preferred_element_type=f32)
        mine[0][pack] = piece.astype(bf16).reshape(chunks, cut // chunks, 3 * size)
        send_piece(bits, 0)
        return carry

    def head_grads():
        total = jnp.zeros((length, size), f32)
        for owner in range(fsdp):
            total = total + lax.dot_general(
                d_ref[:, owner * cut : (owner + 1) * cut],
                out_ref[owner * size : (owner + 1) * size, :],
                NT,
                preferred_element_type=f32,
            )
        dh_buf[...] = total.astype(bf16)

    def unrotated(columns):
        return columns * cos_ref[...] - pltpu.roll(columns, 64, 1) * sin_ref[...]

    def attend_back(head):
        at = slice(head * 128, (head + 1) * 128)
        query, keys, values = q_ref[:, at], k_ref[:, at], v_ref[:, at]
        d_head = dh_buf[:, at]
        scores = lax.dot_general(query, keys, NT, preferred_element_type=f32) * scale
        line = lax.broadcasted_iota(jnp.int32, (length, length), 0)
        column = lax.broadcasted_iota(jnp.int32, (length, length), 1)
        allowed = (line >= column) & (seg_col_ref[...] == seg_row_ref[...])
        probs = jnp.exp(jnp.where(allowed, scores, -1e30) - lt_ref[:, head : head + 1])
        d_values = lax.dot_general(probs.astype(bf16), d_head, TN, preferred_element_type=f32)
        d_probs = lax.dot_general(d_head, values, NT, preferred_element_type=f32)
        delta = jnp.sum(
            d_head.astype(f32) * ho_ref[:, at].astype(f32), axis=-1, keepdims=True
        )
        d_scores = (probs * (d_probs - delta)).astype(bf16)
        d_query = jnp.dot(d_scores, keys, preferred_element_type=f32) * scale
        d_keys = lax.dot_general(d_scores, query, TN, preferred_element_type=f32) * scale
        for which, grad in enumerate((unrotated(d_query), unrotated(d_keys), d_values)):
            base = which * size + head * 128
            dqkv_buf[:, base : base + 128] = grad.astype(bf16)
            here = which * heads + head
            mine[2][0, 0, here : here + 1] = jnp.sum(grad, axis=0, keepdims=True)

    def row_grads(half):
        at = pl.ds(pl.multiple_of(half * 2 * rows, 2 * rows), 2 * rows)
        grads = lax.dot_general(dqkv_buf[at, :], qkv_ref[...], NT, preferred_element_type=f32)
        dn_buf[pl.ds(2 * half, 2)] = grads.astype(bf16).reshape(2, rows, width)

    ends = (rank == 0) | (rank == tp - 1)
    for bits in (6, 7, 2, 4):
        shared_up(bits).start()
        shared_down(bits).start()
    own_up.start()
    own_down.start()
    loads = [
        pltpu.make_async_copy(src, dst, in_sem.at[i])
        for i, (src, dst) in enumerate(
            ((out_in, out_ref), (qkv_in, qkv_ref), (normed_in, normed_ref))
        )
    ]
    for load in loads:
        load.start()
    lax.fori_loop(0, fsdp, out_piece, 0)
    loads[0].wait()
    head_grads()
    mine[2][...] = jnp.zeros_like(mine[2])
    for head in range(heads):
        attend_back(head)
    loads[1].wait()
    row_grads(1 - near)

    @pl.when(ends)
    def _():
        front(0)
        front(1)

    row_grads(near)
    for owner in range(1, fsdp):
        mine[2][owner] = mine[2][0]
    loads[2].wait()
    lax.fori_loop(0, fsdp, qkv_piece, 0)
    for n in range(fsdp):
        send_piece(jnp.int32(fsdp - 1 - n), 2)

    @pl.when(jnp.logical_not(ends))
    def _():
        front(0)

    second(0)

    @pl.when(jnp.logical_not(ends))
    def _():
        front(1)

    second(1)
    for bits in (3, 5, 1):
        shared_up(bits).start()
        shared_down(bits).start()
    front(2)
    front(3)
    d_normed = hidden_grad_ref[...]
    hidden = hidden_ref[...].astype(f32)
    inverse = lax.rsqrt(jnp.mean(hidden * hidden, axis=-1, keepdims=True) + epsilon)
    hat = hidden * inverse
    v_send[...] = jnp.zeros_like(v_send)
    attn_gain = jnp.sum(d_normed * hat, axis=0, keepdims=True)
    for owner in range(fsdp):
        at = slice(owner * share, (owner + 1) * share)
        v_send[owner, 0:1] = attn_gain[:, at]
        v_send[owner, 1:3] = sums_ref[:, at]
    for bits in range(1, fsdp):
        gains_plane(bits).start()
    d_hat = d_normed * gain_ref[...]
    mean = jnp.mean(d_hat * hat, axis=-1, keepdims=True)
    hidden_grad_ref[...] = grad_ref[...] + inverse * (d_hat - hat * mean)
    third(0)
    total = v_send[me]
    for bits in range(1, fsdp):
        gains_plane(bits).wait_recv()
        total = total + v_in[plane(bits)]
    w_send[...] = jnp.zeros_like(w_send)
    for owner in range(tp):
        w_send[owner, :, :part] = total[:, owner * part : (owner + 1) * part]
    for bits in range(1, tp):
        gains_line(bits).start()
    third(1)
    own_up.wait()
    own_down.wait()
    for bits in range(1, fsdp):
        shared_up(bits).wait_recv()
        shared_down(bits).wait_recv()
    units = gs_in.shape[3]
    for owner in range(fsdp):
        at = slice(owner * units, (owner + 1) * units)
        gs_out[:, :, at] = gs_in[owner].astype(f32)
        ds_out[at] = ds_in[owner].astype(f32)
    total = w_send[rank]
    for bits in range(1, tp):
        gains_line(bits).wait_recv()
        total = total + w_in[line(bits)]
    gains_ref[...] = total

    for j in range(chunks):
        for i in every:
            for k in range(4):
                core(k, j, i).wait_send()
            for copy in (diag_x, diag_y, direct_x, direct_y, summed_x, summed_y):
                copy(j, i).wait_send()
    for bits in range(1, fsdp):
        shared_up(bits).wait_send()
        shared_down(bits).wait_send()
        gains_plane(bits).wait_send()
    for bits in range(1, tp):
        gains_line(bits).wait_send()
    for j in range(tp - 1):
        block = blocks[j]

        @pl.when(block > rank)
        def _():
            front_z(j, True).wait_send()

        @pl.when(block < rank)
        def _():
            front_z(j, False).wait_send()


def backward(
    d_rows, heads_out, query, keys, values, log_total, cos, sin, segments, normed, qkv, out,
    shared_up, shared_down, hidden, grad, gain, sums, fsdp, tp, heads, number,
):
    chunks = 2
    rows, width = hidden.shape
    length = rows * tp
    units = shared_up.shape[2]
    span = shared_down.shape[2]
    size = heads * 128
    bf16 = jnp.bfloat16
    f32 = jnp.float32
    shapes = [(width // (fsdp * chunks), 3 * size, bf16), (span // chunks, size, bf16), (16, 128, f32)]
    scratch = [pltpu.VMEM((fsdp, chunks, count, w), kind) for count, w, kind in shapes]
    scratch += [pltpu.VMEM((4, chunks, count, w), kind) for count, w, kind in shapes]
    scratch += [pltpu.VMEM((chunks, 2, count // 2, w), kind) for count, w, kind in shapes]
    scratch += [pltpu.VMEM((chunks, 2, count, w), kind) for count, w, kind in shapes]
    dma = pltpu.SemaphoreType.DMA
    anywhere = pl.BlockSpec(memory_space=pl.ANY)
    vmem = pl.BlockSpec(memory_space=pltpu.VMEM)
    out_shape = [jax.ShapeDtypeStruct((chunks, count, w), f32) for count, w, _ in shapes]
    out_shape += [
        jax.ShapeDtypeStruct((2, span, fsdp * units), f32),
        jax.ShapeDtypeStruct((fsdp * units, span), f32),
        jax.ShapeDtypeStruct((rows, width), f32),
        jax.ShapeDtypeStruct((8, 128), f32),
    ]
    return pl.pallas_call(
        functools.partial(backward_kernel, fsdp, tp, heads),
        out_shape=out_shape,
        in_specs=[vmem] * 10 + [anywhere] * 5 + [vmem] * 4,
        out_specs=[vmem] * len(out_shape),
        scratch_shapes=scratch
        + [
            pltpu.VMEM(normed.shape, bf16),
            pltpu.VMEM(qkv.shape, bf16),
            pltpu.VMEM(out.shape, bf16),
            dma((3,)),
            pltpu.VMEM((length, size), bf16),
            pltpu.VMEM((length, 3 * size), bf16),
            pltpu.VMEM((fsdp, 2, span, units), shared_up.dtype),
            pltpu.VMEM((fsdp, units, span), shared_down.dtype),
            pltpu.VMEM((tp, rows, width), bf16),
            pltpu.VMEM((2, tp, rows, width), bf16),
            pltpu.VMEM((fsdp, 8, width // fsdp), f32),
            pltpu.VMEM((fsdp, 8, width // fsdp), f32),
            pltpu.VMEM((tp, 8, 128), f32),
            pltpu.VMEM((tp, 8, 128), f32),
            dma((4, chunks, 3)), dma((4, chunks, 3)),
            dma((6, chunks, 3)), dma((6, chunks, 3)),
            dma((2,)), dma((2, fsdp)), dma((2, fsdp)),
            dma((2, tp)), dma((2, tp)),
            dma((fsdp,)), dma((fsdp,)), dma((tp,)), dma((tp,)),
        ],
        compiler_params=pltpu.CompilerParams(
            collective_id=number, has_side_effects=True, vmem_limit_bytes=61 << 20
        ),
        name="backward",
    )(
        d_rows, heads_out, query, keys, values, log_total, cos, sin, segments.reshape(1, -1),
        segments.reshape(-1, 1), normed, qkv, out, shared_up, shared_down, hidden, grad, gain, sums,
    )


def attend_kernel(tp, heads, halved, *refs):
    parts = len(halved)
    hidden_ref, gain_ref, grad_ref, seg_row_ref, seg_col_ref, cos_ref, sin_ref = refs[:7]
    pieces, refs = refs[7 : 7 + parts], refs[7 + parts :]
    rows_out, grads_ref, q_ref, k_ref, v_ref, lt_ref, heads_ref, part_ref = refs[:8]
    fulls_out, refs = refs[8 : 8 + parts], refs[8 + parts :]
    rows_ref, fulls, refs = refs[0], refs[1 : 1 + parts], refs[1 + parts :]
    (
        l_sem, e_sem, z_send, z_recv, g_send, g_recv, p_send, p_recv, gp_send, gp_recv,
    ) = refs
    me, rank = place()
    f32 = jnp.float32
    bf16 = jnp.bfloat16
    rows, width = hidden_ref.shape
    length = rows * tp

    greet(me, rank, tp)

    def along_z(spot, sends, recvs, block, to_right):
        way = 0 if to_right else 1
        return pltpu.make_async_remote_copy(
            src_ref=spot,
            dst_ref=spot,
            send_sem=sends.at[way, block],
            recv_sem=recvs.at[way, block],
            device_id=(me, rank + 1 if to_right else rank - 1),
            device_id_type=MESH,
        )

    def row_z(block, to_right):
        spot = rows_ref.at[pl.ds(block * rows, rows)]
        return along_z(spot, z_send, z_recv, block, to_right)

    def grad_z(block, to_right):
        return along_z(grad_region(me, block), g_send, g_recv, block, to_right)

    def z_start(copy):
        @pl.when(rank < tp - 1)
        def _():
            copy(rank, True).start()

        @pl.when(rank > 0)
        def _():
            copy(rank, False).start()

    def z_step(copy, step, then=None):
        @pl.when(rank >= step)
        def _():
            copy(rank - step, True).wait_recv()

            @pl.when(rank < tp - 1)
            def _():
                copy(rank - step, True).start()

            if then is not None:
                then(rank - step)

        @pl.when(rank + step < tp)
        def _():
            copy(rank + step, False).wait_recv()

            @pl.when(rank > 0)
            def _():
                copy(rank + step, False).start()

            if then is not None:
                then(rank + step)

    def z_end(copy):
        for block in range(tp):

            @pl.when((block <= rank) & (rank < tp - 1))
            def _():
                copy(block, True).wait_send()

            @pl.when((block >= rank) & (rank > 0))
            def _():
                copy(block, False).wait_send()

    def region(i, owner_bits, start=0, count=None):
        size = pieces[i].shape[0]
        count = size if count is None else count
        return fulls[i].at[pl.ds(plane_peer(me, owner_bits) * size + start, count)]

    def across(i, bit, owner_bits, slot, start=0, count=None):
        spot = region(i, owner_bits, start, count)
        return pltpu.make_async_remote_copy(
            src_ref=pieces[i] if owner_bits == 0 else spot,
            dst_ref=spot,
            send_sem=p_send.at[slot, i],
            recv_sem=p_recv.at[slot, i],
            device_id=(flipped(me, bit), rank),
            device_id_type=MESH,
        )

    def to_core(q, i):
        return across(i, 1, 2 * q, q)

    def own_x(i):
        return across(i, 2, 0, 4)

    def own_y(i):
        return across(i, 4, 0, 5)

    def x_to_y(i):
        size = pieces[i].shape[0]
        return across(i, 4, 2, 6, 0, size // 2 if halved[i] else size)

    def y_to_x(i):
        size = pieces[i].shape[0]
        return across(i, 2, 4, 7, size // 2, size // 2)

    def local(i):
        return pltpu.make_async_copy(pieces[i], region(i, 0), l_sem.at[i])

    def export(i):
        return pltpu.make_async_copy(fulls[i], fulls_out[i], e_sem.at[i])

    def forward(i):
        own_x(i).wait_recv()
        x_to_y(i).start()
        to_core(1, i).start()
        own_y(i).wait_recv()
        if halved[i]:
            y_to_x(i).start()
        to_core(2, i).start()

    def finish(i):
        x_to_y(i).wait_recv()
        if halved[i]:
            y_to_x(i).wait_recv()
        to_core(3, i).start()

    def arrived(i):
        local(i).wait()
        for q in range(4):
            to_core(q, i).wait_recv()
        export(i).start()

    order = [rank]
    for bit in (1, 2):
        order = order + [flipped(one, bit) for one in order]

    def grad_region(pack, block, start=0, count=None):
        count = rows if count is None else count
        return grads_ref.at[pl.ds(pack * length + block * rows + start, count)]

    def grad_across(bit, pack_bits, block, slot, start=0, count=None):
        spot = grad_region(plane_peer(me, pack_bits), block, start, count)
        return pltpu.make_async_remote_copy(
            src_ref=spot,
            dst_ref=spot,
            send_sem=gp_send.at[slot, block],
            recv_sem=gp_recv.at[slot, block],
            device_id=(flipped(me, bit), rank),
            device_id_type=MESH,
        )

    def grad_core(q, block):
        return grad_across(1, 2 * q, block, q)

    def grad_x(block):
        return grad_across(2, 0, block, 4)

    def grad_y(block):
        return grad_across(4, 0, block, 5)

    def grad_x_to_y(block):
        return grad_across(4, 2, block, 6, 0, rows // 2)

    def grad_y_to_x(block):
        return grad_across(2, 4, block, 7, rows // 2, rows // 2)

    def grad_plane(block):
        grad_x(block).start()
        grad_y(block).start()
        grad_core(0, block).start()

    def grad_forward(block):
        grad_x(block).wait_recv()
        grad_x_to_y(block).start()
        grad_core(1, block).start()
        grad_y(block).wait_recv()
        grad_y_to_x(block).start()
        grad_core(2, block).start()

    def grad_finish(block):
        grad_x_to_y(block).wait_recv()
        grad_y_to_x(block).wait_recv()
        grad_core(3, block).start()

    def project(which):
        at = slice(which * heads * 128, (which + 1) * heads * 128)
        return jnp.dot(rows_ref[...], fulls[0][:, at], preferred_element_type=f32)

    def bias(which, head):
        line = which * heads + head
        size = pieces[3].shape[0]
        share = 128 // 8
        return jnp.concatenate(
            [fulls[3][owner * size + line : owner * size + line + 1, :share] for owner in range(8)],
            axis=1,
        )

    def rotated(columns):
        return columns * cos_ref[...] + pltpu.roll(columns, 64, 1) * sin_ref[...]

    def make_heads():
        for which, ref in ((0, q_ref), (1, k_ref), (2, v_ref)):
            all_heads = project(which)
            for head in range(heads):
                at = slice(head * 128, (head + 1) * 128)
                one = all_heads[:, at] + bias(which, head)
                if which < 2:
                    one = rotated(one)
                ref[:, at] = one.astype(bf16)

    def attend(head):
        at = slice(head * 128, (head + 1) * 128)
        scores = lax.dot_general(q_ref[:, at], k_ref[:, at], NT, preferred_element_type=f32)
        line = lax.broadcasted_iota(jnp.int32, (length, length), 0)
        column = lax.broadcasted_iota(jnp.int32, (length, length), 1)
        allowed = (line >= column) & (seg_col_ref[...] == seg_row_ref[...])
        scores = jnp.where(allowed, scores * 128 ** (-0.5), -1e30)
        peak = jnp.max(scores, axis=-1, keepdims=True)
        log_total = peak + jnp.log(jnp.sum(jnp.exp(scores - peak), axis=-1, keepdims=True))
        probs = jnp.exp(scores - log_total).astype(bf16)
        lane = lax.broadcasted_iota(jnp.int32, (length, 128), 1)
        before = jnp.zeros((length, 128), f32) if head == 0 else lt_ref[...]
        lt_ref[...] = jnp.where(lane == head, log_total, before)
        heads_ref[:, at] = jnp.dot(probs, v_ref[:, at], preferred_element_type=f32).astype(bf16)

    def project_out():
        size = pieces[1].shape[0]
        share = width // 8
        for owner in range(8):
            part_ref[:, owner * share : (owner + 1) * share] = jnp.dot(
                heads_ref[...],
                fulls[1][owner * size : (owner + 1) * size, :],
                preferred_element_type=f32,
            ).astype(bf16)

    for i in range(parts):
        own_x(i).start()
        own_y(i).start()
        to_core(0, i).start()
    hidden = hidden_ref[...].astype(f32)
    inverse = lax.rsqrt(jnp.mean(hidden * hidden, axis=-1, keepdims=True) + epsilon)
    own_rows = pl.ds(pl.multiple_of(rank * rows, rows), rows)
    rows_ref[own_rows, :] = (hidden * inverse * gain_ref[...]).astype(bf16)
    z_start(row_z)
    own_grad = pltpu.make_async_copy(grad_ref, grad_region(me, rank), l_sem.at[parts])
    own_grad.start()
    for i in range(parts):
        local(i).start()
    own_grad.wait()
    grad_plane(rank)
    z_step(row_z, 1)
    forward(0)
    z_step(row_z, 2)
    z_start(grad_z)
    for i in range(1, parts):
        forward(i)
    finish(0)
    z_step(row_z, 3)
    rows_export = pltpu.make_async_copy(rows_ref, rows_out, e_sem.at[parts])
    rows_export.start()
    for i in range(1, parts):
        finish(i)
    grad_forward(order[0])
    z_step(grad_z, 1, grad_plane)
    for i in range(parts):
        arrived(i)
    make_heads()
    grad_finish(order[0])
    z_step(grad_z, 2, grad_plane)
    attend(0)
    attend(1)
    grad_forward(order[1])
    z_step(grad_z, 3, grad_plane)
    for head in range(2, heads):
        attend(head)
    grad_finish(order[1])
    grad_forward(order[2])
    project_out()
    grad_finish(order[2])
    grad_forward(order[3])
    grad_finish(order[3])
    for block in order:
        for q in range(4):
            grad_core(q, block).wait_recv()

    rows_export.wait()
    for i in range(parts):
        export(i).wait()
        for q in range(4):
            to_core(q, i).wait_send()
        own_x(i).wait_send()
        own_y(i).wait_send()
        x_to_y(i).wait_send()
        if halved[i]:
            y_to_x(i).wait_send()
    for block in order:
        for q in range(4):
            grad_core(q, block).wait_send()
        for copy in (grad_x, grad_y, grad_x_to_y, grad_y_to_x):
            copy(block).wait_send()
    z_end(row_z)
    z_end(grad_z)


def attend_pack(hidden, gain, grad, segments, cos, sin, pieces, fsdp, tp, heads, number):
    rows, width = hidden.shape
    length = rows * tp
    parts = len(pieces)
    halved = [one.shape[0] >= 32 for one in pieces]
    bf16 = jnp.bfloat16
    f32 = jnp.float32
    dma = pltpu.SemaphoreType.DMA
    anywhere = pl.BlockSpec(memory_space=pl.ANY)
    vmem = pl.BlockSpec(memory_space=pltpu.VMEM)
    fulls = [(one.shape[0] * fsdp, one.shape[1]) for one in pieces]
    of_heads = jax.ShapeDtypeStruct((length, heads * 128), bf16)
    return pl.pallas_call(
        functools.partial(attend_kernel, tp, heads, halved),
        out_shape=[
            jax.ShapeDtypeStruct((length, width), bf16),
            jax.ShapeDtypeStruct((length * fsdp, width), bf16),
            of_heads,
            of_heads,
            of_heads,
            jax.ShapeDtypeStruct((length, 128), f32),
            of_heads,
            jax.ShapeDtypeStruct((length, width), bf16),
        ]
        + [jax.ShapeDtypeStruct(shape, one.dtype) for shape, one in zip(fulls, pieces)],
        in_specs=[vmem] * 7 + [anywhere] * parts,
        out_specs=[anywhere, anywhere] + [vmem] * 6 + [anywhere] * parts,
        scratch_shapes=[pltpu.VMEM((length, width), bf16)]
        + [pltpu.VMEM(shape, one.dtype) for shape, one in zip(fulls, pieces)]
        + [
            dma((parts + 1,)), dma((parts + 1,)),
            dma((2, tp)), dma((2, tp)), dma((2, tp)), dma((2, tp)),
            dma((8, parts)), dma((8, parts)), dma((8, tp)), dma((8, tp)),
        ],
        compiler_params=pltpu.CompilerParams(
            collective_id=number, has_side_effects=True, vmem_limit_bytes=48 << 20
        ),
        name="attend",
    )(
        hidden, gain, grad, segments.reshape(1, -1), segments.reshape(-1, 1), cos, sin,
        *pieces,
    )


def dense_plan(
    hidden_in,
    out_grad,
    segment_ids,
    expert_ids,
    route_weights,
    attn_gain,
    ffn_gain,
    qkv_weight,
    qkv_bias,
    out_weight,
    shared_gate_up,
    shared_down,
    shared_gate_vec,
    expert_gate_up,
    expert_down,
):
    every = ("fsdp", "tp")
    tp_rank = lax.axis_index("tp")
    experts = lax.axis_size("fsdp")
    packs = experts
    length = segment_ids.shape[1]
    own_rows = hidden_in.shape[0]
    own_units = shared_gate_up.shape[0]
    model_width = hidden_in.shape[1]
    bf16 = jnp.bfloat16
    f32 = jnp.float32

    expert_up = expert_gate_up[0]
    expert_dn = expert_down[0]
    expert_width = expert_up.shape[2]
    shared_width = shared_gate_up.shape[2] // experts

    chosen = expert_ids[:, :, None] == jnp.arange(experts, dtype=jnp.int32)
    table = jnp.sum(jnp.where(chosen, route_weights[:, :, None], 0.0), axis=1)
    local_heads = qkv_weight.shape[2]
    head_dim = qkv_weight.shape[3]
    cos_table, sin_table = rope_tables(length, head_dim)
    segments = segment_ids[0]
    hidden_float = hidden_in.astype(f32)
    attn_inverse = inverse_rms(hidden_float)
    bias_rows = 3 * local_heads
    bias_columns = qkv_bias.shape[2]
    bias_piece = jnp.pad(
        qkv_bias.reshape(bias_rows, bias_columns), ((0, 16 - bias_rows), (0, 128 - bias_columns))
    )
    heads_width = local_heads * head_dim
    up_pieces = shared_gate_up.reshape(own_units, 2, experts, shared_width).transpose(2, 1, 0, 3)
    cos_two = jnp.concatenate([cos_table[:, 0], cos_table[:, 0]], axis=1)
    sin_two = jnp.concatenate([-sin_table[:, 0], sin_table[:, 0]], axis=1)
    (
        normed_one,
        grad_all,
        query,
        keys,
        values,
        log_total,
        heads_out,
        projected,
        qkv_flat,
        out_pieces,
        tables,
        bias_pieces,
    ) = attend_pack(
        hidden_in,
        attn_gain[None],
        out_grad,
        segments,
        cos_two,
        sin_two,
        [qkv_weight.reshape(-1, 3 * heads_width), out_weight, table.T, bias_piece],
        experts,
        lax.axis_size("tp"),
        local_heads,
        4,
    )
    expert_scale = lax.dynamic_index_in_dim(
        tables.reshape(packs, experts, length), lax.axis_index("fsdp"), axis=1, keepdims=False
    ).reshape(-1)
    scales = expert_scale.reshape(packs, lax.axis_size("tp"), 2, own_rows // 2)
    scales = scales.transpose(0, 2, 1, 3).reshape(packs, 2, 1, length // 2)
    middle, normed_all, _, d_all, hidden_all, token_part, d_normed_two, lines = ffn(
        projected,
        hidden_in,
        ffn_gain[None],
        shared_gate_vec[None],
        scales,
        grad_all,
        expert_up.transpose(1, 0, 2),
        up_pieces,
        expert_dn,
        shared_down.reshape(experts, shared_width, -1),
        experts,
        lax.axis_size("tp"),
        1,
    )
    tokens = token_part.shape[0]
    middle = middle.reshape(own_rows, model_width)
    normed_all = normed_all.reshape(tokens, model_width)
    d_all = d_all.reshape(tokens, -1)
    hidden_all = hidden_all.reshape(tokens, -1)
    d_normed_two = d_normed_two.reshape(own_rows, model_width)
    lines = lax.dynamic_slice_in_dim(lines, tp_rank * (own_rows // 2), own_rows // 2, axis=2)
    extra_sum = lines.transpose(1, 0, 2).reshape(16, own_rows)
    own_start = tp_rank * own_rows
    ids_own = lax.dynamic_slice_in_dim(expert_ids, own_start, own_rows)
    picked = ids_own[:, :, None] == jnp.arange(experts, dtype=jnp.int32)
    route_grad = jnp.sum(jnp.where(picked, extra_sum[:experts].T[:, None, :], 0.0), axis=-1)
    gate_grad = extra_sum[experts]
    (
        hidden_out,
        middle_grad,
        norm_sums,
        d_rows,
        g_expert_up,
        g_shared_up,
        g_expert_down,
        g_shared_down,
    ) = outputs(
        token_part,
        normed_all,
        d_all,
        hidden_all,
        grad_all,
        middle,
        d_normed_two,
        gate_grad[:, None],
        out_grad,
        ffn_gain[None],
        shared_gate_vec[None],
        experts,
        lax.axis_size("tp"),
        expert_width,
        shared_width,
        2,
    )
    g_qkv, g_out, g_bias, g_shared_up, g_shared_down, hidden_grad, gains = backward(
        d_rows,
        heads_out,
        query,
        keys,
        values,
        log_total,
        cos_two,
        sin_two,
        segments,
        normed_one,
        qkv_flat,
        out_pieces,
        g_shared_up,
        g_shared_down,
        hidden_in,
        middle_grad,
        attn_gain[None],
        norm_sums,
        experts,
        lax.axis_size("tp"),
        local_heads,
        3,
    )
    share = model_width // (experts * lax.axis_size("tp"))
    g_bias = lax.dynamic_slice_in_dim(
        g_bias.reshape(32, 128)[:bias_rows], lax.axis_index("fsdp") * bias_columns, bias_columns, 1
    )
    return (
        hidden_out,
        hidden_grad,
        route_grad,
        gains[0, :share],
        gains[1, :share],
        g_qkv.reshape(-1, 3, local_heads, head_dim),
        g_bias.reshape(qkv_bias.shape),
        g_out.reshape(out_weight.shape[::-1]).T,
        g_shared_up.transpose(1, 0, 2),
        g_shared_down,
        gains[2, :share],
        g_expert_up.transpose(1, 0, 2)[None],
        g_expert_down[None],
    )


def on_device(*arrays):
    if lax.axis_size("fsdp") == 8 and lax.axis_size("tp") == 4 and arrays[3].shape[1] >= 3:
        return dense_plan(*arrays)
    return routed_plan(*arrays)


def solution(mesh):
    placed = (
        P(("fsdp", "tp"), None),
        P(("fsdp", "tp"), None),
        P("fsdp", None),
        P("fsdp", None),
        P("fsdp", None),
        P(),
        P(),
        P("fsdp", None, "tp", None),
        P(None, "tp", "fsdp"),
        P("tp", "fsdp"),
        P("fsdp", None, "tp"),
        P("tp", "fsdp"),
        P(),
        P("fsdp", None, None, "tp"),
        P("fsdp", "tp", None),
    )
    return jax.shard_map(
        on_device,
        mesh=mesh,
        in_specs=placed,
        out_specs=(
            P(("fsdp", "tp"), None),
            P(("fsdp", "tp"), None),
            P(("fsdp", "tp"), None),
            P(("fsdp", "tp")),
            P(("fsdp", "tp")),
            P("fsdp", None, "tp", None),
            P(None, "tp", "fsdp"),
            P("tp", "fsdp"),
            P("fsdp", None, "tp"),
            P("tp", "fsdp"),
            P(("fsdp", "tp")),
            P("fsdp", None, None, "tp"),
            P("fsdp", "tp", None),
        ),
        check_vma=False,
    )
```
